32 devices in a mesh: seq: 32 (over z, y, x, core).
Axes of the slice: x: 2, y: 2, z: 4, core: 2. Of those that a mesh axis runs over, the one named last changes fastest.
Arguments:
- tokens: bfloat16 [32768, 1024], P('seq'), may hold values from -6 to 6
- norm_gain: bfloat16 [1024], P('seq'), may hold values from 0.5 to 1.5
- query_weight: bfloat16 [1024, 512], P('seq'), may hold values from -0.1875 to 0.1875
- key_weight: bfloat16 [1024, 512], P('seq'), may hold values from -0.1875 to 0.1875
- value_weight: bfloat16 [1024, 1024], P('seq'), may hold values from -0.1875 to 0.1875
- gate_weight: bfloat16 [1024, 1024], P('seq'), may hold values from -0.1875 to 0.1875
- rank_down: bfloat16 [1024, 16], P('seq'), may hold values from -0.1875 to 0.1875
- rank_up: bfloat16 [16, 512], P(None, 'seq'), may hold values from -1.5 to 1.5
- gate_bias: bfloat16 [512], P('seq'), may hold values from 1 to 12
- head_gain: bfloat16 [1024], P('seq'), may hold values from 0.5 to 1.5
- out_weight: bfloat16 [1024, 1024], P('seq'), may hold values from -0.1875 to 0.1875
- ffn_gain: bfloat16 [1024], P('seq'), may hold values from 0.5 to 1.5
- ffn_gate: bfloat16 [1024, 2816], P('seq'), may hold values from -0.1875 to 0.1875
- ffn_up: bfloat16 [1024, 2816], P('seq'), may hold values from -0.1875 to 0.1875
- ffn_down: bfloat16 [2816, 1024], P('seq'), may hold values from -0.109375 to 0.109375
- cotangent: bfloat16 [32768, 1024], P('seq'), may hold values from -6 to 6
Outputs:
- block_output: float32 [32768, 1024], P('seq')
- tokens_grad: float32 [32768, 1024], P('seq')
- norm_gain_grad: float32 [1024], P('seq')
- query_grad: float32 [1024, 512], P('seq')
- key_grad: float32 [1024, 512], P('seq')
- value_grad: float32 [1024, 1024], P('seq')
- gate_grad: float32 [1024, 1024], P('seq')
- rank_down_grad: float32 [1024, 16], P('seq')
- rank_up_grad: float32 [16, 512], P(None, 'seq')
- gate_bias_grad: float32 [512], P('seq')
- head_gain_grad: float32 [1024], P('seq')
- out_grad: float32 [1024, 1024], P('seq')
- ffn_gain_grad: float32 [1024], P('seq')
- ffn_gate_grad: float32 [1024, 2816], P('seq')
- ffn_up_grad: float32 [1024, 2816], P('seq')
- ffn_down_grad: float32 [2816, 1024], P('seq')
The draws below stay inside these ranges and needn't reach their ends.
All inputs are finite; a program needn't handle non-finite values.
Results may differ from the reference program's by a relative error of at most 0.038.
Values may be sent and summed in bfloat16 or wider, within the bound.
A program may use at most 384 MiB of HBM per device.

```python
import jax
import jax.numpy as jnp
from jax import lax

D = 1024
HEADS = 4
HK = 128
HV = 256
FF = 2816
RANK = 16
GROUP = 64
SEQS = 1
TOKENS = 32768
KEYS = 512
VALS = 1024


def block_levels(own_key, shape, pieces, least, high):
    factor_of, own = 1.0, jax.random.fold_in(own_key, 6)
    for position, blocks in pieces:
        draws = jnp.exp(jax.random.uniform(jax.random.fold_in(own, position), (blocks,), jnp.float32, least / len(pieces), high / len(pieces)))
        factor_of = factor_of * jnp.repeat(draws, shape[position] // blocks).reshape([-1 if axis == position else 1 for axis in range(len(shape))])
    return factor_of


def normal_values(own_key, dims, scale, limit, shards=(), held_as=jnp.bfloat16):
    drawn = scale * jax.random.normal(own_key, dims, jnp.float32)
    if shards:
        drawn = drawn * block_levels(own_key, dims, shards, -0.22, 0.18)
    return jnp.clip(drawn, -limit, limit).astype(held_as)


def setup_inputs(seed: int = 0) -> dict:
    key_of = jax.random.split(jax.random.key(seed), 17)
    tokens = normal_values(key_of[0], (TOKENS, D), 1.0, 6.0, ((0, 32),))
    norm_gain = jnp.clip(1.0 + 0.1 * jax.random.normal(key_of[1], (D,), jnp.float32), 0.5, 1.5).astype(jnp.bfloat16)
    query_weight = normal_values(key_of[2], (D, KEYS), D ** -0.5, 0.1875, ((0, 32),))
    key_weight = normal_values(key_of[3], (D, KEYS), D ** -0.5, 0.1875, ((0, 32),))
    value_weight = normal_values(key_of[4], (D, VALS), D ** -0.5, 0.1875, ((0, 32),))
    gate_weight = normal_values(key_of[5], (D, VALS), D ** -0.5, 0.1875, ((0, 32),))
    rank_down = normal_values(key_of[6], (D, RANK), D ** -0.5, 0.1875, ((0, 32),))
    rank_up = normal_values(key_of[7], (RANK, KEYS), RANK ** -0.5, 1.5, ((1, 32),))
    gate_bias = jnp.clip(1.0 + 11.0 * jax.random.uniform(key_of[8], (KEYS,), jnp.float32) ** block_levels(key_of[8], (KEYS,), ((0, 32),), -0.2, 0.2), 1.0, 12.0).astype(jnp.bfloat16)
    head_gain = jnp.clip(1.0 + 0.1 * jax.random.normal(key_of[9], (VALS,), jnp.float32), 0.5, 1.5).astype(jnp.bfloat16)
    out_weight = normal_values(key_of[10], (VALS, D), VALS ** -0.5, 0.1875, ((0, 32),))
    ffn_gain = jnp.clip(1.0 + 0.1 * jax.random.normal(key_of[11], (D,), jnp.float32), 0.5, 1.5).astype(jnp.bfloat16)
    ffn_gate = normal_values(key_of[12], (D, FF), D ** -0.5, 0.1875, ((0, 32),))
    ffn_up = normal_values(key_of[13], (D, FF), D ** -0.5, 0.1875, ((0, 32),))
    ffn_down = normal_values(key_of[14], (FF, D), FF ** -0.5, 0.109375, ((0, 32),))
    cotangent = normal_values(key_of[15], (TOKENS, D), 1.0, 6.0, ((0, 32),))
    return {"tokens": tokens, "norm_gain": norm_gain, "query_weight": query_weight, "key_weight": key_weight, "value_weight": value_weight, "gate_weight": gate_weight, "rank_down": rank_down, "rank_up": rank_up, "gate_bias": gate_bias, "head_gain": head_gain, "out_weight": out_weight, "ffn_gain": ffn_gain, "ffn_gate": ffn_gate, "ffn_up": ffn_up, "ffn_down": ffn_down, "cotangent": cotangent}


@jax.custom_vjp
def low(v):
    return lax.optimization_barrier(v.astype(jnp.bfloat16)).astype(jnp.float32)

@jax.custom_vjp
def low_back(v):
    return v

def low_keep(v):
    return (low(v), None)

def low_pass(kept, grad):
    return (grad,)

def back_keep(v):
    return (v, None)

def back_low(kept, grad):
    return (low(grad),)
low.defvjp(low_keep, low_pass)
low_back.defvjp(back_keep, back_low)

def matmul(left, right):
    return jnp.dot(left, right, precision=lax.Precision.HIGHEST, preferred_element_type=jnp.float32)

def rms_norm(values, gain):
    return values * lax.rsqrt(lax.optimization_barrier(jnp.mean(values * values, axis=-1, keepdims=True)) + 1e-06) * gain

def mixer_block(state_matrix, inputs):
    query, key, value_rows, decay = inputs
    within = jnp.cumsum(decay, axis=0)
    total = within[-1]
    query_with_decay = query * jnp.exp(within)
    k_decayed = key * jnp.exp(-within)
    key_to_segment_end = key * jnp.exp(total[None] - within)
    size = query.shape[0]
    causal = (jnp.arange(size)[:, None] >= jnp.arange(size)[None, :]).astype(jnp.float32)
    scores = jnp.einsum('ihk,jhk->hij', query_with_decay, k_decayed, precision=lax.Precision.HIGHEST) * causal[None]
    segment_result = jnp.einsum('hij,jhv->ihv', scores, value_rows, precision=lax.Precision.HIGHEST)
    segment_result = segment_result + jnp.einsum('xds,dsa->xda', query_with_decay, state_matrix, precision=lax.Precision.HIGHEST)
    state_increment = jnp.einsum('qcu,qcp->cup', key_to_segment_end, value_rows, precision=lax.Precision.HIGHEST)
    state_matrix = jnp.exp(total)[:, :, None] * state_matrix + state_increment
    return (state_matrix, segment_result)

def run_sequence(q_blocks, k_blocks, v_blocks, d_blocks):
    start = jnp.zeros((HEADS, HK, HV), jnp.float32)
    return lax.scan(jax.checkpoint(mixer_block), start, (q_blocks, k_blocks, v_blocks, d_blocks))[1]

def forward(tokens, norm_gain, query_weight, key_weight, value_weight, gate_weight, rank_down, rank_up, gate_bias, head_gain, out_weight, ffn_gain, ffn_gate, ffn_up, ffn_down):
    length = tokens.shape[0]
    normed = low(rms_norm(tokens, norm_gain))
    query = low(low_back(matmul(normed, query_weight)))
    key = low(low_back(matmul(normed, key_weight)))
    value_rows = low(low_back(matmul(normed, value_weight)))
    rank_mid = low(low_back(matmul(normed, rank_down)))
    logit = low_back(matmul(rank_mid, rank_up)) + gate_bias
    decay = jax.nn.log_sigmoid(logit) / 16.0
    gate = low_back(matmul(normed, gate_weight))
    per_seq = length // GROUP // SEQS
    q_blocks = query.reshape(SEQS, per_seq, GROUP, HEADS, HK) * HK ** (-0.5)
    k_blocks = key.reshape(SEQS, per_seq, GROUP, HEADS, HK)
    v_blocks = value_rows.reshape(SEQS, per_seq, GROUP, HEADS, HV)
    d_blocks = decay.reshape(SEQS, per_seq, GROUP, HEADS, HK)
    mixed = jax.vmap(run_sequence)(q_blocks, k_blocks, v_blocks, d_blocks)
    mixed = mixed.reshape(length, HEADS, HV)
    headed = mixed * lax.rsqrt(lax.optimization_barrier(jnp.mean(mixed * mixed, axis=-1, keepdims=True)) + 1e-06)
    gated = low(headed.reshape(length, HEADS * HV) * head_gain * jax.nn.silu(gate))
    hidden_state = tokens + low_back(matmul(gated, out_weight))
    ffn_in = low(rms_norm(hidden_state, ffn_gain))
    fgate = low_back(matmul(ffn_in, ffn_gate))
    fup = low_back(matmul(ffn_in, ffn_up))
    inner = low(jax.nn.silu(fgate) * fup)
    return hidden_state + low_back(matmul(inner, ffn_down))

def reference(tokens, norm_gain, query_weight, key_weight, value_weight, gate_weight, rank_down, rank_up, gate_bias, head_gain, out_weight, ffn_gain, ffn_gate, ffn_up, ffn_down, cotangent):
    inputs = [a.astype(jnp.float32) for a in (tokens, norm_gain, query_weight, key_weight, value_weight, gate_weight, rank_down, rank_up, gate_bias, head_gain, out_weight, ffn_gain, ffn_gate, ffn_up, ffn_down)]
    segment_result, pullback = jax.vjp(forward, *inputs)
    grads = pullback(cotangent.astype(jnp.float32))
    return (segment_result, grads[0], grads[1], grads[2], grads[3], grads[4], grads[5], grads[6], grads[7], grads[8], grads[9], grads[10], grads[11], grads[12], grads[13], grads[14])
```

```python
import functools

import jax
import jax.numpy as jnp
from jax import lax
from jax.experimental import pallas as pl
from jax.experimental.pallas import tpu as pltpu
from jax.sharding import PartitionSpec as P

HEADS = 4
HK = 128
HV = 256
GROUP = 64

MESH = pl.DeviceIdType.MESH
LINE = 0
CORE = 3


def grid_of(count):
    core = 2 if count % 2 == 0 else 1
    rest = count // core
    third = max(k for k in range(1, rest + 1) if rest % k == 0 and k**3 <= rest)
    rest //= third
    second = max(k for k in range(1, rest + 1) if rest % k == 0 and k * k <= rest)
    return (rest // second, second, third, core)


class Place:
    def __init__(self, sizes):
        self.sizes = sizes
        rest = lax.axis_index("seq")
        here = []
        for size in sizes[::-1]:
            here.append(lax.rem(rest, size))
            rest = lax.div(rest, size)
        self.here = here[::-1]

    def index(self, **moved):
        out = 0
        for axis, size in enumerate(self.sizes):
            out = out * size + moved.get(f"a{axis}", self.here[axis])
        return out

    def toward(self, axis, step):
        return (self.index(**{f"a{axis}": self.here[axis] + step}),)

    def can(self, axis, step):
        return self.here[axis] > 0 if step < 0 else self.here[axis] < self.sizes[axis] - 1

    def greet(self):
        barrier = pltpu.get_barrier_semaphore()
        total = 0
        for axis, size in enumerate(self.sizes):
            for step in (-1, 1):
                if size == 1:
                    continue
                able = self.can(axis, step)

                @pl.when(able)
                def _(axis=axis, step=step):
                    pl.semaphore_signal(
                        barrier, inc=1, device_id=self.toward(axis, step), device_id_type=MESH
                    )

                total = total + able.astype(jnp.int32)
        pl.semaphore_wait(barrier, total)


def run_all(coroutines):
    active = list(coroutines)
    while active:
        still = []
        for coroutine in active:
            try:
                next(coroutine)
                still.append(coroutine)
            except StopIteration:
                pass
        active = still


class Gather:
    def __init__(self, place, part, order, buffer, columns, send, recv):
        self.place, self.part, self.order = place, part, order + (CORE,)
        self.buffer, self.columns, self.send, self.recv = buffer, columns, send, recv

    def copy(self, stage, line, along, step):
        place, axis = self.place, self.order[stage]
        where = []
        for a in range(4):
            if a == axis:
                where.append(along)
            elif a == LINE and LINE in self.order[:stage]:
                where.append(line)
            elif a in self.order[:stage]:
                where.append(slice(None))
            else:
                where.append(place.here[a])
        first, width = self.columns
        block = self.buffer.at[tuple(where) + (slice(None), pl.ds(first, width))]
        lane = 0 if place.sizes[axis] == 2 and axis != LINE else along
        if axis == LINE:
            line, lane = along, 0
        return pltpu.make_async_remote_copy(
            src_ref=block,
            dst_ref=block,
            send_sem=self.send.at[self.part, stage, line, lane, (step + 1) // 2],
            recv_sem=self.recv.at[self.part, stage, line, lane],
            device_id=place.toward(axis, step),
            device_id_type=MESH,
        )

    def each_step(self, stage, do):
        axis, place = self.order[stage], self.place
        if place.sizes[axis] == 1:
            return
        if place.sizes[axis] == 2 and axis != LINE:
            do(1 - 2 * place.here[axis], None)
            return
        for step in (-1, 1):
            do(step, place.can(axis, step))

    def launch(self, stage, line):
        axis, place = self.order[stage], self.place

        def do(step, able):
            def go():
                self.copy(stage, line, place.here[axis], step).start()

            go() if able is None else pl.when(able)(go)

        self.each_step(stage, do)

    def finish(self, stage, line):
        axis, place = self.order[stage], self.place
        size, here = place.sizes[axis], place.here[axis]
        if size == 1:
            return
        if size == 2:
            self.copy(stage, line, 1 - here, 1 - 2 * here).wait_recv()
            return
        for hop in range(1, size):
            for step in (-1, 1):
                along = here - step * hop
                valid = (along >= 0) & (along < size)

                @pl.when(valid)
                def _(along=along, step=step):
                    self.copy(stage, line, along, step).wait_recv()

                @pl.when(valid & place.can(axis, step))
                def _(along=along, step=step):
                    self.copy(stage, line, along, step).start()

    def steps(self):
        place = self.place
        size, here = place.sizes[LINE], place.here[LINE]
        spot = self.order.index(LINE)
        for stage in range(spot):
            self.launch(stage, here)
            yield
            self.finish(stage, here)
        for step in (-1, 1):

            @pl.when(place.can(LINE, step))
            def _(step=step):
                self.copy(spot, here, here, step).start()

        later = list(range(spot + 1, 4))
        for turn in range(size + len(later)):
            for age in range(min(turn, len(later)), -1, -1):
                far = turn - age
                if far >= size:
                    continue
                for step in (-1, 1) if far else (1,):
                    line = here - step * far
                    valid = (line >= 0) & (line < size)

                    def advance(line=line, step=step, far=far, age=age):
                        if age == 0 and far:
                            self.copy(spot, line, line, step).wait_recv()

                            @pl.when(place.can(LINE, step))
                            def _():
                                self.copy(spot, line, line, step).start()

                        if age:
                            self.finish(later[age - 1], line)
                        if age < len(later):
                            self.launch(later[age], line)

                    pl.when(valid)(advance) if far else advance()
            yield

    def drain(self):
        place = self.place
        size, here = place.sizes[LINE], place.here[LINE]
        spot = self.order.index(LINE)
        for line in range(size):
            for step in (-1, 1):

                @pl.when(place.can(LINE, step) & ((line <= here) if step > 0 else (line >= here)))
                def _(line=line, step=step):
                    self.copy(spot, line, line, step).wait_send()

        for stage in range(4):
            if stage == spot:
                continue
            axis = self.order[stage]
            lines = [here] if stage < spot else list(range(size))
            for line in lines:
                if place.sizes[axis] == 1:
                    continue
                if place.sizes[axis] == 2:
                    self.copy(stage, line, place.here[axis], 1 - 2 * place.here[axis]).wait_send()
                    continue
                for step in (-1, 1):
                    for along in range(place.sizes[axis]):
                        at = place.here[axis]

                        @pl.when(place.can(axis, step) & ((along <= at) if step > 0 else (along >= at)))
                        def _(line=line, step=step, along=along, stage=stage):
                            self.copy(stage, line, along, step).wait_send()


ORDERS = ((2, 0, 1), (1, 0, 2), (0, 2, 1), (0, 1, 2))


def gather_kernel(sizes, parts, count, *refs):
    shards, buffers = refs[:count], refs[count : 2 * count]
    send, recv, own = refs[2 * count :]
    place = Place(sizes)
    locals_ = [
        pltpu.make_async_copy(shard, buffer.at[tuple(place.here)], own.at[k])
        for k, (shard, buffer) in enumerate(zip(shards, buffers))
    ]
    for copy in locals_:
        copy.start()
    place.greet()
    for copy in locals_:
        copy.wait()
    gathers = [
        Gather(place, k, order, buffers[which], columns, send, recv)
        for k, (which, columns, order) in enumerate(parts)
    ]
    run_all([g.steps() for g in gathers])
    for g in gathers:
        g.drain()


def lanes_of(sizes):
    return max([1] + [size for size in sizes[1:] if size > 2])


def gather_all(shards, parts, sizes, collective_id):
    lanes = lanes_of(sizes)
    out = pl.pallas_call(
        functools.partial(gather_kernel, sizes, parts, len(shards)),
        out_shape=[jax.ShapeDtypeStruct(sizes + s.shape, s.dtype) for s in shards],
        in_specs=[pl.BlockSpec(memory_space=pltpu.VMEM)] * len(shards),
        out_specs=[pl.BlockSpec(memory_space=pl.ANY)] * len(shards),
        scratch_shapes=[
            pltpu.SemaphoreType.DMA((len(parts), 4, sizes[0], lanes, 2)),
            pltpu.SemaphoreType.DMA((len(parts), 4, sizes[0], lanes)),
            pltpu.SemaphoreType.DMA((len(shards),)),
        ],
        compiler_params=pltpu.CompilerParams(collective_id=collective_id, has_side_effects=True),
    )(*shards)
    return [o.reshape((-1,) + o.shape[5:]) for o in out]


class Scatter:
    def __init__(self, place, part, order, partial, columns, held, bufs, out, load, send, recv):
        self.place, self.part, self.order = place, part, (CORE,) + order
        self.partial, self.columns, self.held, self.bufs, self.out = partial, columns, held, bufs, out
        self.load, self.send, self.recv = load, send, recv

    def own(self, line):
        first, width = self.columns
        where = (line, slice(None), slice(None), self.place.here[CORE], slice(None), pl.ds(first, width))
        return pltpu.make_async_copy(self.partial.at[where], self.held.at[line], self.load.at[self.part, line])

    def block(self, stage, line, along):
        where, done = [], self.order[:stage]
        for a in range(3):
            if a == self.order[stage]:
                where.append(along)
            elif a in done:
                where.append(self.place.here[a])
            elif a == LINE:
                where.append(line)
            else:
                where.append(slice(None))
        return tuple(where)

    def slot(self, stage, line, slot):
        axis = self.order[stage]
        if axis == LINE:
            return (slot,)
        if LINE in self.order[:stage]:
            line = 0
        return (line, 0 if self.place.sizes[axis] == 2 else slot)

    def copy(self, stage, line, along, step):
        place, axis = self.place, self.order[stage]
        size = place.sizes[axis]
        first, width = self.columns
        if axis == CORE:
            where = (line, slice(None), slice(None), along, slice(None), pl.ds(first, width))
            source = self.partial.at[where]
        else:
            source = self.held.at[self.block(stage, line, along)]
        arrives = place.here[axis] + step == along
        number = jnp.where(arrives & (step < 0), size, along) if size > 2 else 0
        sem = self.slot(stage, line, along)
        if axis == LINE:
            sem = sem + (0,)
        there = self.slot(stage, line, number)
        return pltpu.make_async_remote_copy(
            src_ref=source,
            dst_ref=self.bufs[stage].at[there],
            send_sem=self.send.at[(self.part, stage) + sem],
            recv_sem=self.recv.at[(self.part, stage) + there + ((0,) if axis == LINE else ())],
            device_id=place.toward(axis, step),
            device_id_type=MESH,
        )

    def wait(self, stage, line, number):
        there = self.slot(stage, line, number)
        buf = self.bufs[stage].at[there]
        axis = self.order[stage]
        pltpu.make_async_copy(
            buf, buf, self.recv.at[(self.part, stage) + there + ((0,) if axis == LINE else ())]
        ).wait()
        return self.bufs[stage], there

    def add(self, stage, line, along, number, last=False):
        buf, there = self.wait(stage, line, number)
        if last:
            first, width = self.columns
            self.out[:, pl.ds(first, width)] += buf[there].astype(jnp.float32)
            return
        where = self.block(stage, line, along)
        if self.order[stage] == CORE:
            where = (line, slice(None), slice(None))
        total = self.held[where].astype(jnp.float32) + buf[there].astype(jnp.float32)
        self.held[where] = total.astype(self.held.dtype)

    def launch(self, stage, line):
        axis, place = self.order[stage], self.place
        size, here = place.sizes[axis], place.here[axis]
        if size == 2:
            self.copy(stage, line, 1 - here, 1 - 2 * here).start()
        elif size > 2:
            for turn in range(1, size):
                for step, along in ((1, size - turn), (-1, turn - 1)):

                    @pl.when((here == (0 if step > 0 else size - 1)))
                    def _(step=step, along=along):
                        self.copy(stage, line, along, step).start()

    def pass_on(self, stage, line, turn):
        axis, place = self.order[stage], self.place
        size, here = place.sizes[axis], place.here[axis]
        for step, along in ((1, size - turn), (-1, turn - 1)):
            ahead = (along > here) if step > 0 else (along < here)

            @pl.when(ahead & place.can(axis, -step))
            def _(step=step, along=along):
                self.add(stage, line, along, along)
                self.copy(stage, line, along, step).start()

    def finish(self, stage, line):
        axis, place = self.order[stage], self.place
        size, here = place.sizes[axis], place.here[axis]
        if size == 2:
            self.add(stage, line, here, 0, stage == 3)
        elif size > 2:
            for step, number in ((-1, here), (1, size)):

                @pl.when(place.can(axis, step))
                def _(number=number):
                    self.add(stage, line, here, number, stage == 3)

    def whole(self, stage, line):
        for turn in range(1, self.place.sizes[self.order[stage]]):
            if self.place.sizes[self.order[stage]] > 2:
                self.pass_on(stage, line, turn)
        self.finish(stage, line)

    def line_hop(self, along, hop):
        place, stage = self.place, self.order.index(LINE)
        size, here = place.sizes[LINE], place.here[LINE]
        for step, at, ahead in ((1, hop, along > hop), (-1, size - 1 - hop, along < size - 1 - hop)):
            if not ahead:
                continue

            @pl.when(here == at)
            def _(step=step):
                if hop:
                    self.add(stage, here, along, along)
                self.copy(stage, here, along, step).start()

    def steps(self):
        place = self.place
        size, here = place.sizes[LINE], place.here[LINE]
        lines = []
        for k in range(size):
            lines.append(k // 2 if k % 2 == 0 else size - 1 - k // 2)
        spot = self.order.index(LINE)

        def begin(k):
            self.own(lines[k]).start()
            self.launch(0, lines[k])

        begin(0)
        yield
        for turn in range(2 * size + spot - 2):
            if turn + 1 < size:
                begin(turn + 1)
            for k in range(size):
                hop = turn - k - spot
                if 0 <= hop < size - 1:
                    self.line_hop(lines[k], hop)
            for stage in range(spot - 1, -1, -1):
                k = turn - stage
                if not 0 <= k < size:
                    continue
                if stage == 0:
                    self.own(lines[k]).wait()
                self.whole(stage, lines[k])
                if stage + 1 < spot:
                    self.launch(stage + 1, lines[k])
            yield
        if spot == 3:
            self.begin_out()
        self.finish(spot, here)
        for stage in range(spot + 1, 4):
            if stage == 3:
                self.begin_out()
            self.launch(stage, here)
            yield
            self.whole(stage, here)

    def begin_out(self):
        first, width = self.columns
        mine = self.held[tuple(self.place.here[:3])]
        self.out[:, pl.ds(first, width)] = mine.astype(jnp.float32)

    def drain(self):
        place = self.place
        spot = self.order.index(LINE)
        for stage in range(4):
            axis = self.order[stage]
            size, here = place.sizes[axis], place.here[axis]
            for line in range(place.sizes[LINE]) if stage < spot else [place.here[LINE]]:
                if size == 2:
                    self.copy(stage, line, 1 - here, 1 - 2 * here).wait_send()
                elif size > 2:
                    for along in range(size):
                        for step in (-1, 1):

                            @pl.when((along > here) if step > 0 else (along < here))
                            def _(along=along, step=step, line=line, stage=stage):
                                self.copy(stage, line, along, step).wait_send()


def scatter_kernel(sizes, parts, count, *refs):
    partials, outs = refs[:count], refs[count : 2 * count]
    load, send, recv = refs[2 * count : 2 * count + 3]
    scratch = list(refs[2 * count + 3 :])
    place = Place(sizes)
    place.greet()
    scatters = []
    for k, (which, columns, order) in enumerate(parts):
        held, *bufs = scratch[5 * k : 5 * k + 5]
        scatters.append(
            Scatter(place, k, order, partials[which], columns, held, bufs, outs[which], load, send, recv)
        )
    run_all([s.steps() for s in scatters])
    for s in scatters:
        s.drain()


def scatter_scratch(sizes, parts, shapes, dtype):
    scratch = []
    for which, (_, width), order in parts:
        rows = shapes[which][-2]
        scratch.append(pltpu.VMEM(sizes[:3] + (rows, width), dtype))
        stages = (CORE,) + order
        for stage, axis in enumerate(stages):
            free = tuple(sizes[a] for a in range(1, 3) if a not in stages[: stage + 1])
            slots = 1 if sizes[axis] <= 2 else sizes[axis] + 1
            if axis == LINE:
                lead = (slots,)
            else:
                lead = (1 if LINE in stages[:stage] else sizes[LINE], slots)
            scratch.append(pltpu.VMEM(lead + free + (rows, width), dtype))
    return scratch


def scatter_all(partials, parts, sizes, collective_id):
    count = 1
    for size in sizes:
        count *= size
    partials = [p.reshape(sizes + (p.shape[0] // count, p.shape[1])) for p in partials]
    lanes = max([1] + [size + 1 for size in sizes[1:] if size > 2])
    sems = (len(parts), 4, sizes[0] + 1, lanes)
    return pl.pallas_call(
        functools.partial(scatter_kernel, sizes, parts, len(partials)),
        out_shape=[jax.ShapeDtypeStruct(p.shape[4:], jnp.float32) for p in partials],
        in_specs=[pl.BlockSpec(memory_space=pl.ANY)] * len(partials),
        out_specs=[pl.BlockSpec(memory_space=pltpu.VMEM)] * len(partials),
        scratch_shapes=[
            pltpu.SemaphoreType.DMA((len(parts), sizes[0])),
            pltpu.SemaphoreType.DMA(sems),
            pltpu.SemaphoreType.DMA(sems),
        ]
        + scatter_scratch(sizes, parts, [p.shape for p in partials], partials[0].dtype),
        compiler_params=pltpu.CompilerParams(
            collective_id=collective_id, has_side_effects=True, vmem_limit_bytes=60 << 20
        ),
    )(*partials)


def partners_of(sizes):
    hops = []
    for axis in (2, 1, 0):
        stride = 1
        while stride < sizes[axis]:
            hops.append((axis, stride))
            stride *= 2
    return hops


def scan_kernel(
    sizes, backward, state_ref, logs_ref, out_ref,
    sib, sib_logs, first, first_logs, pre, pre_logs, total, total_logs, wire, wire_logs, got, got_logs, other, send, recv,
):
    place = Place(sizes)
    core = place.here[CORE]
    hops = partners_of(sizes)
    half = HEADS // 2
    mine, theirs = pl.ds(half * core, half), pl.ds(half * (1 - core), half)
    sibling = place.toward(CORE, 1 - 2 * core)

    def bit(axis, stride):
        return lax.rem(lax.div(place.here[axis], stride), 2)

    def partner(axis, stride):
        return place.toward(axis, (1 - 2 * bit(axis, stride)) * stride)

    barrier = pltpu.get_barrier_semaphore()
    for device in [sibling] + [partner(*hop) for hop in hops]:
        pl.semaphore_signal(barrier, inc=1, device_id=device, device_id_type=MESH)
    pl.semaphore_wait(barrier, 1 + len(hops))

    def remote(source, target, number, device):
        return pltpu.make_async_remote_copy(
            src_ref=source, dst_ref=target, send_sem=send.at[number], recv_sem=recv.at[number],
            device_id=device, device_id_type=MESH,
        )

    def scaled(logs, states, added):
        return [jnp.exp(logs[h, 0:1, :]) * states[h] + added[h] for h in range(half)]

    swap = [
        remote(state_ref.at[theirs], sib, 0, sibling),
        remote(logs_ref.at[theirs], sib_logs, 1, sibling),
    ]
    for copy in swap:
        copy.start()
    for copy in swap:
        copy.wait_recv()
    starts = core == (1 if backward else 0)

    @pl.when(starts)
    def _():
        first[...] = state_ref[mine]
        first_logs[...] = logs_ref[mine]
        new = scaled(sib_logs, first, sib)
        for h in range(half):
            total[h] = new[h]

    @pl.when(jnp.logical_not(starts))
    def _():
        first[...] = sib[...]
        first_logs[...] = sib_logs[...]
        new = scaled(logs_ref.at[mine], first, state_ref.at[mine])
        for h in range(half):
            total[h] = new[h]

    total_logs[...] = logs_ref[mine] + sib_logs[...]
    pre[...] = jnp.zeros_like(pre)
    pre_logs[...] = jnp.zeros_like(pre_logs)
    pending = list(swap)
    for k, (axis, stride) in enumerate(hops):
        last = k == len(hops) - 1
        wire[k] = total[...].astype(wire.dtype)
        wire_logs[k] = total_logs[...]
        copies = [
            remote(wire.at[k], got.at[k], 2 + 2 * k, partner(axis, stride)),
            remote(wire_logs.at[k], got_logs.at[k], 3 + 2 * k, partner(axis, stride)),
        ]
        for copy in copies:
            copy.start()
        pending += copies
        for copy in copies:
            copy.wait_recv()
        earlier = bit(axis, stride) == (1 if backward else 0)
        arrived = [got[k, h].astype(jnp.float32) for h in range(half)]

        @pl.when(jnp.logical_not(earlier))
        def _(k=k, arrived=arrived, last=last):
            new = scaled(pre_logs, arrived, pre)
            for h in range(half):
                pre[h] = new[h]
            pre_logs[...] = pre_logs[...] + got_logs[k]
            if not last:
                new = scaled(total_logs, arrived, total)
                for h in range(half):
                    total[h] = new[h]

        if not last:

            @pl.when(earlier)
            def _(k=k, arrived=arrived):
                new = scaled(got_logs.at[k], total, arrived)
                for h in range(half):
                    total[h] = new[h]

            total_logs[...] = total_logs[...] + got_logs[k]
    second = scaled(first_logs, pre, first)

    @pl.when(starts)
    def _():
        for h in range(half):
            other[h] = second[h]
        out_ref[mine] = pre[...]

    @pl.when(jnp.logical_not(starts))
    def _():
        other[...] = pre[...]
        for h in range(half):
            out_ref[half * core + h] = second[h]

    back = remote(other, out_ref.at[mine], 2 + 2 * len(hops), sibling)
    back.start()
    back.wait_recv()
    for copy in pending + [back]:
        copy.wait_send()


def entering(state, logs, sizes, backward, collective_id):
    half, hops = HEADS // 2, len(partners_of(sizes))
    block, tile = (half, HV, HK), (half, 8, HK)
    spread = jnp.broadcast_to(logs[:, None, :], (HEADS, 8, HK))
    return pl.pallas_call(
        functools.partial(scan_kernel, sizes, backward),
        out_shape=jax.ShapeDtypeStruct(state.shape, jnp.float32),
        in_specs=[pl.BlockSpec(memory_space=pltpu.VMEM)] * 2,
        out_specs=pl.BlockSpec(memory_space=pltpu.VMEM),
        scratch_shapes=[
            pltpu.VMEM(block, jnp.float32), pltpu.VMEM(tile, jnp.float32),
            pltpu.VMEM(block, jnp.float32), pltpu.VMEM(tile, jnp.float32),
            pltpu.VMEM(block, jnp.float32), pltpu.VMEM(tile, jnp.float32),
            pltpu.VMEM(block, jnp.float32), pltpu.VMEM(tile, jnp.float32),
            pltpu.VMEM((hops,) + block, jnp.bfloat16), pltpu.VMEM((hops,) + tile, jnp.float32),
            pltpu.VMEM((hops,) + block, jnp.bfloat16), pltpu.VMEM((hops,) + tile, jnp.float32),
            pltpu.VMEM(block, jnp.float32),
            pltpu.SemaphoreType.DMA((3 + 2 * hops,)),
            pltpu.SemaphoreType.DMA((3 + 2 * hops,)),
        ],
        compiler_params=pltpu.CompilerParams(
            collective_id=collective_id, has_side_effects=True, vmem_limit_bytes=32 << 20
        ),
    )(state, spread)


def matmul(left, right):
    return jnp.dot(left, right, preferred_element_type=jnp.float32)


def left_t(left, right):
    return lax.dot_general(
        left, right, (((0,), (0,)), ((), ())), preferred_element_type=jnp.float32
    )


def right_t(left, right):
    return lax.dot_general(
        left, right, (((1,), (1,)), ((), ())), preferred_element_type=jnp.float32
    )


def rms_norm(values, gain):
    return values * lax.rsqrt(jnp.mean(values * values, axis=-1, keepdims=True) + 1e-06) * gain


def head_norm(mixed, gain, gate):
    length = mixed.shape[0]
    shaped = mixed.reshape(length, HEADS, HV)
    headed = shaped * lax.rsqrt(jnp.mean(shaped * shaped, axis=-1, keepdims=True) + 1e-06)
    return headed.reshape(length, HEADS * HV) * gain * jax.nn.silu(gate)


def swiglu(fgate, fup):
    return jax.nn.silu(fgate) * fup


def mixer_local(query, key, value_rows, decay):
    length = query.shape[0]
    blocks = length // GROUP
    q_blocks = query.reshape(blocks, GROUP, HEADS, HK) * HK ** (-0.5)
    k_blocks = key.reshape(blocks, GROUP, HEADS, HK)
    v_blocks = value_rows.reshape(blocks, GROUP, HEADS, HV)
    within = jnp.cumsum(decay.reshape(blocks, GROUP, HEADS, HK), axis=1)
    total = within[:, -1]
    query_with_decay = q_blocks * jnp.exp(within)
    k_decayed = k_blocks * jnp.exp(-within)
    key_to_segment_end = k_blocks * jnp.exp(total[:, None] - within)
    causal = (jnp.arange(GROUP)[:, None] >= jnp.arange(GROUP)[None, :]).astype(jnp.float32)
    scores = (
        jnp.einsum("nihk,njhk->nhij", query_with_decay, k_decayed, precision=lax.Precision.HIGHEST)
        * causal
    )
    segment_result = jnp.einsum(
        "nhij,njhv->nihv", scores, v_blocks, precision=lax.Precision.HIGHEST
    )
    updates = jnp.einsum(
        "njhk,njhv->nhkv", key_to_segment_end, v_blocks, precision=lax.Precision.HIGHEST
    )

    def advance(state_matrix, pair):
        factor, state_increment = pair
        return (jnp.exp(factor)[:, :, None] * state_matrix + state_increment, state_matrix)

    final, starts = lax.scan(advance, jnp.zeros((HEADS, HK, HV), jnp.float32), (total, updates))
    segment_result = segment_result + jnp.einsum(
        "nihk,nhkv->nihv", query_with_decay, starts, precision=lax.Precision.HIGHEST
    )
    return (segment_result.reshape(length, HEADS * HV), final, jnp.sum(total, axis=0))


def mixer_carried(query, decay, incoming_state):
    length = query.shape[0]
    blocks = length // GROUP
    q_blocks = query.reshape(blocks, GROUP, HEADS, HK) * HK ** (-0.5)
    within = jnp.cumsum(decay.reshape(blocks, GROUP, HEADS, HK), axis=1)
    before = jnp.cumsum(within[:, -1], axis=0) - within[:, -1]
    weighted_scores = q_blocks * jnp.exp(within + before[:, None])
    segment_result = jnp.einsum(
        "blfs,fsq->blfq", weighted_scores, incoming_state, precision=lax.Precision.HIGHEST
    )
    return segment_result.reshape(length, HEADS * HV)


PARTS = (
    (0, (0, 128), ORDERS[0]),
    (1, (0, 1024), ORDERS[0]),
    (1, (1024, 1024), ORDERS[1]),
    (1, (2048, 1024), ORDERS[2]),
    (2, (0, 1024), ORDERS[3]),
    (3, (0, 2816), ORDERS[0]),
    (4, (0, 2816), ORDERS[1]),
    (5, (0, 512), ORDERS[2]),
    (5, (512, 512), ORDERS[3]),
)
BACK_PARTS = tuple((which, columns, order[::-1]) for which, columns, order in PARTS)
TILE = (16, 128)


def packed(pieces):
    count = pieces[0].shape[0]
    flat = jnp.concatenate([p.reshape(count, -1) for p in pieces], axis=1)
    flat = jnp.pad(flat, ((0, 0), (0, TILE[0] * TILE[1] - flat.shape[1])))
    return flat.reshape(count * TILE[0], TILE[1])


def unpacked(tiles, shapes):
    count = tiles.shape[0] // TILE[0]
    flat = tiles.reshape(count, TILE[0] * TILE[1])
    out, at = [], 0
    for shape in shapes:
        size = 1
        for extent in shape:
            size *= extent
        out.append(flat[:, at : at + size].reshape((count,) + shape))
        at += size
    return out


def local(
    tokens,
    norm_gain,
    query_weight,
    key_weight,
    value_weight,
    gate_weight,
    rank_down,
    rank_up,
    gate_bias,
    head_gain,
    out_weight,
    ffn_gain,
    ffn_gate,
    ffn_up,
    ffn_down,
    cotangent,
):
    count = lax.axis_size("seq")
    sizes = grid_of(count)
    small = (norm_gain, rank_down, rank_up, gate_bias, head_gain, ffn_gain)
    shapes = [s.shape for s in small]
    projections = jnp.concatenate([query_weight, key_weight, value_weight, gate_weight], axis=1)
    tiles, full_proj, full_out, full_fgate, full_fup, full_fdown = gather_all(
        [packed([s[None] for s in small]), projections, out_weight, ffn_gate, ffn_up, ffn_down], PARTS, sizes, 0
    )
    pieces = unpacked(tiles, shapes)
    full_gain, full_bias, full_head_gain, full_ffn_gain = (pieces[k].reshape(-1) for k in (0, 3, 4, 5))
    full_down_rank = pieces[1].reshape(-1, rank_down.shape[1])
    full_up_rank = pieces[2].transpose(1, 0, 2).reshape(rank_up.shape[0], -1)
    full_query, full_key = full_proj[:, :512], full_proj[:, 512:1024]
    full_value, full_gate = full_proj[:, 1024:2048], full_proj[:, 2048:]
    gain_one = full_gain.astype(jnp.float32)
    gain_two = full_ffn_gain.astype(jnp.float32)
    heads_gain = full_head_gain.astype(jnp.float32)
    inputs = tokens.astype(jnp.float32)
    normed = rms_norm(inputs, gain_one)
    normed_low = normed.astype(jnp.bfloat16)
    query_low = matmul(normed_low, full_query).astype(jnp.bfloat16)
    key_low = matmul(normed_low, full_key).astype(jnp.bfloat16)
    value_low = matmul(normed_low, full_value).astype(jnp.bfloat16)
    rank_mid = matmul(normed_low, full_down_rank).astype(jnp.bfloat16)
    logit = matmul(rank_mid, full_up_rank) + full_bias.astype(jnp.float32)
    decay = jax.nn.log_sigmoid(logit) / 16.0
    gate = matmul(normed_low, full_gate)
    query_f = query_low.astype(jnp.float32)
    key_f = key_low.astype(jnp.float32)
    value_f = value_low.astype(jnp.float32)
    local_out, local_pull = jax.vjp(mixer_local, query_f, key_f, value_f, decay)
    mixed_local, final_state, log_total = local_out
    factor = jnp.exp(log_total)
    incoming_state = entering(final_state.transpose(0, 2, 1), log_total, sizes, False, 2).transpose(0, 2, 1)
    carried_out, carried_pull = jax.vjp(mixer_carried, query_f, decay, incoming_state)
    mixed = mixed_local + carried_out
    gated, gated_pull = jax.vjp(head_norm, mixed, heads_gain, gate)
    gated_low = gated.astype(jnp.bfloat16)
    hidden_state = inputs + matmul(gated_low, full_out)
    ffn_in, ffn_norm_pull = jax.vjp(rms_norm, hidden_state, gain_two)
    ffn_low = ffn_in.astype(jnp.bfloat16)
    fgate = matmul(ffn_low, full_fgate)
    fup = matmul(ffn_low, full_fup)
    inner, inner_pull = jax.vjp(swiglu, fgate, fup)
    inner_low = inner.astype(jnp.bfloat16)
    block_output = hidden_state + matmul(inner_low, full_fdown)
    upstream = cotangent.astype(jnp.float32)
    down_grad = left_t(inner_low, cotangent)
    inner_grad = right_t(cotangent, full_fdown)
    fgate_grad, fup_grad = inner_pull(inner_grad)
    fgate_low = fgate_grad.astype(jnp.bfloat16)
    fup_low = fup_grad.astype(jnp.bfloat16)
    fgate_wgrad = left_t(ffn_low, fgate_low)
    fup_wgrad = left_t(ffn_low, fup_low)
    ffn_in_grad = right_t(fgate_low, full_fgate) + right_t(fup_low, full_fup)
    hidden_part, gain_two_grad = ffn_norm_pull(ffn_in_grad)
    hidden_grad = upstream + hidden_part
    hidden_low = hidden_grad.astype(jnp.bfloat16)
    out_wgrad = left_t(gated_low, hidden_low)
    gated_grad = right_t(hidden_low, full_out)
    mixed_grad, heads_gain_grad, gate_grad = gated_pull(gated_grad)
    gate_low = gate_grad.astype(jnp.bfloat16)
    gate_wgrad = left_t(normed_low, gate_low)
    query_part, decay_part, entering_grad = carried_pull(mixed_grad)
    leaving_grad = entering(entering_grad.transpose(0, 2, 1), log_total, sizes, True, 3).transpose(0, 2, 1)
    log_total_grad = factor * jnp.sum(incoming_state * leaving_grad, axis=-1)
    query_rest, key_grad, value_grad, decay_rest = local_pull(
        (mixed_grad, leaving_grad, log_total_grad)
    )
    query_low_grad = (query_part + query_rest).astype(jnp.bfloat16)
    key_low_grad = key_grad.astype(jnp.bfloat16)
    value_low_grad = value_grad.astype(jnp.bfloat16)
    logit_grad = (decay_part + decay_rest) * jax.nn.sigmoid(-logit) / 16.0
    bias_grad = jnp.sum(logit_grad, axis=0)
    logit_low = logit_grad.astype(jnp.bfloat16)
    up_rank_grad = left_t(rank_mid, logit_low)
    mid_low = right_t(logit_low, full_up_rank).astype(jnp.bfloat16)
    down_rank_grad = left_t(normed_low, mid_low)
    query_wgrad = left_t(normed_low, query_low_grad)
    key_wgrad = left_t(normed_low, key_low_grad)
    value_wgrad = left_t(normed_low, value_low_grad)
    normed_grad = (
        right_t(query_low_grad, full_query)
        + right_t(key_low_grad, full_key)
        + right_t(value_low_grad, full_value)
        + right_t(gate_low, full_gate)
        + right_t(mid_low, full_down_rank)
    )
    input_part, gain_one_grad = jax.vjp(rms_norm, inputs, gain_one)[1](normed_grad)
    tokens_grad = hidden_grad + input_part
    tiles = packed(
        [
            gain_one_grad.reshape(count, -1),
            down_rank_grad.reshape(count, -1),
            up_rank_grad.reshape(rank_up.shape[0], count, -1).transpose(1, 0, 2),
            bias_grad.reshape(count, -1),
            heads_gain_grad.reshape(count, -1),
            gain_two_grad.reshape(count, -1),
        ]
    ).astype(jnp.bfloat16)
    proj_wgrad = jnp.concatenate([query_wgrad, key_wgrad, value_wgrad, gate_wgrad], axis=1)
    summed = scatter_all(
        [tiles] + [g.astype(jnp.bfloat16) for g in (proj_wgrad, out_wgrad, fgate_wgrad, fup_wgrad, down_grad)],
        BACK_PARTS, sizes, 1,
    )
    gain_sum, down_sum, up_sum, bias_sum, head_sum, ffn_sum = [p[0] for p in unpacked(summed[0], shapes)]
    proj_sum = summed[1]
    return (
        block_output,
        tokens_grad,
        gain_sum,
        proj_sum[:, :512],
        proj_sum[:, 512:1024],
        proj_sum[:, 1024:2048],
        proj_sum[:, 2048:],
        down_sum,
        up_sum,
        bias_sum,
        head_sum,
        summed[2],
        ffn_sum,
        summed[3],
        summed[4],
        summed[5],
    )


def solution(mesh):
    return jax.shard_map(
        local,
        mesh=mesh,
        in_specs=(
            P("seq", None),
            P("seq"),
            P("seq", None),
            P("seq", None),
            P("seq", None),
            P("seq", None),
            P("seq", None),
            P(None, "seq"),
            P("seq"),
            P("seq"),
            P("seq", None),
            P("seq"),
            P("seq", None),
            P("seq", None),
            P("seq", None),
            P("seq", None),
        ),
        out_specs=(
            P("seq", None),
            P("seq", None),
            P("seq"),
            P("seq", None),
            P("seq", None),
            P("seq", None),
            P("seq", None),
            P("seq", None),
            P(None, "seq"),
            P("seq"),
            P("seq"),
            P("seq", None),
            P("seq"),
            P("seq", None),
            P("seq", None),
            P("seq", None),
        ),
        check_vma=False,
    )
```

```python
import functools

import jax
import jax.numpy as jnp
from jax import lax
from jax.experimental import pallas as pl
from jax.experimental.pallas import tpu as pltpu
from jax.sharding import PartitionSpec as P

HEADS = 4
HK = 128
HV = 256

MESH = pl.DeviceIdType.MESH
LINE = 0
CORE = 3


def grid_of(count):
    core = 2 if count % 2 == 0 else 1
    rest = count // core
    third = max(k for k in range(1, rest + 1) if rest % k == 0 and k**3 <= rest)
    rest //= third
    second = max(k for k in range(1, rest + 1) if rest % k == 0 and k * k <= rest)
    return (rest // second, second, third, core)


class Place:
    def __init__(self, sizes):
        self.sizes = sizes
        rest = lax.axis_index("seq")
        here = []
        for size in sizes[::-1]:
            here.append(lax.rem(rest, size))
            rest = lax.div(rest, size)
        self.here = here[::-1]

    def index(self, **moved):
        out = 0
        for axis, size in enumerate(self.sizes):
            out = out * size + moved.get(f"a{axis}", self.here[axis])
        return out

    def toward(self, axis, step):
        return (self.index(**{f"a{axis}": self.here[axis] + step}),)

    def can(self, axis, step):
        return self.here[axis] > 0 if step < 0 else self.here[axis] < self.sizes[axis] - 1

    def greet(self):
        barrier = pltpu.get_barrier_semaphore()
        total = 0
        for axis, size in enumerate(self.sizes):
            for step in (-1, 1):
                if size == 1:
                    continue
                able = self.can(axis, step)

                @pl.when(able)
                def _(axis=axis, step=step):
                    pl.semaphore_signal(
                        barrier, inc=1, device_id=self.toward(axis, step), device_id_type=MESH
                    )

                total = total + able.astype(jnp.int32)
        pl.semaphore_wait(barrier, total)


def run_all(coroutines):
    active = list(coroutines)
    while active:
        still = []
        for coroutine in active:
            try:
                next(coroutine)
                still.append(coroutine)
            except StopIteration:
                pass
        active = still


class Gather:
    def __init__(self, place, part, order, buffer, columns, send, recv):
        self.place, self.part, self.order = place, part, order + (CORE,)
        self.buffer, self.columns, self.send, self.recv = buffer, columns, send, recv

    def copy(self, stage, line, along, step):
        place, axis = self.place, self.order[stage]
        where = []
        for a in range(4):
            if a == axis:
                where.append(along)
            elif a == LINE and LINE in self.order[:stage]:
                where.append(line)
            elif a in self.order[:stage]:
                where.append(slice(None))
            else:
                where.append(place.here[a])
        first, width = self.columns
        block = self.buffer.at[tuple(where) + (slice(None), pl.ds(first, width))]
        lane = 0 if place.sizes[axis] == 2 and axis != LINE else along
        if axis == LINE:
            line, lane = along, 0
        return pltpu.make_async_remote_copy(
            src_ref=block,
            dst_ref=block,
            send_sem=self.send.at[self.part, stage, line, lane, (step + 1) // 2],
            recv_sem=self.recv.at[self.part, stage, line, lane],
            device_id=place.toward(axis, step),
            device_id_type=MESH,
        )

    def each_step(self, stage, do):
        axis, place = self.order[stage], self.place
        if place.sizes[axis] == 1:
            return
        if place.sizes[axis] == 2 and axis != LINE:
            do(1 - 2 * place.here[axis], None)
            return
        for step in (-1, 1):
            do(step, place.can(axis, step))

    def launch(self, stage, line):
        axis, place = self.order[stage], self.place

        def do(step, able):
            def go():
                self.copy(stage, line, place.here[axis], step).start()

            go() if able is None else pl.when(able)(go)

        self.each_step(stage, do)

    def finish(self, stage, line):
        axis, place = self.order[stage], self.place
        size, here = place.sizes[axis], place.here[axis]
        if size == 1:
            return
        if size == 2:
            self.copy(stage, line, 1 - here, 1 - 2 * here).wait_recv()
            return
        for hop in range(1, size):
            for step in (-1, 1):
                along = here - step * hop
                valid = (along >= 0) & (along < size)

                @pl.when(valid)
                def _(along=along, step=step):
                    self.copy(stage, line, along, step).wait_recv()

                @pl.when(valid & place.can(axis, step))
                def _(along=along, step=step):
                    self.copy(stage, line, along, step).start()

    def steps(self):
        place = self.place
        size, here = place.sizes[LINE], place.here[LINE]
        spot = self.order.index(LINE)
        for stage in range(spot):
            self.launch(stage, here)
            yield
            self.finish(stage, here)
        for step in (-1, 1):

            @pl.when(place.can(LINE, step))
            def _(step=step):
                self.copy(spot, here, here, step).start()

        later = list(range(spot + 1, 4))
        for turn in range(size + len(later)):
            for age in range(min(turn, len(later)), -1, -1):
                far = turn - age
                if far >= size:
                    continue
                for step in (-1, 1) if far else (1,):
                    line = here - step * far
                    valid = (line >= 0) & (line < size)

                    def advance(line=line, step=step, far=far, age=age):
                        if age == 0 and far:
                            self.copy(spot, line, line, step).wait_recv()

                            @pl.when(place.can(LINE, step))
                            def _():
                                self.copy(spot, line, line, step).start()

                        if age:
                            self.finish(later[age - 1], line)
                        if age < len(later):
                            self.launch(later[age], line)

                    pl.when(valid)(advance) if far else advance()
            yield

    def drain(self):
        place = self.place
        size, here = place.sizes[LINE], place.here[LINE]
        spot = self.order.index(LINE)
        for line in range(size):
            for step in (-1, 1):

                @pl.when(place.can(LINE, step) & ((line <= here) if step > 0 else (line >= here)))
                def _(line=line, step=step):
                    self.copy(spot, line, line, step).wait_send()

        for stage in range(4):
            if stage == spot:
                continue
            axis = self.order[stage]
            lines = [here] if stage < spot else list(range(size))
            for line in lines:
                if place.sizes[axis] == 1:
                    continue
                if place.sizes[axis] == 2:
                    self.copy(stage, line, place.here[axis], 1 - 2 * place.here[axis]).wait_send()
                    continue
                for step in (-1, 1):
                    for along in range(place.sizes[axis]):
                        at = place.here[axis]

                        @pl.when(place.can(axis, step) & ((along <= at) if step > 0 else (along >= at)))
                        def _(line=line, step=step, along=along, stage=stage):
                            self.copy(stage, line, along, step).wait_send()


ORDERS = ((2, 0, 1), (1, 0, 2), (0, 2, 1), (0, 1, 2))


def gather_kernel(sizes, parts, count, *refs):
    shards, buffers = refs[:count], refs[count : 2 * count]
    send, recv, own = refs[2 * count :]
    place = Place(sizes)
    locals_ = [
        pltpu.make_async_copy(shard, buffer.at[tuple(place.here)], own.at[k])
        for k, (shard, buffer) in enumerate(zip(shards, buffers))
    ]
    for copy in locals_:
        copy.start()
    place.greet()
    for copy in locals_:
        copy.wait()
    gathers = [
        Gather(place, k, order, buffers[which], columns, send, recv)
        for k, (which, columns, order) in enumerate(parts)
    ]
    run_all([g.steps() for g in gathers])
    for g in gathers:
        g.drain()


def lanes_of(sizes):
    return max([1] + [size for size in sizes[1:] if size > 2])


def gather_all(shards, parts, sizes, collective_id):
    lanes = lanes_of(sizes)
    out = pl.pallas_call(
        functools.partial(gather_kernel, sizes, parts, len(shards)),
        out_shape=[jax.ShapeDtypeStruct(sizes + s.shape, s.dtype) for s in shards],
        in_specs=[pl.BlockSpec(memory_space=pltpu.VMEM)] * len(shards),
        out_specs=[pl.BlockSpec(memory_space=pl.ANY)] * len(shards),
        scratch_shapes=[
            pltpu.SemaphoreType.DMA((len(parts), 4, sizes[0], lanes, 2)),
            pltpu.SemaphoreType.DMA((len(parts), 4, sizes[0], lanes)),
            pltpu.SemaphoreType.DMA((len(shards),)),
        ],
        compiler_params=pltpu.CompilerParams(collective_id=collective_id, has_side_effects=True),
    )(*shards)
    return [o.reshape((-1,) + o.shape[5:]) for o in out]


class Scatter:
    def __init__(self, place, part, order, partial, columns, held, bufs, out, load, send, recv):
        self.place, self.part, self.order = place, part, (CORE,) + order
        self.partial, self.columns, self.held, self.bufs, self.out = partial, columns, held, bufs, out
        self.load, self.send, self.recv = load, send, recv

    def own(self, line):
        first, width = self.columns
        where = (line, slice(None), slice(None), self.place.here[CORE], slice(None), pl.ds(first, width))
        return pltpu.make_async_copy(self.partial.at[where], self.held.at[line], self.load.at[self.part, line])

    def block(self, stage, line, along):
        where, done = [], self.order[:stage]
        for a in range(3):
            if a == self.order[stage]:
                where.append(along)
            elif a in done:
                where.append(self.place.here[a])
            elif a == LINE:
                where.append(line)
            else:
                where.append(slice(None))
        return tuple(where)

    def slot(self, stage, line, slot):
        axis = self.order[stage]
        if axis == LINE:
            return (slot,)
        if LINE in self.order[:stage]:
            line = 0
        return (line, 0 if self.place.sizes[axis] == 2 else slot)

    def copy(self, stage, line, along, step):
        place, axis = self.place, self.order[stage]
        size = place.sizes[axis]
        first, width = self.columns
        if axis == CORE:
            where = (line, slice(None), slice(None), along, slice(None), pl.ds(first, width))
            source = self.partial.at[where]
        else:
            source = self.held.at[self.block(stage, line, along)]
        arrives = place.here[axis] + step == along
        number = jnp.where(arrives & (step < 0), size, along) if size > 2 else 0
        sem = self.slot(stage, line, along)
        if axis == LINE:
            sem = sem + (0,)
        there = self.slot(stage, line, number)
        return pltpu.make_async_remote_copy(
            src_ref=source,
            dst_ref=self.bufs[stage].at[there],
            send_sem=self.send.at[(self.part, stage) + sem],
            recv_sem=self.recv.at[(self.part, stage) + there + ((0,) if axis == LINE else ())],
            device_id=place.toward(axis, step),
            device_id_type=MESH,
        )

    def wait(self, stage, line, number):
        there = self.slot(stage, line, number)
        buf = self.bufs[stage].at[there]
        axis = self.order[stage]
        pltpu.make_async_copy(
            buf, buf, self.recv.at[(self.part, stage) + there + ((0,) if axis == LINE else ())]
        ).wait()
        return self.bufs[stage], there

    def add(self, stage, line, along, number, last=False):
        buf, there = self.wait(stage, line, number)
        if last:
            first, width = self.columns
            self.out[:, pl.ds(first, width)] += buf[there].astype(jnp.float32)
            return
        where = self.block(stage, line, along)
        if self.order[stage] == CORE:
            where = (line, slice(None), slice(None))
        total = self.held[where].astype(jnp.float32) + buf[there].astype(jnp.float32)
        self.held[where] = total.astype(self.held.dtype)

    def launch(self, stage, line):
        axis, place = self.order[stage], self.place
        size, here = place.sizes[axis], place.here[axis]
        if size == 2:
            self.copy(stage, line, 1 - here, 1 - 2 * here).start()
        elif size > 2:
            for turn in range(1, size):
                for step, along in ((1, size - turn), (-1, turn - 1)):

                    @pl.when((here == (0 if step > 0 else size - 1)))
                    def _(step=step, along=along):
                        self.copy(stage, line, along, step).start()

    def pass_on(self, stage, line, turn):
        axis, place = self.order[stage], self.place
        size, here = place.sizes[axis], place.here[axis]
        for step, along in ((1, size - turn), (-1, turn - 1)):
            ahead = (along > here) if step > 0 else (along < here)

            @pl.when(ahead & place.can(axis, -step))
            def _(step=step, along=along):
                self.add(stage, line, along, along)
                self.copy(stage, line, along, step).start()

    def finish(self, stage, line):
        axis, place = self.order[stage], self.place
        size, here = place.sizes[axis], place.here[axis]
        if size == 2:
            self.add(stage, line, here, 0, stage == 3)
        elif size > 2:
            for step, number in ((-1, here), (1, size)):

                @pl.when(place.can(axis, step))
                def _(number=number):
                    self.add(stage, line, here, number, stage == 3)

    def whole(self, stage, line):
        for turn in range(1, self.place.sizes[self.order[stage]]):
            if self.place.sizes[self.order[stage]] > 2:
                self.pass_on(stage, line, turn)
        self.finish(stage, line)

    def line_hop(self, along, hop):
        place, stage = self.place, self.order.index(LINE)
        size, here = place.sizes[LINE], place.here[LINE]
        for step, at, ahead in ((1, hop, along > hop), (-1, size - 1 - hop, along < size - 1 - hop)):
            if not ahead:
                continue

            @pl.when(here == at)
            def _(step=step):
                if hop:
                    self.add(stage, here, along, along)
                self.copy(stage, here, along, step).start()

    def steps(self):
        place = self.place
        size, here = place.sizes[LINE], place.here[LINE]
        lines = []
        for k in range(size):
            lines.append(k // 2 if k % 2 == 0 else size - 1 - k // 2)
        spot = self.order.index(LINE)

        def begin(k):
            self.own(lines[k]).start()
            self.launch(0, lines[k])

        begin(0)
        yield
        for turn in range(2 * size + spot - 2):
            if turn + 1 < size:
                begin(turn + 1)
            for k in range(size):
                hop = turn - k - spot
                if 0 <= hop < size - 1:
                    self.line_hop(lines[k], hop)
            for stage in range(spot - 1, -1, -1):
                k = turn - stage
                if not 0 <= k < size:
                    continue
                if stage == 0:
                    self.own(lines[k]).wait()
                self.whole(stage, lines[k])
                if stage + 1 < spot:
                    self.launch(stage + 1, lines[k])
            yield
        if spot == 3:
            self.begin_out()
        self.finish(spot, here)
        for stage in range(spot + 1, 4):
            if stage == 3:
                self.begin_out()
            self.launch(stage, here)
            yield
            self.whole(stage, here)

    def begin_out(self):
        first, width = self.columns
        mine = self.held[tuple(self.place.here[:3])]
        self.out[:, pl.ds(first, width)] = mine.astype(jnp.float32)

    def drain(self):
        place = self.place
        spot = self.order.index(LINE)
        for stage in range(4):
            axis = self.order[stage]
            size, here = place.sizes[axis], place.here[axis]
            for line in range(place.sizes[LINE]) if stage < spot else [place.here[LINE]]:
                if size == 2:
                    self.copy(stage, line, 1 - here, 1 - 2 * here).wait_send()
                elif size > 2:
                    for along in range(size):
                        for step in (-1, 1):

                            @pl.when((along > here) if step > 0 else (along < here))
                            def _(along=along, step=step, line=line, stage=stage):
                                self.copy(stage, line, along, step).wait_send()


def scatter_kernel(sizes, parts, count, *refs):
    partials, outs = refs[:count], refs[count : 2 * count]
    load, send, recv = refs[2 * count : 2 * count + 3]
    scratch = list(refs[2 * count + 3 :])
    place = Place(sizes)
    place.greet()
    scatters = []
    for k, (which, columns, order) in enumerate(parts):
        held, *bufs = scratch[5 * k : 5 * k + 5]
        scatters.append(
            Scatter(place, k, order, partials[which], columns, held, bufs, outs[which], load, send, recv)
        )
    run_all([s.steps() for s in scatters])
    for s in scatters:
        s.drain()


def scatter_scratch(sizes, parts, shapes, dtype):
    scratch = []
    for which, (_, width), order in parts:
        rows = shapes[which][-2]
        scratch.append(pltpu.VMEM(sizes[:3] + (rows, width), dtype))
        stages = (CORE,) + order
        for stage, axis in enumerate(stages):
            free = tuple(sizes[a] for a in range(1, 3) if a not in stages[: stage + 1])
            slots = 1 if sizes[axis] <= 2 else sizes[axis] + 1
            if axis == LINE:
                lead = (slots,)
            else:
                lead = (1 if LINE in stages[:stage] else sizes[LINE], slots)
            scratch.append(pltpu.VMEM(lead + free + (rows, width), dtype))
    return scratch


def scatter_all(partials, parts, sizes, collective_id):
    count = 1
    for size in sizes:
        count *= size
    partials = [p.reshape(sizes + (p.shape[0] // count, p.shape[1])) for p in partials]
    lanes = max([1] + [size + 1 for size in sizes[1:] if size > 2])
    sems = (len(parts), 4, sizes[0] + 1, lanes)
    return pl.pallas_call(
        functools.partial(scatter_kernel, sizes, parts, len(partials)),
        out_shape=[jax.ShapeDtypeStruct(p.shape[4:], jnp.float32) for p in partials],
        in_specs=[pl.BlockSpec(memory_space=pl.ANY)] * len(partials),
        out_specs=[pl.BlockSpec(memory_space=pltpu.VMEM)] * len(partials),
        scratch_shapes=[
            pltpu.SemaphoreType.DMA((len(parts), sizes[0])),
            pltpu.SemaphoreType.DMA(sems),
            pltpu.SemaphoreType.DMA(sems),
        ]
        + scatter_scratch(sizes, parts, [p.shape for p in partials], partials[0].dtype),
        compiler_params=pltpu.CompilerParams(
            collective_id=collective_id, has_side_effects=True, vmem_limit_bytes=60 << 20
        ),
    )(*partials)


def partners_of(sizes):
    hops = []
    for axis in (2, 1, 0):
        stride = 1
        while stride < sizes[axis]:
            hops.append((axis, stride))
            stride *= 2
    return hops


def scan_kernel(
    sizes, backward, state_ref, logs_ref, out_ref,
    sib, sib_logs, first, first_logs, pre, pre_logs, total, total_logs, wire, wire_logs, got, got_logs, other, send, recv,
):
    place = Place(sizes)
    core = place.here[CORE]
    hops = partners_of(sizes)
    half = HEADS // 2
    mine, theirs = pl.ds(half * core, half), pl.ds(half * (1 - core), half)
    sibling = place.toward(CORE, 1 - 2 * core)

    def bit(axis, stride):
        return lax.rem(lax.div(place.here[axis], stride), 2)

    def partner(axis, stride):
        return place.toward(axis, (1 - 2 * bit(axis, stride)) * stride)

    barrier = pltpu.get_barrier_semaphore()
    for device in [sibling] + [partner(*hop) for hop in hops]:
        pl.semaphore_signal(barrier, inc=1, device_id=device, device_id_type=MESH)
    pl.semaphore_wait(barrier, 1 + len(hops))

    def remote(source, target, number, device):
        return pltpu.make_async_remote_copy(
            src_ref=source, dst_ref=target, send_sem=send.at[number], recv_sem=recv.at[number],
            device_id=device, device_id_type=MESH,
        )

    def scaled(logs, states, added):
        return [jnp.exp(logs[h, 0:1, :]) * states[h] + added[h] for h in range(half)]

    swap = [
        remote(state_ref.at[theirs], sib, 0, sibling),
        remote(logs_ref.at[theirs], sib_logs, 1, sibling),
    ]
    for copy in swap:
        copy.start()
    for copy in swap:
        copy.wait_recv()
    starts = core == (1 if backward else 0)

    @pl.when(starts)
    def _():
        first[...] = state_ref[mine]
        first_logs[...] = logs_ref[mine]
        new = scaled(sib_logs, first, sib)
        for h in range(half):
            total[h] = new[h]

    @pl.when(jnp.logical_not(starts))
    def _():
        first[...] = sib[...]
        first_logs[...] = sib_logs[...]
        new = scaled(logs_ref.at[mine], first, state_ref.at[mine])
        for h in range(half):
            total[h] = new[h]

    total_logs[...] = logs_ref[mine] + sib_logs[...]
    pre[...] = jnp.zeros_like(pre)
    pre_logs[...] = jnp.zeros_like(pre_logs)
    pending = list(swap)
    for k, (axis, stride) in enumerate(hops):
        last = k == len(hops) - 1
        wire[k] = total[...].astype(wire.dtype)
        wire_logs[k] = total_logs[...]
        copies = [
            remote(wire.at[k], got.at[k], 2 + 2 * k, partner(axis, stride)),
            remote(wire_logs.at[k], got_logs.at[k], 3 + 2 * k, partner(axis, stride)),
        ]
        for copy in copies:
            copy.start()
        pending += copies
        for copy in copies:
            copy.wait_recv()
        earlier = bit(axis, stride) == (1 if backward else 0)
        arrived = [got[k, h].astype(jnp.float32) for h in range(half)]

        @pl.when(jnp.logical_not(earlier))
        def _(k=k, arrived=arrived, last=last):
            new = scaled(pre_logs, arrived, pre)
            for h in range(half):
                pre[h] = new[h]
            pre_logs[...] = pre_logs[...] + got_logs[k]
            if not last:
                new = scaled(total_logs, arrived, total)
                for h in range(half):
                    total[h] = new[h]

        if not last:

            @pl.when(earlier)
            def _(k=k, arrived=arrived):
                new = scaled(got_logs.at[k], total, arrived)
                for h in range(half):
                    total[h] = new[h]

            total_logs[...] = total_logs[...] + got_logs[k]
    second = scaled(first_logs, pre, first)

    @pl.when(starts)
    def _():
        for h in range(half):
            other[h] = second[h]
        out_ref[mine] = pre[...]

    @pl.when(jnp.logical_not(starts))
    def _():
        other[...] = pre[...]
        for h in range(half):
            out_ref[half * core + h] = second[h]

    back = remote(other, out_ref.at[mine], 2 + 2 * len(hops), sibling)
    back.start()
    back.wait_recv()
    for copy in pending + [back]:
        copy.wait_send()


def entering(state, logs, sizes, backward, collective_id):
    half, hops = HEADS // 2, len(partners_of(sizes))
    block, tile = (half, HV, HK), (half, 8, HK)
    return pl.pallas_call(
        functools.partial(scan_kernel, sizes, backward),
        out_shape=jax.ShapeDtypeStruct(state.shape, jnp.float32),
        in_specs=[pl.BlockSpec(memory_space=pltpu.VMEM)] * 2,
        out_specs=pl.BlockSpec(memory_space=pltpu.VMEM),
        scratch_shapes=[
            pltpu.VMEM(block, jnp.float32), pltpu.VMEM(tile, jnp.float32),
            pltpu.VMEM(block, jnp.float32), pltpu.VMEM(tile, jnp.float32),
            pltpu.VMEM(block, jnp.float32), pltpu.VMEM(tile, jnp.float32),
            pltpu.VMEM(block, jnp.float32), pltpu.VMEM(tile, jnp.float32),
            pltpu.VMEM((hops,) + block, jnp.bfloat16), pltpu.VMEM((hops,) + tile, jnp.float32),
            pltpu.VMEM((hops,) + block, jnp.bfloat16), pltpu.VMEM((hops,) + tile, jnp.float32),
            pltpu.VMEM(block, jnp.float32),
            pltpu.SemaphoreType.DMA((3 + 2 * hops,)),
            pltpu.SemaphoreType.DMA((3 + 2 * hops,)),
        ],
        compiler_params=pltpu.CompilerParams(
            collective_id=collective_id, has_side_effects=True, vmem_limit_bytes=32 << 20
        ),
    )(state, logs)


CHUNK = 128
ROWS = 256
FTILE = 256
F32, BF16 = jnp.float32, jnp.bfloat16


def nn(left, right):
    return jnp.dot(left, right, preferred_element_type=F32)


def nt(left, right):
    return lax.dot_general(left, right, (((1,), (1,)), ((), ())), preferred_element_type=F32)


def tn(left, right):
    return lax.dot_general(left, right, (((0,), (0,)), ((), ())), preferred_element_type=F32)


def sigmoid(v):
    return 1.0 / (1.0 + jnp.exp(-v))


def causal_mask(size):
    return lax.broadcasted_iota(jnp.int32, (size, size), 0) >= lax.broadcasted_iota(jnp.int32, (size, size), 1)


def triangle(upper):
    rows = lax.broadcasted_iota(jnp.int32, (CHUNK, CHUNK), 0)
    columns = lax.broadcasted_iota(jnp.int32, (CHUNK, CHUNK), 1)
    kept = (columns >= rows) if upper else (columns <= rows)
    return jnp.where(kept, 1.0, 0.0).astype(BF16)


def running(matrix, values):
    high = values.astype(BF16)
    low = (values - high.astype(F32)).astype(BF16)
    return nn(matrix, high) + nn(matrix, low)


def inverse_rms(values):
    return lax.rsqrt(jnp.mean(values * values, axis=-1, keepdims=True) + 1e-06)


def heads_of(width):
    return [slice(h * width, (h + 1) * width) for h in range(HEADS)]


def project_kernel(
    tokens, gain, weights, down, up, bias,
    normed_ref, query_ref, key_ref, value_ref, gate_ref, mid_ref, logit_ref, within_ref, update_ref, final_ref, logs_ref,
):
    @pl.when(pl.program_id(0) == 0)
    def _():
        final_ref[...] = jnp.zeros_like(final_ref)
        logs_ref[...] = jnp.zeros_like(logs_ref)

    inputs = tokens[...].astype(F32)
    normed = (inputs * inverse_rms(inputs) * gain[...]).astype(BF16)
    normed_ref[...] = normed
    keys = HEADS * HK
    values = HEADS * HV
    mid = nn(normed, down[...]).astype(BF16)
    mid_ref[...] = mid
    logit = nn(mid, up[...]) + bias[...]
    logit_ref[...] = logit
    query_ref[...] = nn(normed, weights[:, :keys]).astype(BF16)
    key_ref[...] = nn(normed, weights[:, keys : 2 * keys]).astype(BF16)
    value_ref[...] = nn(normed, weights[:, 2 * keys : 2 * keys + values]).astype(BF16)
    gate_ref[...] = nn(normed, weights[:, 2 * keys + values :]).astype(BF16)
    decay = (jnp.minimum(logit, 0.0) - jnp.log1p(jnp.exp(-jnp.abs(logit)))) * (1.0 / 16.0)
    lower = triangle(False)
    for c in range(ROWS // CHUNK):
        rows = slice(c * CHUNK, (c + 1) * CHUNK)
        within = running(lower, decay[rows])
        within_ref[rows] = within
        total = within[CHUNK - 1 : CHUNK]
        ending = (key_ref[rows].astype(F32) * jnp.exp(total - within)).astype(BF16)
        for h, (ks, vs) in enumerate(zip(heads_of(HK), heads_of(HV))):
            update = tn(value_ref[rows, vs], ending[:, ks])
            update_ref[c, h] = update.astype(BF16)
            final_ref[h] = final_ref[h] * jnp.exp(total[:, ks]) + update
            logs_ref[h] = logs_ref[h] + total[:, ks]


def mix_kernel(
    tokens, query, key, value, gate, within_all, update, entering_ref, head_gain, out_weight, ffn_gain,
    mixed_ref, gated_ref, hidden_ref, ffn_ref, starts_ref, state,
):
    @pl.when(pl.program_id(0) == 0)
    def _():
        state[...] = entering_ref[...]

    mask = causal_mask(CHUNK)
    for c in range(ROWS // CHUNK):
        rows = slice(c * CHUNK, (c + 1) * CHUNK)
        within = within_all[rows]
        middle = within[CHUNK // 2 - 1 : CHUNK // 2]
        total = within[CHUNK - 1 : CHUNK]
        scaled = query[rows].astype(F32) * HK**-0.5
        from_start = (scaled * jnp.exp(within)).astype(BF16)
        left = (scaled * jnp.exp(within - middle)).astype(BF16)
        right = (key[rows].astype(F32) * jnp.exp(middle - within)).astype(BF16)
        for h, (ks, vs) in enumerate(zip(heads_of(HK), heads_of(HV))):
            start = state[h].astype(BF16)
            starts_ref[c, h] = start
            scores = jnp.where(mask, nt(left[:, ks], right[:, ks]), 0.0).astype(BF16)
            mixed = nn(scores, value[rows, vs]) + nt(from_start[:, ks], start)
            state[h] = state[h] * jnp.exp(total[:, ks]) + update[c, h].astype(F32)
            mixed_ref[rows, vs] = mixed.astype(BF16)
            gates = gate[rows, vs].astype(F32)
            gated = mixed * inverse_rms(mixed) * head_gain[:, vs] * (gates * sigmoid(gates))
            gated_ref[rows, vs] = gated.astype(BF16)
    hidden = tokens[...].astype(F32) + nn(gated_ref[...], out_weight[...])
    hidden_ref[...] = hidden
    ffn_ref[...] = (hidden * inverse_rms(hidden) * ffn_gain[...]).astype(BF16)


def ffn_kernel(
    ffn_in, ffn_in_t, cotangent, hidden, gate_weight, up_weight, down_weight,
    out_ref, back_ref, gate_grad, up_grad, down_grad,
):
    @pl.when(pl.program_id(0) == 0)
    def _():
        out_ref[...] = hidden[...]
        back_ref[...] = jnp.zeros_like(back_ref)

    gate, up = nn(ffn_in[...], gate_weight[...]), nn(ffn_in[...], up_weight[...])
    back = nt(cotangent[...], down_weight[...])
    share = sigmoid(gate)
    passed = gate * share
    inner = (passed * up).astype(BF16)
    d_up = (back * passed).astype(BF16)
    d_gate = (back * up * (share * (1.0 + gate * (1.0 - share)))).astype(BF16)
    out_ref[...] += nn(inner, down_weight[...])
    back_ref[...] += nt(d_gate, gate_weight[...]) + nt(d_up, up_weight[...])
    gate_grad[...] = nn(ffn_in_t[...], d_gate).astype(BF16)
    up_grad[...] = nn(ffn_in_t[...], d_up).astype(BF16)
    down_grad[...] = tn(inner, cotangent[...]).astype(BF16)


def norm_back(values, gain, grad):
    scale = inverse_rms(values)
    inner = grad * gain
    along = jnp.mean(inner * values, axis=-1, keepdims=True)
    return scale * inner - values * (scale * scale * scale * along), grad * values * scale


def unmix_kernel(
    ffn_back, hidden, cotangent, gate, mixed, query, within_all, head_gain, out_weight, ffn_gain,
    d_hidden_ref, low_ref, d_gate_ref, d_mixed_ref, update_ref, enters_ref, ffn_gain_ref, head_gain_ref,
):
    @pl.when(pl.program_id(0) == 0)
    def _():
        enters_ref[...] = jnp.zeros_like(enters_ref)
        ffn_gain_ref[...] = jnp.zeros_like(ffn_gain_ref)
        head_gain_ref[...] = jnp.zeros_like(head_gain_ref)

    through, terms = norm_back(hidden[...], ffn_gain[...], ffn_back[...])
    ffn_gain_ref[...] += jnp.sum(terms, axis=0, keepdims=True)
    d_hidden = cotangent[...].astype(F32) + through
    d_hidden_ref[...] = d_hidden
    low = d_hidden.astype(BF16)
    low_ref[...] = low
    d_gated = nt(low, out_weight[...])
    for vs in heads_of(HV):
        value = mixed[:, vs].astype(F32)
        scale = inverse_rms(value)
        headed = value * scale
        gates = gate[:, vs].astype(F32)
        share = sigmoid(gates)
        passed = gates * share
        grad, gain = d_gated[:, vs], head_gain[:, vs]
        head_gain_ref[:, vs] += jnp.sum(grad * headed * passed, axis=0, keepdims=True)
        d_gate_ref[:, vs] = (grad * headed * gain * (share * (1.0 + gates * (1.0 - share)))).astype(BF16)
        d_headed = grad * gain * passed
        along = jnp.mean(d_headed * headed, axis=-1, keepdims=True)
        d_mixed_ref[:, vs] = (scale * (d_headed - headed * along)).astype(BF16)
    for c in reversed(range(ROWS // CHUNK)):
        rows = slice(c * CHUNK, (c + 1) * CHUNK)
        within = within_all[rows]
        total = within[CHUNK - 1 : CHUNK]
        from_start = (query[rows].astype(F32) * HK**-0.5 * jnp.exp(within)).astype(BF16)
        for h, (ks, vs) in enumerate(zip(heads_of(HK), heads_of(HV))):
            update = tn(d_mixed_ref[rows, vs], from_start[:, ks])
            update_ref[c, h] = update.astype(BF16)
            enters_ref[h] = enters_ref[h] * jnp.exp(total[:, ks]) + update


def back_kernel(
    tokens, query, key, value, logit, within_all, d_mixed, starts, update, leaving_ref, d_gate, d_hidden,
    gain, weights, down, up,
    d_qkv_ref, d_logit_ref, d_mid_ref, tokens_grad_ref, gain_ref, bias_ref, state,
):
    @pl.when(pl.program_id(0) == 0)
    def _():
        state[...] = leaving_ref[...]
        gain_ref[...] = jnp.zeros_like(gain_ref)
        bias_ref[...] = jnp.zeros_like(bias_ref)

    mask = causal_mask(CHUNK)
    upper = triangle(True)
    keys = HEADS * HK
    for c in reversed(range(ROWS // CHUNK)):
        rows = slice(c * CHUNK, (c + 1) * CHUNK)
        within = within_all[rows]
        middle = within[CHUNK // 2 - 1 : CHUNK // 2]
        total = within[CHUNK - 1 : CHUNK]
        factor = jnp.exp(total)
        queries, keys_f = query[rows].astype(F32), key[rows].astype(F32)
        q_start, q_middle = jnp.exp(within) * HK**-0.5, jnp.exp(within - middle) * HK**-0.5
        k_middle, k_end = jnp.exp(middle - within), jnp.exp(total - within)
        left = (queries * q_middle).astype(BF16)
        right = (keys_f * k_middle).astype(BF16)
        ending = (keys_f * k_end).astype(BF16)
        moves, extras = [], []
        for h, (ks, vs) in enumerate(zip(heads_of(HK), heads_of(HV))):
            start, after = starts[c, h], state[h].astype(BF16)
            grad, values = d_mixed[rows, vs], value[rows, vs]
            scores = jnp.where(mask, nt(left[:, ks], right[:, ks]), 0.0).astype(BF16)
            d_scores = jnp.where(mask, nt(grad, values), 0.0).astype(BF16)
            d_value = tn(scores, grad) + nt(ending[:, ks], after)
            d_query = nn(d_scores, right[:, ks]) * q_middle[:, ks] + nn(grad, start) * q_start[:, ks]
            d_end = nn(values, after) * k_end[:, ks]
            d_key = tn(d_scores, left[:, ks]) * k_middle[:, ks] + d_end
            d_qkv_ref[rows, ks] = d_query.astype(BF16)
            d_qkv_ref[rows, slice(keys + ks.start, keys + ks.stop)] = d_key.astype(BF16)
            d_qkv_ref[rows, slice(2 * keys + vs.start, 2 * keys + vs.stop)] = d_value.astype(BF16)
            moves.append(queries[:, ks] * d_query - keys_f[:, ks] * d_key)
            extras.append(
                jnp.sum(keys_f[:, ks] * d_end, axis=0, keepdims=True)
                + factor[:, ks] * jnp.sum(start.astype(F32) * state[h], axis=0, keepdims=True)
            )
            state[h] = state[h] * factor[:, ks] + update[c, h].astype(F32)
        d_decay = running(upper, jnp.concatenate(moves, axis=1)) + jnp.concatenate(extras, axis=1)
        d_logit = d_decay * sigmoid(-logit[rows]) * (1.0 / 16.0)
        bias_ref[...] += jnp.sum(d_logit, axis=0, keepdims=True)
        d_logit_ref[rows] = d_logit.astype(BF16)
    d_mid = nt(d_logit_ref[...], up[...]).astype(BF16)
    d_mid_ref[...] = d_mid
    inner = 2 * keys + HEADS * HV
    d_normed = (
        nt(d_qkv_ref[...], weights[:, :inner]) + nt(d_gate[...], weights[:, inner:]) + nt(d_mid, down[...])
    )
    through, terms = norm_back(tokens[...].astype(F32), gain[...], d_normed)
    gain_ref[...] += jnp.sum(terms, axis=0, keepdims=True)
    tokens_grad_ref[...] = d_hidden[...] + through


def rows_spec(width, steps, backward):
    return pl.BlockSpec((ROWS, width), (lambda i: (steps - 1 - i, 0)) if backward else (lambda i: (i, 0)))


def chunks_spec(steps, backward):
    return pl.BlockSpec(
        (ROWS // CHUNK, HEADS, HV, HK),
        (lambda i: (steps - 1 - i, 0, 0, 0)) if backward else (lambda i: (i, 0, 0, 0)),
    )


def kept_spec(shape):
    return pl.BlockSpec(shape, lambda i: (0,) * len(shape), pipeline_mode=pl.Buffered(1))


def kept_out(shape):
    return pl.BlockSpec(shape, lambda i: (0,) * len(shape))


PARAMS = dict(vmem_limit_bytes=60 << 20)
STATE = (HEADS, HV, HK)


def project(tokens, gain, weights, down, up, bias):
    length, width = tokens.shape
    steps, keys, values = length // ROWS, HEADS * HK, HEADS * HV
    row = lambda w: rows_spec(w, steps, False)
    chunks = (length // CHUNK,) + STATE
    shape = jax.ShapeDtypeStruct
    return pl.pallas_call(
        project_kernel,
        grid=(steps,),
        in_specs=[row(width)] + [kept_spec(a.shape) for a in (gain, weights, down, up, bias)],
        out_specs=[row(w) for w in (width, keys, keys, values, values, down.shape[1], keys, keys)]
        + [chunks_spec(steps, False), kept_out(STATE), kept_out((HEADS, 8, HK))],
        out_shape=[shape((length, w), BF16) for w in (width, keys, keys, values, values, down.shape[1])]
        + [shape((length, keys), F32)] * 2
        + [shape(chunks, BF16), shape(STATE, F32), shape((HEADS, 8, HK), F32)],
        compiler_params=pltpu.CompilerParams(**PARAMS),
    )(tokens, gain, weights, down, up, bias)


def mix(tokens, query, key, value, gate, within, update, entered, head_gain, out_weight, ffn_gain):
    length, width = tokens.shape
    steps, keys, values = length // ROWS, HEADS * HK, HEADS * HV
    row = lambda w: rows_spec(w, steps, False)
    shape = jax.ShapeDtypeStruct
    return pl.pallas_call(
        mix_kernel,
        grid=(steps,),
        in_specs=[row(w) for w in (width, keys, keys, values, values, keys)]
        + [chunks_spec(steps, False)]
        + [kept_spec(a.shape) for a in (entered, head_gain, out_weight, ffn_gain)],
        out_specs=[row(w) for w in (values, values, width, width)] + [chunks_spec(steps, False)],
        out_shape=[
            shape((length, values), BF16), shape((length, values), BF16),
            shape((length, width), F32), shape((length, width), BF16), shape(update.shape, BF16),
        ],
        scratch_shapes=[pltpu.VMEM(STATE, F32)],
        compiler_params=pltpu.CompilerParams(**PARAMS),
    )(tokens, query, key, value, gate, within, update, entered, head_gain, out_weight, ffn_gain)


def feed_forward(ffn_in, cotangent, hidden, gate_weight, up_weight, down_weight):
    length, width = ffn_in.shape
    inner = gate_weight.shape[1]
    whole = [ffn_in, ffn_in.T, cotangent, hidden]
    wide = pl.BlockSpec((width, FTILE), lambda i: (0, i))
    tall = pl.BlockSpec((FTILE, width), lambda i: (i, 0))
    shape = jax.ShapeDtypeStruct
    return pl.pallas_call(
        ffn_kernel,
        grid=(inner // FTILE,),
        in_specs=[kept_spec(a.shape) for a in whole] + [wide, wide, tall],
        out_specs=[kept_out((length, width))] * 2 + [wide, wide, tall],
        out_shape=[shape((length, width), F32)] * 2
        + [shape((width, inner), BF16)] * 2 + [shape((inner, width), BF16)],
        compiler_params=pltpu.CompilerParams(**PARAMS),
    )(*whole, gate_weight, up_weight, down_weight)


def unmix(ffn_back, hidden, cotangent, gate, mixed, query, within, head_gain, out_weight, ffn_gain):
    length, width = hidden.shape
    steps, keys, values = length // ROWS, HEADS * HK, HEADS * HV
    row = lambda w: rows_spec(w, steps, True)
    chunks = (length // CHUNK,) + STATE
    shape = jax.ShapeDtypeStruct
    return pl.pallas_call(
        unmix_kernel,
        grid=(steps,),
        in_specs=[row(w) for w in (width, width, width, values, values, keys, keys)]
        + [kept_spec(a.shape) for a in (head_gain, out_weight, ffn_gain)],
        out_specs=[row(w) for w in (width, width, values, values)]
        + [chunks_spec(steps, True), kept_out(STATE), kept_out((1, width)), kept_out((1, values))],
        out_shape=[
            shape((length, width), F32), shape((length, width), BF16), shape((length, values), BF16),
            shape((length, values), BF16), shape(chunks, BF16), shape(STATE, F32),
            shape((1, width), F32), shape((1, values), F32),
        ],
        compiler_params=pltpu.CompilerParams(**PARAMS),
    )(ffn_back, hidden, cotangent, gate, mixed, query, within, head_gain, out_weight, ffn_gain)


def back(tokens, query, key, value, logit, within, d_mixed, starts, update, leaving, d_gate, d_hidden, gain, weights, down, up):
    length, width = tokens.shape
    steps, keys, values = length // ROWS, HEADS * HK, HEADS * HV
    row = lambda w: rows_spec(w, steps, True)
    shape = jax.ShapeDtypeStruct
    inner = 2 * keys + values
    return pl.pallas_call(
        back_kernel,
        grid=(steps,),
        in_specs=[row(w) for w in (width, keys, keys, values, keys, keys, values)]
        + [chunks_spec(steps, True)] * 2 + [kept_spec(leaving.shape), row(values), row(width)]
        + [kept_spec(a.shape) for a in (gain, weights, down, up)],
        out_specs=[row(w) for w in (inner, keys, down.shape[1], width)] + [kept_out((1, width)), kept_out((1, keys))],
        out_shape=[
            shape((length, inner), BF16), shape((length, keys), BF16), shape((length, down.shape[1]), BF16),
            shape((length, width), F32), shape((1, width), F32), shape((1, keys), F32),
        ],
        scratch_shapes=[pltpu.VMEM(STATE, F32)],
        compiler_params=pltpu.CompilerParams(**PARAMS),
    )(tokens, query, key, value, logit, within, d_mixed, starts, update, leaving, d_gate, d_hidden, gain, weights, down, up)


PARTS = (
    (0, (0, 128), ORDERS[0]),
    (1, (0, 1024), ORDERS[0]),
    (1, (1024, 1024), ORDERS[1]),
    (1, (2048, 1024), ORDERS[2]),
    (2, (0, 1024), ORDERS[3]),
    (3, (0, 2816), ORDERS[0]),
    (4, (0, 2816), ORDERS[1]),
    (5, (0, 512), ORDERS[2]),
    (5, (512, 512), ORDERS[3]),
)
BACK_PARTS = tuple((which, columns, order[::-1]) for which, columns, order in PARTS)
TILE = (16, 128)


def packed(pieces):
    count = pieces[0].shape[0]
    flat = jnp.concatenate([p.reshape(count, -1) for p in pieces], axis=1)
    flat = jnp.pad(flat, ((0, 0), (0, TILE[0] * TILE[1] - flat.shape[1])))
    return flat.reshape(count * TILE[0], TILE[1])


def unpacked(tiles, shapes):
    count = tiles.shape[0] // TILE[0]
    flat = tiles.reshape(count, TILE[0] * TILE[1])
    out, at = [], 0
    for shape in shapes:
        size = 1
        for extent in shape:
            size *= extent
        out.append(flat[:, at : at + size].reshape((count,) + shape))
        at += size
    return out


def local(
    tokens,
    norm_gain,
    query_weight,
    key_weight,
    value_weight,
    gate_weight,
    rank_down,
    rank_up,
    gate_bias,
    head_gain,
    out_weight,
    ffn_gain,
    ffn_gate,
    ffn_up,
    ffn_down,
    cotangent,
):
    count = lax.axis_size("seq")
    sizes = grid_of(count)
    small = (norm_gain, rank_down, rank_up, gate_bias, head_gain, ffn_gain)
    shapes = [s.shape for s in small]
    projections = jnp.concatenate([query_weight, key_weight, value_weight, gate_weight], axis=1)
    tiles, full_proj, full_out, full_fgate, full_fup, full_fdown = gather_all(
        [packed([s[None] for s in small]), projections, out_weight, ffn_gate, ffn_up, ffn_down], PARTS, sizes, 0
    )
    pieces = unpacked(tiles, shapes)
    full_gain, full_bias, full_head_gain, full_ffn_gain = (pieces[k].reshape(-1) for k in (0, 3, 4, 5))
    full_down_rank = pieces[1].reshape(-1, rank_down.shape[1])
    full_up_rank = pieces[2].transpose(1, 0, 2).reshape(rank_up.shape[0], -1)
    gain, heads_gain, ffn_gains, bias = (
        v.astype(F32).reshape(1, -1) for v in (full_gain, full_head_gain, full_ffn_gain, full_bias)
    )
    rank = rank_down.shape[1]
    down = jnp.pad(full_down_rank, ((0, 0), (0, 128 - rank)))
    up = jnp.pad(full_up_rank, ((0, 128 - rank), (0, 0)))
    normed, query, key, value, gate, mid, logit, within, update, final, logs = project(
        tokens, gain, full_proj, down, up, bias
    )
    incoming = entering(final, logs, sizes, False, 2)
    mixed, gated, hidden, ffn_in, starts = mix(
        tokens, query, key, value, gate, within, update, incoming, heads_gain, full_out, ffn_gains
    )
    block_output, ffn_back, fgate_wgrad, fup_wgrad, fdown_wgrad = feed_forward(
        ffn_in, cotangent, hidden, full_fgate, full_fup, full_fdown
    )
    d_hidden, hidden_low, d_gate, d_mixed, back_update, enters, ffn_gain_grad, head_gain_grad = unmix(
        ffn_back, hidden, cotangent, gate, mixed, query, within, heads_gain, full_out, ffn_gains
    )
    leaving = entering(enters, logs, sizes, True, 3)
    d_qkv, d_logit, d_mid, tokens_grad, gain_grad, bias_grad = back(
        tokens, query, key, value, logit, within, d_mixed, starts, back_update, leaving, d_gate, d_hidden,
        gain, full_proj, down, up,
    )
    proj_wgrad = jnp.concatenate([tn(normed, d_qkv).astype(BF16), tn(normed, d_gate).astype(BF16)], axis=1)
    out_wgrad = tn(gated, hidden_low).astype(BF16)
    down_rank_grad = tn(normed, d_mid)[:, :rank]
    up_rank_grad = tn(mid, d_logit)[:rank]
    tiles = packed(
        [
            gain_grad.reshape(count, -1),
            down_rank_grad.reshape(count, -1),
            up_rank_grad.reshape(rank, count, -1).transpose(1, 0, 2),
            bias_grad.reshape(count, -1),
            head_gain_grad.reshape(count, -1),
            ffn_gain_grad.reshape(count, -1),
        ]
    ).astype(BF16)
    summed = scatter_all(
        [tiles, proj_wgrad, out_wgrad, fgate_wgrad, fup_wgrad, fdown_wgrad], BACK_PARTS, sizes, 1
    )
    gain_sum, down_sum, up_sum, bias_sum, head_sum, ffn_sum = [p[0] for p in unpacked(summed[0], shapes)]
    proj_sum, keys = summed[1], HEADS * HK
    return (
        block_output,
        tokens_grad,
        gain_sum,
        proj_sum[:, :keys],
        proj_sum[:, keys : 2 * keys],
        proj_sum[:, 2 * keys : 2 * keys + HEADS * HV],
        proj_sum[:, 2 * keys + HEADS * HV :],
        down_sum,
        up_sum,
        bias_sum,
        head_sum,
        summed[2],
        ffn_sum,
        summed[3],
        summed[4],
        summed[5],
    )


def solution(mesh):
    return jax.shard_map(
        local,
        mesh=mesh,
        in_specs=(
            P("seq", None),
            P("seq"),
            P("seq", None),
            P("seq", None),
            P("seq", None),
            P("seq", None),
            P("seq", None),
            P(None, "seq"),
            P("seq"),
            P("seq"),
            P("seq", None),
            P("seq"),
            P("seq", None),
            P("seq", None),
            P("seq", None),
            P("seq", None),
        ),
        out_specs=(
            P("seq", None),
            P("seq", None),
            P("seq"),
            P("seq", None),
            P("seq", None),
            P("seq", None),
            P("seq", None),
            P("seq", None),
            P(None, "seq"),
            P("seq"),
            P("seq"),
            P("seq", None),
            P("seq"),
            P("seq", None),
            P("seq", None),
            P("seq", None),
        ),
        check_vma=False,
    )
```

```python
import functools

import jax
import jax.numpy as jnp
from jax import lax
from jax.experimental import pallas as pl
from jax.experimental.pallas import tpu as pltpu
from jax.sharding import PartitionSpec as P

HEADS = 4
HK = 128
HV = 256
RANK = 16

MESH = pl.DeviceIdType.MESH
LINE = 0
CORE = 3


def grid_of(count):
    core = 2 if count % 2 == 0 else 1
    rest = count // core
    third = max(k for k in range(1, rest + 1) if rest % k == 0 and k**3 <= rest)
    rest //= third
    second = max(k for k in range(1, rest + 1) if rest % k == 0 and k * k <= rest)
    return (rest // second, second, third, core)


class Place:
    def __init__(self, sizes):
        self.sizes = sizes
        rest = lax.axis_index("seq")
        here = []
        for size in sizes[::-1]:
            here.append(lax.rem(rest, size))
            rest = lax.div(rest, size)
        self.here = here[::-1]

    def index(self, **moved):
        out = 0
        for axis, size in enumerate(self.sizes):
            out = out * size + moved.get(f"a{axis}", self.here[axis])
        return out

    def toward(self, axis, step):
        return (self.index(**{f"a{axis}": self.here[axis] + step}),)

    def can(self, axis, step):
        return self.here[axis] > 0 if step < 0 else self.here[axis] < self.sizes[axis] - 1

    def bit(self, axis, stride):
        return lax.rem(lax.div(self.here[axis], stride), 2)

    def partner(self, axis, stride):
        return self.toward(axis, (1 - 2 * self.bit(axis, stride)) * stride)

    def greet(self, hops=()):
        barrier = pltpu.get_barrier_semaphore()
        total = 0
        for axis, stride in hops:
            if stride > 1:
                pl.semaphore_signal(barrier, inc=1, device_id=self.partner(axis, stride), device_id_type=MESH)
                total = total + 1
        for axis, size in enumerate(self.sizes):
            for step in (-1, 1):
                if size == 1:
                    continue
                able = self.can(axis, step)

                @pl.when(able)
                def _(axis=axis, step=step):
                    pl.semaphore_signal(
                        barrier, inc=1, device_id=self.toward(axis, step), device_id_type=MESH
                    )

                total = total + able.astype(jnp.int32)
        pl.semaphore_wait(barrier, total)


def run_all(coroutines):
    active = list(coroutines)
    while active:
        still = []
        for coroutine in active:
            try:
                next(coroutine)
                still.append(coroutine)
            except StopIteration:
                pass
        active = still


class Gather:
    def __init__(self, place, part, order, buffer, columns, send, recv):
        self.place, self.part, self.order = place, part, order + (CORE,)
        self.buffer, self.columns, self.send, self.recv = buffer, columns, send, recv

    def copy(self, stage, line, along, step):
        place, axis = self.place, self.order[stage]
        where = []
        for a in range(4):
            if a == axis:
                where.append(along)
            elif a == LINE and LINE in self.order[:stage]:
                where.append(line)
            elif a in self.order[:stage]:
                where.append(slice(None))
            else:
                where.append(place.here[a])
        first, width = self.columns
        block = self.buffer.at[tuple(where) + (slice(None), pl.ds(first, width))]
        lane = 0 if place.sizes[axis] == 2 and axis != LINE else along
        if axis == LINE:
            line, lane = along, 0
        return pltpu.make_async_remote_copy(
            src_ref=block,
            dst_ref=block,
            send_sem=self.send.at[self.part, stage, line, lane, (step + 1) // 2],
            recv_sem=self.recv.at[self.part, stage, line, lane],
            device_id=place.toward(axis, step),
            device_id_type=MESH,
        )

    def each_step(self, stage, do):
        axis, place = self.order[stage], self.place
        if place.sizes[axis] == 1:
            return
        if place.sizes[axis] == 2 and axis != LINE:
            do(1 - 2 * place.here[axis], None)
            return
        for step in (-1, 1):
            do(step, place.can(axis, step))

    def launch(self, stage, line):
        axis, place = self.order[stage], self.place

        def do(step, able):
            def go():
                self.copy(stage, line, place.here[axis], step).start()

            go() if able is None else pl.when(able)(go)

        self.each_step(stage, do)

    def finish(self, stage, line):
        axis, place = self.order[stage], self.place
        size, here = place.sizes[axis], place.here[axis]
        if size == 1:
            return
        if size == 2:
            self.copy(stage, line, 1 - here, 1 - 2 * here).wait_recv()
            return
        for hop in range(1, size):
            for step in (-1, 1):
                along = here - step * hop
                valid = (along >= 0) & (along < size)

                @pl.when(valid)
                def _(along=along, step=step):
                    self.copy(stage, line, along, step).wait_recv()

                @pl.when(valid & place.can(axis, step))
                def _(along=along, step=step):
                    self.copy(stage, line, along, step).start()

    def steps(self):
        place = self.place
        size, here = place.sizes[LINE], place.here[LINE]
        spot = self.order.index(LINE)
        for stage in range(spot):
            self.launch(stage, here)
            yield
            self.finish(stage, here)
        for step in (-1, 1):

            @pl.when(place.can(LINE, step))
            def _(step=step):
                self.copy(spot, here, here, step).start()

        later = list(range(spot + 1, 4))
        for turn in range(size + len(later)):
            for age in range(min(turn, len(later)), -1, -1):
                far = turn - age
                if far >= size:
                    continue
                for step in (-1, 1) if far else (1,):
                    line = here - step * far
                    valid = (line >= 0) & (line < size)

                    def advance(line=line, step=step, far=far, age=age):
                        if age == 0 and far:
                            self.copy(spot, line, line, step).wait_recv()

                            @pl.when(place.can(LINE, step))
                            def _():
                                self.copy(spot, line, line, step).start()

                        if age:
                            self.finish(later[age - 1], line)
                        if age < len(later):
                            self.launch(later[age], line)

                    pl.when(valid)(advance) if far else advance()
            yield

    def drain(self):
        place = self.place
        size, here = place.sizes[LINE], place.here[LINE]
        spot = self.order.index(LINE)
        for line in range(size):
            for step in (-1, 1):

                @pl.when(place.can(LINE, step) & ((line <= here) if step > 0 else (line >= here)))
                def _(line=line, step=step):
                    self.copy(spot, line, line, step).wait_send()

        for stage in range(4):
            if stage == spot:
                continue
            axis = self.order[stage]
            lines = [here] if stage < spot else list(range(size))
            for line in lines:
                if place.sizes[axis] == 1:
                    continue
                if place.sizes[axis] == 2:
                    self.copy(stage, line, place.here[axis], 1 - 2 * place.here[axis]).wait_send()
                    continue
                for step in (-1, 1):
                    for along in range(place.sizes[axis]):
                        at = place.here[axis]

                        @pl.when(place.can(axis, step) & ((along <= at) if step > 0 else (along >= at)))
                        def _(line=line, step=step, along=along, stage=stage):
                            self.copy(stage, line, along, step).wait_send()


ORDERS = ((2, 0, 1), (1, 0, 2), (0, 2, 1), (0, 1, 2))


def gather_kernel(sizes, parts, count, *refs):
    shards, buffers = refs[:count], refs[count : 2 * count]
    send, recv, own = refs[2 * count :]
    place = Place(sizes)
    locals_ = [
        pltpu.make_async_copy(shard, buffer.at[tuple(place.here)], own.at[k])
        for k, (shard, buffer) in enumerate(zip(shards, buffers))
    ]
    for copy in locals_:
        copy.start()
    place.greet()
    for copy in locals_:
        copy.wait()
    gathers = [
        Gather(place, k, order, buffers[which], columns, send, recv)
        for k, (which, columns, order) in enumerate(parts)
    ]
    run_all([g.steps() for g in gathers])
    for g in gathers:
        g.drain()


def lanes_of(sizes):
    return max([1] + [size for size in sizes[1:] if size > 2])


def gather_all(shards, parts, sizes, collective_id):
    lanes = lanes_of(sizes)
    out = pl.pallas_call(
        functools.partial(gather_kernel, sizes, parts, len(shards)),
        out_shape=[jax.ShapeDtypeStruct(sizes + s.shape, s.dtype) for s in shards],
        in_specs=[pl.BlockSpec(memory_space=pltpu.VMEM)] * len(shards),
        out_specs=[pl.BlockSpec(memory_space=pl.ANY)] * len(shards),
        scratch_shapes=[
            pltpu.SemaphoreType.DMA((len(parts), 4, sizes[0], lanes, 2)),
            pltpu.SemaphoreType.DMA((len(parts), 4, sizes[0], lanes)),
            pltpu.SemaphoreType.DMA((len(shards),)),
        ],
        compiler_params=pltpu.CompilerParams(collective_id=collective_id, has_side_effects=True),
    )(*shards)
    return [o.reshape((-1,) + o.shape[5:]) for o in out]


class Scatter:
    def __init__(self, place, part, order, partial, columns, held, bufs, out, load, send, recv):
        self.place, self.part, self.order = place, part, (CORE,) + order
        self.partial, self.columns, self.held, self.bufs, self.out = partial, columns, held, bufs, out
        self.load, self.send, self.recv = load, send, recv

    def own(self, line):
        first, width = self.columns
        where = (line, slice(None), slice(None), self.place.here[CORE], slice(None), pl.ds(first, width))
        return pltpu.make_async_copy(self.partial.at[where], self.held.at[line], self.load.at[self.part, line])

    def block(self, stage, line, along):
        where, done = [], self.order[:stage]
        for a in range(3):
            if a == self.order[stage]:
                where.append(along)
            elif a in done:
                where.append(self.place.here[a])
            elif a == LINE:
                where.append(line)
            else:
                where.append(slice(None))
        return tuple(where)

    def slot(self, stage, line, slot):
        axis = self.order[stage]
        if axis == LINE:
            return (slot,)
        if LINE in self.order[:stage]:
            line = 0
        return (line, 0 if self.place.sizes[axis] == 2 else slot)

    def copy(self, stage, line, along, step):
        place, axis = self.place, self.order[stage]
        size = place.sizes[axis]
        first, width = self.columns
        if axis == CORE:
            where = (line, slice(None), slice(None), along, slice(None), pl.ds(first, width))
            source = self.partial.at[where]
        else:
            source = self.held.at[self.block(stage, line, along)]
        arrives = place.here[axis] + step == along
        number = jnp.where(arrives & (step < 0), size, along) if size > 2 else 0
        sem = self.slot(stage, line, along)
        if axis == LINE:
            sem = sem + (0,)
        there = self.slot(stage, line, number)
        return pltpu.make_async_remote_copy(
            src_ref=source,
            dst_ref=self.bufs[stage].at[there],
            send_sem=self.send.at[(self.part, stage) + sem],
            recv_sem=self.recv.at[(self.part, stage) + there + ((0,) if axis == LINE else ())],
            device_id=place.toward(axis, step),
            device_id_type=MESH,
        )

    def wait(self, stage, line, number):
        there = self.slot(stage, line, number)
        buf = self.bufs[stage].at[there]
        axis = self.order[stage]
        pltpu.make_async_copy(
            buf, buf, self.recv.at[(self.part, stage) + there + ((0,) if axis == LINE else ())]
        ).wait()
        return self.bufs[stage], there

    def add(self, stage, line, along, number, last=False):
        buf, there = self.wait(stage, line, number)
        if last:
            first, width = self.columns
            self.out[:, pl.ds(first, width)] += buf[there].astype(jnp.float32)
            return
        where = self.block(stage, line, along)
        if self.order[stage] == CORE:
            where = (line, slice(None), slice(None))
        total = self.held[where].astype(jnp.float32) + buf[there].astype(jnp.float32)
        self.held[where] = total.astype(self.held.dtype)

    def launch(self, stage, line):
        axis, place = self.order[stage], self.place
        size, here = place.sizes[axis], place.here[axis]
        if size == 2:
            self.copy(stage, line, 1 - here, 1 - 2 * here).start()
        elif size > 2:
            for turn in range(1, size):
                for step, along in ((1, size - turn), (-1, turn - 1)):

                    @pl.when((here == (0 if step > 0 else size - 1)))
                    def _(step=step, along=along):
                        self.copy(stage, line, along, step).start()

    def pass_on(self, stage, line, turn):
        axis, place = self.order[stage], self.place
        size, here = place.sizes[axis], place.here[axis]
        for step, along in ((1, size - turn), (-1, turn - 1)):
            ahead = (along > here) if step > 0 else (along < here)

            @pl.when(ahead & place.can(axis, -step))
            def _(step=step, along=along):
                self.add(stage, line, along, along)
                self.copy(stage, line, along, step).start()

    def finish(self, stage, line):
        axis, place = self.order[stage], self.place
        size, here = place.sizes[axis], place.here[axis]
        if size == 2:
            self.add(stage, line, here, 0, stage == 3)
        elif size > 2:
            for step, number in ((-1, here), (1, size)):

                @pl.when(place.can(axis, step))
                def _(number=number):
                    self.add(stage, line, here, number, stage == 3)

    def whole(self, stage, line):
        for turn in range(1, self.place.sizes[self.order[stage]]):
            if self.place.sizes[self.order[stage]] > 2:
                self.pass_on(stage, line, turn)
        self.finish(stage, line)

    def line_hop(self, along, hop):
        place, stage = self.place, self.order.index(LINE)
        size, here = place.sizes[LINE], place.here[LINE]
        for step, at, ahead in ((1, hop, along > hop), (-1, size - 1 - hop, along < size - 1 - hop)):
            if not ahead:
                continue

            @pl.when(here == at)
            def _(step=step):
                if hop:
                    self.add(stage, here, along, along)
                self.copy(stage, here, along, step).start()

    def steps(self):
        place = self.place
        size, here = place.sizes[LINE], place.here[LINE]
        lines = []
        for k in range(size):
            lines.append(k // 2 if k % 2 == 0 else size - 1 - k // 2)
        spot = self.order.index(LINE)

        def begin(k):
            self.own(lines[k]).start()
            self.launch(0, lines[k])

        begin(0)
        yield
        for turn in range(2 * size + spot - 2):
            if turn + 1 < size:
                begin(turn + 1)
            for k in range(size):
                hop = turn - k - spot
                if 0 <= hop < size - 1:
                    self.line_hop(lines[k], hop)
            for stage in range(spot - 1, -1, -1):
                k = turn - stage
                if not 0 <= k < size:
                    continue
                if stage == 0:
                    self.own(lines[k]).wait()
                self.whole(stage, lines[k])
                if stage + 1 < spot:
                    self.launch(stage + 1, lines[k])
            yield
        if spot == 3:
            self.begin_out()
        self.finish(spot, here)
        for stage in range(spot + 1, 4):
            if stage == 3:
                self.begin_out()
            self.launch(stage, here)
            yield
            self.whole(stage, here)

    def begin_out(self):
        first, width = self.columns
        mine = self.held[tuple(self.place.here[:3])]
        self.out[:, pl.ds(first, width)] = mine.astype(jnp.float32)

    def drain(self):
        place = self.place
        spot = self.order.index(LINE)
        for stage in range(4):
            axis = self.order[stage]
            size, here = place.sizes[axis], place.here[axis]
            for line in range(place.sizes[LINE]) if stage < spot else [place.here[LINE]]:
                if size == 2:
                    self.copy(stage, line, 1 - here, 1 - 2 * here).wait_send()
                elif size > 2:
                    for along in range(size):
                        for step in (-1, 1):

                            @pl.when((along > here) if step > 0 else (along < here))
                            def _(along=along, step=step, line=line, stage=stage):
                                self.copy(stage, line, along, step).wait_send()


def scatter_kernel(sizes, parts, count, *refs):
    partials, outs = refs[:count], refs[count : 2 * count]
    load, send, recv = refs[2 * count : 2 * count + 3]
    scratch = list(refs[2 * count + 3 :])
    place = Place(sizes)
    place.greet()
    scatters = []
    for k, (which, columns, order) in enumerate(parts):
        held, *bufs = scratch[5 * k : 5 * k + 5]
        scatters.append(
            Scatter(place, k, order, partials[which], columns, held, bufs, outs[which], load, send, recv)
        )
    run_all([s.steps() for s in scatters])
    for s in scatters:
        s.drain()


def scatter_scratch(sizes, parts, shapes, dtype):
    scratch = []
    for which, (_, width), order in parts:
        rows = shapes[which][-2]
        scratch.append(pltpu.VMEM(sizes[:3] + (rows, width), dtype))
        stages = (CORE,) + order
        for stage, axis in enumerate(stages):
            free = tuple(sizes[a] for a in range(1, 3) if a not in stages[: stage + 1])
            slots = 1 if sizes[axis] <= 2 else sizes[axis] + 1
            if axis == LINE:
                lead = (slots,)
            else:
                lead = (1 if LINE in stages[:stage] else sizes[LINE], slots)
            scratch.append(pltpu.VMEM(lead + free + (rows, width), dtype))
    return scratch


def scatter_all(partials, parts, sizes, collective_id):
    count = 1
    for size in sizes:
        count *= size
    partials = [p.reshape(sizes + (p.shape[0] // count, p.shape[1])) for p in partials]
    lanes = max([1] + [size + 1 for size in sizes[1:] if size > 2])
    sems = (len(parts), 4, sizes[0] + 1, lanes)
    return pl.pallas_call(
        functools.partial(scatter_kernel, sizes, parts, len(partials)),
        out_shape=[jax.ShapeDtypeStruct(p.shape[4:], jnp.float32) for p in partials],
        in_specs=[pl.BlockSpec(memory_space=pl.ANY)] * len(partials),
        out_specs=[pl.BlockSpec(memory_space=pltpu.VMEM)] * len(partials),
        scratch_shapes=[
            pltpu.SemaphoreType.DMA((len(parts), sizes[0])),
            pltpu.SemaphoreType.DMA(sems),
            pltpu.SemaphoreType.DMA(sems),
        ]
        + scatter_scratch(sizes, parts, [p.shape for p in partials], partials[0].dtype),
        compiler_params=pltpu.CompilerParams(
            collective_id=collective_id, has_side_effects=True, vmem_limit_bytes=60 << 20
        ),
    )(*partials)


def partners_of(sizes):
    hops = []
    for axis in (2, 1, 0):
        stride = 1
        while stride < sizes[axis]:
            hops.append((axis, stride))
            stride *= 2
    return hops


def scan_kernel(sizes, backward, *refs):
    place = Place(sizes)
    place.greet(partners_of(sizes))
    scan_states(place, backward, lambda hop: None, *refs)


def scan_states(
    place, backward, between, state_ref, logs_ref, out_ref,
    sib, sib_logs, first, first_logs, pre, pre_logs, total, total_logs, wire, wire_logs, got, got_logs, other, send, recv,
):
    core = place.here[CORE]
    hops = partners_of(place.sizes)
    half = HEADS // 2
    mine, theirs = pl.ds(half * core, half), pl.ds(half * (1 - core), half)
    sibling = place.toward(CORE, 1 - 2 * core)
    bit, partner = place.bit, place.partner

    def remote(source, target, number, device):
        return pltpu.make_async_remote_copy(
            src_ref=source, dst_ref=target, send_sem=send.at[number], recv_sem=recv.at[number],
            device_id=device, device_id_type=MESH,
        )

    def scaled(logs, states, added):
        return [jnp.exp(logs[h, 0:1, :]) * states[h] + added[h] for h in range(half)]

    swap = [
        remote(state_ref.at[theirs], sib, 0, sibling),
        remote(logs_ref.at[theirs], sib_logs, 1, sibling),
    ]
    for copy in swap:
        copy.start()
    for copy in swap:
        copy.wait_recv()
    starts = core == (1 if backward else 0)

    @pl.when(starts)
    def _():
        first[...] = state_ref[mine]
        first_logs[...] = logs_ref[mine]
        new = scaled(sib_logs, first, sib)
        for h in range(half):
            total[h] = new[h]

    @pl.when(jnp.logical_not(starts))
    def _():
        first[...] = sib[...]
        first_logs[...] = sib_logs[...]
        new = scaled(logs_ref.at[mine], first, state_ref.at[mine])
        for h in range(half):
            total[h] = new[h]

    total_logs[...] = logs_ref[mine] + sib_logs[...]
    pre[...] = jnp.zeros_like(pre)
    pre_logs[...] = jnp.zeros_like(pre_logs)
    pending = list(swap)
    for k, (axis, stride) in enumerate(hops):
        between(k)
        last = k == len(hops) - 1
        wire[k] = total[...].astype(wire.dtype)
        wire_logs[k] = total_logs[...]
        copies = [
            remote(wire.at[k], got.at[k], 2 + 2 * k, partner(axis, stride)),
            remote(wire_logs.at[k], got_logs.at[k], 3 + 2 * k, partner(axis, stride)),
        ]
        for copy in copies:
            copy.start()
        pending += copies
        for copy in copies:
            copy.wait_recv()
        earlier = bit(axis, stride) == (1 if backward else 0)
        arrived = [got[k, h].astype(jnp.float32) for h in range(half)]

        @pl.when(jnp.logical_not(earlier))
        def _(k=k, arrived=arrived, last=last):
            new = scaled(pre_logs, arrived, pre)
            for h in range(half):
                pre[h] = new[h]
            pre_logs[...] = pre_logs[...] + got_logs[k]
            if not last:
                new = scaled(total_logs, arrived, total)
                for h in range(half):
                    total[h] = new[h]

        if not last:

            @pl.when(earlier)
            def _(k=k, arrived=arrived):
                new = scaled(got_logs.at[k], total, arrived)
                for h in range(half):
                    total[h] = new[h]

            total_logs[...] = total_logs[...] + got_logs[k]
    second = scaled(first_logs, pre, first)

    @pl.when(starts)
    def _():
        for h in range(half):
            other[h] = second[h]
        out_ref[mine] = pre[...]

    @pl.when(jnp.logical_not(starts))
    def _():
        other[...] = pre[...]
        for h in range(half):
            out_ref[half * core + h] = second[h]

    back = remote(other, out_ref.at[mine], 2 + 2 * len(hops), sibling)
    back.start()
    back.wait_recv()
    for copy in pending + [back]:
        copy.wait_send()


def scan_scratch(sizes):
    half, hops = HEADS // 2, len(partners_of(sizes))
    block, tile = (half, HV, HK), (half, 8, HK)
    return [
        pltpu.VMEM(block, jnp.float32), pltpu.VMEM(tile, jnp.float32),
        pltpu.VMEM(block, jnp.float32), pltpu.VMEM(tile, jnp.float32),
        pltpu.VMEM(block, jnp.float32), pltpu.VMEM(tile, jnp.float32),
        pltpu.VMEM(block, jnp.float32), pltpu.VMEM(tile, jnp.float32),
        pltpu.VMEM((hops,) + block, jnp.bfloat16), pltpu.VMEM((hops,) + tile, jnp.float32),
        pltpu.VMEM((hops,) + block, jnp.bfloat16), pltpu.VMEM((hops,) + tile, jnp.float32),
        pltpu.VMEM(block, jnp.float32),
        pltpu.SemaphoreType.DMA((3 + 2 * hops,)),
        pltpu.SemaphoreType.DMA((3 + 2 * hops,)),
    ]


def entering(state, logs, sizes, backward, collective_id):
    return pl.pallas_call(
        functools.partial(scan_kernel, sizes, backward),
        out_shape=jax.ShapeDtypeStruct(state.shape, jnp.float32),
        in_specs=[pl.BlockSpec(memory_space=pltpu.VMEM)] * 2,
        out_specs=pl.BlockSpec(memory_space=pltpu.VMEM),
        scratch_shapes=scan_scratch(sizes),
        compiler_params=pltpu.CompilerParams(
            collective_id=collective_id, has_side_effects=True, vmem_limit_bytes=32 << 20
        ),
    )(state, logs)


CHUNK = 128
ROWS = 256
FTILE = 256
F32, BF16 = jnp.float32, jnp.bfloat16


def nn(left, right):
    return jnp.dot(left, right, preferred_element_type=F32)


def nt(left, right):
    return lax.dot_general(left, right, (((1,), (1,)), ((), ())), preferred_element_type=F32)


def tn(left, right):
    return lax.dot_general(left, right, (((0,), (0,)), ((), ())), preferred_element_type=F32)


def sigmoid(v):
    return 1.0 / (1.0 + jnp.exp(-v))


def causal_mask(size):
    return lax.broadcasted_iota(jnp.int32, (size, size), 0) >= lax.broadcasted_iota(jnp.int32, (size, size), 1)


def triangle(upper):
    rows = lax.broadcasted_iota(jnp.int32, (CHUNK, CHUNK), 0)
    columns = lax.broadcasted_iota(jnp.int32, (CHUNK, CHUNK), 1)
    kept = (columns >= rows) if upper else (columns <= rows)
    return jnp.where(kept, 1.0, 0.0).astype(BF16)


def running(matrix, values):
    high = values.astype(BF16)
    low = (values - high.astype(F32)).astype(BF16)
    return nn(matrix, high) + nn(matrix, low)


def halves(values):
    high = values.astype(BF16)
    return high, (values - high.astype(F32)).astype(BF16)


def fine_nt(left, right):
    (high, low), (other, rest) = left, right
    return nt(high, other) + (nt(high, rest) + nt(low, other))


def inverse_rms(values):
    return lax.rsqrt(jnp.mean(values * values, axis=-1, keepdims=True) + 1e-06)


def heads_of(width):
    return [slice(h * width, (h + 1) * width) for h in range(HEADS)]


def small_rows(extra):
    lanes = lax.broadcasted_iota(jnp.int32, (8, extra.shape[1]), 1)
    rows = lax.broadcasted_iota(jnp.int32, (8, extra.shape[1]), 0)
    return nt(jnp.where(lanes == rows + RANK, 1.0, 0.0).astype(BF16), extra)


def with_one(mid):
    lanes = lax.broadcasted_iota(jnp.int32, mid.shape, 1)
    return jnp.where(lanes < RANK, mid, jnp.where(lanes == RANK, 1.0, 0.0)).astype(BF16)


def project_rows(tokens, gain, weight, up, outs, final_ref, logs_ref):
    normed_ref, query_ref, key_ref, value_ref, gate_ref, mid_ref, logit_ref, within_ref, update_ref = outs
    inputs = tokens[...].astype(F32)
    normed = (inputs * inverse_rms(inputs) * gain).astype(BF16)
    normed_ref[...] = normed
    keys = HEADS * HK
    values = HEADS * HV
    mid = with_one(nn(normed, weight(2 * keys + 2 * values, 128)))
    mid_ref[...] = mid
    logit = nt(mid, up)
    logit_ref[...] = logit
    query_ref[...] = nn(normed, weight(0, keys)).astype(BF16)
    key_ref[...] = nn(normed, weight(keys, keys)).astype(BF16)
    value_ref[...] = nn(normed, weight(2 * keys, values)).astype(BF16)
    gate_ref[...] = nn(normed, weight(2 * keys + values, values)).astype(BF16)
    decay = (jnp.minimum(logit, 0.0) - jnp.log1p(jnp.exp(-jnp.abs(logit)))) * (1.0 / 16.0)
    lower = triangle(False)
    for c in range(ROWS // CHUNK):
        rows = pl.ds(c * CHUNK, CHUNK)
        within = running(lower, decay[c * CHUNK : (c + 1) * CHUNK])
        within_ref[rows, :] = within
        total = within[CHUNK - 1 : CHUNK]
        ending = (key_ref[rows, :].astype(F32) * jnp.exp(total - within)).astype(BF16)
        for h, (ks, vs) in enumerate(zip(heads_of(HK), heads_of(HV))):
            update = tn(value_ref[rows, vs], ending[:, ks])
            update_ref[c, h] = update.astype(BF16)
            final_ref[h] = final_ref[h] * jnp.exp(total[:, ks]) + update
            logs_ref[h] = logs_ref[h] + total[:, ks]


def project_kernel(tokens, gains, weights, up, *refs):
    outs, (final_ref, logs_ref) = refs[:9], refs[9:]

    @pl.when(pl.program_id(0) == 0)
    def _():
        final_ref[...] = jnp.zeros_like(final_ref)
        logs_ref[...] = jnp.zeros_like(logs_ref)

    project_rows(
        tokens, gains[0:1], lambda first, width: weights[:, first : first + width], up[...], outs, final_ref, logs_ref
    )


def mix_rows(tokens, query, key, value, gate, within_all, update, state, head_gain, out_weight, ffn_gain, outs):
    mixed_ref, gated_ref, hidden_ref, ffn_ref, starts_ref = outs
    mask = causal_mask(CHUNK)
    for c in range(ROWS // CHUNK):
        rows = pl.ds(c * CHUNK, CHUNK)
        within = within_all[rows, :]
        middle = within[CHUNK // 2 - 1 : CHUNK // 2]
        total = within[CHUNK - 1 : CHUNK]
        scaled = query[rows, :].astype(F32) * HK**-0.5
        from_start = (scaled * jnp.exp(within)).astype(BF16)
        left = halves(scaled * jnp.exp(within - middle))
        right = halves(key[rows, :].astype(F32) * jnp.exp(middle - within))
        for h, (ks, vs) in enumerate(zip(heads_of(HK), heads_of(HV))):
            start = state[h].astype(BF16)
            starts_ref[c, h] = start
            scores = jnp.where(mask, fine_nt([p[:, ks] for p in left], [p[:, ks] for p in right]), 0.0).astype(BF16)
            mixed = nn(scores, value[rows, vs]) + nt(from_start[:, ks], start)
            state[h] = state[h] * jnp.exp(total[:, ks]) + update[c, h].astype(F32)
            mixed_ref[rows, vs] = mixed
            gates = gate[rows, vs].astype(F32)
            gated = mixed * inverse_rms(mixed) * head_gain[:, vs] * (gates * sigmoid(gates))
            gated_ref[rows, vs] = gated.astype(BF16)
    hidden = tokens[...].astype(F32) + nn(gated_ref[...], out_weight)
    hidden_ref[...] = hidden
    ffn_ref[...] = (hidden * inverse_rms(hidden) * ffn_gain).astype(BF16)


def mix_kernel(tokens, query, key, value, gate, within_all, update, entering_ref, gains, out_weight, *refs):
    outs, state = refs[:5], refs[5]

    @pl.when(pl.program_id(0) == 0)
    def _():
        state[...] = entering_ref[...]

    mix_rows(
        tokens, query, key, value, gate, within_all, update, state, gains[1:2], out_weight[...], gains[2:3], outs
    )


def ffn_kernel(
    ffn_in, ffn_in_t, cotangent, hidden, gate_weight, up_weight, down_weight,
    out_ref, back_ref, gate_grad, up_grad, down_grad,
):
    @pl.when(pl.program_id(0) == 0)
    def _():
        out_ref[...] = hidden[...]
        back_ref[...] = jnp.zeros_like(back_ref)

    gate, up = nn(ffn_in[...], gate_weight[...]), nn(ffn_in[...], up_weight[...])
    back = nt(cotangent[...], down_weight[...])
    share = sigmoid(gate)
    passed = gate * share
    inner = (passed * up).astype(BF16)
    d_up = (back * passed).astype(BF16)
    d_gate = (back * up * (share * (1.0 + gate * (1.0 - share)))).astype(BF16)
    out_ref[...] += nn(inner, down_weight[...])
    back_ref[...] += nt(d_gate, gate_weight[...]) + nt(d_up, up_weight[...])
    gate_grad[...] = nn(ffn_in_t[...], d_gate).astype(BF16)
    up_grad[...] = nn(ffn_in_t[...], d_up).astype(BF16)
    down_grad[...] = tn(inner, cotangent[...]).astype(BF16)


def norm_back(values, gain, grad):
    scale = inverse_rms(values)
    inner = grad * gain
    along = jnp.mean(inner * values, axis=-1, keepdims=True)
    return scale * inner - values * (scale * scale * scale * along), grad * values * scale


def unmix_kernel(
    ffn_back, hidden, cotangent, gate, mixed, query, within_all, gains, out_weight,
    d_hidden_ref, low_ref, d_gate_ref, d_mixed_ref, update_ref, enters_ref, ffn_gain_ref, head_gain_ref,
):
    @pl.when(pl.program_id(0) == 0)
    def _():
        enters_ref[...] = jnp.zeros_like(enters_ref)
        ffn_gain_ref[...] = jnp.zeros_like(ffn_gain_ref)
        head_gain_ref[...] = jnp.zeros_like(head_gain_ref)

    through, terms = norm_back(hidden[...], gains[2:3], ffn_back[...])
    ffn_gain_ref[...] += jnp.sum(terms, axis=0, keepdims=True)
    d_hidden = cotangent[...].astype(F32) + through
    d_hidden_ref[...] = d_hidden
    low = d_hidden.astype(BF16)
    low_ref[...] = low
    d_gated = nt(low, out_weight[...])
    for vs in heads_of(HV):
        value = mixed[:, vs]
        scale = inverse_rms(value)
        headed = value * scale
        gates = gate[:, vs].astype(F32)
        share = sigmoid(gates)
        passed = gates * share
        grad, gain = d_gated[:, vs], gains[1:2, vs]
        head_gain_ref[:, vs] += jnp.sum(grad * headed * passed, axis=0, keepdims=True)
        d_gate_ref[:, vs] = (grad * headed * gain * (share * (1.0 + gates * (1.0 - share)))).astype(BF16)
        d_headed = grad * gain * passed
        along = jnp.mean(d_headed * headed, axis=-1, keepdims=True)
        d_mixed_ref[:, vs] = scale * (d_headed - headed * along)
    for c in reversed(range(ROWS // CHUNK)):
        rows = slice(c * CHUNK, (c + 1) * CHUNK)
        within = within_all[rows]
        total = within[CHUNK - 1 : CHUNK]
        from_start = (query[rows].astype(F32) * HK**-0.5 * jnp.exp(within)).astype(BF16)
        for h, (ks, vs) in enumerate(zip(heads_of(HK), heads_of(HV))):
            update = tn(d_mixed_ref[rows, vs].astype(BF16), from_start[:, ks])
            update_ref[c, h] = update.astype(BF16)
            enters_ref[h] = enters_ref[h] * jnp.exp(total[:, ks]) + update


def back_kernel(
    tokens, query, key, value, logit, within_all, d_mixed, starts, update, leaving_ref, d_gate, d_hidden,
    gains, weights, up,
    d_qkv_ref, d_logit_ref, d_mid_ref, tokens_grad_ref, gain_ref, state,
):
    @pl.when(pl.program_id(0) == 0)
    def _():
        state[...] = leaving_ref[...]
        gain_ref[...] = jnp.zeros_like(gain_ref)

    mask = causal_mask(CHUNK)
    upper = triangle(True)
    keys = HEADS * HK
    for c in reversed(range(ROWS // CHUNK)):
        rows = slice(c * CHUNK, (c + 1) * CHUNK)
        within = within_all[rows]
        middle = within[CHUNK // 2 - 1 : CHUNK // 2]
        total = within[CHUNK - 1 : CHUNK]
        factor = jnp.exp(total)
        queries, keys_f = query[rows].astype(F32), key[rows].astype(F32)
        q_start, q_middle = jnp.exp(within) * HK**-0.5, jnp.exp(within - middle) * HK**-0.5
        k_middle, k_end = jnp.exp(middle - within), jnp.exp(total - within)
        lefts, rights = halves(queries * q_middle), halves(keys_f * k_middle)
        left, right = lefts[0], rights[0]
        ending = (keys_f * k_end).astype(BF16)
        moves, extras = [], []
        for h, (ks, vs) in enumerate(zip(heads_of(HK), heads_of(HV))):
            start, after = starts[c, h], state[h].astype(BF16)
            (grad, rest), values = halves(d_mixed[rows, vs]), value[rows, vs]
            scores = jnp.where(mask, fine_nt([p[:, ks] for p in lefts], [p[:, ks] for p in rights]), 0.0).astype(BF16)
            d_scores = jnp.where(mask, nt(grad, values) + nt(rest, values), 0.0).astype(BF16)
            d_value = tn(scores, grad) + nt(ending[:, ks], after)
            d_query = nn(d_scores, right[:, ks]) * q_middle[:, ks] + nn(grad, start) * q_start[:, ks]
            d_end = nn(values, after) * k_end[:, ks]
            d_key = tn(d_scores, left[:, ks]) * k_middle[:, ks] + d_end
            d_qkv_ref[rows, ks] = d_query.astype(BF16)
            d_qkv_ref[rows, slice(keys + ks.start, keys + ks.stop)] = d_key.astype(BF16)
            d_qkv_ref[rows, slice(2 * keys + vs.start, 2 * keys + vs.stop)] = d_value.astype(BF16)
            moves.append(queries[:, ks] * d_query - keys_f[:, ks] * d_key)
            extras.append(
                jnp.sum(keys_f[:, ks] * d_end, axis=0, keepdims=True)
                + factor[:, ks] * jnp.sum(start.astype(F32) * state[h], axis=0, keepdims=True)
            )
            state[h] = state[h] * factor[:, ks] + update[c, h].astype(F32)
        d_decay = running(upper, jnp.concatenate(moves, axis=1)) + jnp.concatenate(extras, axis=1)
        d_logit = d_decay * sigmoid(-logit[rows]) * (1.0 / 16.0)
        d_logit_ref[rows] = d_logit.astype(BF16)
    d_mid = nn(d_logit_ref[...], up[...])
    d_mid = jnp.where(lax.broadcasted_iota(jnp.int32, d_mid.shape, 1) < RANK, d_mid, 0.0).astype(BF16)
    d_mid_ref[...] = d_mid
    inner = 2 * keys + HEADS * HV
    outer = inner + HEADS * HV
    d_normed = (
        nt(d_qkv_ref[...], weights[:, :inner]) + nt(d_gate[...], weights[:, inner:outer]) + nt(d_mid, weights[:, outer:])
    )
    through, terms = norm_back(tokens[...].astype(F32), gains[0:1], d_normed)
    gain_ref[...] += jnp.sum(terms, axis=0, keepdims=True)
    tokens_grad_ref[...] = d_hidden[...] + through


def rows_spec(width, steps, backward):
    return pl.BlockSpec((ROWS, width), (lambda i: (steps - 1 - i, 0)) if backward else (lambda i: (i, 0)))


def chunks_spec(steps, backward):
    return pl.BlockSpec(
        (ROWS // CHUNK, HEADS, HV, HK),
        (lambda i: (steps - 1 - i, 0, 0, 0)) if backward else (lambda i: (i, 0, 0, 0)),
    )


def kept_spec(shape):
    return pl.BlockSpec(shape, lambda i: (0,) * len(shape), pipeline_mode=pl.Buffered(1))


def kept_out(shape):
    return pl.BlockSpec(shape, lambda i: (0,) * len(shape))


PARAMS = dict(vmem_limit_bytes=60 << 20)
STATE = (HEADS, HV, HK)


def project(tokens, gains, weights, up):
    length, width = tokens.shape
    steps, keys, values = length // ROWS, HEADS * HK, HEADS * HV
    row = lambda w: rows_spec(w, steps, False)
    chunks = (length // CHUNK,) + STATE
    shape = jax.ShapeDtypeStruct
    return pl.pallas_call(
        project_kernel,
        grid=(steps,),
        in_specs=[row(width)] + [kept_spec(a.shape) for a in (gains, weights, up)],
        out_specs=[row(w) for w in (width, keys, keys, values, values, 128, keys, keys)]
        + [chunks_spec(steps, False), kept_out(STATE), kept_out((HEADS, 8, HK))],
        out_shape=[shape((length, w), BF16) for w in (width, keys, keys, values, values, 128)]
        + [shape((length, keys), F32)] * 2
        + [shape(chunks, BF16), shape(STATE, F32), shape((HEADS, 8, HK), F32)],
        compiler_params=pltpu.CompilerParams(**PARAMS),
    )(tokens, gains, weights, up)


def mix(tokens, query, key, value, gate, within, update, entered, gains, out_weight):
    length, width = tokens.shape
    steps, keys, values = length // ROWS, HEADS * HK, HEADS * HV
    row = lambda w: rows_spec(w, steps, False)
    shape = jax.ShapeDtypeStruct
    return pl.pallas_call(
        mix_kernel,
        grid=(steps,),
        in_specs=[row(w) for w in (width, keys, keys, values, values, keys)]
        + [chunks_spec(steps, False)]
        + [kept_spec(a.shape) for a in (entered, gains, out_weight)],
        out_specs=[row(w) for w in (values, values, width, width)] + [chunks_spec(steps, False)],
        out_shape=[
            shape((length, values), F32), shape((length, values), BF16),
            shape((length, width), F32), shape((length, width), BF16), shape(update.shape, BF16),
        ],
        scratch_shapes=[pltpu.VMEM(STATE, F32)],
        compiler_params=pltpu.CompilerParams(**PARAMS),
    )(tokens, query, key, value, gate, within, update, entered, gains, out_weight)


FRONT_PARTS = (
    (0, (0, 128), ORDERS[0]),
    (1, (0, 1024), ORDERS[0]),
    (1, (1024, 1024), ORDERS[1]),
    (1, (2048, 1152), ORDERS[2]),
    (2, (0, 1024), ORDERS[3]),
    (3, (0, 2816), ORDERS[0]),
    (4, (0, 2816), ORDERS[1]),
    (5, (0, 512), ORDERS[2]),
    (5, (512, 512), ORDERS[3]),
)
FIRST_PARTS = 5
FRONT_TURNS = (1, 2, (2,), 1)


def front_kernel(sizes, steps, *refs):
    tokens, shards, refs = refs[0], refs[1:7], refs[7:]
    buffers, refs = refs[:6], refs[6:]
    outs, mixed_outs, (logs_out, gains_out), refs = refs[:8], refs[8:13], refs[13:15], refs[15:]
    up_all, proj_all, out_all, query, key, value, gate, within, update, state, final, logs, gains, refs = *refs[:13], refs[13:]
    send, recv, own, flush = refs[:4]
    scan = refs[4:]
    place = Place(sizes)
    step = pl.program_id(0)
    here = tuple(place.here)
    held = (up_all, proj_all, out_all) + tuple(buffers[3:])
    gathers = [
        Gather(place, k, order, held[which], columns, send, recv)
        for k, (which, columns, order) in enumerate(FRONT_PARTS)
    ]
    owned = [pltpu.make_async_copy(shards[k], buffers[k].at[here], own.at[k]) for k in (3, 4, 5)]
    flushes = [pltpu.make_async_copy(held[k], buffers[k], flush.at[k]) for k in range(3)]
    later = [g.steps() for g in gathers[FIRST_PARTS:]]

    def turn():
        for g in later:
            next(g, None)

    def during(hop):
        if hop in FRONT_TURNS[2]:
            turn()

    @pl.when(step == 0)
    def _():
        for copy in owned:
            copy.start()
        for k in range(3):
            held[k][here] = shards[k][...]
        place.greet(partners_of(sizes))
        for copy in owned:
            copy.wait()
        run_all([g.steps() for g in gathers[:FIRST_PARTS]])
        turn()
        flushes[0].start()
        flushes[1].start()
        flushes[2].start()
        extra = 2 * HEADS * (HK + HV)
        gains[...] = small_rows(proj_all[..., pl.ds(extra, 128)].reshape(-1, 128))
        gains_out[...] = gains[...]
        final[...] = jnp.zeros_like(final)
        logs[...] = jnp.zeros_like(logs)
        for _ in range(FRONT_TURNS[0]):
            turn()

    @pl.when(step < steps)
    def _():
        rows = pl.ds(pl.multiple_of(step * ROWS, ROWS), ROWS)
        chunks = pl.ds(step * (ROWS // CHUNK), ROWS // CHUNK)
        normed_ref, query_ref, key_ref, value_ref, gate_ref, mid_ref, logit_ref, within_ref = outs
        kept = (query, key, value, gate, within)
        tiles = (query_ref, key_ref, value_ref, gate_ref, within_ref)
        project_rows(
            tokens, gains[0:1],
            lambda first, width: proj_all[..., pl.ds(first, width)].reshape(-1, width),
            up_all[...].reshape(-1, 128),
            (normed_ref, query_ref, key_ref, value_ref, gate_ref, mid_ref, logit_ref, within_ref, update.at[chunks]),
            final, logs,
        )
        for whole, tile in zip(kept, tiles):
            whole[rows, :] = tile[...]

    @pl.when(step == steps)
    def _():
        for _ in range(FRONT_TURNS[1]):
            turn()
        logs_out[...] = logs[...]
        scan_states(place, False, during, final, logs, state, *scan)
        for _ in range(FRONT_TURNS[3]):
            turn()

    @pl.when(step >= steps)
    def _():
        at = step - steps
        rows = pl.ds(pl.multiple_of(at * ROWS, ROWS), ROWS)
        chunks = pl.ds(at * (ROWS // CHUNK), ROWS // CHUNK)
        mix_rows(
            tokens, query.at[rows], key.at[rows], value.at[rows], gate.at[rows], within.at[rows], update.at[chunks], state,
            gains[1:2], out_all[...].reshape(-1, out_all.shape[-1]), gains[2:3], mixed_outs,
        )

    @pl.when(step == 2 * steps - 1)
    def _():
        run_all(later)
        for g in gathers:
            g.drain()
        for copy in flushes:
            copy.wait()


def front(tokens, shards, sizes, collective_id):
    length, width = tokens.shape
    steps, keys, values = length // ROWS, HEADS * HK, HEADS * HV
    shape, chunks = jax.ShapeDtypeStruct, (length // CHUNK,) + STATE
    first = lambda w: pl.BlockSpec((ROWS, w), lambda i: (jnp.minimum(i, steps - 1), 0))
    second = lambda w: pl.BlockSpec((ROWS, w), lambda i: (jnp.maximum(i - steps, 0), 0))
    lanes = lanes_of(sizes)
    parts = len(FRONT_PARTS)
    one = lambda w, t: ((length, w), t)
    results = [one(width, BF16), one(keys, BF16), one(keys, BF16), one(values, BF16), one(values, BF16), one(128, BF16), one(keys, F32), one(keys, F32)]
    mixes = [one(values, F32), one(values, BF16), one(width, F32), one(width, BF16)]
    out = pl.pallas_call(
        functools.partial(front_kernel, sizes, steps),
        grid=(2 * steps,),
        in_specs=[pl.BlockSpec((ROWS, width), lambda i: (lax.rem(i, steps), 0))] + [kept_spec(s.shape) for s in shards],
        out_specs=[pl.BlockSpec(memory_space=pl.ANY)] * len(shards)
        + [first(s[1]) for s, _ in results]
        + [second(s[1]) for s, _ in mixes]
        + [pl.BlockSpec((ROWS // CHUNK,) + STATE, lambda i: (jnp.maximum(i - steps, 0), 0, 0, 0))]
        + [kept_out((HEADS, 8, HK)), kept_out((8, width))],
        out_shape=[shape(sizes + s.shape, s.dtype) for s in shards]
        + [shape(s, t) for s, t in results + mixes]
        + [shape(chunks, BF16), shape((HEADS, 8, HK), F32), shape((8, width), F32)],
        scratch_shapes=[pltpu.VMEM(sizes + s.shape, s.dtype) for s in shards[:3]]
        + [pltpu.VMEM((length, w), t) for w, t in ((keys, BF16), (keys, BF16), (values, BF16), (values, BF16), (keys, F32))]
        + [pltpu.VMEM(chunks, BF16), pltpu.VMEM(STATE, F32), pltpu.VMEM(STATE, F32), pltpu.VMEM((HEADS, 8, HK), F32), pltpu.VMEM((8, width), F32)]
        + [
            pltpu.SemaphoreType.DMA((parts, 4, sizes[0], lanes, 2)),
            pltpu.SemaphoreType.DMA((parts, 4, sizes[0], lanes)),
            pltpu.SemaphoreType.DMA((len(shards),)),
            pltpu.SemaphoreType.DMA((3,)),
        ]
        + scan_scratch(sizes),
        compiler_params=pltpu.CompilerParams(collective_id=collective_id, has_side_effects=True, **PARAMS),
    )(tokens, *shards)
    weights = [o.reshape(-1, o.shape[-1]) for o in out[: len(shards)]]
    return weights, out[len(shards) :]


def feed_forward(ffn_in, cotangent, hidden, gate_weight, up_weight, down_weight):
    length, width = ffn_in.shape
    inner = gate_weight.shape[1]
    whole = [ffn_in, ffn_in.T, cotangent, hidden]
    wide = pl.BlockSpec((width, FTILE), lambda i: (0, i))
    tall = pl.BlockSpec((FTILE, width), lambda i: (i, 0))
    shape = jax.ShapeDtypeStruct
    return pl.pallas_call(
        ffn_kernel,
        grid=(inner // FTILE,),
        in_specs=[kept_spec(a.shape) for a in whole] + [wide, wide, tall],
        out_specs=[kept_out((length, width))] * 2 + [wide, wide, tall],
        out_shape=[shape((length, width), F32)] * 2
        + [shape((width, inner), BF16)] * 2 + [shape((inner, width), BF16)],
        compiler_params=pltpu.CompilerParams(**PARAMS),
    )(*whole, gate_weight, up_weight, down_weight)


def unmix(ffn_back, hidden, cotangent, gate, mixed, query, within, gains, out_weight):
    length, width = hidden.shape
    steps, keys, values = length // ROWS, HEADS * HK, HEADS * HV
    row = lambda w: rows_spec(w, steps, True)
    chunks = (length // CHUNK,) + STATE
    shape = jax.ShapeDtypeStruct
    return pl.pallas_call(
        unmix_kernel,
        grid=(steps,),
        in_specs=[row(w) for w in (width, width, width, values, values, keys, keys)]
        + [kept_spec(a.shape) for a in (gains, out_weight)],
        out_specs=[row(w) for w in (width, width, values, values)]
        + [chunks_spec(steps, True), kept_out(STATE), kept_out((1, width)), kept_out((1, values))],
        out_shape=[
            shape((length, width), F32), shape((length, width), BF16), shape((length, values), BF16),
            shape((length, values), F32), shape(chunks, BF16), shape(STATE, F32),
            shape((1, width), F32), shape((1, values), F32),
        ],
        compiler_params=pltpu.CompilerParams(**PARAMS),
    )(ffn_back, hidden, cotangent, gate, mixed, query, within, gains, out_weight)


def back(tokens, query, key, value, logit, within, d_mixed, starts, update, leaving, d_gate, d_hidden, gains, weights, up):
    length, width = tokens.shape
    steps, keys, values = length // ROWS, HEADS * HK, HEADS * HV
    row = lambda w: rows_spec(w, steps, True)
    shape = jax.ShapeDtypeStruct
    inner = 2 * keys + values
    return pl.pallas_call(
        back_kernel,
        grid=(steps,),
        in_specs=[row(w) for w in (width, keys, keys, values, keys, keys, values)]
        + [chunks_spec(steps, True)] * 2 + [kept_spec(leaving.shape), row(values), row(width)]
        + [kept_spec(a.shape) for a in (gains, weights, up)],
        out_specs=[row(w) for w in (inner, keys, 128, width)] + [kept_out((1, width))],
        out_shape=[
            shape((length, inner), BF16), shape((length, keys), BF16), shape((length, 128), BF16),
            shape((length, width), F32), shape((1, width), F32),
        ],
        scratch_shapes=[pltpu.VMEM(STATE, F32)],
        compiler_params=pltpu.CompilerParams(**PARAMS),
    )(tokens, query, key, value, logit, within, d_mixed, starts, update, leaving, d_gate, d_hidden, gains, weights, up)


BACK_PARTS = tuple((which, columns, order[::-1]) for which, columns, order in FRONT_PARTS)


def beside(pieces):
    rows, used = pieces[0].shape[0], sum(p.shape[1] for p in pieces)
    return jnp.concatenate(pieces + [jnp.zeros((rows, 128 - used), pieces[0].dtype)], axis=1)


def local(
    tokens,
    norm_gain,
    query_weight,
    key_weight,
    value_weight,
    gate_weight,
    rank_down,
    rank_up,
    gate_bias,
    head_gain,
    out_weight,
    ffn_gain,
    ffn_gate,
    ffn_up,
    ffn_down,
    cotangent,
):
    sizes = grid_of(lax.axis_size("seq"))
    extra = beside([rank_down] + [g[:, None] for g in (norm_gain, head_gain, ffn_gain)])
    projections = jnp.concatenate([query_weight, key_weight, value_weight, gate_weight, extra], axis=1)
    shards = [beside([rank_up.T, gate_bias[:, None]]), projections, out_weight, ffn_gate, ffn_up, ffn_down]
    if rank_up.shape[1] % 16 == 0:
        weights, kept = front(tokens, shards, sizes, 0)
        up, proj, out, full_fgate, full_fup, full_fdown = weights
        normed, query, key, value, gate, mid, logit, within, mixed, gated, hidden, ffn_in, starts, logs, gains = kept
    else:
        up, proj, out, full_fgate, full_fup, full_fdown = gather_all(shards, FRONT_PARTS, sizes, 0)
        gains = jnp.pad(proj[:, -128 + RANK : -128 + RANK + 3].astype(F32).T, ((0, 5), (0, 0)))
        normed, query, key, value, gate, mid, logit, within, update, final, logs = project(tokens, gains, proj, up)
        incoming = entering(final, logs, sizes, False, 2)
        mixed, gated, hidden, ffn_in, starts = mix(
            tokens, query, key, value, gate, within, update, incoming, gains, out
        )
    block_output, ffn_back, fgate_wgrad, fup_wgrad, fdown_wgrad = feed_forward(
        ffn_in, cotangent, hidden, full_fgate, full_fup, full_fdown
    )
    d_hidden, hidden_low, d_gate, d_mixed, back_update, enters, ffn_gain_grad, head_gain_grad = unmix(
        ffn_back, hidden, cotangent, gate, mixed, query, within, gains, out
    )
    leaving = entering(enters, logs, sizes, True, 3)
    d_qkv, d_logit, d_mid, tokens_grad, gain_grad = back(
        tokens, query, key, value, logit, within, d_mixed, starts, back_update, leaving, d_gate, d_hidden,
        gains, proj, up,
    )
    rank_grad = tn(normed, d_mid)[:, :RANK]
    extra_grad = beside([rank_grad] + [g.reshape(-1, 1) for g in (gain_grad, head_gain_grad, ffn_gain_grad)])
    proj_wgrad = jnp.concatenate(
        [tn(normed, d_qkv).astype(BF16), tn(normed, d_gate).astype(BF16), extra_grad.astype(BF16)], axis=1
    )
    out_wgrad = tn(gated, hidden_low).astype(BF16)
    up_wgrad = tn(d_logit, mid).astype(BF16)
    up_sum, proj_sum, out_sum, fgate_sum, fup_sum, fdown_sum = scatter_all(
        [up_wgrad, proj_wgrad, out_wgrad, fgate_wgrad, fup_wgrad, fdown_wgrad], BACK_PARTS, sizes, 1
    )
    keys, values = HEADS * HK, HEADS * HV
    last = 2 * (keys + values)
    gain_sum, head_sum, ffn_sum = (proj_sum[:, last + RANK + k] for k in range(3))
    return (
        block_output,
        tokens_grad,
        gain_sum,
        proj_sum[:, :keys],
        proj_sum[:, keys : 2 * keys],
        proj_sum[:, 2 * keys : 2 * keys + values],
        proj_sum[:, 2 * keys + values : last],
        proj_sum[:, last : last + RANK],
        up_sum[:, :RANK].T,
        up_sum[:, RANK],
        head_sum,
        out_sum,
        ffn_sum,
        fgate_sum,
        fup_sum,
        fdown_sum,
    )


def solution(mesh):
    return jax.shard_map(
        local,
        mesh=mesh,
        in_specs=(
            P("seq", None),
            P("seq"),
            P("seq", None),
            P("seq", None),
            P("seq", None),
            P("seq", None),
            P("seq", None),
            P(None, "seq"),
            P("seq"),
            P("seq"),
            P("seq", None),
            P("seq"),
            P("seq", None),
            P("seq", None),
            P("seq", None),
            P("seq", None),
        ),
        out_specs=(
            P("seq", None),
            P("seq", None),
            P("seq"),
            P("seq", None),
            P("seq", None),
            P("seq", None),
            P("seq", None),
            P("seq", None),
            P(None, "seq"),
            P("seq"),
            P("seq"),
            P("seq", None),
            P("seq"),
            P("seq", None),
            P("seq", None),
            P("seq", None),
        ),
        check_vma=False,
    )
```

```python
import functools

import jax
import jax.numpy as jnp
from jax import lax
from jax.experimental import pallas as pl
from jax.experimental.pallas import tpu as pltpu
from jax.sharding import PartitionSpec as P

HEADS = 4
HK = 128
HV = 256
RANK = 16

MESH = pl.DeviceIdType.MESH
LINE = 0
CORE = 3


def grid_of(count):
    core = 2 if count % 2 == 0 else 1
    rest = count // core
    third = max(k for k in range(1, rest + 1) if rest % k == 0 and k**3 <= rest)
    rest //= third
    second = max(k for k in range(1, rest + 1) if rest % k == 0 and k * k <= rest)
    return (rest // second, second, third, core)


class Place:
    def __init__(self, sizes):
        self.sizes = sizes
        rest = lax.axis_index("seq")
        here = []
        for size in sizes[::-1]:
            here.append(lax.rem(rest, size))
            rest = lax.div(rest, size)
        self.here = here[::-1]

    def index(self, **moved):
        out = 0
        for axis, size in enumerate(self.sizes):
            out = out * size + moved.get(f"a{axis}", self.here[axis])
        return out

    def toward(self, axis, step):
        return (self.index(**{f"a{axis}": self.here[axis] + step}),)

    def can(self, axis, step):
        return self.here[axis] > 0 if step < 0 else self.here[axis] < self.sizes[axis] - 1

    def bit(self, axis, stride):
        return lax.rem(lax.div(self.here[axis], stride), 2)

    def partner(self, axis, stride):
        return self.toward(axis, (1 - 2 * self.bit(axis, stride)) * stride)

    def greet(self, hops=()):
        barrier = pltpu.get_barrier_semaphore()
        total = 0
        for axis, stride in hops:
            if stride > 1:
                pl.semaphore_signal(barrier, inc=1, device_id=self.partner(axis, stride), device_id_type=MESH)
                total = total + 1
        for axis, size in enumerate(self.sizes):
            for step in (-1, 1):
                if size == 1:
                    continue
                able = self.can(axis, step)

                @pl.when(able)
                def _(axis=axis, step=step):
                    pl.semaphore_signal(
                        barrier, inc=1, device_id=self.toward(axis, step), device_id_type=MESH
                    )

                total = total + able.astype(jnp.int32)
        pl.semaphore_wait(barrier, total)


def run_all(coroutines):
    active = list(coroutines)
    while active:
        still = []
        for coroutine in active:
            try:
                next(coroutine)
                still.append(coroutine)
            except StopIteration:
                pass
        active = still


class Gather:
    def __init__(self, place, part, order, buffer, columns, send, recv):
        self.place, self.part, self.order = place, part, order + (CORE,)
        self.buffer, self.columns, self.send, self.recv = buffer, columns, send, recv

    def copy(self, stage, line, along, step):
        place, axis = self.place, self.order[stage]
        where = []
        for a in range(4):
            if a == axis:
                where.append(along)
            elif a == LINE and LINE in self.order[:stage]:
                where.append(line)
            elif a in self.order[:stage]:
                where.append(slice(None))
            else:
                where.append(place.here[a])
        first, width = self.columns
        block = self.buffer.at[tuple(where) + (slice(None), pl.ds(first, width))]
        lane = 0 if place.sizes[axis] == 2 and axis != LINE else along
        if axis == LINE:
            line, lane = along, 0
        return pltpu.make_async_remote_copy(
            src_ref=block,
            dst_ref=block,
            send_sem=self.send.at[self.part, stage, line, lane, (step + 1) // 2],
            recv_sem=self.recv.at[self.part, stage, line, lane],
            device_id=place.toward(axis, step),
            device_id_type=MESH,
        )

    def each_step(self, stage, do):
        axis, place = self.order[stage], self.place
        if place.sizes[axis] == 1:
            return
        if place.sizes[axis] == 2 and axis != LINE:
            do(1 - 2 * place.here[axis], None)
            return
        for step in (-1, 1):
            do(step, place.can(axis, step))

    def launch(self, stage, line):
        axis, place = self.order[stage], self.place

        def do(step, able):
            def go():
                self.copy(stage, line, place.here[axis], step).start()

            go() if able is None else pl.when(able)(go)

        self.each_step(stage, do)

    def finish(self, stage, line):
        axis, place = self.order[stage], self.place
        size, here = place.sizes[axis], place.here[axis]
        if size == 1:
            return
        if size == 2:
            self.copy(stage, line, 1 - here, 1 - 2 * here).wait_recv()
            return
        for hop in range(1, size):
            for step in (-1, 1):
                along = here - step * hop
                valid = (along >= 0) & (along < size)

                @pl.when(valid)
                def _(along=along, step=step):
                    self.copy(stage, line, along, step).wait_recv()

                @pl.when(valid & place.can(axis, step))
                def _(along=along, step=step):
                    self.copy(stage, line, along, step).start()

    def steps(self):
        place = self.place
        size, here = place.sizes[LINE], place.here[LINE]
        spot = self.order.index(LINE)
        for stage in range(spot):
            self.launch(stage, here)
            yield
            self.finish(stage, here)
        for step in (-1, 1):

            @pl.when(place.can(LINE, step))
            def _(step=step):
                self.copy(spot, here, here, step).start()

        later = list(range(spot + 1, 4))
        for turn in range(size + len(later)):
            for age in range(min(turn, len(later)), -1, -1):
                far = turn - age
                if far >= size:
                    continue
                for step in (-1, 1) if far else (1,):
                    line = here - step * far
                    valid = (line >= 0) & (line < size)

                    def advance(line=line, step=step, far=far, age=age):
                        if age == 0 and far:
                            self.copy(spot, line, line, step).wait_recv()

                            @pl.when(place.can(LINE, step))
                            def _():
                                self.copy(spot, line, line, step).start()

                        if age:
                            self.finish(later[age - 1], line)
                        if age < len(later):
                            self.launch(later[age], line)

                    pl.when(valid)(advance) if far else advance()
            yield

    def drain(self):
        place = self.place
        size, here = place.sizes[LINE], place.here[LINE]
        spot = self.order.index(LINE)
        for line in range(size):
            for step in (-1, 1):

                @pl.when(place.can(LINE, step) & ((line <= here) if step > 0 else (line >= here)))
                def _(line=line, step=step):
                    self.copy(spot, line, line, step).wait_send()

        for stage in range(4):
            if stage == spot:
                continue
            axis = self.order[stage]
            lines = [here] if stage < spot else list(range(size))
            for line in lines:
                if place.sizes[axis] == 1:
                    continue
                if place.sizes[axis] == 2:
                    self.copy(stage, line, place.here[axis], 1 - 2 * place.here[axis]).wait_send()
                    continue
                for step in (-1, 1):
                    for along in range(place.sizes[axis]):
                        at = place.here[axis]

                        @pl.when(place.can(axis, step) & ((along <= at) if step > 0 else (along >= at)))
                        def _(line=line, step=step, along=along, stage=stage):
                            self.copy(stage, line, along, step).wait_send()


ORDERS = ((2, 0, 1), (1, 0, 2), (0, 2, 1), (0, 1, 2))


def gather_kernel(sizes, parts, count, *refs):
    shards, buffers = refs[:count], refs[count : 2 * count]
    send, recv, own = refs[2 * count :]
    place = Place(sizes)
    locals_ = [
        pltpu.make_async_copy(shard, buffer.at[tuple(place.here)], own.at[k])
        for k, (shard, buffer) in enumerate(zip(shards, buffers))
    ]
    for copy in locals_:
        copy.start()
    place.greet()
    for copy in locals_:
        copy.wait()
    gathers = [
        Gather(place, k, order, buffers[which], columns, send, recv)
        for k, (which, columns, order) in enumerate(parts)
    ]
    run_all([g.steps() for g in gathers])
    for g in gathers:
        g.drain()


def lanes_of(sizes):
    return max([1] + [size for size in sizes[1:] if size > 2])


def gather_all(shards, parts, sizes, collective_id):
    lanes = lanes_of(sizes)
    out = pl.pallas_call(
        functools.partial(gather_kernel, sizes, parts, len(shards)),
        out_shape=[jax.ShapeDtypeStruct(sizes + s.shape, s.dtype) for s in shards],
        in_specs=[pl.BlockSpec(memory_space=pltpu.VMEM)] * len(shards),
        out_specs=[pl.BlockSpec(memory_space=pl.ANY)] * len(shards),
        scratch_shapes=[
            pltpu.SemaphoreType.DMA((len(parts), 4, sizes[0], lanes, 2)),
            pltpu.SemaphoreType.DMA((len(parts), 4, sizes[0], lanes)),
            pltpu.SemaphoreType.DMA((len(shards),)),
        ],
        compiler_params=pltpu.CompilerParams(collective_id=collective_id, has_side_effects=True),
    )(*shards)
    return [o.reshape((-1,) + o.shape[5:]) for o in out]


class Scatter:
    def __init__(self, place, part, order, partial, columns, held, bufs, out, load, send, recv):
        self.place, self.part, self.order = place, part, (CORE,) + order
        self.partial, self.columns, self.held, self.bufs, self.out = partial, columns, held, bufs, out
        self.load, self.send, self.recv = load, send, recv

    def lines(self):
        size = self.place.sizes[LINE]
        return [k // 2 if k % 2 == 0 else size - 1 - k // 2 for k in range(size)]

    def own(self, line):
        first, width = self.columns
        where = (line, slice(None), slice(None), self.place.here[CORE], slice(None), pl.ds(first, width))
        return pltpu.make_async_copy(
            self.partial.at[where], self.bufs[0].at[self.lines().index(line) % 2], self.load.at[self.part, line]
        )

    def block(self, stage, line, along):
        where, done = [], self.order[:stage]
        for a in range(3):
            if a == self.order[stage]:
                where.append(along)
            elif a in done:
                where.append(self.place.here[a])
            elif a == LINE:
                where.append(line)
            else:
                where.append(slice(None))
        return tuple(where)

    def slot(self, stage, line, slot):
        axis = self.order[stage]
        if axis == LINE:
            return (slot,)
        if LINE in self.order[:stage]:
            line = 0
        return (line, 0 if self.place.sizes[axis] == 2 else slot)

    def copy(self, stage, line, along, step):
        place, axis = self.place, self.order[stage]
        size = place.sizes[axis]
        first, width = self.columns
        if axis == CORE:
            where = (line, slice(None), slice(None), along, slice(None), pl.ds(first, width))
            source = self.partial.at[where]
        else:
            source = self.held.at[self.block(stage, line, along)]
        arrives = place.here[axis] + step == along
        number = jnp.where(arrives & (step < 0), size, along) if size > 2 else 0
        sem = self.slot(stage, line, along)
        if axis == LINE:
            sem = sem + (0,)
        there = self.slot(stage, line, number)
        return pltpu.make_async_remote_copy(
            src_ref=source,
            dst_ref=self.held.at[line] if axis == CORE else self.bufs[stage].at[there],
            send_sem=self.send.at[(self.part, stage) + sem],
            recv_sem=self.recv.at[(self.part, stage) + there + ((0,) if axis == LINE else ())],
            device_id=place.toward(axis, step),
            device_id_type=MESH,
        )

    def wait(self, stage, line, number):
        there = self.slot(stage, line, number)
        axis = self.order[stage]
        buf = self.held.at[line] if axis == CORE else self.bufs[stage].at[there]
        pltpu.make_async_copy(
            buf, buf, self.recv.at[(self.part, stage) + there + ((0,) if axis == LINE else ())]
        ).wait()
        return self.bufs[stage], there

    def add(self, stage, line, along, number, last=False):
        buf, there = self.wait(stage, line, number)
        if last:
            first, width = self.columns
            self.out[:, pl.ds(first, width)] += buf[there].astype(jnp.float32)
            return
        where = self.block(stage, line, along)
        if self.order[stage] == CORE:
            where = (line, slice(None), slice(None))
            there = (self.lines().index(line) % 2,)
        total = self.held[where].astype(jnp.float32) + buf[there].astype(jnp.float32)
        self.held[where] = total.astype(self.held.dtype)

    def launch(self, stage, line):
        axis, place = self.order[stage], self.place
        size, here = place.sizes[axis], place.here[axis]
        if size == 2:
            self.copy(stage, line, 1 - here, 1 - 2 * here).start()
        elif size > 2:
            for turn in range(1, size):
                for step, along in ((1, size - turn), (-1, turn - 1)):

                    @pl.when((here == (0 if step > 0 else size - 1)))
                    def _(step=step, along=along):
                        self.copy(stage, line, along, step).start()

    def pass_on(self, stage, line, turn):
        axis, place = self.order[stage], self.place
        size, here = place.sizes[axis], place.here[axis]
        for step, along in ((1, size - turn), (-1, turn - 1)):
            ahead = (along > here) if step > 0 else (along < here)

            @pl.when(ahead & place.can(axis, -step))
            def _(step=step, along=along):
                self.add(stage, line, along, along)
                self.copy(stage, line, along, step).start()

    def finish(self, stage, line):
        axis, place = self.order[stage], self.place
        size, here = place.sizes[axis], place.here[axis]
        if size == 2:
            self.add(stage, line, here, 0, stage == 3)
        elif size > 2:
            for step, number in ((-1, here), (1, size)):

                @pl.when(place.can(axis, step))
                def _(number=number):
                    self.add(stage, line, here, number, stage == 3)

    def whole(self, stage, line):
        for turn in range(1, self.place.sizes[self.order[stage]]):
            if self.place.sizes[self.order[stage]] > 2:
                self.pass_on(stage, line, turn)
        self.finish(stage, line)

    def line_hop(self, along, hop):
        place, stage = self.place, self.order.index(LINE)
        size, here = place.sizes[LINE], place.here[LINE]
        for step, at, ahead in ((1, hop, along > hop), (-1, size - 1 - hop, along < size - 1 - hop)):
            if not ahead:
                continue

            @pl.when(here == at)
            def _(step=step):
                if hop:
                    self.add(stage, here, along, along)
                self.copy(stage, here, along, step).start()

    def steps(self):
        place = self.place
        size, here = place.sizes[LINE], place.here[LINE]
        lines = self.lines()
        spot = self.order.index(LINE)

        def begin(k):
            self.own(lines[k]).start()
            self.launch(0, lines[k])

        begin(0)
        yield
        for turn in range(2 * size + spot - 2):
            if turn + 1 < size:
                begin(turn + 1)
            for k in range(size):
                hop = turn - k - spot
                if 0 <= hop < size - 1:
                    self.line_hop(lines[k], hop)
            for stage in range(spot - 1, -1, -1):
                k = turn - stage
                if not 0 <= k < size:
                    continue
                if stage == 0:
                    self.own(lines[k]).wait()
                self.whole(stage, lines[k])
                if stage + 1 < spot:
                    self.launch(stage + 1, lines[k])
            yield
        if spot == 3:
            self.begin_out()
        self.finish(spot, here)
        for stage in range(spot + 1, 4):
            if stage == 3:
                self.begin_out()
            self.launch(stage, here)
            yield
            self.whole(stage, here)

    def begin_out(self):
        first, width = self.columns
        mine = self.held[tuple(self.place.here[:3])]
        self.out[:, pl.ds(first, width)] = mine.astype(jnp.float32)

    def drain(self):
        place = self.place
        spot = self.order.index(LINE)
        for stage in range(4):
            axis = self.order[stage]
            size, here = place.sizes[axis], place.here[axis]
            for line in range(place.sizes[LINE]) if stage < spot else [place.here[LINE]]:
                if size == 2:
                    self.copy(stage, line, 1 - here, 1 - 2 * here).wait_send()
                elif size > 2:
                    for along in range(size):
                        for step in (-1, 1):

                            @pl.when((along > here) if step > 0 else (along < here))
                            def _(along=along, step=step, line=line, stage=stage):
                                self.copy(stage, line, along, step).wait_send()


def scatter_kernel(sizes, parts, count, *refs):
    partials, outs = refs[:count], refs[count : 2 * count]
    load, send, recv = refs[2 * count : 2 * count + 3]
    scratch = list(refs[2 * count + 3 :])
    place = Place(sizes)
    place.greet()
    scatters = []
    for k, (which, columns, order) in enumerate(parts):
        held, *bufs = scratch[5 * k : 5 * k + 5]
        scatters.append(
            Scatter(place, k, order, partials[which], columns, held, bufs, outs[which], load, send, recv)
        )
    run_all([s.steps() for s in scatters])
    for s in scatters:
        s.drain()


def scatter_scratch(sizes, parts, shapes, dtype):
    scratch = []
    for which, (_, width), order in parts:
        rows = shapes[which][-2]
        scratch.append(pltpu.VMEM(sizes[:3] + (rows, width), dtype))
        stages = (CORE,) + order
        for stage, axis in enumerate(stages):
            free = tuple(sizes[a] for a in range(1, 3) if a not in stages[: stage + 1])
            slots = 1 if sizes[axis] <= 2 else sizes[axis] + 1
            if axis == LINE:
                lead = (slots,)
            elif axis == CORE:
                lead = (2,)
            else:
                lead = (1 if LINE in stages[:stage] else sizes[LINE], slots)
            scratch.append(pltpu.VMEM(lead + free + (rows, width), dtype))
    return scratch


def scatter_all(partials, parts, sizes, collective_id):
    count = 1
    for size in sizes:
        count *= size
    partials = [p.reshape(sizes + (p.shape[0] // count, p.shape[1])) for p in partials]
    lanes = max([1] + [size + 1 for size in sizes[1:] if size > 2])
    sems = (len(parts), 4, sizes[0] + 1, lanes)
    return pl.pallas_call(
        functools.partial(scatter_kernel, sizes, parts, len(partials)),
        out_shape=[jax.ShapeDtypeStruct(p.shape[4:], jnp.float32) for p in partials],
        in_specs=[pl.BlockSpec(memory_space=pl.ANY)] * len(partials),
        out_specs=[pl.BlockSpec(memory_space=pltpu.VMEM)] * len(partials),
        scratch_shapes=[
            pltpu.SemaphoreType.DMA((len(parts), sizes[0])),
            pltpu.SemaphoreType.DMA(sems),
            pltpu.SemaphoreType.DMA(sems),
        ]
        + scatter_scratch(sizes, parts, [p.shape for p in partials], partials[0].dtype),
        compiler_params=pltpu.CompilerParams(
            collective_id=collective_id, has_side_effects=True, vmem_limit_bytes=60 << 20
        ),
    )(*partials)


def partners_of(sizes):
    hops = []
    for axis in (2, 1, 0):
        stride = 1
        while stride < sizes[axis]:
            hops.append((axis, stride))
            stride *= 2
    return hops


def scan_kernel(sizes, backward, *refs):
    place = Place(sizes)
    place.greet(partners_of(sizes))
    scan_states(place, backward, lambda hop: None, *refs)


def scan_states(
    place, backward, between, state_ref, logs_ref, out_ref,
    sib, sib_logs, first, first_logs, pre, pre_logs, total, total_logs, wire, wire_logs, got, got_logs, other, send, recv,
):
    core = place.here[CORE]
    hops = partners_of(place.sizes)
    half = HEADS // 2
    mine, theirs = pl.ds(half * core, half), pl.ds(half * (1 - core), half)
    sibling = place.toward(CORE, 1 - 2 * core)
    bit, partner = place.bit, place.partner

    def remote(source, target, number, device):
        return pltpu.make_async_remote_copy(
            src_ref=source, dst_ref=target, send_sem=send.at[number], recv_sem=recv.at[number],
            device_id=device, device_id_type=MESH,
        )

    def scaled(logs, states, added):
        return [jnp.exp(logs[h, 0:1, :]) * states[h] + added[h] for h in range(half)]

    swap = [
        remote(state_ref.at[theirs], sib, 0, sibling),
        remote(logs_ref.at[theirs], sib_logs, 1, sibling),
    ]
    for copy in swap:
        copy.start()
    for copy in swap:
        copy.wait_recv()
    starts = core == (1 if backward else 0)

    @pl.when(starts)
    def _():
        first[...] = state_ref[mine]
        first_logs[...] = logs_ref[mine]
        new = scaled(sib_logs, first, sib)
        for h in range(half):
            total[h] = new[h]

    @pl.when(jnp.logical_not(starts))
    def _():
        first[...] = sib[...]
        first_logs[...] = sib_logs[...]
        new = scaled(logs_ref.at[mine], first, state_ref.at[mine])
        for h in range(half):
            total[h] = new[h]

    total_logs[...] = logs_ref[mine] + sib_logs[...]
    pre[...] = jnp.zeros_like(pre)
    pre_logs[...] = jnp.zeros_like(pre_logs)
    pending = list(swap)
    for k, (axis, stride) in enumerate(hops):
        between(k)
        last = k == len(hops) - 1
        wire[k] = total[...].astype(wire.dtype)
        wire_logs[k] = total_logs[...]
        copies = [
            remote(wire.at[k], got.at[k], 2 + 2 * k, partner(axis, stride)),
            remote(wire_logs.at[k], got_logs.at[k], 3 + 2 * k, partner(axis, stride)),
        ]
        for copy in copies:
            copy.start()
        pending += copies
        for copy in copies:
            copy.wait_recv()
        earlier = bit(axis, stride) == (1 if backward else 0)
        arrived = [got[k, h].astype(jnp.float32) for h in range(half)]

        @pl.when(jnp.logical_not(earlier))
        def _(k=k, arrived=arrived, last=last):
            new = scaled(pre_logs, arrived, pre)
            for h in range(half):
                pre[h] = new[h]
            pre_logs[...] = pre_logs[...] + got_logs[k]
            if not last:
                new = scaled(total_logs, arrived, total)
                for h in range(half):
                    total[h] = new[h]

        if not last:

            @pl.when(earlier)
            def _(k=k, arrived=arrived):
                new = scaled(got_logs.at[k], total, arrived)
                for h in range(half):
                    total[h] = new[h]

            total_logs[...] = total_logs[...] + got_logs[k]
    second = scaled(first_logs, pre, first)

    @pl.when(starts)
    def _():
        for h in range(half):
            other[h] = second[h]
        out_ref[mine] = pre[...]

    @pl.when(jnp.logical_not(starts))
    def _():
        other[...] = pre[...]
        for h in range(half):
            out_ref[half * core + h] = second[h]

    back = remote(other, out_ref.at[mine], 2 + 2 * len(hops), sibling)
    back.start()
    back.wait_recv()
    for copy in pending + [back]:
        copy.wait_send()


def scan_scratch(sizes):
    half, hops = HEADS // 2, len(partners_of(sizes))
    block, tile = (half, HV, HK), (half, 8, HK)
    return [
        pltpu.VMEM(block, jnp.float32), pltpu.VMEM(tile, jnp.float32),
        pltpu.VMEM(block, jnp.float32), pltpu.VMEM(tile, jnp.float32),
        pltpu.VMEM(block, jnp.float32), pltpu.VMEM(tile, jnp.float32),
        pltpu.VMEM(block, jnp.float32), pltpu.VMEM(tile, jnp.float32),
        pltpu.VMEM((hops,) + block, jnp.bfloat16), pltpu.VMEM((hops,) + tile, jnp.float32),
        pltpu.VMEM((hops,) + block, jnp.bfloat16), pltpu.VMEM((hops,) + tile, jnp.float32),
        pltpu.VMEM(block, jnp.float32),
        pltpu.SemaphoreType.DMA((3 + 2 * hops,)),
        pltpu.SemaphoreType.DMA((3 + 2 * hops,)),
    ]


def entering(state, logs, sizes, backward, collective_id):
    return pl.pallas_call(
        functools.partial(scan_kernel, sizes, backward),
        out_shape=jax.ShapeDtypeStruct(state.shape, jnp.float32),
        in_specs=[pl.BlockSpec(memory_space=pltpu.VMEM)] * 2,
        out_specs=pl.BlockSpec(memory_space=pltpu.VMEM),
        scratch_shapes=scan_scratch(sizes),
        compiler_params=pltpu.CompilerParams(
            collective_id=collective_id, has_side_effects=True, vmem_limit_bytes=32 << 20
        ),
    )(state, logs)


CHUNK = 128
ROWS = 256
FTILE = 256
F32, BF16 = jnp.float32, jnp.bfloat16


def nn(left, right):
    return jnp.dot(left, right, preferred_element_type=F32)


def nt(left, right):
    return lax.dot_general(left, right, (((1,), (1,)), ((), ())), preferred_element_type=F32)


def tn(left, right):
    return lax.dot_general(left, right, (((0,), (0,)), ((), ())), preferred_element_type=F32)


def sigmoid(v):
    return 1.0 / (1.0 + jnp.exp(-v))


def causal_mask(size):
    return lax.broadcasted_iota(jnp.int32, (size, size), 0) >= lax.broadcasted_iota(jnp.int32, (size, size), 1)


def triangle(upper):
    rows = lax.broadcasted_iota(jnp.int32, (CHUNK, CHUNK), 0)
    columns = lax.broadcasted_iota(jnp.int32, (CHUNK, CHUNK), 1)
    kept = (columns >= rows) if upper else (columns <= rows)
    return jnp.where(kept, 1.0, 0.0).astype(BF16)


def running(matrix, values):
    high = values.astype(BF16)
    low = (values - high.astype(F32)).astype(BF16)
    return nn(matrix, high) + nn(matrix, low)


def halves(values):
    high = values.astype(BF16)
    return high, (values - high.astype(F32)).astype(BF16)


def fine_nt(left, right):
    (high, low), (other, rest) = left, right
    return nt(high, other) + (nt(high, rest) + nt(low, other))


def inverse_rms(values):
    return lax.rsqrt(jnp.mean(values * values, axis=-1, keepdims=True) + 1e-06)


def heads_of(width):
    return [slice(h * width, (h + 1) * width) for h in range(HEADS)]


def small_rows(extra):
    lanes = lax.broadcasted_iota(jnp.int32, (8, extra.shape[1]), 1)
    rows = lax.broadcasted_iota(jnp.int32, (8, extra.shape[1]), 0)
    return nt(jnp.where(lanes == rows + RANK, 1.0, 0.0).astype(BF16), extra)


def with_one(mid):
    lanes = lax.broadcasted_iota(jnp.int32, mid.shape, 1)
    return jnp.where(lanes < RANK, mid, jnp.where(lanes == RANK, 1.0, 0.0)).astype(BF16)


def project_rows(tokens, gain, weight, up, outs, final_ref, logs_ref):
    normed_ref, query_ref, key_ref, value_ref, gate_ref, mid_ref, logit_ref, within_ref, update_ref = outs
    inputs = tokens[...].astype(F32)
    normed = (inputs * inverse_rms(inputs) * gain).astype(BF16)
    normed_ref[...] = normed
    keys = HEADS * HK
    values = HEADS * HV
    mid = with_one(nn(normed, weight(2 * keys + 2 * values, 128)))
    mid_ref[...] = mid
    logit = nt(mid, up)
    logit_ref[...] = logit
    query_ref[...] = nn(normed, weight(0, keys)).astype(BF16)
    key_ref[...] = nn(normed, weight(keys, keys)).astype(BF16)
    value_ref[...] = nn(normed, weight(2 * keys, values)).astype(BF16)
    gate_ref[...] = nn(normed, weight(2 * keys + values, values)).astype(BF16)
    decay = (jnp.minimum(logit, 0.0) - jnp.log1p(jnp.exp(-jnp.abs(logit)))) * (1.0 / 16.0)
    lower = triangle(False)
    for c in range(ROWS // CHUNK):
        rows = pl.ds(c * CHUNK, CHUNK)
        within = running(lower, decay[c * CHUNK : (c + 1) * CHUNK])
        within_ref[rows, :] = within
        total = within[CHUNK - 1 : CHUNK]
        ending = (key_ref[rows, :].astype(F32) * jnp.exp(total - within)).astype(BF16)
        for h, (ks, vs) in enumerate(zip(heads_of(HK), heads_of(HV))):
            update = tn(value_ref[rows, vs], ending[:, ks])
            update_ref[c, h] = update.astype(BF16)
            final_ref[h] = final_ref[h] * jnp.exp(total[:, ks]) + update
            logs_ref[h] = logs_ref[h] + total[:, ks]


def project_kernel(tokens, gains, weights, up, *refs):
    outs, (final_ref, logs_ref) = refs[:9], refs[9:]

    @pl.when(pl.program_id(0) == 0)
    def _():
        final_ref[...] = jnp.zeros_like(final_ref)
        logs_ref[...] = jnp.zeros_like(logs_ref)

    project_rows(
        tokens, gains[0:1], lambda first, width: weights[:, first : first + width], up[...], outs, final_ref, logs_ref
    )


def mix_rows(tokens, query, key, value, gate, within_all, update, state, head_gain, out_weight, ffn_gain, outs):
    mixed_ref, gated_ref, hidden_ref, ffn_ref, starts_ref = outs
    mask = causal_mask(CHUNK)
    for c in range(ROWS // CHUNK):
        rows = pl.ds(c * CHUNK, CHUNK)
        within = within_all[rows, :]
        middle = within[CHUNK // 2 - 1 : CHUNK // 2]
        total = within[CHUNK - 1 : CHUNK]
        scaled = query[rows, :].astype(F32) * HK**-0.5
        from_start = (scaled * jnp.exp(within)).astype(BF16)
        left = halves(scaled * jnp.exp(within - middle))
        right = halves(key[rows, :].astype(F32) * jnp.exp(middle - within))
        for h, (ks, vs) in enumerate(zip(heads_of(HK), heads_of(HV))):
            start = state[h].astype(BF16)
            starts_ref[c, h] = start
            scores = jnp.where(mask, fine_nt([p[:, ks] for p in left], [p[:, ks] for p in right]), 0.0).astype(BF16)
            mixed = nn(scores, value[rows, vs]) + nt(from_start[:, ks], start)
            state[h] = state[h] * jnp.exp(total[:, ks]) + update[c, h].astype(F32)
            mixed_ref[rows, vs] = mixed
            gates = gate[rows, vs].astype(F32)
            gated = mixed * inverse_rms(mixed) * head_gain[:, vs] * (gates * sigmoid(gates))
            gated_ref[rows, vs] = gated.astype(BF16)
    hidden = tokens[...].astype(F32) + nn(gated_ref[...], out_weight)
    hidden_ref[...] = hidden
    ffn_ref[...] = (hidden * inverse_rms(hidden) * ffn_gain).astype(BF16)


def mix_kernel(tokens, query, key, value, gate, within_all, update, entering_ref, gains, out_weight, *refs):
    outs, state = refs[:5], refs[5]

    @pl.when(pl.program_id(0) == 0)
    def _():
        state[...] = entering_ref[...]

    mix_rows(
        tokens, query, key, value, gate, within_all, update, state, gains[1:2], out_weight[...], gains[2:3], outs
    )


def ffn_kernel(
    ffn_in, ffn_in_t, cotangent, hidden, gate_weight, up_weight, down_weight,
    out_ref, back_ref, gate_grad, up_grad, down_grad,
):
    @pl.when(pl.program_id(0) == 0)
    def _():
        out_ref[...] = hidden[...]
        back_ref[...] = jnp.zeros_like(back_ref)

    gate, up = nn(ffn_in[...], gate_weight[...]), nn(ffn_in[...], up_weight[...])
    back = nt(cotangent[...], down_weight[...])
    share = sigmoid(gate)
    passed = gate * share
    inner = (passed * up).astype(BF16)
    d_up = (back * passed).astype(BF16)
    d_gate = (back * up * (share * (1.0 + gate * (1.0 - share)))).astype(BF16)
    out_ref[...] += nn(inner, down_weight[...])
    back_ref[...] += nt(d_gate, gate_weight[...]) + nt(d_up, up_weight[...])
    gate_grad[...] = nn(ffn_in_t[...], d_gate).astype(BF16)
    up_grad[...] = nn(ffn_in_t[...], d_up).astype(BF16)
    down_grad[...] = tn(inner, cotangent[...]).astype(BF16)


def norm_back(values, gain, grad):
    scale = inverse_rms(values)
    inner = grad * gain
    along = jnp.mean(inner * values, axis=-1, keepdims=True)
    return scale * inner - values * (scale * scale * scale * along), grad * values * scale


def unmix_kernel(
    ffn_back, hidden, cotangent, gate, mixed, query, within_all, gains, out_weight,
    d_hidden_ref, low_ref, d_gate_ref, d_mixed_ref, update_ref, enters_ref, ffn_gain_ref, head_gain_ref,
):
    @pl.when(pl.program_id(0) == 0)
    def _():
        enters_ref[...] = jnp.zeros_like(enters_ref)
        ffn_gain_ref[...] = jnp.zeros_like(ffn_gain_ref)
        head_gain_ref[...] = jnp.zeros_like(head_gain_ref)

    through, terms = norm_back(hidden[...], gains[2:3], ffn_back[...])
    ffn_gain_ref[...] += jnp.sum(terms, axis=0, keepdims=True)
    d_hidden = cotangent[...].astype(F32) + through
    d_hidden_ref[...] = d_hidden
    low = d_hidden.astype(BF16)
    low_ref[...] = low
    d_gated = nt(low, out_weight[...])
    for vs in heads_of(HV):
        value = mixed[:, vs]
        scale = inverse_rms(value)
        headed = value * scale
        gates = gate[:, vs].astype(F32)
        share = sigmoid(gates)
        passed = gates * share
        grad, gain = d_gated[:, vs], gains[1:2, vs]
        head_gain_ref[:, vs] += jnp.sum(grad * headed * passed, axis=0, keepdims=True)
        d_gate_ref[:, vs] = (grad * headed * gain * (share * (1.0 + gates * (1.0 - share)))).astype(BF16)
        d_headed = grad * gain * passed
        along = jnp.mean(d_headed * headed, axis=-1, keepdims=True)
        d_mixed_ref[:, vs] = scale * (d_headed - headed * along)
    for c in reversed(range(ROWS // CHUNK)):
        rows = slice(c * CHUNK, (c + 1) * CHUNK)
        within = within_all[rows]
        total = within[CHUNK - 1 : CHUNK]
        from_start = (query[rows].astype(F32) * HK**-0.5 * jnp.exp(within)).astype(BF16)
        for h, (ks, vs) in enumerate(zip(heads_of(HK), heads_of(HV))):
            update = tn(d_mixed_ref[rows, vs].astype(BF16), from_start[:, ks])
            update_ref[c, h] = update.astype(BF16)
            enters_ref[h] = enters_ref[h] * jnp.exp(total[:, ks]) + update


def back_rows(
    tokens, query, key, value, logit, within_all, d_mixed, starts, update, d_gate, d_hidden, gains, weights, up,
    d_proj_ref, d_logit_ref, tokens_grad_ref, gain_ref, state,
):
    mask = causal_mask(CHUNK)
    upper = triangle(True)
    keys = HEADS * HK
    for c in reversed(range(ROWS // CHUNK)):
        rows = slice(c * CHUNK, (c + 1) * CHUNK)
        within = within_all[rows]
        middle = within[CHUNK // 2 - 1 : CHUNK // 2]
        total = within[CHUNK - 1 : CHUNK]
        factor = jnp.exp(total)
        queries, keys_f = query[rows].astype(F32), key[rows].astype(F32)
        q_start, q_middle = jnp.exp(within) * HK**-0.5, jnp.exp(within - middle) * HK**-0.5
        k_middle, k_end = jnp.exp(middle - within), jnp.exp(total - within)
        lefts, rights = halves(queries * q_middle), halves(keys_f * k_middle)
        left, right = lefts[0], rights[0]
        ending = (keys_f * k_end).astype(BF16)
        moves, extras = [], []
        for h, (ks, vs) in enumerate(zip(heads_of(HK), heads_of(HV))):
            start, after = starts[c, h], state[h].astype(BF16)
            (grad, rest), values = halves(d_mixed[rows, vs]), value[rows, vs]
            scores = jnp.where(mask, fine_nt([p[:, ks] for p in lefts], [p[:, ks] for p in rights]), 0.0).astype(BF16)
            d_scores = jnp.where(mask, nt(grad, values) + nt(rest, values), 0.0).astype(BF16)
            d_value = tn(scores, grad) + nt(ending[:, ks], after)
            d_query = nn(d_scores, right[:, ks]) * q_middle[:, ks] + nn(grad, start) * q_start[:, ks]
            d_end = nn(values, after) * k_end[:, ks]
            d_key = tn(d_scores, left[:, ks]) * k_middle[:, ks] + d_end
            d_proj_ref[rows, ks] = d_query.astype(BF16)
            d_proj_ref[rows, slice(keys + ks.start, keys + ks.stop)] = d_key.astype(BF16)
            d_proj_ref[rows, slice(2 * keys + vs.start, 2 * keys + vs.stop)] = d_value.astype(BF16)
            moves.append(queries[:, ks] * d_query - keys_f[:, ks] * d_key)
            extras.append(
                jnp.sum(keys_f[:, ks] * d_end, axis=0, keepdims=True)
                + factor[:, ks] * jnp.sum(start.astype(F32) * state[h], axis=0, keepdims=True)
            )
            state[h] = state[h] * factor[:, ks] + update[c, h].astype(F32)
        d_decay = running(upper, jnp.concatenate(moves, axis=1)) + jnp.concatenate(extras, axis=1)
        d_logit = d_decay * sigmoid(-logit[rows]) * (1.0 / 16.0)
        d_logit_ref[rows] = d_logit.astype(BF16)
    d_mid = nn(d_logit_ref[...], up[...])
    d_mid = jnp.where(lax.broadcasted_iota(jnp.int32, d_mid.shape, 1) < RANK, d_mid, 0.0).astype(BF16)
    inner = 2 * keys + HEADS * HV
    outer = inner + HEADS * HV
    d_proj_ref[:, inner:outer] = d_gate[...]
    d_proj_ref[:, outer:] = d_mid
    d_normed = nt(d_proj_ref[...], weights[...])
    through, terms = norm_back(tokens[...].astype(F32), gains[0:1], d_normed)
    gain_ref[...] += jnp.sum(terms, axis=0, keepdims=True)
    tokens_grad_ref[...] = d_hidden[...] + through


def back_kernel(*refs):
    tiles, leaving_ref, refs = refs[:11], refs[11], refs[12:]
    gain_ref, state = refs[-2:]

    @pl.when(pl.program_id(0) == 0)
    def _():
        state[...] = leaving_ref[...]
        gain_ref[...] = jnp.zeros_like(gain_ref)

    back_rows(*tiles, *refs)


def tail_kernel(sizes, steps, count, *refs):
    tiles, (enters, logs), refs = refs[:11], refs[11:13], refs[13:]
    kept, partials, refs = refs[:3], refs[3 : 3 + count], refs[3 + count :]
    outs, gain_ref, sums, refs = refs[:3], refs[3], refs[4 : 4 + count], refs[4 + count :]
    state, load, send, recv = refs[:4]
    scratch, scan = refs[4 : 4 + 5 * len(TAIL_PARTS)], refs[4 + 5 * len(TAIL_PARTS) :]
    place = Place(sizes)
    step = pl.program_id(0)
    scatters = []
    for k, (which, columns, order) in enumerate(TAIL_PARTS):
        held, *bufs = scratch[5 * k : 5 * k + 5]
        scatters.append(
            Scatter(place, k, order, partials[which], columns, held, bufs, sums[which], load, send, recv)
        )
    moves = [s.steps() for s in scatters]

    def turn():
        for move in moves:
            next(move, None)

    def during(hop):
        for _ in range(TAIL_TURNS[0].count(hop)):
            turn()

    @pl.when(step == 0)
    def _():
        gain_ref[...] = jnp.zeros_like(gain_ref)
        place.greet(partners_of(sizes))
        turn()
        scan_states(place, True, during, enters, logs, state, *scan)

    for k in range(1, steps + 1):

        @pl.when(step == k)
        def _(k=k):
            for _ in range(TAIL_TURNS[1].count(k)):
                turn()

    @pl.when(step > 0)
    def _():
        back_rows(*tiles, *kept, *outs, gain_ref, state)

    @pl.when(step == steps)
    def _():
        run_all(moves)
        for s in scatters:
            s.drain()


def rows_spec(width, steps, backward):
    return pl.BlockSpec((ROWS, width), (lambda i: (steps - 1 - i, 0)) if backward else (lambda i: (i, 0)))


def chunks_spec(steps, backward):
    return pl.BlockSpec(
        (ROWS // CHUNK, HEADS, HV, HK),
        (lambda i: (steps - 1 - i, 0, 0, 0)) if backward else (lambda i: (i, 0, 0, 0)),
    )


def kept_spec(shape):
    return pl.BlockSpec(shape, lambda i: (0,) * len(shape), pipeline_mode=pl.Buffered(1))


def kept_out(shape):
    return pl.BlockSpec(shape, lambda i: (0,) * len(shape))


PARAMS = dict(vmem_limit_bytes=60 << 20)
STATE = (HEADS, HV, HK)


def project(tokens, gains, weights, up):
    length, width = tokens.shape
    steps, keys, values = length // ROWS, HEADS * HK, HEADS * HV
    row = lambda w: rows_spec(w, steps, False)
    chunks = (length // CHUNK,) + STATE
    shape = jax.ShapeDtypeStruct
    return pl.pallas_call(
        project_kernel,
        grid=(steps,),
        in_specs=[row(width)] + [kept_spec(a.shape) for a in (gains, weights, up)],
        out_specs=[row(w) for w in (width, keys, keys, values, values, 128, keys, keys)]
        + [chunks_spec(steps, False), kept_out(STATE), kept_out((HEADS, 8, HK))],
        out_shape=[shape((length, w), BF16) for w in (width, keys, keys, values, values, 128)]
        + [shape((length, keys), F32)] * 2
        + [shape(chunks, BF16), shape(STATE, F32), shape((HEADS, 8, HK), F32)],
        compiler_params=pltpu.CompilerParams(**PARAMS),
    )(tokens, gains, weights, up)


def mix(tokens, query, key, value, gate, within, update, entered, gains, out_weight):
    length, width = tokens.shape
    steps, keys, values = length // ROWS, HEADS * HK, HEADS * HV
    row = lambda w: rows_spec(w, steps, False)
    shape = jax.ShapeDtypeStruct
    return pl.pallas_call(
        mix_kernel,
        grid=(steps,),
        in_specs=[row(w) for w in (width, keys, keys, values, values, keys)]
        + [chunks_spec(steps, False)]
        + [kept_spec(a.shape) for a in (entered, gains, out_weight)],
        out_specs=[row(w) for w in (values, values, width, width)] + [chunks_spec(steps, False)],
        out_shape=[
            shape((length, values), F32), shape((length, values), BF16),
            shape((length, width), F32), shape((length, width), BF16), shape(update.shape, BF16),
        ],
        scratch_shapes=[pltpu.VMEM(STATE, F32)],
        compiler_params=pltpu.CompilerParams(**PARAMS),
    )(tokens, query, key, value, gate, within, update, entered, gains, out_weight)


FRONT_PARTS = (
    (0, (0, 128), ORDERS[0]),
    (1, (0, 1024), ORDERS[0]),
    (1, (1024, 1024), ORDERS[1]),
    (1, (2048, 1152), ORDERS[2]),
    (2, (0, 1024), ORDERS[3]),
    (3, (0, 2816), ORDERS[0]),
    (4, (0, 2816), ORDERS[1]),
    (5, (0, 512), ORDERS[2]),
    (5, (512, 512), ORDERS[3]),
)
FIRST_PARTS = 5
FRONT_TURNS = (1, 2, (2,), 1)


def front_kernel(sizes, steps, *refs):
    tokens, shards, refs = refs[0], refs[1:7], refs[7:]
    buffers, refs = refs[:6], refs[6:]
    outs, mixed_outs, (logs_out, gains_out), refs = refs[:8], refs[8:13], refs[13:15], refs[15:]
    up_all, proj_all, out_all, query, key, value, gate, within, update, state, final, logs, gains, refs = *refs[:13], refs[13:]
    send, recv, own, flush = refs[:4]
    scan = refs[4:]
    place = Place(sizes)
    step = pl.program_id(0)
    here = tuple(place.here)
    held = (up_all, proj_all, out_all) + tuple(buffers[3:])
    gathers = [
        Gather(place, k, order, held[which], columns, send, recv)
        for k, (which, columns, order) in enumerate(FRONT_PARTS)
    ]
    owned = [pltpu.make_async_copy(shards[k], buffers[k].at[here], own.at[k]) for k in (3, 4, 5)]
    flushes = [pltpu.make_async_copy(held[k], buffers[k], flush.at[k]) for k in range(3)]
    later = [g.steps() for g in gathers[FIRST_PARTS:]]

    def turn():
        for g in later:
            next(g, None)

    def during(hop):
        if hop in FRONT_TURNS[2]:
            turn()

    @pl.when(step == 0)
    def _():
        for copy in owned:
            copy.start()
        for k in range(3):
            held[k][here] = shards[k][...]
        place.greet(partners_of(sizes))
        for copy in owned:
            copy.wait()
        run_all([g.steps() for g in gathers[:FIRST_PARTS]])
        turn()
        flushes[0].start()
        flushes[1].start()
        flushes[2].start()
        extra = 2 * HEADS * (HK + HV)
        gains[...] = small_rows(proj_all[..., pl.ds(extra, 128)].reshape(-1, 128))
        gains_out[...] = gains[...]
        final[...] = jnp.zeros_like(final)
        logs[...] = jnp.zeros_like(logs)
        for _ in range(FRONT_TURNS[0]):
            turn()

    @pl.when(step < steps)
    def _():
        rows = pl.ds(pl.multiple_of(step * ROWS, ROWS), ROWS)
        chunks = pl.ds(step * (ROWS // CHUNK), ROWS // CHUNK)
        normed_ref, query_ref, key_ref, value_ref, gate_ref, mid_ref, logit_ref, within_ref = outs
        kept = (query, key, value, gate, within)
        tiles = (query_ref, key_ref, value_ref, gate_ref, within_ref)
        project_rows(
            tokens, gains[0:1],
            lambda first, width: proj_all[..., pl.ds(first, width)].reshape(-1, width),
            up_all[...].reshape(-1, 128),
            (normed_ref, query_ref, key_ref, value_ref, gate_ref, mid_ref, logit_ref, within_ref, update.at[chunks]),
            final, logs,
        )
        for whole, tile in zip(kept, tiles):
            whole[rows, :] = tile[...]

    @pl.when(step == steps)
    def _():
        for _ in range(FRONT_TURNS[1]):
            turn()
        logs_out[...] = logs[...]
        scan_states(place, False, during, final, logs, state, *scan)
        for _ in range(FRONT_TURNS[3]):
            turn()

    @pl.when(step >= steps)
    def _():
        at = step - steps
        rows = pl.ds(pl.multiple_of(at * ROWS, ROWS), ROWS)
        chunks = pl.ds(at * (ROWS // CHUNK), ROWS // CHUNK)
        mix_rows(
            tokens, query.at[rows], key.at[rows], value.at[rows], gate.at[rows], within.at[rows], update.at[chunks], state,
            gains[1:2], out_all[...].reshape(-1, out_all.shape[-1]), gains[2:3], mixed_outs,
        )

    @pl.when(step == 2 * steps - 1)
    def _():
        run_all(later)
        for g in gathers:
            g.drain()
        for copy in flushes:
            copy.wait()


def front(tokens, shards, sizes, collective_id):
    length, width = tokens.shape
    steps, keys, values = length // ROWS, HEADS * HK, HEADS * HV
    shape, chunks = jax.ShapeDtypeStruct, (length // CHUNK,) + STATE
    first = lambda w: pl.BlockSpec((ROWS, w), lambda i: (jnp.minimum(i, steps - 1), 0))
    second = lambda w: pl.BlockSpec((ROWS, w), lambda i: (jnp.maximum(i - steps, 0), 0))
    lanes = lanes_of(sizes)
    parts = len(FRONT_PARTS)
    one = lambda w, t: ((length, w), t)
    results = [one(width, BF16), one(keys, BF16), one(keys, BF16), one(values, BF16), one(values, BF16), one(128, BF16), one(keys, F32), one(keys, F32)]
    mixes = [one(values, F32), one(values, BF16), one(width, F32), one(width, BF16)]
    out = pl.pallas_call(
        functools.partial(front_kernel, sizes, steps),
        grid=(2 * steps,),
        in_specs=[pl.BlockSpec((ROWS, width), lambda i: (lax.rem(i, steps), 0))] + [kept_spec(s.shape) for s in shards],
        out_specs=[pl.BlockSpec(memory_space=pl.ANY)] * len(shards)
        + [first(s[1]) for s, _ in results]
        + [second(s[1]) for s, _ in mixes]
        + [pl.BlockSpec((ROWS // CHUNK,) + STATE, lambda i: (jnp.maximum(i - steps, 0), 0, 0, 0))]
        + [kept_out((HEADS, 8, HK)), kept_out((8, width))],
        out_shape=[shape(sizes + s.shape, s.dtype) for s in shards]
        + [shape(s, t) for s, t in results + mixes]
        + [shape(chunks, BF16), shape((HEADS, 8, HK), F32), shape((8, width), F32)],
        scratch_shapes=[pltpu.VMEM(sizes + s.shape, s.dtype) for s in shards[:3]]
        + [pltpu.VMEM((length, w), t) for w, t in ((keys, BF16), (keys, BF16), (values, BF16), (values, BF16), (keys, F32))]
        + [pltpu.VMEM(chunks, BF16), pltpu.VMEM(STATE, F32), pltpu.VMEM(STATE, F32), pltpu.VMEM((HEADS, 8, HK), F32), pltpu.VMEM((8, width), F32)]
        + [
            pltpu.SemaphoreType.DMA((parts, 4, sizes[0], lanes, 2)),
            pltpu.SemaphoreType.DMA((parts, 4, sizes[0], lanes)),
            pltpu.SemaphoreType.DMA((len(shards),)),
            pltpu.SemaphoreType.DMA((3,)),
        ]
        + scan_scratch(sizes),
        compiler_params=pltpu.CompilerParams(collective_id=collective_id, has_side_effects=True, **PARAMS),
    )(tokens, *shards)
    weights = [o.reshape(-1, o.shape[-1]) for o in out[: len(shards)]]
    return weights, out[len(shards) :]


def feed_forward(ffn_in, cotangent, hidden, gate_weight, up_weight, down_weight):
    length, width = ffn_in.shape
    inner = gate_weight.shape[1]
    whole = [ffn_in, ffn_in.T, cotangent, hidden]
    wide = pl.BlockSpec((width, FTILE), lambda i: (0, i))
    tall = pl.BlockSpec((FTILE, width), lambda i: (i, 0))
    shape = jax.ShapeDtypeStruct
    return pl.pallas_call(
        ffn_kernel,
        grid=(inner // FTILE,),
        in_specs=[kept_spec(a.shape) for a in whole] + [wide, wide, tall],
        out_specs=[kept_out((length, width))] * 2 + [wide, wide, tall],
        out_shape=[shape((length, width), F32)] * 2
        + [shape((width, inner), BF16)] * 2 + [shape((inner, width), BF16)],
        compiler_params=pltpu.CompilerParams(**PARAMS),
    )(*whole, gate_weight, up_weight, down_weight)


def unmix(ffn_back, hidden, cotangent, gate, mixed, query, within, gains, out_weight):
    length, width = hidden.shape
    steps, keys, values = length // ROWS, HEADS * HK, HEADS * HV
    row = lambda w: rows_spec(w, steps, True)
    chunks = (length // CHUNK,) + STATE
    shape = jax.ShapeDtypeStruct
    return pl.pallas_call(
        unmix_kernel,
        grid=(steps,),
        in_specs=[row(w) for w in (width, width, width, values, values, keys, keys)]
        + [kept_spec(a.shape) for a in (gains, out_weight)],
        out_specs=[row(w) for w in (width, width, values, values)]
        + [chunks_spec(steps, True), kept_out(STATE), kept_out((1, width)), kept_out((1, values))],
        out_shape=[
            shape((length, width), F32), shape((length, width), BF16), shape((length, values), BF16),
            shape((length, values), F32), shape(chunks, BF16), shape(STATE, F32),
            shape((1, width), F32), shape((1, values), F32),
        ],
        compiler_params=pltpu.CompilerParams(**PARAMS),
    )(ffn_back, hidden, cotangent, gate, mixed, query, within, gains, out_weight)


def back(tiles, leaving, gains, weights, up):
    length, width = tiles[0].shape
    steps, keys, values = length // ROWS, HEADS * HK, HEADS * HV
    row = lambda w: rows_spec(w, steps, True)
    shape = jax.ShapeDtypeStruct
    return pl.pallas_call(
        back_kernel,
        grid=(steps,),
        in_specs=[row(w) for w in (width, keys, keys, values, keys, keys, values)]
        + [chunks_spec(steps, True)] * 2 + [row(values), row(width)]
        + [kept_spec(a.shape) for a in (leaving, gains, weights, up)],
        out_specs=[row(w) for w in (weights.shape[1], keys, width)] + [kept_out((1, width))],
        out_shape=[
            shape((length, weights.shape[1]), BF16), shape((length, keys), BF16),
            shape((length, width), F32), shape((1, width), F32),
        ],
        scratch_shapes=[pltpu.VMEM(STATE, F32)],
        compiler_params=pltpu.CompilerParams(**PARAMS),
    )(*tiles, leaving, gains, weights, up)


TAIL_PARTS = (
    (0, (0, 2816), ORDERS[1][::-1]),
    (1, (0, 2816), ORDERS[0][::-1]),
    (2, (0, 512), ORDERS[2][::-1]),
    (2, (512, 512), ORDERS[3][::-1]),
    (3, (0, 512), ORDERS[2][::-1]),
    (3, (512, 512), ORDERS[3][::-1]),
)
TAIL_TURNS = ((1, 2, 3), (1, 2, 3, 4))
LAST_PARTS = (
    (0, (0, 128), ORDERS[0][::-1]),
    (1, (0, 1024), ORDERS[0][::-1]),
    (1, (1024, 1024), ORDERS[1][::-1]),
    (1, (2048, 640), ORDERS[2][::-1]),
    (1, (2688, 512), ORDERS[3][::-1]),
)


def tail(tiles, enters, logs, gains, weights, up, partials, sizes, collective_id):
    length, width = tiles[0].shape
    steps, keys, values = length // ROWS, HEADS * HK, HEADS * HV
    shape, at = jax.ShapeDtypeStruct, lambda i: steps - jnp.maximum(i, 1)
    row = lambda w: pl.BlockSpec((ROWS, w), lambda i: (at(i), 0))
    chunk = pl.BlockSpec((ROWS // CHUNK,) + STATE, lambda i: (at(i), 0, 0, 0))
    count = len(partials)
    devices = sizes[0] * sizes[1] * sizes[2] * sizes[3]
    partials = [p.reshape(sizes + (p.shape[0] // devices, p.shape[1])) for p in partials]
    lanes = max([1] + [size + 1 for size in sizes[1:] if size > 2])
    sems = (len(TAIL_PARTS), 4, sizes[0] + 1, lanes)
    out = pl.pallas_call(
        functools.partial(tail_kernel, sizes, steps, count),
        grid=(steps + 1,),
        in_specs=[row(w) for w in (width, keys, keys, values, keys, keys, values)]
        + [chunk] * 2 + [row(values), row(width)]
        + [kept_spec(a.shape) for a in (enters, logs, gains, weights, up)]
        + [pl.BlockSpec(memory_space=pl.ANY)] * count,
        out_specs=[row(w) for w in (weights.shape[1], keys, width)] + [kept_out((1, width))]
        + [kept_out(p.shape[4:]) for p in partials],
        out_shape=[
            shape((length, weights.shape[1]), BF16), shape((length, keys), BF16),
            shape((length, width), F32), shape((1, width), F32),
        ] + [shape(p.shape[4:], F32) for p in partials],
        scratch_shapes=[
            pltpu.VMEM(STATE, F32),
            pltpu.SemaphoreType.DMA((len(TAIL_PARTS), sizes[0])),
            pltpu.SemaphoreType.DMA(sems),
            pltpu.SemaphoreType.DMA(sems),
        ]
        + scatter_scratch(sizes, TAIL_PARTS, [p.shape for p in partials], BF16)
        + scan_scratch(sizes),
        compiler_params=pltpu.CompilerParams(collective_id=collective_id, has_side_effects=True, **PARAMS),
    )(*tiles, enters, logs, gains, weights, up, *partials)
    return out[:4], out[4:]


def beside(pieces):
    rows, used = pieces[0].shape[0], sum(p.shape[1] for p in pieces)
    return jnp.concatenate(pieces + [jnp.zeros((rows, 128 - used), pieces[0].dtype)], axis=1)


def local(
    tokens,
    norm_gain,
    query_weight,
    key_weight,
    value_weight,
    gate_weight,
    rank_down,
    rank_up,
    gate_bias,
    head_gain,
    out_weight,
    ffn_gain,
    ffn_gate,
    ffn_up,
    ffn_down,
    cotangent,
):
    sizes = grid_of(lax.axis_size("seq"))
    extra = beside([rank_down] + [g[:, None] for g in (norm_gain, head_gain, ffn_gain)])
    projections = jnp.concatenate([query_weight, key_weight, value_weight, gate_weight, extra], axis=1)
    shards = [beside([rank_up.T, gate_bias[:, None]]), projections, out_weight, ffn_gate, ffn_up, ffn_down]
    if rank_up.shape[1] % 16 == 0:
        weights, kept = front(tokens, shards, sizes, 0)
        up, proj, out, full_fgate, full_fup, full_fdown = weights
        normed, query, key, value, gate, mid, logit, within, mixed, gated, hidden, ffn_in, starts, logs, gains = kept
    else:
        up, proj, out, full_fgate, full_fup, full_fdown = gather_all(shards, FRONT_PARTS, sizes, 0)
        gains = jnp.pad(proj[:, -128 + RANK : -128 + RANK + 3].astype(F32).T, ((0, 5), (0, 0)))
        normed, query, key, value, gate, mid, logit, within, update, final, logs = project(tokens, gains, proj, up)
        incoming = entering(final, logs, sizes, False, 2)
        mixed, gated, hidden, ffn_in, starts = mix(
            tokens, query, key, value, gate, within, update, incoming, gains, out
        )
    block_output, ffn_back, fgate_wgrad, fup_wgrad, fdown_wgrad = feed_forward(
        ffn_in, cotangent, hidden, full_fgate, full_fup, full_fdown
    )
    d_hidden, hidden_low, d_gate, d_mixed, back_update, enters, ffn_gain_grad, head_gain_grad = unmix(
        ffn_back, hidden, cotangent, gate, mixed, query, within, gains, out
    )
    out_wgrad = tn(gated, hidden_low).astype(BF16)
    early = [fgate_wgrad, fup_wgrad, fdown_wgrad, out_wgrad]
    tiles = (tokens, query, key, value, logit, within, d_mixed, starts, back_update, d_gate, d_hidden)
    if rank_up.shape[1] % 16 == 0:
        backs, early_sums = tail(tiles, enters, logs, gains, proj, up, early, sizes, 3)
    else:
        leaving = entering(enters, logs, sizes, True, 3)
        backs = back(tiles, leaving, gains, proj, up)
        early_sums = scatter_all(early, TAIL_PARTS, sizes, 4)
    d_proj, d_logit, tokens_grad, gain_grad = backs
    fgate_sum, fup_sum, fdown_sum, out_sum = early_sums
    proj_wgrad = tn(normed, d_proj).astype(BF16)
    keys_here = rank_up.shape[1]
    gain_grads = jnp.concatenate([gain_grad, head_gain_grad, ffn_gain_grad]).reshape(3, -1, norm_gain.shape[0] // keys_here, keys_here)
    gain_grads = gain_grads.transpose(1, 3, 0, 2).reshape(HEADS * HK, -1)
    up_wgrad = beside([tn(d_logit, mid)[:, : RANK + 1], gain_grads]).astype(BF16)
    up_sum, proj_sum = scatter_all([up_wgrad, proj_wgrad], LAST_PARTS, sizes, 1)
    keys, values = HEADS * HK, HEADS * HV
    last = 2 * (keys + values)
    gain_sum, head_sum, ffn_sum = (
        up_sum[:, RANK + 1 : RANK + 1 + 3 * (norm_gain.shape[0] // keys_here)].reshape(keys_here, 3, -1).transpose(1, 2, 0).reshape(3, -1)
    )
    return (
        block_output,
        tokens_grad,
        gain_sum,
        proj_sum[:, :keys],
        proj_sum[:, keys : 2 * keys],
        proj_sum[:, 2 * keys : 2 * keys + values],
        proj_sum[:, 2 * keys + values : last],
        proj_sum[:, last : last + RANK],
        up_sum[:, :RANK].T,
        up_sum[:, RANK],
        head_sum,
        out_sum,
        ffn_sum,
        fgate_sum,
        fup_sum,
        fdown_sum,
    )


def solution(mesh):
    return jax.shard_map(
        local,
        mesh=mesh,
        in_specs=(
            P("seq", None),
            P("seq"),
            P("seq", None),
            P("seq", None),
            P("seq", None),
            P("seq", None),
            P("seq", None),
            P(None, "seq"),
            P("seq"),
            P("seq"),
            P("seq", None),
            P("seq"),
            P("seq", None),
            P("seq", None),
            P("seq", None),
            P("seq", None),
        ),
        out_specs=(
            P("seq", None),
            P("seq", None),
            P("seq"),
            P("seq", None),
            P("seq", None),
            P("seq", None),
            P("seq", None),
            P("seq", None),
            P(None, "seq"),
            P("seq"),
            P("seq"),
            P("seq", None),
            P("seq"),
            P("seq", None),
            P("seq", None),
            P("seq", None),
        ),
        check_vma=False,
    )
```

```python
import functools

import jax
import jax.numpy as jnp
from jax import lax
from jax.experimental import pallas as pl
from jax.experimental.pallas import tpu as pltpu
from jax.sharding import PartitionSpec as P

HEADS = 4
HK = 128
HV = 256
RANK = 16

MESH = pl.DeviceIdType.MESH
LINE = 0
CORE = 3


def grid_of(count):
    core = 2 if count % 2 == 0 else 1
    rest = count // core
    third = max(k for k in range(1, rest + 1) if rest % k == 0 and k**3 <= rest)
    rest //= third
    second = max(k for k in range(1, rest + 1) if rest % k == 0 and k * k <= rest)
    return (rest // second, second, third, core)


class Place:
    def __init__(self, sizes):
        self.sizes = sizes
        rest = lax.axis_index("seq")
        here = []
        for size in sizes[::-1]:
            here.append(lax.rem(rest, size))
            rest = lax.div(rest, size)
        self.here = here[::-1]

    def index(self, **moved):
        out = 0
        for axis, size in enumerate(self.sizes):
            out = out * size + moved.get(f"a{axis}", self.here[axis])
        return out

    def toward(self, axis, step):
        return (self.index(**{f"a{axis}": self.here[axis] + step}),)

    def can(self, axis, step):
        return self.here[axis] > 0 if step < 0 else self.here[axis] < self.sizes[axis] - 1

    def bit(self, axis, stride):
        return lax.rem(lax.div(self.here[axis], stride), 2)

    def partner(self, axis, stride):
        return self.toward(axis, (1 - 2 * self.bit(axis, stride)) * stride)

    def greet(self, hops=()):
        barrier = pltpu.get_barrier_semaphore()
        total = 0
        for axis, stride in hops:
            if stride > 1:
                pl.semaphore_signal(barrier, inc=1, device_id=self.partner(axis, stride), device_id_type=MESH)
                total = total + 1
        for axis, size in enumerate(self.sizes):
            for step in (-1, 1):
                if size == 1:
                    continue
                able = self.can(axis, step)

                @pl.when(able)
                def _(axis=axis, step=step):
                    pl.semaphore_signal(
                        barrier, inc=1, device_id=self.toward(axis, step), device_id_type=MESH
                    )

                total = total + able.astype(jnp.int32)
        pl.semaphore_wait(barrier, total)


def run_all(coroutines):
    active = list(coroutines)
    while active:
        still = []
        for coroutine in active:
            try:
                next(coroutine)
                still.append(coroutine)
            except StopIteration:
                pass
        active = still


class Gather:
    def __init__(self, place, part, order, buffer, columns, send, recv):
        self.place, self.part, self.order = place, part, order + (CORE,)
        self.buffer, self.columns, self.send, self.recv = buffer, columns, send, recv

    def copy(self, stage, line, along, step):
        place, axis = self.place, self.order[stage]
        where = []
        for a in range(4):
            if a == axis:
                where.append(along)
            elif a == LINE and LINE in self.order[:stage]:
                where.append(line)
            elif a in self.order[:stage]:
                where.append(slice(None))
            else:
                where.append(place.here[a])
        first, width = self.columns
        block = self.buffer.at[tuple(where) + (slice(None), pl.ds(first, width))]
        lane = 0 if place.sizes[axis] == 2 and axis != LINE else along
        if axis == LINE:
            line, lane = along, 0
        return pltpu.make_async_remote_copy(
            src_ref=block,
            dst_ref=block,
            send_sem=self.send.at[self.part, stage, line, lane, (step + 1) // 2],
            recv_sem=self.recv.at[self.part, stage, line, lane],
            device_id=place.toward(axis, step),
            device_id_type=MESH,
        )

    def each_step(self, stage, do):
        axis, place = self.order[stage], self.place
        if place.sizes[axis] == 1:
            return
        if place.sizes[axis] == 2 and axis != LINE:
            do(1 - 2 * place.here[axis], None)
            return
        for step in (-1, 1):
            do(step, place.can(axis, step))

    def launch(self, stage, line):
        axis, place = self.order[stage], self.place

        def do(step, able):
            def go():
                self.copy(stage, line, place.here[axis], step).start()

            go() if able is None else pl.when(able)(go)

        self.each_step(stage, do)

    def finish(self, stage, line):
        axis, place = self.order[stage], self.place
        size, here = place.sizes[axis], place.here[axis]
        if size == 1:
            return
        if size == 2:
            self.copy(stage, line, 1 - here, 1 - 2 * here).wait_recv()
            return
        for hop in range(1, size):
            for step in (-1, 1):
                along = here - step * hop
                valid = (along >= 0) & (along < size)

                @pl.when(valid)
                def _(along=along, step=step):
                    self.copy(stage, line, along, step).wait_recv()

                @pl.when(valid & place.can(axis, step))
                def _(along=along, step=step):
                    self.copy(stage, line, along, step).start()

    def steps(self):
        place = self.place
        size, here = place.sizes[LINE], place.here[LINE]
        spot = self.order.index(LINE)
        for stage in range(spot):
            self.launch(stage, here)
            yield
            self.finish(stage, here)
        for step in (-1, 1):

            @pl.when(place.can(LINE, step))
            def _(step=step):
                self.copy(spot, here, here, step).start()

        later = list(range(spot + 1, 4))
        for turn in range(size + len(later)):
            for age in range(min(turn, len(later)), -1, -1):
                far = turn - age
                if far >= size:
                    continue
                for step in (-1, 1) if far else (1,):
                    line = here - step * far
                    valid = (line >= 0) & (line < size)

                    def advance(line=line, step=step, far=far, age=age):
                        if age == 0 and far:
                            self.copy(spot, line, line, step).wait_recv()

                            @pl.when(place.can(LINE, step))
                            def _():
                                self.copy(spot, line, line, step).start()

                        if age:
                            self.finish(later[age - 1], line)
                        if age < len(later):
                            self.launch(later[age], line)

                    pl.when(valid)(advance) if far else advance()
            yield

    def drain(self):
        place = self.place
        size, here = place.sizes[LINE], place.here[LINE]
        spot = self.order.index(LINE)
        for line in range(size):
            for step in (-1, 1):

                @pl.when(place.can(LINE, step) & ((line <= here) if step > 0 else (line >= here)))
                def _(line=line, step=step):
                    self.copy(spot, line, line, step).wait_send()

        for stage in range(4):
            if stage == spot:
                continue
            axis = self.order[stage]
            lines = [here] if stage < spot else list(range(size))
            for line in lines:
                if place.sizes[axis] == 1:
                    continue
                if place.sizes[axis] == 2:
                    self.copy(stage, line, place.here[axis], 1 - 2 * place.here[axis]).wait_send()
                    continue
                for step in (-1, 1):
                    for along in range(place.sizes[axis]):
                        at = place.here[axis]

                        @pl.when(place.can(axis, step) & ((along <= at) if step > 0 else (along >= at)))
                        def _(line=line, step=step, along=along, stage=stage):
                            self.copy(stage, line, along, step).wait_send()


ORDERS = ((2, 0, 1), (1, 0, 2), (0, 2, 1), (0, 1, 2))


def gather_kernel(sizes, parts, count, *refs):
    shards, buffers = refs[:count], refs[count : 2 * count]
    send, recv, own = refs[2 * count :]
    place = Place(sizes)
    locals_ = [
        pltpu.make_async_copy(shard, buffer.at[tuple(place.here)], own.at[k])
        for k, (shard, buffer) in enumerate(zip(shards, buffers))
    ]
    for copy in locals_:
        copy.start()
    place.greet()
    for copy in locals_:
        copy.wait()
    gathers = [
        Gather(place, k, order, buffers[which], columns, send, recv)
        for k, (which, columns, order) in enumerate(parts)
    ]
    run_all([g.steps() for g in gathers])
    for g in gathers:
        g.drain()


def lanes_of(sizes):
    return max([1] + [size for size in sizes[1:] if size > 2])


def gather_all(shards, parts, sizes, collective_id):
    lanes = lanes_of(sizes)
    out = pl.pallas_call(
        functools.partial(gather_kernel, sizes, parts, len(shards)),
        out_shape=[jax.ShapeDtypeStruct(sizes + s.shape, s.dtype) for s in shards],
        in_specs=[pl.BlockSpec(memory_space=pltpu.VMEM)] * len(shards),
        out_specs=[pl.BlockSpec(memory_space=pl.ANY)] * len(shards),
        scratch_shapes=[
            pltpu.SemaphoreType.DMA((len(parts), 4, sizes[0], lanes, 2)),
            pltpu.SemaphoreType.DMA((len(parts), 4, sizes[0], lanes)),
            pltpu.SemaphoreType.DMA((len(shards),)),
        ],
        compiler_params=pltpu.CompilerParams(collective_id=collective_id, has_side_effects=True),
    )(*shards)
    return [o.reshape((-1,) + o.shape[5:]) for o in out]


PACE = 1


class Scatter:
    def __init__(self, place, part, order, partial, columns, held, bufs, out, load, send, recv):
        self.place, self.part, self.order = place, part, (CORE,) + order
        self.partial, self.columns, self.held, self.bufs, self.out = partial, columns, held, bufs, out
        self.load, self.send, self.recv = load, send, recv

    def lines(self):
        size = self.place.sizes[LINE]
        return [k // 2 if k % 2 == 0 else size - 1 - k // 2 for k in range(size)]

    def own(self, line):
        first, width = self.columns
        where = (line, slice(None), slice(None), self.place.here[CORE], slice(None), pl.ds(first, width))
        return pltpu.make_async_copy(
            self.partial.at[where], self.bufs[0].at[self.lines().index(line) % (2 * PACE)], self.load.at[self.part, line]
        )

    def block(self, stage, line, along):
        where, done = [], self.order[:stage]
        for a in range(3):
            if a == self.order[stage]:
                where.append(along)
            elif a in done:
                where.append(self.place.here[a])
            elif a == LINE:
                where.append(line)
            else:
                where.append(slice(None))
        return tuple(where)

    def slot(self, stage, line, slot):
        axis = self.order[stage]
        if axis == LINE:
            return (slot,)
        if LINE in self.order[:stage]:
            line = 0
        return (line, 0 if self.place.sizes[axis] == 2 else slot)

    def copy(self, stage, line, along, step):
        place, axis = self.place, self.order[stage]
        size = place.sizes[axis]
        first, width = self.columns
        if axis == CORE:
            where = (line, slice(None), slice(None), along, slice(None), pl.ds(first, width))
            source = self.partial.at[where]
        else:
            source = self.held.at[self.block(stage, line, along)]
        arrives = place.here[axis] + step == along
        number = jnp.where(arrives & (step < 0), size, along) if size > 2 else 0
        sem = self.slot(stage, line, along)
        if axis == LINE:
            sem = sem + (0,)
        there = self.slot(stage, line, number)
        return pltpu.make_async_remote_copy(
            src_ref=source,
            dst_ref=self.held.at[line] if axis == CORE else self.bufs[stage].at[there],
            send_sem=self.send.at[(self.part, stage) + sem],
            recv_sem=self.recv.at[(self.part, stage) + there + ((0,) if axis == LINE else ())],
            device_id=place.toward(axis, step),
            device_id_type=MESH,
        )

    def wait(self, stage, line, number):
        there = self.slot(stage, line, number)
        axis = self.order[stage]
        buf = self.held.at[line] if axis == CORE else self.bufs[stage].at[there]
        pltpu.make_async_copy(
            buf, buf, self.recv.at[(self.part, stage) + there + ((0,) if axis == LINE else ())]
        ).wait()
        return self.bufs[stage], there

    def add(self, stage, line, along, number, last=False):
        buf, there = self.wait(stage, line, number)
        if last:
            first, width = self.columns
            self.out[:, pl.ds(first, width)] += buf[there].astype(jnp.float32)
            return
        where = self.block(stage, line, along)
        if self.order[stage] == CORE:
            where = (line, slice(None), slice(None))
            there = (self.lines().index(line) % (2 * PACE),)
        total = self.held[where].astype(jnp.float32) + buf[there].astype(jnp.float32)
        self.held[where] = total.astype(self.held.dtype)

    def launch(self, stage, line):
        axis, place = self.order[stage], self.place
        size, here = place.sizes[axis], place.here[axis]
        if size == 2:
            self.copy(stage, line, 1 - here, 1 - 2 * here).start()
        elif size > 2:
            for turn in range(1, size):
                for step, along in ((1, size - turn), (-1, turn - 1)):

                    @pl.when((here == (0 if step > 0 else size - 1)))
                    def _(step=step, along=along):
                        self.copy(stage, line, along, step).start()

    def pass_on(self, stage, line, turn):
        axis, place = self.order[stage], self.place
        size, here = place.sizes[axis], place.here[axis]
        for step, along in ((1, size - turn), (-1, turn - 1)):
            ahead = (along > here) if step > 0 else (along < here)

            @pl.when(ahead & place.can(axis, -step))
            def _(step=step, along=along):
                self.add(stage, line, along, along)
                self.copy(stage, line, along, step).start()

    def finish(self, stage, line):
        axis, place = self.order[stage], self.place
        size, here = place.sizes[axis], place.here[axis]
        if size == 2:
            self.add(stage, line, here, 0, stage == 3)
        elif size > 2:
            for step, number in ((-1, here), (1, size)):

                @pl.when(place.can(axis, step))
                def _(number=number):
                    self.add(stage, line, here, number, stage == 3)

    def whole(self, stage, line):
        for turn in range(1, self.place.sizes[self.order[stage]]):
            if self.place.sizes[self.order[stage]] > 2:
                self.pass_on(stage, line, turn)
        self.finish(stage, line)

    def line_hop(self, along, hop):
        place, stage = self.place, self.order.index(LINE)
        size, here = place.sizes[LINE], place.here[LINE]
        for step, at, ahead in ((1, hop, along > hop), (-1, size - 1 - hop, along < size - 1 - hop)):
            if not ahead:
                continue

            @pl.when(here == at)
            def _(step=step):
                if hop:
                    self.add(stage, here, along, along)
                self.copy(stage, here, along, step).start()

    def steps(self):
        place = self.place
        size, here = place.sizes[LINE], place.here[LINE]
        lines = self.lines()
        spot = self.order.index(LINE)

        groups = [lines[k : k + PACE] for k in range(0, size, PACE)]

        def begin(group):
            for line in group:
                self.own(line).start()
                self.launch(0, line)

        begin(groups[0])
        yield
        for turn in range(len(groups) + spot + size - 2):
            if turn + 1 < len(groups):
                begin(groups[turn + 1])
            for k, group in enumerate(groups):
                hop = turn - k - spot
                if 0 <= hop < size - 1:
                    for line in group:
                        self.line_hop(line, hop)
            for stage in range(spot - 1, -1, -1):
                k = turn - stage
                if not 0 <= k < len(groups):
                    continue
                for line in groups[k]:
                    if stage == 0:
                        self.own(line).wait()
                    self.whole(stage, line)
                    if stage + 1 < spot:
                        self.launch(stage + 1, line)
            yield
        if spot == 3:
            self.begin_out()
        self.finish(spot, here)
        for stage in range(spot + 1, 4):
            if stage == 3:
                self.begin_out()
            self.launch(stage, here)
            yield
            self.whole(stage, here)

    def begin_out(self):
        first, width = self.columns
        mine = self.held[tuple(self.place.here[:3])]
        self.out[:, pl.ds(first, width)] = mine.astype(jnp.float32)

    def drain(self):
        place = self.place
        spot = self.order.index(LINE)
        for stage in range(4):
            axis = self.order[stage]
            size, here = place.sizes[axis], place.here[axis]
            for line in range(place.sizes[LINE]) if stage < spot else [place.here[LINE]]:
                if size == 2:
                    self.copy(stage, line, 1 - here, 1 - 2 * here).wait_send()
                elif size > 2:
                    for along in range(size):
                        for step in (-1, 1):

                            @pl.when((along > here) if step > 0 else (along < here))
                            def _(along=along, step=step, line=line, stage=stage):
                                self.copy(stage, line, along, step).wait_send()


def scatter_kernel(sizes, parts, count, *refs):
    partials, outs = refs[:count], refs[count : 2 * count]
    load, send, recv = refs[2 * count : 2 * count + 3]
    scratch = list(refs[2 * count + 3 :])
    place = Place(sizes)
    place.greet()
    scatters = []
    for k, (which, columns, order) in enumerate(parts):
        held, *bufs = scratch[5 * k : 5 * k + 5]
        scatters.append(
            Scatter(place, k, order, partials[which], columns, held, bufs, outs[which], load, send, recv)
        )
    run_all([s.steps() for s in scatters])
    for s in scatters:
        s.drain()


def scatter_scratch(sizes, parts, shapes, dtype):
    scratch = []
    for which, (_, width), order in parts:
        rows = shapes[which][-2]
        scratch.append(pltpu.VMEM(sizes[:3] + (rows, width), dtype))
        stages = (CORE,) + order
        for stage, axis in enumerate(stages):
            free = tuple(sizes[a] for a in range(1, 3) if a not in stages[: stage + 1])
            slots = 1 if sizes[axis] <= 2 else sizes[axis] + 1
            if axis == LINE:
                lead = (slots,)
            elif axis == CORE:
                lead = (2 * PACE,)
            else:
                lead = (1 if LINE in stages[:stage] else sizes[LINE], slots)
            scratch.append(pltpu.VMEM(lead + free + (rows, width), dtype))
    return scratch


def scatter_all(partials, parts, sizes, collective_id):
    count = 1
    for size in sizes:
        count *= size
    partials = [p.reshape(sizes + (p.shape[0] // count, p.shape[1])) for p in partials]
    lanes = max([1] + [size + 1 for size in sizes[1:] if size > 2])
    sems = (len(parts), 4, sizes[0] + 1, lanes)
    return pl.pallas_call(
        functools.partial(scatter_kernel, sizes, parts, len(partials)),
        out_shape=[jax.ShapeDtypeStruct(p.shape[4:], jnp.float32) for p in partials],
        in_specs=[pl.BlockSpec(memory_space=pl.ANY)] * len(partials),
        out_specs=[pl.BlockSpec(memory_space=pltpu.VMEM)] * len(partials),
        scratch_shapes=[
            pltpu.SemaphoreType.DMA((len(parts), sizes[0])),
            pltpu.SemaphoreType.DMA(sems),
            pltpu.SemaphoreType.DMA(sems),
        ]
        + scatter_scratch(sizes, parts, [p.shape for p in partials], partials[0].dtype),
        compiler_params=pltpu.CompilerParams(
            collective_id=collective_id, has_side_effects=True, vmem_limit_bytes=60 << 20
        ),
    )(*partials)


def partners_of(sizes):
    hops = []
    for axis in (2, 1, 0):
        stride = 1
        while stride < sizes[axis]:
            hops.append((axis, stride))
            stride *= 2
    return hops


def scan_kernel(sizes, backward, *refs):
    place = Place(sizes)
    place.greet(partners_of(sizes))
    scan_states(place, backward, lambda hop: None, *refs)


def scan_states(
    place, backward, between, state_ref, logs_ref, out_ref,
    sib, sib_logs, first, first_logs, pre, pre_logs, total, total_logs, wire, wire_logs, got, got_logs, other, send, recv,
):
    core = place.here[CORE]
    hops = partners_of(place.sizes)
    half = HEADS // 2
    mine, theirs = pl.ds(half * core, half), pl.ds(half * (1 - core), half)
    sibling = place.toward(CORE, 1 - 2 * core)
    bit, partner = place.bit, place.partner

    def remote(source, target, number, device):
        return pltpu.make_async_remote_copy(
            src_ref=source, dst_ref=target, send_sem=send.at[number], recv_sem=recv.at[number],
            device_id=device, device_id_type=MESH,
        )

    def scaled(logs, states, added):
        return [jnp.exp(logs[h, 0:1, :]) * states[h] + added[h] for h in range(half)]

    swap = [
        remote(state_ref.at[theirs], sib, 0, sibling),
        remote(logs_ref.at[theirs], sib_logs, 1, sibling),
    ]
    for copy in swap:
        copy.start()
    for copy in swap:
        copy.wait_recv()
    starts = core == (1 if backward else 0)

    @pl.when(starts)
    def _():
        first[...] = state_ref[mine]
        first_logs[...] = logs_ref[mine]
        new = scaled(sib_logs, first, sib)
        for h in range(half):
            total[h] = new[h]

    @pl.when(jnp.logical_not(starts))
    def _():
        first[...] = sib[...]
        first_logs[...] = sib_logs[...]
        new = scaled(logs_ref.at[mine], first, state_ref.at[mine])
        for h in range(half):
            total[h] = new[h]

    total_logs[...] = logs_ref[mine] + sib_logs[...]
    pre[...] = jnp.zeros_like(pre)
    pre_logs[...] = jnp.zeros_like(pre_logs)
    pending = list(swap)
    for k, (axis, stride) in enumerate(hops):
        between(k)
        last = k == len(hops) - 1
        wire[k] = total[...].astype(wire.dtype)
        wire_logs[k] = total_logs[...]
        copies = [
            remote(wire.at[k], got.at[k], 2 + 2 * k, partner(axis, stride)),
            remote(wire_logs.at[k], got_logs.at[k], 3 + 2 * k, partner(axis, stride)),
        ]
        for copy in copies:
            copy.start()
        pending += copies
        for copy in copies:
            copy.wait_recv()
        earlier = bit(axis, stride) == (1 if backward else 0)
        arrived = [got[k, h].astype(jnp.float32) for h in range(half)]

        @pl.when(jnp.logical_not(earlier))
        def _(k=k, arrived=arrived, last=last):
            new = scaled(pre_logs, arrived, pre)
            for h in range(half):
                pre[h] = new[h]
            pre_logs[...] = pre_logs[...] + got_logs[k]
            if not last:
                new = scaled(total_logs, arrived, total)
                for h in range(half):
                    total[h] = new[h]

        if not last:

            @pl.when(earlier)
            def _(k=k, arrived=arrived):
                new = scaled(got_logs.at[k], total, arrived)
                for h in range(half):
                    total[h] = new[h]

            total_logs[...] = total_logs[...] + got_logs[k]
    second = scaled(first_logs, pre, first)

    @pl.when(starts)
    def _():
        for h in range(half):
            other[h] = second[h]
        out_ref[mine] = pre[...]

    @pl.when(jnp.logical_not(starts))
    def _():
        other[...] = pre[...]
        for h in range(half):
            out_ref[half * core + h] = second[h]

    back = remote(other, out_ref.at[mine], 2 + 2 * len(hops), sibling)
    back.start()
    back.wait_recv()
    for copy in pending + [back]:
        copy.wait_send()


def scan_scratch(sizes):
    half, hops = HEADS // 2, len(partners_of(sizes))
    block, tile = (half, HV, HK), (half, 8, HK)
    return [
        pltpu.VMEM(block, jnp.float32), pltpu.VMEM(tile, jnp.float32),
        pltpu.VMEM(block, jnp.float32), pltpu.VMEM(tile, jnp.float32),
        pltpu.VMEM(block, jnp.float32), pltpu.VMEM(tile, jnp.float32),
        pltpu.VMEM(block, jnp.float32), pltpu.VMEM(tile, jnp.float32),
        pltpu.VMEM((hops,) + block, jnp.bfloat16), pltpu.VMEM((hops,) + tile, jnp.float32),
        pltpu.VMEM((hops,) + block, jnp.bfloat16), pltpu.VMEM((hops,) + tile, jnp.float32),
        pltpu.VMEM(block, jnp.float32),
        pltpu.SemaphoreType.DMA((3 + 2 * hops,)),
        pltpu.SemaphoreType.DMA((3 + 2 * hops,)),
    ]


def entering(state, logs, sizes, backward, collective_id):
    return pl.pallas_call(
        functools.partial(scan_kernel, sizes, backward),
        out_shape=jax.ShapeDtypeStruct(state.shape, jnp.float32),
        in_specs=[pl.BlockSpec(memory_space=pltpu.VMEM)] * 2,
        out_specs=pl.BlockSpec(memory_space=pltpu.VMEM),
        scratch_shapes=scan_scratch(sizes),
        compiler_params=pltpu.CompilerParams(
            collective_id=collective_id, has_side_effects=True, vmem_limit_bytes=32 << 20
        ),
    )(state, logs)


CHUNK = 128
ROWS = 256
FTILE = 256
F32, BF16 = jnp.float32, jnp.bfloat16


def nn(left, right):
    return jnp.dot(left, right, preferred_element_type=F32)


def nt(left, right):
    return lax.dot_general(left, right, (((1,), (1,)), ((), ())), preferred_element_type=F32)


def tn(left, right):
    return lax.dot_general(left, right, (((0,), (0,)), ((), ())), preferred_element_type=F32)


def sigmoid(v):
    return 1.0 / (1.0 + jnp.exp(-v))


def causal_mask(size):
    return lax.broadcasted_iota(jnp.int32, (size, size), 0) >= lax.broadcasted_iota(jnp.int32, (size, size), 1)


def triangle(upper):
    rows = lax.broadcasted_iota(jnp.int32, (CHUNK, CHUNK), 0)
    columns = lax.broadcasted_iota(jnp.int32, (CHUNK, CHUNK), 1)
    kept = (columns >= rows) if upper else (columns <= rows)
    return jnp.where(kept, 1.0, 0.0).astype(BF16)


def running(matrix, values):
    high = values.astype(BF16)
    low = (values - high.astype(F32)).astype(BF16)
    return nn(matrix, high) + nn(matrix, low)


def halves(values):
    high = values.astype(BF16)
    return high, (values - high.astype(F32)).astype(BF16)


def fine_nt(left, right):
    (high, low), (other, rest) = left, right
    return nt(high, other) + (nt(high, rest) + nt(low, other))


def inverse_rms(values):
    return lax.rsqrt(jnp.mean(values * values, axis=-1, keepdims=True) + 1e-06)


def heads_of(width):
    return [slice(h * width, (h + 1) * width) for h in range(HEADS)]


def small_rows(extra):
    lanes = lax.broadcasted_iota(jnp.int32, (8, extra.shape[1]), 1)
    rows = lax.broadcasted_iota(jnp.int32, (8, extra.shape[1]), 0)
    return nt(jnp.where(lanes == rows + RANK, 1.0, 0.0).astype(BF16), extra)


def with_one(mid):
    lanes = lax.broadcasted_iota(jnp.int32, mid.shape, 1)
    return jnp.where(lanes < RANK, mid, jnp.where(lanes == RANK, 1.0, 0.0)).astype(BF16)


def project_rows(tokens, gain, weight, up, outs, final_ref, logs_ref):
    normed_ref, query_ref, key_ref, value_ref, gate_ref, mid_ref, logit_ref, within_ref, update_ref = outs
    inputs = tokens[...].astype(F32)
    normed = inputs * inverse_rms(inputs) * gain
    normed_ref[...] = (normed.T if normed_ref.shape[0] != tokens.shape[0] else normed).astype(BF16)
    normed = normed.astype(BF16)
    keys = HEADS * HK
    values = HEADS * HV
    mid = with_one(nn(normed, weight(2 * keys + 2 * values, 128)))
    mid_ref[...] = mid
    logit = nt(mid, up)
    logit_ref[...] = logit
    query_ref[...] = nn(normed, weight(0, keys)).astype(BF16)
    key_ref[...] = nn(normed, weight(keys, keys)).astype(BF16)
    value_ref[...] = nn(normed, weight(2 * keys, values)).astype(BF16)
    gate_ref[...] = nn(normed, weight(2 * keys + values, values)).astype(BF16)
    decay = (jnp.minimum(logit, 0.0) - jnp.log1p(jnp.exp(-jnp.abs(logit)))) * (1.0 / 16.0)
    lower = triangle(False)
    for c in range(ROWS // CHUNK):
        rows = pl.ds(c * CHUNK, CHUNK)
        within = running(lower, decay[c * CHUNK : (c + 1) * CHUNK])
        within_ref[rows, :] = within
        total = within[CHUNK - 1 : CHUNK]
        ending = (key_ref[rows, :].astype(F32) * jnp.exp(total - within)).astype(BF16)
        for h, (ks, vs) in enumerate(zip(heads_of(HK), heads_of(HV))):
            update = tn(value_ref[rows, vs], ending[:, ks])
            update_ref[c, h] = update.astype(BF16)
            final_ref[h] = final_ref[h] * jnp.exp(total[:, ks]) + update
            logs_ref[h] = logs_ref[h] + total[:, ks]


def project_kernel(tokens, gains, weights, up, *refs):
    outs, (final_ref, logs_ref) = refs[:9], refs[9:]

    @pl.when(pl.program_id(0) == 0)
    def _():
        final_ref[...] = jnp.zeros_like(final_ref)
        logs_ref[...] = jnp.zeros_like(logs_ref)

    project_rows(
        tokens, gains[0:1], lambda first, width: weights[:, first : first + width], up[...], outs, final_ref, logs_ref
    )


def mix_rows(tokens, query, key, value, gate, within_all, update, state, head_gain, out_weight, ffn_gain, outs):
    mixed_ref, gated_ref, hidden_ref, ffn_ref, starts_ref = outs
    mask = causal_mask(CHUNK)
    for c in range(ROWS // CHUNK):
        rows = pl.ds(c * CHUNK, CHUNK)
        within = within_all[rows, :]
        middle = within[CHUNK // 2 - 1 : CHUNK // 2]
        total = within[CHUNK - 1 : CHUNK]
        scaled = query[rows, :].astype(F32) * HK**-0.5
        from_start = (scaled * jnp.exp(within)).astype(BF16)
        left = halves(scaled * jnp.exp(within - middle))
        right = halves(key[rows, :].astype(F32) * jnp.exp(middle - within))
        for h, (ks, vs) in enumerate(zip(heads_of(HK), heads_of(HV))):
            start = state[h].astype(BF16)
            starts_ref[c, h] = start
            scores = jnp.where(mask, fine_nt([p[:, ks] for p in left], [p[:, ks] for p in right]), 0.0).astype(BF16)
            mixed = nn(scores, value[rows, vs]) + nt(from_start[:, ks], start)
            state[h] = state[h] * jnp.exp(total[:, ks]) + update[c, h].astype(F32)
            mixed_ref[rows, vs] = mixed
            gates = gate[rows, vs].astype(F32)
            gated = mixed * inverse_rms(mixed) * head_gain[:, vs] * (gates * sigmoid(gates))
            gated_ref[rows, vs] = gated.astype(BF16)
    hidden = tokens[...].astype(F32) + nn(gated_ref[...], out_weight)
    hidden_ref[...] = hidden
    ffn_in = hidden * inverse_rms(hidden) * ffn_gain
    ffn_ref[...] = ffn_in.astype(BF16)
    return ffn_in


def mix_kernel(tokens, query, key, value, gate, within_all, update, entering_ref, gains, out_weight, *refs):
    outs, state = refs[:5], refs[5]

    @pl.when(pl.program_id(0) == 0)
    def _():
        state[...] = entering_ref[...]

    mix_rows(
        tokens, query, key, value, gate, within_all, update, state, gains[1:2], out_weight[...], gains[2:3], outs
    )


def ffn_kernel(
    ffn_in, ffn_in_t, cotangent, hidden, gate_weight, up_weight, down_weight,
    out_ref, back_ref, gate_grad, up_grad, down_grad,
):
    @pl.when(pl.program_id(0) == 0)
    def _():
        out_ref[...] = hidden[...]
        back_ref[...] = jnp.zeros_like(back_ref)

    gate, up = nn(ffn_in[...], gate_weight[...]), nn(ffn_in[...], up_weight[...])
    back = nt(cotangent[...], down_weight[...])
    share = sigmoid(gate)
    passed = gate * share
    inner = (passed * up).astype(BF16)
    d_up = (back * passed).astype(BF16)
    d_gate = (back * up * (share * (1.0 + gate * (1.0 - share)))).astype(BF16)
    out_ref[...] += nn(inner, down_weight[...])
    back_ref[...] += nt(d_gate, gate_weight[...]) + nt(d_up, up_weight[...])
    gate_grad[...] = nn(ffn_in_t[...], d_gate).astype(BF16)
    up_grad[...] = nn(ffn_in_t[...], d_up).astype(BF16)
    down_grad[...] = tn(inner, cotangent[...]).astype(BF16)


def norm_back(values, gain, grad):
    scale = inverse_rms(values)
    inner = grad * gain
    along = jnp.mean(inner * values, axis=-1, keepdims=True)
    return scale * inner - values * (scale * scale * scale * along), grad * values * scale


def unmix_kernel(
    ffn_back, hidden, cotangent, gate, mixed, query, within_all, gains, out_weight,
    d_hidden_ref, low_ref, d_gate_ref, d_mixed_ref, update_ref, enters_ref, ffn_gain_ref, head_gain_ref,
):
    @pl.when(pl.program_id(0) == 0)
    def _():
        enters_ref[...] = jnp.zeros_like(enters_ref)
        ffn_gain_ref[...] = jnp.zeros_like(ffn_gain_ref)
        head_gain_ref[...] = jnp.zeros_like(head_gain_ref)

    through, terms = norm_back(hidden[...], gains[2:3], ffn_back[...])
    ffn_gain_ref[...] += jnp.sum(terms, axis=0, keepdims=True)
    d_hidden = cotangent[...].astype(F32) + through
    d_hidden_ref[...] = d_hidden
    low = d_hidden.astype(BF16)
    low_ref[...] = low
    d_gated = nt(low, out_weight[...])
    for vs in heads_of(HV):
        value = mixed[:, vs]
        scale = inverse_rms(value)
        headed = value * scale
        gates = gate[:, vs].astype(F32)
        share = sigmoid(gates)
        passed = gates * share
        grad, gain = d_gated[:, vs], gains[1:2, vs]
        head_gain_ref[:, vs] += jnp.sum(grad * headed * passed, axis=0, keepdims=True)
        d_gate_ref[:, vs] = (grad * headed * gain * (share * (1.0 + gates * (1.0 - share)))).astype(BF16)
        d_headed = grad * gain * passed
        along = jnp.mean(d_headed * headed, axis=-1, keepdims=True)
        d_mixed_ref[:, vs] = scale * (d_headed - headed * along)
    for c in reversed(range(ROWS // CHUNK)):
        rows = slice(c * CHUNK, (c + 1) * CHUNK)
        within = within_all[rows]
        total = within[CHUNK - 1 : CHUNK]
        from_start = (query[rows].astype(F32) * HK**-0.5 * jnp.exp(within)).astype(BF16)
        for h, (ks, vs) in enumerate(zip(heads_of(HK), heads_of(HV))):
            update = tn(d_mixed_ref[rows, vs].astype(BF16), from_start[:, ks])
            update_ref[c, h] = update.astype(BF16)
            enters_ref[h] = enters_ref[h] * jnp.exp(total[:, ks]) + update


def back_rows(
    tokens, query, key, value, logit, within_all, d_mixed, starts, update, d_gate, d_hidden, gains, weights, up,
    d_proj_ref, d_logit_ref, tokens_grad_ref, gain_ref, state,
):
    mask = causal_mask(CHUNK)
    upper = triangle(True)
    keys = HEADS * HK
    for c in reversed(range(ROWS // CHUNK)):
        rows = slice(c * CHUNK, (c + 1) * CHUNK)
        within = within_all[rows]
        middle = within[CHUNK // 2 - 1 : CHUNK // 2]
        total = within[CHUNK - 1 : CHUNK]
        factor = jnp.exp(total)
        queries, keys_f = query[rows].astype(F32), key[rows].astype(F32)
        q_start, q_middle = jnp.exp(within) * HK**-0.5, jnp.exp(within - middle) * HK**-0.5
        k_middle, k_end = jnp.exp(middle - within), jnp.exp(total - within)
        lefts, rights = halves(queries * q_middle), halves(keys_f * k_middle)
        left, right = lefts[0], rights[0]
        ending = (keys_f * k_end).astype(BF16)
        moves, extras = [], []
        for h, (ks, vs) in enumerate(zip(heads_of(HK), heads_of(HV))):
            start, after = starts[c, h], state[h].astype(BF16)
            (grad, rest), values = halves(d_mixed[rows, vs]), value[rows, vs]
            scores = jnp.where(mask, fine_nt([p[:, ks] for p in lefts], [p[:, ks] for p in rights]), 0.0).astype(BF16)
            d_scores = jnp.where(mask, nt(grad, values) + nt(rest, values), 0.0).astype(BF16)
            d_value = tn(scores, grad) + nt(ending[:, ks], after)
            d_query = nn(d_scores, right[:, ks]) * q_middle[:, ks] + nn(grad, start) * q_start[:, ks]
            d_end = nn(values, after) * k_end[:, ks]
            d_key = tn(d_scores, left[:, ks]) * k_middle[:, ks] + d_end
            d_proj_ref[rows, ks] = d_query.astype(BF16)
            d_proj_ref[rows, slice(keys + ks.start, keys + ks.stop)] = d_key.astype(BF16)
            d_proj_ref[rows, slice(2 * keys + vs.start, 2 * keys + vs.stop)] = d_value.astype(BF16)
            moves.append(queries[:, ks] * d_query - keys_f[:, ks] * d_key)
            extras.append(
                jnp.sum(keys_f[:, ks] * d_end, axis=0, keepdims=True)
                + factor[:, ks] * jnp.sum(start.astype(F32) * state[h], axis=0, keepdims=True)
            )
            state[h] = state[h] * factor[:, ks] + update[c, h].astype(F32)
        d_decay = running(upper, jnp.concatenate(moves, axis=1)) + jnp.concatenate(extras, axis=1)
        d_logit = d_decay * sigmoid(-logit[rows]) * (1.0 / 16.0)
        d_logit_ref[rows] = d_logit.astype(BF16)
    d_mid = nn(d_logit_ref[...], up[...])
    d_mid = jnp.where(lax.broadcasted_iota(jnp.int32, d_mid.shape, 1) < RANK, d_mid, 0.0).astype(BF16)
    inner = 2 * keys + HEADS * HV
    outer = inner + HEADS * HV
    d_proj_ref[:, inner:outer] = d_gate[...]
    d_proj_ref[:, outer:] = d_mid
    d_normed = nt(d_proj_ref[...], weights[...])
    through, terms = norm_back(tokens[...].astype(F32), gains[0:1], d_normed)
    gain_ref[...] += jnp.sum(terms, axis=0, keepdims=True)
    tokens_grad_ref[...] = d_hidden[...] + through


def back_kernel(*refs):
    tiles, leaving_ref, refs = refs[:11], refs[11], refs[12:]
    gain_ref, state = refs[-2:]

    @pl.when(pl.program_id(0) == 0)
    def _():
        state[...] = leaving_ref[...]
        gain_ref[...] = jnp.zeros_like(gain_ref)

    back_rows(*tiles, *refs)


def tail_kernel(sizes, steps, count, *refs):
    tiles, (enters, logs), refs = refs[:11], refs[11:13], refs[13:]
    kept, partials, refs = refs[:3], refs[3 : 3 + count], refs[3 + count :]
    outs, gain_ref, sums, refs = refs[:3], refs[3], refs[4 : 4 + count], refs[4 + count :]
    state, load, send, recv = refs[:4]
    scratch, scan = refs[4 : 4 + 5 * len(TAIL_PARTS)], refs[4 + 5 * len(TAIL_PARTS) :]
    place = Place(sizes)
    step = pl.program_id(0)
    scatters = []
    for k, (which, columns, order) in enumerate(TAIL_PARTS):
        held, *bufs = scratch[5 * k : 5 * k + 5]
        scatters.append(
            Scatter(place, k, order, partials[which], columns, held, bufs, sums[which], load, send, recv)
        )
    moves = [s.steps() for s in scatters]

    def turn():
        for move in moves:
            next(move, None)

    def during(hop):
        for _ in range(TAIL_TURNS[0].count(hop)):
            turn()

    @pl.when(step == 0)
    def _():
        gain_ref[...] = jnp.zeros_like(gain_ref)
        place.greet(partners_of(sizes))
        turn()
        scan_states(place, True, during, enters, logs, state, *scan)

    for k in range(1, steps + 1):

        @pl.when(step == k)
        def _(k=k):
            for _ in range(TAIL_TURNS[1].count(k)):
                turn()

    @pl.when(step > 0)
    def _():
        back_rows(*tiles, *kept, *outs, gain_ref, state)

    @pl.when(step == steps)
    def _():
        run_all(moves)
        for s in scatters:
            s.drain()


def rows_spec(width, steps, backward):
    return pl.BlockSpec((ROWS, width), (lambda i: (steps - 1 - i, 0)) if backward else (lambda i: (i, 0)))


def chunks_spec(steps, backward):
    return pl.BlockSpec(
        (ROWS // CHUNK, HEADS, HV, HK),
        (lambda i: (steps - 1 - i, 0, 0, 0)) if backward else (lambda i: (i, 0, 0, 0)),
    )


def kept_spec(shape):
    return pl.BlockSpec(shape, lambda i: (0,) * len(shape), pipeline_mode=pl.Buffered(1))


def kept_out(shape):
    return pl.BlockSpec(shape, lambda i: (0,) * len(shape))


PARAMS = dict(vmem_limit_bytes=60 << 20)
STATE = (HEADS, HV, HK)


def project(tokens, gains, weights, up):
    length, width = tokens.shape
    steps, keys, values = length // ROWS, HEADS * HK, HEADS * HV
    row = lambda w: rows_spec(w, steps, False)
    chunks = (length // CHUNK,) + STATE
    shape = jax.ShapeDtypeStruct
    return pl.pallas_call(
        project_kernel,
        grid=(steps,),
        in_specs=[row(width)] + [kept_spec(a.shape) for a in (gains, weights, up)],
        out_specs=[row(w) for w in (width, keys, keys, values, values, 128, keys, keys)]
        + [chunks_spec(steps, False), kept_out(STATE), kept_out((HEADS, 8, HK))],
        out_shape=[shape((length, w), BF16) for w in (width, keys, keys, values, values, 128)]
        + [shape((length, keys), F32)] * 2
        + [shape(chunks, BF16), shape(STATE, F32), shape((HEADS, 8, HK), F32)],
        compiler_params=pltpu.CompilerParams(**PARAMS),
    )(tokens, gains, weights, up)


def mix(tokens, query, key, value, gate, within, update, entered, gains, out_weight):
    length, width = tokens.shape
    steps, keys, values = length // ROWS, HEADS * HK, HEADS * HV
    row = lambda w: rows_spec(w, steps, False)
    shape = jax.ShapeDtypeStruct
    return pl.pallas_call(
        mix_kernel,
        grid=(steps,),
        in_specs=[row(w) for w in (width, keys, keys, values, values, keys)]
        + [chunks_spec(steps, False)]
        + [kept_spec(a.shape) for a in (entered, gains, out_weight)],
        out_specs=[row(w) for w in (values, values, width, width)] + [chunks_spec(steps, False)],
        out_shape=[
            shape((length, values), F32), shape((length, values), BF16),
            shape((length, width), F32), shape((length, width), BF16), shape(update.shape, BF16),
        ],
        scratch_shapes=[pltpu.VMEM(STATE, F32)],
        compiler_params=pltpu.CompilerParams(**PARAMS),
    )(tokens, query, key, value, gate, within, update, entered, gains, out_weight)


FRONT_PARTS = (
    (0, (0, 128), ORDERS[0]),
    (1, (0, 1024), ORDERS[0]),
    (1, (1024, 1024), ORDERS[1]),
    (1, (2048, 1152), ORDERS[2]),
    (2, (0, 1024), ORDERS[3]),
    (3, (0, 2816), ORDERS[0]),
    (4, (0, 2816), ORDERS[1]),
    (5, (0, 512), ORDERS[2]),
    (5, (512, 512), ORDERS[3]),
)
FIRST_PARTS = 5
FRONT_TURNS = (1, 2, (2,), 1)


def front_kernel(sizes, steps, *refs):
    tokens, shards, refs = refs[0], refs[1:7], refs[7:]
    buffers, refs = refs[:6], refs[6:]
    outs, mixed_outs, (logs_out, gains_out, ffn_t_ref), refs = refs[:8], refs[8:13], refs[13:16], refs[16:]
    up_all, proj_all, out_all, query, key, value, gate, within, update, state, final, logs, gains, refs = *refs[:13], refs[13:]
    send, recv, own, flush = refs[:4]
    scan = refs[4:]
    place = Place(sizes)
    step = pl.program_id(0)
    here = tuple(place.here)
    held = (up_all, proj_all, out_all) + tuple(buffers[3:])
    gathers = [
        Gather(place, k, order, held[which], columns, send, recv)
        for k, (which, columns, order) in enumerate(FRONT_PARTS)
    ]
    owned = [pltpu.make_async_copy(shards[k], buffers[k].at[here], own.at[k]) for k in (3, 4, 5)]
    flushes = [pltpu.make_async_copy(held[k], buffers[k], flush.at[k]) for k in range(3)]
    later = [g.steps() for g in gathers[FIRST_PARTS:]]

    def turn():
        for g in later:
            next(g, None)

    def during(hop):
        if hop in FRONT_TURNS[2]:
            turn()

    @pl.when(step == 0)
    def _():
        for copy in owned:
            copy.start()
        for k in range(3):
            held[k][here] = shards[k][...]
        place.greet(partners_of(sizes))
        for copy in owned:
            copy.wait()
        run_all([g.steps() for g in gathers[:FIRST_PARTS]])
        turn()
        flushes[0].start()
        flushes[1].start()
        flushes[2].start()
        extra = 2 * HEADS * (HK + HV)
        gains[...] = small_rows(proj_all[..., pl.ds(extra, 128)].reshape(-1, 128))
        gains_out[...] = gains[...]
        final[...] = jnp.zeros_like(final)
        logs[...] = jnp.zeros_like(logs)
        for _ in range(FRONT_TURNS[0]):
            turn()

    @pl.when(step < steps)
    def _():
        rows = pl.ds(pl.multiple_of(step * ROWS, ROWS), ROWS)
        chunks = pl.ds(step * (ROWS // CHUNK), ROWS // CHUNK)
        normed_ref, query_ref, key_ref, value_ref, gate_ref, mid_ref, logit_ref, within_ref = outs
        kept = (query, key, value, gate, within)
        tiles = (query_ref, key_ref, value_ref, gate_ref, within_ref)
        project_rows(
            tokens, gains[0:1],
            lambda first, width: proj_all[..., pl.ds(first, width)].reshape(-1, width),
            up_all[...].reshape(-1, 128),
            (normed_ref, query_ref, key_ref, value_ref, gate_ref, mid_ref, logit_ref, within_ref, update.at[chunks]),
            final, logs,
        )
        for whole, tile in zip(kept, tiles):
            whole[rows, :] = tile[...]

    @pl.when(step == steps)
    def _():
        for _ in range(FRONT_TURNS[1]):
            turn()
        logs_out[...] = logs[...]
        scan_states(place, False, during, final, logs, state, *scan)
        for _ in range(FRONT_TURNS[3]):
            turn()

    @pl.when(step >= steps)
    def _():
        at = step - steps
        rows = pl.ds(pl.multiple_of(at * ROWS, ROWS), ROWS)
        chunks = pl.ds(at * (ROWS // CHUNK), ROWS // CHUNK)
        ffn_in = mix_rows(
            tokens, query.at[rows], key.at[rows], value.at[rows], gate.at[rows], within.at[rows], update.at[chunks], state,
            gains[1:2], out_all[...].reshape(-1, out_all.shape[-1]), gains[2:3], mixed_outs,
        )
        ffn_t_ref[...] = ffn_in.T.astype(BF16)

    @pl.when(step == 2 * steps - 1)
    def _():
        run_all(later)
        for g in gathers:
            g.drain()
        for copy in flushes:
            copy.wait()


def front(tokens, shards, sizes, collective_id):
    length, width = tokens.shape
    steps, keys, values = length // ROWS, HEADS * HK, HEADS * HV
    shape, chunks = jax.ShapeDtypeStruct, (length // CHUNK,) + STATE
    first = lambda w: pl.BlockSpec((ROWS, w), lambda i: (jnp.minimum(i, steps - 1), 0))
    second = lambda w: pl.BlockSpec((ROWS, w), lambda i: (jnp.maximum(i - steps, 0), 0))
    lanes = lanes_of(sizes)
    parts = len(FRONT_PARTS)
    one = lambda w, t: ((length, w), t)
    turned = lambda first: pl.BlockSpec((width, ROWS), lambda i: (0, jnp.minimum(i, steps - 1) if first else jnp.maximum(i - steps, 0)))
    results = [one(keys, BF16), one(keys, BF16), one(values, BF16), one(values, BF16), one(128, BF16), one(keys, F32), one(keys, F32)]
    mixes = [one(values, F32), one(values, BF16), one(width, F32), one(width, BF16)]
    out = pl.pallas_call(
        functools.partial(front_kernel, sizes, steps),
        grid=(2 * steps,),
        in_specs=[pl.BlockSpec((ROWS, width), lambda i: (lax.rem(i, steps), 0))] + [kept_spec(s.shape) for s in shards],
        out_specs=[pl.BlockSpec(memory_space=pl.ANY)] * len(shards)
        + [turned(True)] + [first(s[1]) for s, _ in results]
        + [second(s[1]) for s, _ in mixes]
        + [pl.BlockSpec((ROWS // CHUNK,) + STATE, lambda i: (jnp.maximum(i - steps, 0), 0, 0, 0))]
        + [kept_out((HEADS, 8, HK)), kept_out((8, width)), turned(False)],
        out_shape=[shape(sizes + s.shape, s.dtype) for s in shards]
        + [shape((width, length), BF16)]
        + [shape(s, t) for s, t in results + mixes]
        + [shape(chunks, BF16), shape((HEADS, 8, HK), F32), shape((8, width), F32), shape((width, length), BF16)],
        scratch_shapes=[pltpu.VMEM(sizes + s.shape, s.dtype) for s in shards[:3]]
        + [pltpu.VMEM((length, w), t) for w, t in ((keys, BF16), (keys, BF16), (values, BF16), (values, BF16), (keys, F32))]
        + [pltpu.VMEM(chunks, BF16), pltpu.VMEM(STATE, F32), pltpu.VMEM(STATE, F32), pltpu.VMEM((HEADS, 8, HK), F32), pltpu.VMEM((8, width), F32)]
        + [
            pltpu.SemaphoreType.DMA((parts, 4, sizes[0], lanes, 2)),
            pltpu.SemaphoreType.DMA((parts, 4, sizes[0], lanes)),
            pltpu.SemaphoreType.DMA((len(shards),)),
            pltpu.SemaphoreType.DMA((3,)),
        ]
        + scan_scratch(sizes),
        compiler_params=pltpu.CompilerParams(collective_id=collective_id, has_side_effects=True, **PARAMS),
    )(tokens, *shards)
    weights = [o.reshape(-1, o.shape[-1]) for o in out[: len(shards)]]
    return weights, out[len(shards) :]


def feed_forward(ffn_in, ffn_t, cotangent, hidden, gate_weight, up_weight, down_weight):
    length, width = ffn_in.shape
    inner = gate_weight.shape[1]
    whole = [ffn_in, ffn_t, cotangent, hidden]
    wide = pl.BlockSpec((width, FTILE), lambda i: (0, i))
    tall = pl.BlockSpec((FTILE, width), lambda i: (i, 0))
    shape = jax.ShapeDtypeStruct
    return pl.pallas_call(
        ffn_kernel,
        grid=(inner // FTILE,),
        in_specs=[kept_spec(a.shape) for a in whole] + [wide, wide, tall],
        out_specs=[kept_out((length, width))] * 2 + [wide, wide, tall],
        out_shape=[shape((length, width), F32)] * 2
        + [shape((width, inner), BF16)] * 2 + [shape((inner, width), BF16)],
        compiler_params=pltpu.CompilerParams(**PARAMS),
    )(*whole, gate_weight, up_weight, down_weight)


def unmix(ffn_back, hidden, cotangent, gate, mixed, query, within, gains, out_weight):
    length, width = hidden.shape
    steps, keys, values = length // ROWS, HEADS * HK, HEADS * HV
    row = lambda w: rows_spec(w, steps, True)
    chunks = (length // CHUNK,) + STATE
    shape = jax.ShapeDtypeStruct
    return pl.pallas_call(
        unmix_kernel,
        grid=(steps,),
        in_specs=[row(w) for w in (width, width, width, values, values, keys, keys)]
        + [kept_spec(a.shape) for a in (gains, out_weight)],
        out_specs=[row(w) for w in (width, width, values, values)]
        + [chunks_spec(steps, True), kept_out(STATE), kept_out((1, width)), kept_out((1, values))],
        out_shape=[
            shape((length, width), F32), shape((length, width), BF16), shape((length, values), BF16),
            shape((length, values), F32), shape(chunks, BF16), shape(STATE, F32),
            shape((1, width), F32), shape((1, values), F32),
        ],
        compiler_params=pltpu.CompilerParams(**PARAMS),
    )(ffn_back, hidden, cotangent, gate, mixed, query, within, gains, out_weight)


def back(tiles, leaving, gains, weights, up):
    length, width = tiles[0].shape
    steps, keys, values = length // ROWS, HEADS * HK, HEADS * HV
    row = lambda w: rows_spec(w, steps, True)
    shape = jax.ShapeDtypeStruct
    return pl.pallas_call(
        back_kernel,
        grid=(steps,),
        in_specs=[row(w) for w in (width, keys, keys, values, keys, keys, values)]
        + [chunks_spec(steps, True)] * 2 + [row(values), row(width)]
        + [kept_spec(a.shape) for a in (leaving, gains, weights, up)],
        out_specs=[row(w) for w in (weights.shape[1], keys, width)] + [kept_out((1, width))],
        out_shape=[
            shape((length, weights.shape[1]), BF16), shape((length, keys), BF16),
            shape((length, width), F32), shape((1, width), F32),
        ],
        scratch_shapes=[pltpu.VMEM(STATE, F32)],
        compiler_params=pltpu.CompilerParams(**PARAMS),
    )(*tiles, leaving, gains, weights, up)


TAIL_PARTS = (
    (0, (0, 2816), ORDERS[1][::-1]),
    (1, (0, 2816), ORDERS[0][::-1]),
    (2, (0, 512), ORDERS[2][::-1]),
    (2, (512, 512), ORDERS[3][::-1]),
    (3, (0, 512), ORDERS[2][::-1]),
    (3, (512, 512), ORDERS[3][::-1]),
)
TAIL_TURNS = ((2, 4), (1, 2, 3, 4))
LAST_PARTS = (
    (0, (0, 128), ORDERS[0][::-1]),
    (1, (0, 1024), ORDERS[0][::-1]),
    (1, (1024, 1024), ORDERS[1][::-1]),
    (1, (2048, 640), ORDERS[2][::-1]),
    (1, (2688, 512), ORDERS[3][::-1]),
)


def tail(tiles, enters, logs, gains, weights, up, partials, sizes, collective_id):
    length, width = tiles[0].shape
    steps, keys, values = length // ROWS, HEADS * HK, HEADS * HV
    shape, at = jax.ShapeDtypeStruct, lambda i: steps - jnp.maximum(i, 1)
    row = lambda w: pl.BlockSpec((ROWS, w), lambda i: (at(i), 0))
    chunk = pl.BlockSpec((ROWS // CHUNK,) + STATE, lambda i: (at(i), 0, 0, 0))
    count = len(partials)
    devices = sizes[0] * sizes[1] * sizes[2] * sizes[3]
    partials = [p.reshape(sizes + (p.shape[0] // devices, p.shape[1])) for p in partials]
    lanes = max([1] + [size + 1 for size in sizes[1:] if size > 2])
    sems = (len(TAIL_PARTS), 4, sizes[0] + 1, lanes)
    out = pl.pallas_call(
        functools.partial(tail_kernel, sizes, steps, count),
        grid=(steps + 1,),
        in_specs=[row(w) for w in (width, keys, keys, values, keys, keys, values)]
        + [chunk] * 2 + [row(values), row(width)]
        + [kept_spec(a.shape) for a in (enters, logs, gains, weights, up)]
        + [pl.BlockSpec(memory_space=pl.ANY)] * count,
        out_specs=[row(w) for w in (weights.shape[1], keys, width)] + [kept_out((1, width))]
        + [kept_out(p.shape[4:]) for p in partials],
        out_shape=[
            shape((length, weights.shape[1]), BF16), shape((length, keys), BF16),
            shape((length, width), F32), shape((1, width), F32),
        ] + [shape(p.shape[4:], F32) for p in partials],
        scratch_shapes=[
            pltpu.VMEM(STATE, F32),
            pltpu.SemaphoreType.DMA((len(TAIL_PARTS), sizes[0])),
            pltpu.SemaphoreType.DMA(sems),
            pltpu.SemaphoreType.DMA(sems),
        ]
        + scatter_scratch(sizes, TAIL_PARTS, [p.shape for p in partials], BF16)
        + scan_scratch(sizes),
        compiler_params=pltpu.CompilerParams(collective_id=collective_id, has_side_effects=True, **PARAMS),
    )(*tiles, enters, logs, gains, weights, up, *partials)
    return out[:4], out[4:]


def last_kernel(sizes, *refs):
    normed_t, d_proj, small, small_out, proj_out, load, send, recv = refs[:8]
    scratch = refs[8 : 8 + 5 * len(LAST_PARTS)]
    partials = [small] + list(refs[8 + 5 * len(LAST_PARTS) :])
    place = Place(sizes)
    place.greet()
    moves, scatters = [], []
    for k, (which, (first, width), order) in enumerate(LAST_PARTS):
        for move in moves:
            next(move, None)
        out = small_out
        if which:
            out = proj_out.at[:, pl.ds(first, width)]
            for at in range(0, width, 512):
                tile = min(512, width - at)
                grad = nn(normed_t[...], d_proj[:, first + at : first + at + tile]).astype(BF16)
                partials[k][..., pl.ds(at, tile)] = grad.reshape(partials[k].shape[:-1] + (tile,))
        held, *bufs = scratch[5 * k : 5 * k + 5]
        scatters.append(Scatter(place, k, order, partials[k], (0, width), held, bufs, out, load, send, recv))
        moves.append(scatters[-1].steps())
        next(moves[-1])
    run_all(moves)
    for s in scatters:
        s.drain()


def project_grads(normed_t, d_proj, small, sizes, collective_id):
    devices = sizes[0] * sizes[1] * sizes[2] * sizes[3]
    small = small.reshape(sizes + (small.shape[0] // devices, small.shape[1]))
    rows = d_proj.shape[1], normed_t.shape[0] // devices
    shapes = [small.shape, sizes + (rows[1], rows[0])]
    lanes = max([1] + [size + 1 for size in sizes[1:] if size > 2])
    sems = (len(LAST_PARTS), 4, sizes[0] + 1, lanes)
    vmem = pl.BlockSpec(memory_space=pltpu.VMEM)
    return pl.pallas_call(
        functools.partial(last_kernel, sizes),
        out_shape=[jax.ShapeDtypeStruct(s[4:], F32) for s in shapes],
        in_specs=[vmem, vmem, pl.BlockSpec(memory_space=pl.ANY)],
        out_specs=[vmem] * 2,
        scratch_shapes=[
            pltpu.SemaphoreType.DMA((len(LAST_PARTS), sizes[0])),
            pltpu.SemaphoreType.DMA(sems),
            pltpu.SemaphoreType.DMA(sems),
        ]
        + scatter_scratch(sizes, LAST_PARTS, shapes, BF16)
        + [pltpu.VMEM(shapes[1][:-1] + (width,), BF16) for which, (_, width), _ in LAST_PARTS if which],
        compiler_params=pltpu.CompilerParams(collective_id=collective_id, has_side_effects=True, **PARAMS),
    )(normed_t, d_proj, small)


def beside(pieces):
    rows, used = pieces[0].shape[0], sum(p.shape[1] for p in pieces)
    return jnp.concatenate(pieces + [jnp.zeros((rows, 128 - used), pieces[0].dtype)], axis=1)


def local(
    tokens,
    norm_gain,
    query_weight,
    key_weight,
    value_weight,
    gate_weight,
    rank_down,
    rank_up,
    gate_bias,
    head_gain,
    out_weight,
    ffn_gain,
    ffn_gate,
    ffn_up,
    ffn_down,
    cotangent,
):
    sizes = grid_of(lax.axis_size("seq"))
    extra = beside([rank_down] + [g[:, None] for g in (norm_gain, head_gain, ffn_gain)])
    projections = jnp.concatenate([query_weight, key_weight, value_weight, gate_weight, extra], axis=1)
    shards = [beside([rank_up.T, gate_bias[:, None]]), projections, out_weight, ffn_gate, ffn_up, ffn_down]
    if rank_up.shape[1] % 16 == 0:
        weights, kept = front(tokens, shards, sizes, 0)
        up, proj, out, full_fgate, full_fup, full_fdown = weights
        normed_t, query, key, value, gate, mid, logit, within, mixed, gated, hidden, ffn_in, starts, logs, gains, ffn_t = kept
    else:
        up, proj, out, full_fgate, full_fup, full_fdown = gather_all(shards, FRONT_PARTS, sizes, 0)
        gains = jnp.pad(proj[:, -128 + RANK : -128 + RANK + 3].astype(F32).T, ((0, 5), (0, 0)))
        normed, query, key, value, gate, mid, logit, within, update, final, logs = project(tokens, gains, proj, up)
        incoming = entering(final, logs, sizes, False, 2)
        mixed, gated, hidden, ffn_in, starts = mix(
            tokens, query, key, value, gate, within, update, incoming, gains, out
        )
        normed_t, ffn_t = normed.T, ffn_in.T
    block_output, ffn_back, fgate_wgrad, fup_wgrad, fdown_wgrad = feed_forward(
        ffn_in, ffn_t, cotangent, hidden, full_fgate, full_fup, full_fdown
    )
    d_hidden, hidden_low, d_gate, d_mixed, back_update, enters, ffn_gain_grad, head_gain_grad = unmix(
        ffn_back, hidden, cotangent, gate, mixed, query, within, gains, out
    )
    out_wgrad = tn(gated, hidden_low).astype(BF16)
    early = [fgate_wgrad, fup_wgrad, fdown_wgrad, out_wgrad]
    tiles = (tokens, query, key, value, logit, within, d_mixed, starts, back_update, d_gate, d_hidden)
    if rank_up.shape[1] % 16 == 0:
        backs, early_sums = tail(tiles, enters, logs, gains, proj, up, early, sizes, 3)
    else:
        leaving = entering(enters, logs, sizes, True, 3)
        backs = back(tiles, leaving, gains, proj, up)
        early_sums = scatter_all(early, TAIL_PARTS, sizes, 4)
    d_proj, d_logit, tokens_grad, gain_grad = backs
    fgate_sum, fup_sum, fdown_sum, out_sum = early_sums
    keys_here = rank_up.shape[1]
    gain_grads = jnp.concatenate([gain_grad, head_gain_grad, ffn_gain_grad]).reshape(3, -1, norm_gain.shape[0] // keys_here, keys_here)
    gain_grads = gain_grads.transpose(1, 3, 0, 2).reshape(HEADS * HK, -1)
    up_wgrad = beside([tn(d_logit, mid)[:, : RANK + 1], gain_grads]).astype(BF16)
    if keys_here % 16 == 0:
        up_sum, proj_sum = project_grads(normed_t, d_proj, up_wgrad, sizes, 1)
    else:
        up_sum, proj_sum = scatter_all([up_wgrad, nn(normed_t, d_proj).astype(BF16)], LAST_PARTS, sizes, 1)
    keys, values = HEADS * HK, HEADS * HV
    last = 2 * (keys + values)
    gain_sum, head_sum, ffn_sum = (
        up_sum[:, RANK + 1 : RANK + 1 + 3 * (norm_gain.shape[0] // keys_here)].reshape(keys_here, 3, -1).transpose(1, 2, 0).reshape(3, -1)
    )
    return (
        block_output,
        tokens_grad,
        gain_sum,
        proj_sum[:, :keys],
        proj_sum[:, keys : 2 * keys],
        proj_sum[:, 2 * keys : 2 * keys + values],
        proj_sum[:, 2 * keys + values : last],
        proj_sum[:, last : last + RANK],
        up_sum[:, :RANK].T,
        up_sum[:, RANK],
        head_sum,
        out_sum,
        ffn_sum,
        fgate_sum,
        fup_sum,
        fdown_sum,
    )


def solution(mesh):
    return jax.shard_map(
        local,
        mesh=mesh,
        in_specs=(
            P("seq", None),
            P("seq"),
            P("seq", None),
            P("seq", None),
            P("seq", None),
            P("seq", None),
            P("seq", None),
            P(None, "seq"),
            P("seq"),
            P("seq"),
            P("seq", None),
            P("seq"),
            P("seq", None),
            P("seq", None),
            P("seq", None),
            P("seq", None),
        ),
        out_specs=(
            P("seq", None),
            P("seq", None),
            P("seq"),
            P("seq", None),
            P("seq", None),
            P("seq", None),
            P("seq", None),
            P("seq", None),
            P(None, "seq"),
            P("seq"),
            P("seq"),
            P("seq", None),
            P("seq"),
            P("seq", None),
            P("seq", None),
            P("seq", None),
        ),
        check_vma=False,
    )
```

```python
import functools

import jax
import jax.numpy as jnp
from jax import lax
from jax.experimental import pallas as pl
from jax.experimental.pallas import tpu as pltpu
from jax.sharding import PartitionSpec as P

HEADS = 4
HK = 128
HV = 256
RANK = 16

MESH = pl.DeviceIdType.MESH
LINE = 0
CORE = 3


def grid_of(count):
    core = 2 if count % 2 == 0 else 1
    rest = count // core
    third = max(k for k in range(1, rest + 1) if rest % k == 0 and k**3 <= rest)
    rest //= third
    second = max(k for k in range(1, rest + 1) if rest % k == 0 and k * k <= rest)
    return (rest // second, second, third, core)


class Place:
    def __init__(self, sizes):
        self.sizes = sizes
        rest = lax.axis_index("seq")
        here = []
        for size in sizes[::-1]:
            here.append(lax.rem(rest, size))
            rest = lax.div(rest, size)
        self.here = here[::-1]

    def index(self, **moved):
        out = 0
        for axis, size in enumerate(self.sizes):
            out = out * size + moved.get(f"a{axis}", self.here[axis])
        return out

    def toward(self, axis, step):
        return (self.index(**{f"a{axis}": self.here[axis] + step}),)

    def can(self, axis, step):
        return self.here[axis] > 0 if step < 0 else self.here[axis] < self.sizes[axis] - 1

    def bit(self, axis, stride):
        return lax.rem(lax.div(self.here[axis], stride), 2)

    def partner(self, axis, stride):
        return self.toward(axis, (1 - 2 * self.bit(axis, stride)) * stride)

    def greet(self, hops=()):
        barrier = pltpu.get_barrier_semaphore()
        total = 0
        for axis, stride in hops:
            if stride > 1:
                pl.semaphore_signal(barrier, inc=1, device_id=self.partner(axis, stride), device_id_type=MESH)
                total = total + 1
        for axis, size in enumerate(self.sizes):
            for step in (-1, 1):
                if size == 1:
                    continue
                able = self.can(axis, step)

                @pl.when(able)
                def _(axis=axis, step=step):
                    pl.semaphore_signal(
                        barrier, inc=1, device_id=self.toward(axis, step), device_id_type=MESH
                    )

                total = total + able.astype(jnp.int32)
        pl.semaphore_wait(barrier, total)


def run_all(coroutines):
    active = list(coroutines)
    while active:
        still = []
        for coroutine in active:
            try:
                next(coroutine)
                still.append(coroutine)
            except StopIteration:
                pass
        active = still


class Gather:
    def __init__(self, place, part, order, buffer, columns, send, recv):
        self.place, self.part, self.order = place, part, order + (CORE,)
        self.buffer, self.columns, self.send, self.recv = buffer, columns, send, recv

    def copy(self, stage, line, along, step):
        place, axis = self.place, self.order[stage]
        where = []
        for a in range(4):
            if a == axis:
                where.append(along)
            elif a == LINE and LINE in self.order[:stage]:
                where.append(line)
            elif a in self.order[:stage]:
                where.append(slice(None))
            else:
                where.append(place.here[a])
        first, width = self.columns
        block = self.buffer.at[tuple(where) + (slice(None), pl.ds(first, width))]
        lane = 0 if place.sizes[axis] == 2 and axis != LINE else along
        if axis == LINE:
            line, lane = along, 0
        return pltpu.make_async_remote_copy(
            src_ref=block,
            dst_ref=block,
            send_sem=self.send.at[self.part, stage, line, lane, (step + 1) // 2],
            recv_sem=self.recv.at[self.part, stage, line, lane],
            device_id=place.toward(axis, step),
            device_id_type=MESH,
        )

    def each_step(self, stage, do):
        axis, place = self.order[stage], self.place
        if place.sizes[axis] == 1:
            return
        if place.sizes[axis] == 2 and axis != LINE:
            do(1 - 2 * place.here[axis], None)
            return
        for step in (-1, 1):
            do(step, place.can(axis, step))

    def launch(self, stage, line):
        axis, place = self.order[stage], self.place

        def do(step, able):
            def go():
                self.copy(stage, line, place.here[axis], step).start()

            go() if able is None else pl.when(able)(go)

        self.each_step(stage, do)

    def finish(self, stage, line):
        axis, place = self.order[stage], self.place
        size, here = place.sizes[axis], place.here[axis]
        if size == 1:
            return
        if size == 2:
            self.copy(stage, line, 1 - here, 1 - 2 * here).wait_recv()
            return
        for hop in range(1, size):
            for step in (-1, 1):
                along = here - step * hop
                valid = (along >= 0) & (along < size)

                @pl.when(valid)
                def _(along=along, step=step):
                    self.copy(stage, line, along, step).wait_recv()

                @pl.when(valid & place.can(axis, step))
                def _(along=along, step=step):
                    self.copy(stage, line, along, step).start()

    def steps(self):
        place = self.place
        size, here = place.sizes[LINE], place.here[LINE]
        spot = self.order.index(LINE)
        for stage in range(spot):
            self.launch(stage, here)
            yield
            self.finish(stage, here)
        for step in (-1, 1):

            @pl.when(place.can(LINE, step))
            def _(step=step):
                self.copy(spot, here, here, step).start()

        later = list(range(spot + 1, 4))
        for turn in range(size + len(later)):
            for age in range(min(turn, len(later)), -1, -1):
                far = turn - age
                if far >= size:
                    continue
                for step in (-1, 1) if far else (1,):
                    line = here - step * far
                    valid = (line >= 0) & (line < size)

                    def advance(line=line, step=step, far=far, age=age):
                        if age == 0 and far:
                            self.copy(spot, line, line, step).wait_recv()

                            @pl.when(place.can(LINE, step))
                            def _():
                                self.copy(spot, line, line, step).start()

                        if age:
                            self.finish(later[age - 1], line)
                        if age < len(later):
                            self.launch(later[age], line)

                    pl.when(valid)(advance) if far else advance()
            yield

    def drain(self):
        place = self.place
        size, here = place.sizes[LINE], place.here[LINE]
        spot = self.order.index(LINE)
        for line in range(size):
            for step in (-1, 1):

                @pl.when(place.can(LINE, step) & ((line <= here) if step > 0 else (line >= here)))
                def _(line=line, step=step):
                    self.copy(spot, line, line, step).wait_send()

        for stage in range(4):
            if stage == spot:
                continue
            axis = self.order[stage]
            lines = [here] if stage < spot else list(range(size))
            for line in lines:
                if place.sizes[axis] == 1:
                    continue
                if place.sizes[axis] == 2:
                    self.copy(stage, line, place.here[axis], 1 - 2 * place.here[axis]).wait_send()
                    continue
                for step in (-1, 1):
                    for along in range(place.sizes[axis]):
                        at = place.here[axis]

                        @pl.when(place.can(axis, step) & ((along <= at) if step > 0 else (along >= at)))
                        def _(line=line, step=step, along=along, stage=stage):
                            self.copy(stage, line, along, step).wait_send()


ORDERS = ((2, 0, 1), (1, 0, 2), (0, 2, 1), (0, 1, 2))


def gather_kernel(sizes, parts, count, *refs):
    shards, buffers = refs[:count], refs[count : 2 * count]
    send, recv, own = refs[2 * count :]
    place = Place(sizes)
    locals_ = [
        pltpu.make_async_copy(shard, buffer.at[tuple(place.here)], own.at[k])
        for k, (shard, buffer) in enumerate(zip(shards, buffers))
    ]
    for copy in locals_:
        copy.start()
    place.greet()
    for copy in locals_:
        copy.wait()
    gathers = [
        Gather(place, k, order, buffers[which], columns, send, recv)
        for k, (which, columns, order) in enumerate(parts)
    ]
    run_all([g.steps() for g in gathers])
    for g in gathers:
        g.drain()


def lanes_of(sizes):
    return max([1] + [size for size in sizes[1:] if size > 2])


def gather_all(shards, parts, sizes, collective_id):
    lanes = lanes_of(sizes)
    out = pl.pallas_call(
        functools.partial(gather_kernel, sizes, parts, len(shards)),
        out_shape=[jax.ShapeDtypeStruct(sizes + s.shape, s.dtype) for s in shards],
        in_specs=[pl.BlockSpec(memory_space=pltpu.VMEM)] * len(shards),
        out_specs=[pl.BlockSpec(memory_space=pl.ANY)] * len(shards),
        scratch_shapes=[
            pltpu.SemaphoreType.DMA((len(parts), 4, sizes[0], lanes, 2)),
            pltpu.SemaphoreType.DMA((len(parts), 4, sizes[0], lanes)),
            pltpu.SemaphoreType.DMA((len(shards),)),
        ],
        compiler_params=pltpu.CompilerParams(collective_id=collective_id, has_side_effects=True),
    )(*shards)
    return [o.reshape((-1,) + o.shape[5:]) for o in out]


PACE = 1


class Scatter:
    def __init__(self, place, part, order, partial, columns, held, bufs, out, load, send, recv):
        self.place, self.part, self.order = place, part, (CORE,) + order
        self.partial, self.columns, self.held, self.bufs, self.out = partial, columns, held, bufs, out
        self.load, self.send, self.recv = load, send, recv

    def lines(self):
        size = self.place.sizes[LINE]
        return [k // 2 if k % 2 == 0 else size - 1 - k // 2 for k in range(size)]

    def own(self, line):
        first, width = self.columns
        where = (line, slice(None), slice(None), self.place.here[CORE], slice(None), pl.ds(first, width))
        return pltpu.make_async_copy(
            self.partial.at[where], self.bufs[0].at[self.lines().index(line) % (2 * PACE)], self.load.at[self.part, line]
        )

    def block(self, stage, line, along):
        where, done = [], self.order[:stage]
        for a in range(3):
            if a == self.order[stage]:
                where.append(along)
            elif a in done:
                where.append(self.place.here[a])
            elif a == LINE:
                where.append(line)
            else:
                where.append(slice(None))
        return tuple(where)

    def slot(self, stage, line, slot):
        axis = self.order[stage]
        if axis == LINE:
            return (slot,)
        if LINE in self.order[:stage]:
            line = 0
        return (line, 0 if self.place.sizes[axis] == 2 else slot)

    def copy(self, stage, line, along, step):
        place, axis = self.place, self.order[stage]
        size = place.sizes[axis]
        first, width = self.columns
        if axis == CORE:
            where = (line, slice(None), slice(None), along, slice(None), pl.ds(first, width))
            source = self.partial.at[where]
        else:
            source = self.held.at[self.block(stage, line, along)]
        arrives = place.here[axis] + step == along
        number = jnp.where(arrives & (step < 0), size, along) if size > 2 else 0
        sem = self.slot(stage, line, along)
        if axis == LINE:
            sem = sem + (0,)
        there = self.slot(stage, line, number)
        return pltpu.make_async_remote_copy(
            src_ref=source,
            dst_ref=self.held.at[line] if axis == CORE else self.bufs[stage].at[there],
            send_sem=self.send.at[(self.part, stage) + sem],
            recv_sem=self.recv.at[(self.part, stage) + there + ((0,) if axis == LINE else ())],
            device_id=place.toward(axis, step),
            device_id_type=MESH,
        )

    def wait(self, stage, line, number):
        there = self.slot(stage, line, number)
        axis = self.order[stage]
        buf = self.held.at[line] if axis == CORE else self.bufs[stage].at[there]
        pltpu.make_async_copy(
            buf, buf, self.recv.at[(self.part, stage) + there + ((0,) if axis == LINE else ())]
        ).wait()
        return self.bufs[stage], there

    def add(self, stage, line, along, number, last=False):
        buf, there = self.wait(stage, line, number)
        if last:
            first, width = self.columns
            self.out[:, pl.ds(first, width)] += buf[there].astype(jnp.float32)
            return
        where = self.block(stage, line, along)
        if self.order[stage] == CORE:
            where = (line, slice(None), slice(None))
            there = (self.lines().index(line) % (2 * PACE),)
        total = self.held[where].astype(jnp.float32) + buf[there].astype(jnp.float32)
        self.held[where] = total.astype(self.held.dtype)

    def launch(self, stage, line):
        axis, place = self.order[stage], self.place
        size, here = place.sizes[axis], place.here[axis]
        if size == 2:
            self.copy(stage, line, 1 - here, 1 - 2 * here).start()
        elif size > 2:
            for turn in range(1, size):
                for step, along in ((1, size - turn), (-1, turn - 1)):

                    @pl.when((here == (0 if step > 0 else size - 1)))
                    def _(step=step, along=along):
                        self.copy(stage, line, along, step).start()

    def pass_on(self, stage, line, turn):
        axis, place = self.order[stage], self.place
        size, here = place.sizes[axis], place.here[axis]
        for step, along in ((1, size - turn), (-1, turn - 1)):
            ahead = (along > here) if step > 0 else (along < here)

            @pl.when(ahead & place.can(axis, -step))
            def _(step=step, along=along):
                self.add(stage, line, along, along)
                self.copy(stage, line, along, step).start()

    def finish(self, stage, line):
        axis, place = self.order[stage], self.place
        size, here = place.sizes[axis], place.here[axis]
        if size == 2:
            self.add(stage, line, here, 0, stage == 3)
        elif size > 2:
            for step, number in ((-1, here), (1, size)):

                @pl.when(place.can(axis, step))
                def _(number=number):
                    self.add(stage, line, here, number, stage == 3)

    def whole(self, stage, line):
        for turn in range(1, self.place.sizes[self.order[stage]]):
            if self.place.sizes[self.order[stage]] > 2:
                self.pass_on(stage, line, turn)
        self.finish(stage, line)

    def line_hop(self, along, hop):
        place, stage = self.place, self.order.index(LINE)
        size, here = place.sizes[LINE], place.here[LINE]
        for step, at, ahead in ((1, hop, along > hop), (-1, size - 1 - hop, along < size - 1 - hop)):
            if not ahead:
                continue

            @pl.when(here == at)
            def _(step=step):
                if hop:
                    self.add(stage, here, along, along)
                self.copy(stage, here, along, step).start()

    def steps(self):
        place = self.place
        size, here = place.sizes[LINE], place.here[LINE]
        lines = self.lines()
        spot = self.order.index(LINE)

        groups = [lines[k : k + PACE] for k in range(0, size, PACE)]

        def begin(group):
            for line in group:
                self.own(line).start()
                self.launch(0, line)

        begin(groups[0])
        yield
        for turn in range(len(groups) + spot + size - 2):
            if turn + 1 < len(groups):
                begin(groups[turn + 1])
            for k, group in enumerate(groups):
                hop = turn - k - spot
                if 0 <= hop < size - 1:
                    for line in group:
                        self.line_hop(line, hop)
            for stage in range(spot - 1, -1, -1):
                k = turn - stage
                if not 0 <= k < len(groups):
                    continue
                for line in groups[k]:
                    if stage == 0:
                        self.own(line).wait()
                    self.whole(stage, line)
                    if stage + 1 < spot:
                        self.launch(stage + 1, line)
            yield
        if spot == 3:
            self.begin_out()
        self.finish(spot, here)
        for stage in range(spot + 1, 4):
            if stage == 3:
                self.begin_out()
            self.launch(stage, here)
            yield
            self.whole(stage, here)

    def begin_out(self):
        first, width = self.columns
        mine = self.held[tuple(self.place.here[:3])]
        self.out[:, pl.ds(first, width)] = mine.astype(jnp.float32)

    def drain(self):
        place = self.place
        spot = self.order.index(LINE)
        for stage in range(4):
            axis = self.order[stage]
            size, here = place.sizes[axis], place.here[axis]
            for line in range(place.sizes[LINE]) if stage < spot else [place.here[LINE]]:
                if size == 2:
                    self.copy(stage, line, 1 - here, 1 - 2 * here).wait_send()
                elif size > 2:
                    for along in range(size):
                        for step in (-1, 1):

                            @pl.when((along > here) if step > 0 else (along < here))
                            def _(along=along, step=step, line=line, stage=stage):
                                self.copy(stage, line, along, step).wait_send()


def scatter_kernel(sizes, parts, count, *refs):
    partials, outs = refs[:count], refs[count : 2 * count]
    load, send, recv = refs[2 * count : 2 * count + 3]
    scratch = list(refs[2 * count + 3 :])
    place = Place(sizes)
    place.greet()
    scatters = []
    for k, (which, columns, order) in enumerate(parts):
        held, *bufs = scratch[5 * k : 5 * k + 5]
        scatters.append(
            Scatter(place, k, order, partials[which], columns, held, bufs, outs[which], load, send, recv)
        )
    run_all([s.steps() for s in scatters])
    for s in scatters:
        s.drain()


def scatter_scratch(sizes, parts, shapes, dtype):
    scratch = []
    for which, (_, width), order in parts:
        rows = shapes[which][-2]
        scratch.append(pltpu.VMEM(sizes[:3] + (rows, width), dtype))
        stages = (CORE,) + order
        for stage, axis in enumerate(stages):
            free = tuple(sizes[a] for a in range(1, 3) if a not in stages[: stage + 1])
            slots = 1 if sizes[axis] <= 2 else sizes[axis] + 1
            if axis == LINE:
                lead = (slots,)
            elif axis == CORE:
                lead = (2 * PACE,)
            else:
                lead = (1 if LINE in stages[:stage] else sizes[LINE], slots)
            scratch.append(pltpu.VMEM(lead + free + (rows, width), dtype))
    return scratch


def scatter_all(partials, parts, sizes, collective_id):
    count = 1
    for size in sizes:
        count *= size
    partials = [p.reshape(sizes + (p.shape[0] // count, p.shape[1])) for p in partials]
    lanes = max([1] + [size + 1 for size in sizes[1:] if size > 2])
    sems = (len(parts), 4, sizes[0] + 1, lanes)
    return pl.pallas_call(
        functools.partial(scatter_kernel, sizes, parts, len(partials)),
        out_shape=[jax.ShapeDtypeStruct(p.shape[4:], jnp.float32) for p in partials],
        in_specs=[pl.BlockSpec(memory_space=pl.ANY)] * len(partials),
        out_specs=[pl.BlockSpec(memory_space=pltpu.VMEM)] * len(partials),
        scratch_shapes=[
            pltpu.SemaphoreType.DMA((len(parts), sizes[0])),
            pltpu.SemaphoreType.DMA(sems),
            pltpu.SemaphoreType.DMA(sems),
        ]
        + scatter_scratch(sizes, parts, [p.shape for p in partials], partials[0].dtype),
        compiler_params=pltpu.CompilerParams(
            collective_id=collective_id, has_side_effects=True, vmem_limit_bytes=60 << 20
        ),
    )(*partials)


def partners_of(sizes):
    hops = []
    for axis in (2, 1, 0):
        stride = 1
        while stride < sizes[axis]:
            hops.append((axis, stride))
            stride *= 2
    return hops


def scan_kernel(sizes, backward, *refs):
    place = Place(sizes)
    place.greet(partners_of(sizes))
    scan_states(place, backward, lambda hop: None, *refs)


def scan_states(
    place, backward, between, state_ref, logs_ref, out_ref,
    sib, sib_logs, first, first_logs, pre, pre_logs, total, total_logs, wire, wire_logs, got, got_logs, other, send, recv,
):
    core = place.here[CORE]
    hops = partners_of(place.sizes)
    half = HEADS // 2
    mine, theirs = pl.ds(half * core, half), pl.ds(half * (1 - core), half)
    sibling = place.toward(CORE, 1 - 2 * core)
    bit, partner = place.bit, place.partner

    def remote(source, target, number, device):
        return pltpu.make_async_remote_copy(
            src_ref=source, dst_ref=target, send_sem=send.at[number], recv_sem=recv.at[number],
            device_id=device, device_id_type=MESH,
        )

    def scaled(logs, states, added):
        return [jnp.exp(logs[h, 0:1, :]) * states[h] + added[h] for h in range(half)]

    swap = [
        remote(state_ref.at[theirs], sib, 0, sibling),
        remote(logs_ref.at[theirs], sib_logs, 1, sibling),
    ]
    for copy in swap:
        copy.start()
    for copy in swap:
        copy.wait_recv()
    starts = core == (1 if backward else 0)

    @pl.when(starts)
    def _():
        first[...] = state_ref[mine]
        first_logs[...] = logs_ref[mine]
        new = scaled(sib_logs, first, sib)
        for h in range(half):
            total[h] = new[h]

    @pl.when(jnp.logical_not(starts))
    def _():
        first[...] = sib[...]
        first_logs[...] = sib_logs[...]
        new = scaled(logs_ref.at[mine], first, state_ref.at[mine])
        for h in range(half):
            total[h] = new[h]

    total_logs[...] = logs_ref[mine] + sib_logs[...]
    pre[...] = jnp.zeros_like(pre)
    pre_logs[...] = jnp.zeros_like(pre_logs)
    pending = list(swap)
    for k, (axis, stride) in enumerate(hops):
        between(k)
        last = k == len(hops) - 1
        wire[k] = total[...].astype(wire.dtype)
        wire_logs[k] = total_logs[...]
        copies = [
            remote(wire.at[k], got.at[k], 2 + 2 * k, partner(axis, stride)),
            remote(wire_logs.at[k], got_logs.at[k], 3 + 2 * k, partner(axis, stride)),
        ]
        for copy in copies:
            copy.start()
        pending += copies
        for copy in copies:
            copy.wait_recv()
        earlier = bit(axis, stride) == (1 if backward else 0)
        arrived = [got[k, h].astype(jnp.float32) for h in range(half)]

        @pl.when(jnp.logical_not(earlier))
        def _(k=k, arrived=arrived, last=last):
            new = scaled(pre_logs, arrived, pre)
            for h in range(half):
                pre[h] = new[h]
            pre_logs[...] = pre_logs[...] + got_logs[k]
            if not last:
                new = scaled(total_logs, arrived, total)
                for h in range(half):
                    total[h] = new[h]

        if not last:

            @pl.when(earlier)
            def _(k=k, arrived=arrived):
                new = scaled(got_logs.at[k], total, arrived)
                for h in range(half):
                    total[h] = new[h]

            total_logs[...] = total_logs[...] + got_logs[k]
    second = scaled(first_logs, pre, first)

    @pl.when(starts)
    def _():
        for h in range(half):
            other[h] = second[h]
        out_ref[mine] = pre[...]

    @pl.when(jnp.logical_not(starts))
    def _():
        other[...] = pre[...]
        for h in range(half):
            out_ref[half * core + h] = second[h]

    back = remote(other, out_ref.at[mine], 2 + 2 * len(hops), sibling)
    back.start()
    back.wait_recv()
    for copy in pending + [back]:
        copy.wait_send()


def scan_scratch(sizes):
    half, hops = HEADS // 2, len(partners_of(sizes))
    block, tile = (half, HV, HK), (half, 8, HK)
    return [
        pltpu.VMEM(block, jnp.float32), pltpu.VMEM(tile, jnp.float32),
        pltpu.VMEM(block, jnp.float32), pltpu.VMEM(tile, jnp.float32),
        pltpu.VMEM(block, jnp.float32), pltpu.VMEM(tile, jnp.float32),
        pltpu.VMEM(block, jnp.float32), pltpu.VMEM(tile, jnp.float32),
        pltpu.VMEM((hops,) + block, jnp.bfloat16), pltpu.VMEM((hops,) + tile, jnp.float32),
        pltpu.VMEM((hops,) + block, jnp.bfloat16), pltpu.VMEM((hops,) + tile, jnp.float32),
        pltpu.VMEM(block, jnp.float32),
        pltpu.SemaphoreType.DMA((3 + 2 * hops,)),
        pltpu.SemaphoreType.DMA((3 + 2 * hops,)),
    ]


def entering(state, logs, sizes, backward, collective_id):
    return pl.pallas_call(
        functools.partial(scan_kernel, sizes, backward),
        out_shape=jax.ShapeDtypeStruct(state.shape, jnp.float32),
        in_specs=[pl.BlockSpec(memory_space=pltpu.VMEM)] * 2,
        out_specs=pl.BlockSpec(memory_space=pltpu.VMEM),
        scratch_shapes=scan_scratch(sizes),
        compiler_params=pltpu.CompilerParams(
            collective_id=collective_id, has_side_effects=True, vmem_limit_bytes=32 << 20
        ),
    )(state, logs)


CHUNK = 128
ROWS = 256
FTILE = 256
F32, BF16 = jnp.float32, jnp.bfloat16


def nn(left, right):
    return jnp.dot(left, right, preferred_element_type=F32)


def nt(left, right):
    return lax.dot_general(left, right, (((1,), (1,)), ((), ())), preferred_element_type=F32)


def tn(left, right):
    return lax.dot_general(left, right, (((0,), (0,)), ((), ())), preferred_element_type=F32)


def sigmoid(v):
    return 1.0 / (1.0 + jnp.exp(-v))


def causal_mask(size):
    return lax.broadcasted_iota(jnp.int32, (size, size), 0) >= lax.broadcasted_iota(jnp.int32, (size, size), 1)


def triangle(upper):
    rows = lax.broadcasted_iota(jnp.int32, (CHUNK, CHUNK), 0)
    columns = lax.broadcasted_iota(jnp.int32, (CHUNK, CHUNK), 1)
    kept = (columns >= rows) if upper else (columns <= rows)
    return jnp.where(kept, 1.0, 0.0).astype(BF16)


def running(matrix, values):
    high = values.astype(BF16)
    low = (values - high.astype(F32)).astype(BF16)
    return nn(matrix, high) + nn(matrix, low)


def halves(values):
    high = values.astype(BF16)
    return high, (values - high.astype(F32)).astype(BF16)


def fine_nt(left, right):
    (high, low), (other, rest) = left, right
    return nt(high, other) + (nt(high, rest) + nt(low, other))


def inverse_rms(values):
    return lax.rsqrt(jnp.mean(values * values, axis=-1, keepdims=True) + 1e-06)


def heads_of(width):
    return [slice(h * width, (h + 1) * width) for h in range(HEADS)]


def small_rows(extra):
    lanes = lax.broadcasted_iota(jnp.int32, (8, extra.shape[1]), 1)
    rows = lax.broadcasted_iota(jnp.int32, (8, extra.shape[1]), 0)
    return nt(jnp.where(lanes == rows + RANK, 1.0, 0.0).astype(BF16), extra)


def with_one(mid):
    lanes = lax.broadcasted_iota(jnp.int32, mid.shape, 1)
    return jnp.where(lanes < RANK, mid, jnp.where(lanes == RANK, 1.0, 0.0)).astype(BF16)


def project_rows(tokens, gain, weight, up, outs, final_ref, logs_ref):
    normed_ref, query_ref, key_ref, value_ref, gate_ref, mid_ref, logit_ref, within_ref, update_ref = outs
    inputs = tokens[...].astype(F32)
    normed = inputs * inverse_rms(inputs) * gain
    normed_ref[...] = (normed.T if normed_ref.shape[0] != tokens.shape[0] else normed).astype(BF16)
    normed = normed.astype(BF16)
    keys = HEADS * HK
    values = HEADS * HV
    mid = with_one(nn(normed, weight(2 * keys + 2 * values, 128)))
    mid_ref[...] = mid
    logit = nt(mid, up)
    logit_ref[...] = logit
    query_ref[...] = nn(normed, weight(0, keys)).astype(BF16)
    key_ref[...] = nn(normed, weight(keys, keys)).astype(BF16)
    value_ref[...] = nn(normed, weight(2 * keys, values)).astype(BF16)
    gate_ref[...] = nn(normed, weight(2 * keys + values, values)).astype(BF16)
    decay = (jnp.minimum(logit, 0.0) - jnp.log1p(jnp.exp(-jnp.abs(logit)))) * (1.0 / 16.0)
    lower = triangle(False)
    for c in range(ROWS // CHUNK):
        rows = pl.ds(c * CHUNK, CHUNK)
        within = running(lower, decay[c * CHUNK : (c + 1) * CHUNK])
        within_ref[rows, :] = within
        total = within[CHUNK - 1 : CHUNK]
        ending = (key_ref[rows, :].astype(F32) * jnp.exp(total - within)).astype(BF16)
        for h, (ks, vs) in enumerate(zip(heads_of(HK), heads_of(HV))):
            update = tn(value_ref[rows, vs], ending[:, ks])
            update_ref[c, h] = update.astype(BF16)
            final_ref[h] = final_ref[h] * jnp.exp(total[:, ks]) + update
            logs_ref[h] = logs_ref[h] + total[:, ks]


def project_kernel(tokens, gains, weights, up, *refs):
    outs, (final_ref, logs_ref) = refs[:9], refs[9:]

    @pl.when(pl.program_id(0) == 0)
    def _():
        final_ref[...] = jnp.zeros_like(final_ref)
        logs_ref[...] = jnp.zeros_like(logs_ref)

    project_rows(
        tokens, gains[0:1], lambda first, width: weights[:, first : first + width], up[...], outs, final_ref, logs_ref
    )


def mix_rows(tokens, query, key, value, gate, within_all, update, state, head_gain, out_weight, ffn_gain, outs):
    mixed_ref, gated_ref, hidden_ref, ffn_ref, starts_ref = outs
    mask = causal_mask(CHUNK)
    for c in range(ROWS // CHUNK):
        rows = pl.ds(c * CHUNK, CHUNK)
        within = within_all[rows, :]
        middle = within[CHUNK // 2 - 1 : CHUNK // 2]
        total = within[CHUNK - 1 : CHUNK]
        scaled = query[rows, :].astype(F32) * HK**-0.5
        from_start = (scaled * jnp.exp(within)).astype(BF16)
        left = halves(scaled * jnp.exp(within - middle))
        right = halves(key[rows, :].astype(F32) * jnp.exp(middle - within))
        for h, (ks, vs) in enumerate(zip(heads_of(HK), heads_of(HV))):
            start = state[h].astype(BF16)
            starts_ref[c, h] = start
            scores = jnp.where(mask, fine_nt([p[:, ks] for p in left], [p[:, ks] for p in right]), 0.0).astype(BF16)
            mixed = nn(scores, value[rows, vs]) + nt(from_start[:, ks], start)
            state[h] = state[h] * jnp.exp(total[:, ks]) + update[c, h].astype(F32)
            mixed_ref[rows, vs] = mixed
            gates = gate[rows, vs].astype(F32)
            gated = mixed * inverse_rms(mixed) * head_gain[:, vs] * (gates * sigmoid(gates))
            gated_ref[rows, vs] = gated.astype(BF16)
    hidden = tokens[...].astype(F32) + nn(gated_ref[...], out_weight)
    hidden_ref[...] = hidden
    ffn_in = hidden * inverse_rms(hidden) * ffn_gain
    ffn_ref[...] = ffn_in.astype(BF16)
    return ffn_in


def mix_kernel(tokens, query, key, value, gate, within_all, update, entering_ref, gains, out_weight, *refs):
    outs, state = refs[:5], refs[5]

    @pl.when(pl.program_id(0) == 0)
    def _():
        state[...] = entering_ref[...]

    mix_rows(
        tokens, query, key, value, gate, within_all, update, state, gains[1:2], out_weight[...], gains[2:3], outs
    )


def ffn_kernel(
    ffn_in, ffn_in_t, cotangent, hidden, gate_weight, up_weight, down_weight,
    out_ref, back_ref, gate_grad, up_grad, down_grad,
):
    @pl.when(pl.program_id(0) == 0)
    def _():
        out_ref[...] = hidden[...]
        back_ref[...] = jnp.zeros_like(back_ref)

    gate, up = nn(ffn_in[...], gate_weight[...]), nn(ffn_in[...], up_weight[...])
    back = nt(cotangent[...], down_weight[...])
    share = sigmoid(gate)
    passed = gate * share
    inner = (passed * up).astype(BF16)
    d_up = (back * passed).astype(BF16)
    d_gate = (back * up * (share * (1.0 + gate * (1.0 - share)))).astype(BF16)
    out_ref[...] += nn(inner, down_weight[...])
    back_ref[...] += nt(d_gate, gate_weight[...]) + nt(d_up, up_weight[...])
    gate_grad[...] = nn(ffn_in_t[...], d_gate).astype(BF16)
    up_grad[...] = nn(ffn_in_t[...], d_up).astype(BF16)
    down_grad[...] = tn(inner, cotangent[...]).astype(BF16)


def norm_back(values, gain, grad):
    scale = inverse_rms(values)
    inner = grad * gain
    along = jnp.mean(inner * values, axis=-1, keepdims=True)
    return scale * inner - values * (scale * scale * scale * along), grad * values * scale


def unmix_kernel(
    ffn_back, hidden, cotangent, gate, mixed, query, within_all, gains, out_weight,
    d_hidden_ref, low_ref, d_gate_ref, d_mixed_ref, update_ref, enters_ref, ffn_gain_ref, head_gain_ref,
):
    @pl.when(pl.program_id(0) == 0)
    def _():
        enters_ref[...] = jnp.zeros_like(enters_ref)
        ffn_gain_ref[...] = jnp.zeros_like(ffn_gain_ref)
        head_gain_ref[...] = jnp.zeros_like(head_gain_ref)

    through, terms = norm_back(hidden[...], gains[2:3], ffn_back[...])
    ffn_gain_ref[...] += jnp.sum(terms, axis=0, keepdims=True)
    d_hidden = cotangent[...].astype(F32) + through
    d_hidden_ref[...] = d_hidden
    low = d_hidden.astype(BF16)
    low_ref[...] = low
    d_gated = nt(low, out_weight[...])
    for vs in heads_of(HV):
        value = mixed[:, vs]
        scale = inverse_rms(value)
        headed = value * scale
        gates = gate[:, vs].astype(F32)
        share = sigmoid(gates)
        passed = gates * share
        grad, gain = d_gated[:, vs], gains[1:2, vs]
        head_gain_ref[:, vs] += jnp.sum(grad * headed * passed, axis=0, keepdims=True)
        d_gate_ref[:, vs] = (grad * headed * gain * (share * (1.0 + gates * (1.0 - share)))).astype(BF16)
        d_headed = grad * gain * passed
        along = jnp.mean(d_headed * headed, axis=-1, keepdims=True)
        d_mixed_ref[:, vs] = scale * (d_headed - headed * along)
    for c in reversed(range(ROWS // CHUNK)):
        rows = slice(c * CHUNK, (c + 1) * CHUNK)
        within = within_all[rows]
        total = within[CHUNK - 1 : CHUNK]
        from_start = (query[rows].astype(F32) * HK**-0.5 * jnp.exp(within)).astype(BF16)
        for h, (ks, vs) in enumerate(zip(heads_of(HK), heads_of(HV))):
            update = tn(d_mixed_ref[rows, vs].astype(BF16), from_start[:, ks])
            update_ref[c, h] = update.astype(BF16)
            enters_ref[h] = enters_ref[h] * jnp.exp(total[:, ks]) + update


def back_rows(
    tokens, query, key, value, logit, within_all, d_mixed, starts, update, d_gate, d_hidden, gains, weights, up,
    d_proj_ref, d_logit_ref, tokens_grad_ref, gain_ref, state,
):
    mask = causal_mask(CHUNK)
    upper = triangle(True)
    keys = HEADS * HK
    for c in reversed(range(ROWS // CHUNK)):
        rows = slice(c * CHUNK, (c + 1) * CHUNK)
        within = within_all[rows]
        middle = within[CHUNK // 2 - 1 : CHUNK // 2]
        total = within[CHUNK - 1 : CHUNK]
        factor = jnp.exp(total)
        queries, keys_f = query[rows].astype(F32), key[rows].astype(F32)
        q_start, q_middle = jnp.exp(within) * HK**-0.5, jnp.exp(within - middle) * HK**-0.5
        k_middle, k_end = jnp.exp(middle - within), jnp.exp(total - within)
        lefts, rights = halves(queries * q_middle), halves(keys_f * k_middle)
        left, right = lefts[0], rights[0]
        ending = (keys_f * k_end).astype(BF16)
        moves, extras = [], []
        for h, (ks, vs) in enumerate(zip(heads_of(HK), heads_of(HV))):
            start, after = starts[c, h], state[h].astype(BF16)
            (grad, rest), values = halves(d_mixed[rows, vs]), value[rows, vs]
            scores = jnp.where(mask, fine_nt([p[:, ks] for p in lefts], [p[:, ks] for p in rights]), 0.0).astype(BF16)
            d_scores = jnp.where(mask, nt(grad, values) + nt(rest, values), 0.0).astype(BF16)
            d_value = tn(scores, grad) + nt(ending[:, ks], after)
            d_query = nn(d_scores, right[:, ks]) * q_middle[:, ks] + nn(grad, start) * q_start[:, ks]
            d_end = nn(values, after) * k_end[:, ks]
            d_key = tn(d_scores, left[:, ks]) * k_middle[:, ks] + d_end
            d_proj_ref[rows, ks] = d_query.astype(BF16)
            d_proj_ref[rows, slice(keys + ks.start, keys + ks.stop)] = d_key.astype(BF16)
            d_proj_ref[rows, slice(2 * keys + vs.start, 2 * keys + vs.stop)] = d_value.astype(BF16)
            moves.append(queries[:, ks] * d_query - keys_f[:, ks] * d_key)
            extras.append(
                jnp.sum(keys_f[:, ks] * d_end, axis=0, keepdims=True)
                + factor[:, ks] * jnp.sum(start.astype(F32) * state[h], axis=0, keepdims=True)
            )
            state[h] = state[h] * factor[:, ks] + update[c, h].astype(F32)
        d_decay = running(upper, jnp.concatenate(moves, axis=1)) + jnp.concatenate(extras, axis=1)
        d_logit = d_decay * sigmoid(-logit[rows]) * (1.0 / 16.0)
        d_logit_ref[rows] = d_logit.astype(BF16)
    d_mid = nn(d_logit_ref[...], up[...])
    d_mid = jnp.where(lax.broadcasted_iota(jnp.int32, d_mid.shape, 1) < RANK, d_mid, 0.0).astype(BF16)
    inner = 2 * keys + HEADS * HV
    outer = inner + HEADS * HV
    d_proj_ref[:, inner:outer] = d_gate[...]
    d_proj_ref[:, outer:] = d_mid
    d_normed = nt(d_proj_ref[...], weights[...])
    through, terms = norm_back(tokens[...].astype(F32), gains[0:1], d_normed)
    gain_ref[...] += jnp.sum(terms, axis=0, keepdims=True)
    tokens_grad_ref[...] = d_hidden[...] + through


def back_kernel(*refs):
    tiles, leaving_ref, refs = refs[:11], refs[11], refs[12:]
    gain_ref, state = refs[-2:]

    @pl.when(pl.program_id(0) == 0)
    def _():
        state[...] = leaving_ref[...]
        gain_ref[...] = jnp.zeros_like(gain_ref)

    back_rows(*tiles, *refs)


def tail_kernel(sizes, steps, count, *refs):
    tiles, (enters, logs), refs = refs[:11], refs[11:13], refs[13:]
    kept, partials, refs = refs[:3], refs[3 : 3 + count], refs[3 + count :]
    outs, gain_ref, sums, refs = refs[:3], refs[3], refs[4 : 4 + count], refs[4 + count :]
    state, load, send, recv = refs[:4]
    scratch, scan = refs[4 : 4 + 5 * len(TAIL_PARTS)], refs[4 + 5 * len(TAIL_PARTS) :]
    place = Place(sizes)
    step = pl.program_id(0)
    scatters = []
    for k, (which, columns, order) in enumerate(TAIL_PARTS):
        held, *bufs = scratch[5 * k : 5 * k + 5]
        scatters.append(
            Scatter(place, k, order, partials[which], columns, held, bufs, sums[which], load, send, recv)
        )
    moves = [s.steps() for s in scatters]

    def turn():
        for move in moves:
            next(move, None)

    def during(hop):
        for _ in range(TAIL_TURNS[0].count(hop)):
            turn()

    @pl.when(step == 0)
    def _():
        gain_ref[...] = jnp.zeros_like(gain_ref)
        place.greet(partners_of(sizes))
        turn()
        scan_states(place, True, during, enters, logs, state, *scan)

    for k in range(1, steps + 1):

        @pl.when(step == k)
        def _(k=k):
            for _ in range(TAIL_TURNS[1].count(k)):
                turn()

    @pl.when(step > 0)
    def _():
        back_rows(*tiles, *kept, *outs, gain_ref, state)

    @pl.when(step == steps)
    def _():
        run_all(moves)
        for s in scatters:
            s.drain()


def rows_spec(width, steps, backward):
    return pl.BlockSpec((ROWS, width), (lambda i: (steps - 1 - i, 0)) if backward else (lambda i: (i, 0)))


def chunks_spec(steps, backward):
    return pl.BlockSpec(
        (ROWS // CHUNK, HEADS, HV, HK),
        (lambda i: (steps - 1 - i, 0, 0, 0)) if backward else (lambda i: (i, 0, 0, 0)),
    )


def kept_spec(shape):
    return pl.BlockSpec(shape, lambda i: (0,) * len(shape), pipeline_mode=pl.Buffered(1))


def kept_out(shape):
    return pl.BlockSpec(shape, lambda i: (0,) * len(shape))


PARAMS = dict(vmem_limit_bytes=60 << 20)
STATE = (HEADS, HV, HK)


def project(tokens, gains, weights, up):
    length, width = tokens.shape
    steps, keys, values = length // ROWS, HEADS * HK, HEADS * HV
    row = lambda w: rows_spec(w, steps, False)
    chunks = (length // CHUNK,) + STATE
    shape = jax.ShapeDtypeStruct
    return pl.pallas_call(
        project_kernel,
        grid=(steps,),
        in_specs=[row(width)] + [kept_spec(a.shape) for a in (gains, weights, up)],
        out_specs=[row(w) for w in (width, keys, keys, values, values, 128, keys, keys)]
        + [chunks_spec(steps, False), kept_out(STATE), kept_out((HEADS, 8, HK))],
        out_shape=[shape((length, w), BF16) for w in (width, keys, keys, values, values, 128)]
        + [shape((length, keys), F32)] * 2
        + [shape(chunks, BF16), shape(STATE, F32), shape((HEADS, 8, HK), F32)],
        compiler_params=pltpu.CompilerParams(**PARAMS),
    )(tokens, gains, weights, up)


def mix(tokens, query, key, value, gate, within, update, entered, gains, out_weight):
    length, width = tokens.shape
    steps, keys, values = length // ROWS, HEADS * HK, HEADS * HV
    row = lambda w: rows_spec(w, steps, False)
    shape = jax.ShapeDtypeStruct
    return pl.pallas_call(
        mix_kernel,
        grid=(steps,),
        in_specs=[row(w) for w in (width, keys, keys, values, values, keys)]
        + [chunks_spec(steps, False)]
        + [kept_spec(a.shape) for a in (entered, gains, out_weight)],
        out_specs=[row(w) for w in (values, values, width, width)] + [chunks_spec(steps, False)],
        out_shape=[
            shape((length, values), F32), shape((length, values), BF16),
            shape((length, width), F32), shape((length, width), BF16), shape(update.shape, BF16),
        ],
        scratch_shapes=[pltpu.VMEM(STATE, F32)],
        compiler_params=pltpu.CompilerParams(**PARAMS),
    )(tokens, query, key, value, gate, within, update, entered, gains, out_weight)


FRONT_PARTS = (
    (0, (0, 128), ORDERS[0]),
    (1, (0, 1024), ORDERS[0]),
    (1, (1024, 1024), ORDERS[1]),
    (1, (2048, 1152), ORDERS[2]),
    (2, (0, 1024), ORDERS[3]),
    (3, (0, 2816), ORDERS[0]),
    (4, (0, 2816), ORDERS[1]),
    (5, (0, 512), ORDERS[2]),
    (5, (512, 512), ORDERS[3]),
)
FIRST_PARTS = 5
FRONT_TURNS = (1, 2, (2,), 1)


def front_kernel(sizes, steps, *refs):
    tokens, shards, refs = refs[0], refs[1:7], refs[7:]
    buffers, refs = refs[:6], refs[6:]
    outs, mixed_outs, (logs_out, gains_out, ffn_t_ref), refs = refs[:8], refs[8:13], refs[13:16], refs[16:]
    up_all, proj_all, out_all, query, key, value, gate, within, update, state, final, logs, gains, refs = *refs[:13], refs[13:]
    send, recv, own, flush = refs[:4]
    scan = refs[4:]
    place = Place(sizes)
    step = pl.program_id(0)
    here = tuple(place.here)
    held = (up_all, proj_all, out_all) + tuple(buffers[3:])
    gathers = [
        Gather(place, k, order, held[which], columns, send, recv)
        for k, (which, columns, order) in enumerate(FRONT_PARTS)
    ]
    owned = [pltpu.make_async_copy(shards[k], buffers[k].at[here], own.at[k]) for k in (3, 4, 5)]
    flushes = [pltpu.make_async_copy(held[k], buffers[k], flush.at[k]) for k in range(3)]
    later = [g.steps() for g in gathers[FIRST_PARTS:]]

    def turn():
        for g in later:
            next(g, None)

    def during(hop):
        if hop in FRONT_TURNS[2]:
            turn()

    @pl.when(step == 0)
    def _():
        for copy in owned:
            copy.start()
        for k in range(3):
            held[k][here] = shards[k][...]
        place.greet(partners_of(sizes))
        for copy in owned:
            copy.wait()
        run_all([g.steps() for g in gathers[:FIRST_PARTS]])
        turn()
        flushes[0].start()
        flushes[1].start()
        flushes[2].start()
        extra = 2 * HEADS * (HK + HV)
        gains[...] = small_rows(proj_all[..., pl.ds(extra, 128)].reshape(-1, 128))
        gains_out[...] = gains[...]
        final[...] = jnp.zeros_like(final)
        logs[...] = jnp.zeros_like(logs)
        for _ in range(FRONT_TURNS[0]):
            turn()

    @pl.when(step < steps)
    def _():
        rows = pl.ds(pl.multiple_of(step * ROWS, ROWS), ROWS)
        chunks = pl.ds(step * (ROWS // CHUNK), ROWS // CHUNK)
        normed_ref, query_ref, key_ref, value_ref, gate_ref, mid_ref, logit_ref, within_ref = outs
        kept = (query, key, value, gate, within)
        tiles = (query_ref, key_ref, value_ref, gate_ref, within_ref)
        project_rows(
            tokens, gains[0:1],
            lambda first, width: proj_all[..., pl.ds(first, width)].reshape(-1, width),
            up_all[...].reshape(-1, 128),
            (normed_ref, query_ref, key_ref, value_ref, gate_ref, mid_ref, logit_ref, within_ref, update.at[chunks]),
            final, logs,
        )
        for whole, tile in zip(kept, tiles):
            whole[rows, :] = tile[...]

    @pl.when(step == steps)
    def _():
        for _ in range(FRONT_TURNS[1]):
            turn()
        logs_out[...] = logs[...]
        scan_states(place, False, during, final, logs, state, *scan)
        for _ in range(FRONT_TURNS[3]):
            turn()

    @pl.when(step >= steps)
    def _():
        at = step - steps
        rows = pl.ds(pl.multiple_of(at * ROWS, ROWS), ROWS)
        chunks = pl.ds(at * (ROWS // CHUNK), ROWS // CHUNK)
        ffn_in = mix_rows(
            tokens, query.at[rows], key.at[rows], value.at[rows], gate.at[rows], within.at[rows], update.at[chunks], state,
            gains[1:2], out_all[...].reshape(-1, out_all.shape[-1]), gains[2:3], mixed_outs,
        )
        ffn_t_ref[...] = ffn_in.T.astype(BF16)

    @pl.when(step == 2 * steps - 1)
    def _():
        run_all(later)
        for g in gathers:
            g.drain()
        for copy in flushes:
            copy.wait()


def front(tokens, shards, sizes, collective_id):
    length, width = tokens.shape
    steps, keys, values = length // ROWS, HEADS * HK, HEADS * HV
    shape, chunks = jax.ShapeDtypeStruct, (length // CHUNK,) + STATE
    first = lambda w: pl.BlockSpec((ROWS, w), lambda i: (jnp.minimum(i, steps - 1), 0))
    second = lambda w: pl.BlockSpec((ROWS, w), lambda i: (jnp.maximum(i - steps, 0), 0))
    lanes = lanes_of(sizes)
    parts = len(FRONT_PARTS)
    one = lambda w, t: ((length, w), t)
    turned = lambda first: pl.BlockSpec((width, ROWS), lambda i: (0, jnp.minimum(i, steps - 1) if first else jnp.maximum(i - steps, 0)))
    results = [one(keys, BF16), one(keys, BF16), one(values, BF16), one(values, BF16), one(128, BF16), one(keys, F32), one(keys, F32)]
    mixes = [one(values, F32), one(values, BF16), one(width, F32), one(width, BF16)]
    out = pl.pallas_call(
        functools.partial(front_kernel, sizes, steps),
        grid=(2 * steps,),
        in_specs=[pl.BlockSpec((ROWS, width), lambda i: (lax.rem(i, steps), 0))] + [kept_spec(s.shape) for s in shards],
        out_specs=[pl.BlockSpec(memory_space=pl.ANY)] * len(shards)
        + [turned(True)] + [first(s[1]) for s, _ in results]
        + [second(s[1]) for s, _ in mixes]
        + [pl.BlockSpec((ROWS // CHUNK,) + STATE, lambda i: (jnp.maximum(i - steps, 0), 0, 0, 0))]
        + [kept_out((HEADS, 8, HK)), kept_out((8, width)), turned(False)],
        out_shape=[shape(sizes + s.shape, s.dtype) for s in shards]
        + [shape((width, length), BF16)]
        + [shape(s, t) for s, t in results + mixes]
        + [shape(chunks, BF16), shape((HEADS, 8, HK), F32), shape((8, width), F32), shape((width, length), BF16)],
        scratch_shapes=[pltpu.VMEM(sizes + s.shape, s.dtype) for s in shards[:3]]
        + [pltpu.VMEM((length, w), t) for w, t in ((keys, BF16), (keys, BF16), (values, BF16), (values, BF16), (keys, F32))]
        + [pltpu.VMEM(chunks, BF16), pltpu.VMEM(STATE, F32), pltpu.VMEM(STATE, F32), pltpu.VMEM((HEADS, 8, HK), F32), pltpu.VMEM((8, width), F32)]
        + [
            pltpu.SemaphoreType.DMA((parts, 4, sizes[0], lanes, 2)),
            pltpu.SemaphoreType.DMA((parts, 4, sizes[0], lanes)),
            pltpu.SemaphoreType.DMA((len(shards),)),
            pltpu.SemaphoreType.DMA((3,)),
        ]
        + scan_scratch(sizes),
        compiler_params=pltpu.CompilerParams(collective_id=collective_id, has_side_effects=True, **PARAMS),
    )(tokens, *shards)
    weights = [o.reshape(-1, o.shape[-1]) for o in out[: len(shards)]]
    return weights, out[len(shards) :]


def feed_forward(ffn_in, ffn_t, cotangent, hidden, gate_weight, up_weight, down_weight):
    length, width = ffn_in.shape
    inner = gate_weight.shape[1]
    whole = [ffn_in, ffn_t, cotangent, hidden]
    wide = pl.BlockSpec((width, FTILE), lambda i: (0, i))
    tall = pl.BlockSpec((FTILE, width), lambda i: (i, 0))
    shape = jax.ShapeDtypeStruct
    return pl.pallas_call(
        ffn_kernel,
        grid=(inner // FTILE,),
        in_specs=[kept_spec(a.shape) for a in whole] + [wide, wide, tall],
        out_specs=[kept_out((length, width))] * 2 + [wide, wide, tall],
        out_shape=[shape((length, width), F32)] * 2
        + [shape((width, inner), BF16)] * 2 + [shape((inner, width), BF16)],
        compiler_params=pltpu.CompilerParams(**PARAMS),
    )(*whole, gate_weight, up_weight, down_weight)


def unmix(ffn_back, hidden, cotangent, gate, mixed, query, within, gains, out_weight):
    length, width = hidden.shape
    steps, keys, values = length // ROWS, HEADS * HK, HEADS * HV
    row = lambda w: rows_spec(w, steps, True)
    chunks = (length // CHUNK,) + STATE
    shape = jax.ShapeDtypeStruct
    return pl.pallas_call(
        unmix_kernel,
        grid=(steps,),
        in_specs=[row(w) for w in (width, width, width, values, values, keys, keys)]
        + [kept_spec(a.shape) for a in (gains, out_weight)],
        out_specs=[row(w) for w in (width, width, values, values)]
        + [chunks_spec(steps, True), kept_out(STATE), kept_out((1, width)), kept_out((1, values))],
        out_shape=[
            shape((length, width), F32), shape((length, width), BF16), shape((length, values), BF16),
            shape((length, values), F32), shape(chunks, BF16), shape(STATE, F32),
            shape((1, width), F32), shape((1, values), F32),
        ],
        compiler_params=pltpu.CompilerParams(**PARAMS),
    )(ffn_back, hidden, cotangent, gate, mixed, query, within, gains, out_weight)


def back(tiles, leaving, gains, weights, up):
    length, width = tiles[0].shape
    steps, keys, values = length // ROWS, HEADS * HK, HEADS * HV
    row = lambda w: rows_spec(w, steps, True)
    shape = jax.ShapeDtypeStruct
    return pl.pallas_call(
        back_kernel,
        grid=(steps,),
        in_specs=[row(w) for w in (width, keys, keys, values, keys, keys, values)]
        + [chunks_spec(steps, True)] * 2 + [row(values), row(width)]
        + [kept_spec(a.shape) for a in (leaving, gains, weights, up)],
        out_specs=[row(w) for w in (weights.shape[1], keys, width)] + [kept_out((1, width))],
        out_shape=[
            shape((length, weights.shape[1]), BF16), shape((length, keys), BF16),
            shape((length, width), F32), shape((1, width), F32),
        ],
        scratch_shapes=[pltpu.VMEM(STATE, F32)],
        compiler_params=pltpu.CompilerParams(**PARAMS),
    )(*tiles, leaving, gains, weights, up)


TAIL_PARTS = (
    (2, (0, 512), (0, 2, 1)),
    (3, (0, 1024), (0, 1, 2)),
    (0, (0, 2816), (1, 2, 0)),
    (1, (0, 2816), (2, 1, 0)),
    (2, (512, 512), (1, 2, 0)),
)
TAIL_TURNS = ((2, 4), (1, 2, 3, 4))
LAST_PARTS = (
    (0, (0, 128), ORDERS[0][::-1]),
    (1, (0, 1024), ORDERS[0][::-1]),
    (1, (1024, 1024), ORDERS[1][::-1]),
    (1, (2048, 640), ORDERS[2][::-1]),
    (1, (2688, 512), ORDERS[3][::-1]),
)


def tail(tiles, enters, logs, gains, weights, up, partials, sizes, collective_id):
    length, width = tiles[0].shape
    steps, keys, values = length // ROWS, HEADS * HK, HEADS * HV
    shape, at = jax.ShapeDtypeStruct, lambda i: steps - jnp.maximum(i, 1)
    row = lambda w: pl.BlockSpec((ROWS, w), lambda i: (at(i), 0))
    chunk = pl.BlockSpec((ROWS // CHUNK,) + STATE, lambda i: (at(i), 0, 0, 0))
    count = len(partials)
    devices = sizes[0] * sizes[1] * sizes[2] * sizes[3]
    partials = [p.reshape(sizes + (p.shape[0] // devices, p.shape[1])) for p in partials]
    lanes = max([1] + [size + 1 for size in sizes[1:] if size > 2])
    sems = (len(TAIL_PARTS), 4, sizes[0] + 1, lanes)
    out = pl.pallas_call(
        functools.partial(tail_kernel, sizes, steps, count),
        grid=(steps + 1,),
        in_specs=[row(w) for w in (width, keys, keys, values, keys, keys, values)]
        + [chunk] * 2 + [row(values), row(width)]
        + [kept_spec(a.shape) for a in (enters, logs, gains, weights, up)]
        + [pl.BlockSpec(memory_space=pl.ANY)] * count,
        out_specs=[row(w) for w in (weights.shape[1], keys, width)] + [kept_out((1, width))]
        + [kept_out(p.shape[4:]) for p in partials],
        out_shape=[
            shape((length, weights.shape[1]), BF16), shape((length, keys), BF16),
            shape((length, width), F32), shape((1, width), F32),
        ] + [shape(p.shape[4:], F32) for p in partials],
        scratch_shapes=[
            pltpu.VMEM(STATE, F32),
            pltpu.SemaphoreType.DMA((len(TAIL_PARTS), sizes[0])),
            pltpu.SemaphoreType.DMA(sems),
            pltpu.SemaphoreType.DMA(sems),
        ]
        + scatter_scratch(sizes, TAIL_PARTS, [p.shape for p in partials], BF16)
        + scan_scratch(sizes),
        compiler_params=pltpu.CompilerParams(collective_id=collective_id, has_side_effects=True, **PARAMS),
    )(*tiles, enters, logs, gains, weights, up, *partials)
    return out[:4], out[4:]


def last_kernel(sizes, *refs):
    normed_t, d_proj, small, small_out, proj_out, load, send, recv = refs[:8]
    scratch = refs[8 : 8 + 5 * len(LAST_PARTS)]
    partials = [small] + list(refs[8 + 5 * len(LAST_PARTS) :])
    place = Place(sizes)
    place.greet()
    moves, scatters = [], []
    for k, (which, (first, width), order) in enumerate(LAST_PARTS):
        for move in moves:
            next(move, None)
        out = small_out
        if which:
            out = proj_out.at[:, pl.ds(first, width)]
            for at in range(0, width, 512):
                tile = min(512, width - at)
                grad = nn(normed_t[...], d_proj[:, first + at : first + at + tile]).astype(BF16)
                partials[k][..., pl.ds(at, tile)] = grad.reshape(partials[k].shape[:-1] + (tile,))
        held, *bufs = scratch[5 * k : 5 * k + 5]
        scatters.append(Scatter(place, k, order, partials[k], (0, width), held, bufs, out, load, send, recv))
        moves.append(scatters[-1].steps())
        next(moves[-1])
    run_all(moves)
    for s in scatters:
        s.drain()


def project_grads(normed_t, d_proj, small, sizes, collective_id):
    devices = sizes[0] * sizes[1] * sizes[2] * sizes[3]
    small = small.reshape(sizes + (small.shape[0] // devices, small.shape[1]))
    rows = d_proj.shape[1], normed_t.shape[0] // devices
    shapes = [small.shape, sizes + (rows[1], rows[0])]
    lanes = max([1] + [size + 1 for size in sizes[1:] if size > 2])
    sems = (len(LAST_PARTS), 4, sizes[0] + 1, lanes)
    vmem = pl.BlockSpec(memory_space=pltpu.VMEM)
    return pl.pallas_call(
        functools.partial(last_kernel, sizes),
        out_shape=[jax.ShapeDtypeStruct(s[4:], F32) for s in shapes],
        in_specs=[vmem, vmem, pl.BlockSpec(memory_space=pl.ANY)],
        out_specs=[vmem] * 2,
        scratch_shapes=[
            pltpu.SemaphoreType.DMA((len(LAST_PARTS), sizes[0])),
            pltpu.SemaphoreType.DMA(sems),
            pltpu.SemaphoreType.DMA(sems),
        ]
        + scatter_scratch(sizes, LAST_PARTS, shapes, BF16)
        + [pltpu.VMEM(shapes[1][:-1] + (width,), BF16) for which, (_, width), _ in LAST_PARTS if which],
        compiler_params=pltpu.CompilerParams(collective_id=collective_id, has_side_effects=True, **PARAMS),
    )(normed_t, d_proj, small)


def beside(pieces):
    rows, used = pieces[0].shape[0], sum(p.shape[1] for p in pieces)
    return jnp.concatenate(pieces + [jnp.zeros((rows, 128 - used), pieces[0].dtype)], axis=1)


def local(
    tokens,
    norm_gain,
    query_weight,
    key_weight,
    value_weight,
    gate_weight,
    rank_down,
    rank_up,
    gate_bias,
    head_gain,
    out_weight,
    ffn_gain,
    ffn_gate,
    ffn_up,
    ffn_down,
    cotangent,
):
    sizes = grid_of(lax.axis_size("seq"))
    extra = beside([rank_down] + [g[:, None] for g in (norm_gain, head_gain, ffn_gain)])
    projections = jnp.concatenate([query_weight, key_weight, value_weight, gate_weight, extra], axis=1)
    shards = [beside([rank_up.T, gate_bias[:, None]]), projections, out_weight, ffn_gate, ffn_up, ffn_down]
    if rank_up.shape[1] % 16 == 0:
        weights, kept = front(tokens, shards, sizes, 0)
        up, proj, out, full_fgate, full_fup, full_fdown = weights
        normed_t, query, key, value, gate, mid, logit, within, mixed, gated, hidden, ffn_in, starts, logs, gains, ffn_t = kept
    else:
        up, proj, out, full_fgate, full_fup, full_fdown = gather_all(shards, FRONT_PARTS, sizes, 0)
        gains = jnp.pad(proj[:, -128 + RANK : -128 + RANK + 3].astype(F32).T, ((0, 5), (0, 0)))
        normed, query, key, value, gate, mid, logit, within, update, final, logs = project(tokens, gains, proj, up)
        incoming = entering(final, logs, sizes, False, 2)
        mixed, gated, hidden, ffn_in, starts = mix(
            tokens, query, key, value, gate, within, update, incoming, gains, out
        )
        normed_t, ffn_t = normed.T, ffn_in.T
    block_output, ffn_back, fgate_wgrad, fup_wgrad, fdown_wgrad = feed_forward(
        ffn_in, ffn_t, cotangent, hidden, full_fgate, full_fup, full_fdown
    )
    d_hidden, hidden_low, d_gate, d_mixed, back_update, enters, ffn_gain_grad, head_gain_grad = unmix(
        ffn_back, hidden, cotangent, gate, mixed, query, within, gains, out
    )
    out_wgrad = tn(gated, hidden_low).astype(BF16)
    early = [fgate_wgrad, fup_wgrad, fdown_wgrad, out_wgrad]
    tiles = (tokens, query, key, value, logit, within, d_mixed, starts, back_update, d_gate, d_hidden)
    if rank_up.shape[1] % 16 == 0:
        backs, early_sums = tail(tiles, enters, logs, gains, proj, up, early, sizes, 3)
    else:
        leaving = entering(enters, logs, sizes, True, 3)
        backs = back(tiles, leaving, gains, proj, up)
        early_sums = scatter_all(early, TAIL_PARTS, sizes, 4)
    d_proj, d_logit, tokens_grad, gain_grad = backs
    fgate_sum, fup_sum, fdown_sum, out_sum = early_sums
    keys_here = rank_up.shape[1]
    gain_grads = jnp.concatenate([gain_grad, head_gain_grad, ffn_gain_grad]).reshape(3, -1, norm_gain.shape[0] // keys_here, keys_here)
    gain_grads = gain_grads.transpose(1, 3, 0, 2).reshape(HEADS * HK, -1)
    up_wgrad = beside([tn(d_logit, mid)[:, : RANK + 1], gain_grads]).astype(BF16)
    if keys_here % 16 == 0:
        up_sum, proj_sum = project_grads(normed_t, d_proj, up_wgrad, sizes, 1)
    else:
        up_sum, proj_sum = scatter_all([up_wgrad, nn(normed_t, d_proj).astype(BF16)], LAST_PARTS, sizes, 1)
    keys, values = HEADS * HK, HEADS * HV
    last = 2 * (keys + values)
    gain_sum, head_sum, ffn_sum = (
        up_sum[:, RANK + 1 : RANK + 1 + 3 * (norm_gain.shape[0] // keys_here)].reshape(keys_here, 3, -1).transpose(1, 2, 0).reshape(3, -1)
    )
    return (
        block_output,
        tokens_grad,
        gain_sum,
        proj_sum[:, :keys],
        proj_sum[:, keys : 2 * keys],
        proj_sum[:, 2 * keys : 2 * keys + values],
        proj_sum[:, 2 * keys + values : last],
        proj_sum[:, last : last + RANK],
        up_sum[:, :RANK].T,
        up_sum[:, RANK],
        head_sum,
        out_sum,
        ffn_sum,
        fgate_sum,
        fup_sum,
        fdown_sum,
    )


def solution(mesh):
    return jax.shard_map(
        local,
        mesh=mesh,
        in_specs=(
            P("seq", None),
            P("seq"),
            P("seq", None),
            P("seq", None),
            P("seq", None),
            P("seq", None),
            P("seq", None),
            P(None, "seq"),
            P("seq"),
            P("seq"),
            P("seq", None),
            P("seq"),
            P("seq", None),
            P("seq", None),
            P("seq", None),
            P("seq", None),
        ),
        out_specs=(
            P("seq", None),
            P("seq", None),
            P("seq"),
            P("seq", None),
            P("seq", None),
            P("seq", None),
            P("seq", None),
            P("seq", None),
            P(None, "seq"),
            P("seq"),
            P("seq"),
            P("seq", None),
            P("seq"),
            P("seq", None),
            P("seq", None),
            P("seq", None),
        ),
        check_vma=False,
    )
```

```python
import functools

import jax
import jax.numpy as jnp
from jax import lax
from jax.experimental import pallas as pl
from jax.experimental.pallas import tpu as pltpu
from jax.sharding import PartitionSpec as P

HEADS = 4
HK = 128
HV = 256
RANK = 16

MESH = pl.DeviceIdType.MESH
LINE = 0
CORE = 3


def grid_of(count):
    core = 2 if count % 2 == 0 else 1
    rest = count // core
    third = max(k for k in range(1, rest + 1) if rest % k == 0 and k**3 <= rest)
    rest //= third
    second = max(k for k in range(1, rest + 1) if rest % k == 0 and k * k <= rest)
    return (rest // second, second, third, core)


class Place:
    def __init__(self, sizes):
        self.sizes = sizes
        rest = lax.axis_index("seq")
        here = []
        for size in sizes[::-1]:
            here.append(lax.rem(rest, size))
            rest = lax.div(rest, size)
        self.here = here[::-1]

    def index(self, **moved):
        out = 0
        for axis, size in enumerate(self.sizes):
            out = out * size + moved.get(f"a{axis}", self.here[axis])
        return out

    def toward(self, axis, step):
        return (self.index(**{f"a{axis}": self.here[axis] + step}),)

    def can(self, axis, step):
        return self.here[axis] > 0 if step < 0 else self.here[axis] < self.sizes[axis] - 1

    def bit(self, axis, stride):
        return lax.rem(lax.div(self.here[axis], stride), 2)

    def partner(self, axis, stride):
        return self.toward(axis, (1 - 2 * self.bit(axis, stride)) * stride)

    def greet(self, hops=()):
        barrier = pltpu.get_barrier_semaphore()
        total = 0
        for axis, stride in hops:
            if stride > 1:
                pl.semaphore_signal(barrier, inc=1, device_id=self.partner(axis, stride), device_id_type=MESH)
                total = total + 1
        for axis, size in enumerate(self.sizes):
            for step in (-1, 1):
                if size == 1:
                    continue
                able = self.can(axis, step)

                @pl.when(able)
                def _(axis=axis, step=step):
                    pl.semaphore_signal(
                        barrier, inc=1, device_id=self.toward(axis, step), device_id_type=MESH
                    )

                total = total + able.astype(jnp.int32)
        pl.semaphore_wait(barrier, total)


def run_all(coroutines):
    active = list(coroutines)
    while active:
        still = []
        for coroutine in active:
            try:
                next(coroutine)
                still.append(coroutine)
            except StopIteration:
                pass
        active = still


class Gather:
    def __init__(self, place, part, order, buffer, columns, send, recv):
        self.place, self.part, self.order = place, part, order + (CORE,)
        self.buffer, self.columns, self.send, self.recv = buffer, columns, send, recv

    def copy(self, stage, line, along, step):
        place, axis = self.place, self.order[stage]
        where = []
        for a in range(4):
            if a == axis:
                where.append(along)
            elif a == LINE and LINE in self.order[:stage]:
                where.append(line)
            elif a in self.order[:stage]:
                where.append(slice(None))
            else:
                where.append(place.here[a])
        first, width = self.columns
        block = self.buffer.at[tuple(where) + (slice(None), pl.ds(first, width))]
        lane = 0 if place.sizes[axis] == 2 and axis != LINE else along
        if axis == LINE:
            line, lane = along, 0
        return pltpu.make_async_remote_copy(
            src_ref=block,
            dst_ref=block,
            send_sem=self.send.at[self.part, stage, line, lane, (step + 1) // 2],
            recv_sem=self.recv.at[self.part, stage, line, lane],
            device_id=place.toward(axis, step),
            device_id_type=MESH,
        )

    def each_step(self, stage, do):
        axis, place = self.order[stage], self.place
        if place.sizes[axis] == 1:
            return
        if place.sizes[axis] == 2 and axis != LINE:
            do(1 - 2 * place.here[axis], None)
            return
        for step in (-1, 1):
            do(step, place.can(axis, step))

    def launch(self, stage, line):
        axis, place = self.order[stage], self.place

        def do(step, able):
            def go():
                self.copy(stage, line, place.here[axis], step).start()

            go() if able is None else pl.when(able)(go)

        self.each_step(stage, do)

    def finish(self, stage, line):
        axis, place = self.order[stage], self.place
        size, here = place.sizes[axis], place.here[axis]
        if size == 1:
            return
        if size == 2:
            self.copy(stage, line, 1 - here, 1 - 2 * here).wait_recv()
            return
        for hop in range(1, size):
            for step in (-1, 1):
                along = here - step * hop
                valid = (along >= 0) & (along < size)

                @pl.when(valid)
                def _(along=along, step=step):
                    self.copy(stage, line, along, step).wait_recv()

                @pl.when(valid & place.can(axis, step))
                def _(along=along, step=step):
                    self.copy(stage, line, along, step).start()

    def steps(self):
        place = self.place
        size, here = place.sizes[LINE], place.here[LINE]
        spot = self.order.index(LINE)
        for stage in range(spot):
            self.launch(stage, here)
            yield
            self.finish(stage, here)
        for step in (-1, 1):

            @pl.when(place.can(LINE, step))
            def _(step=step):
                self.copy(spot, here, here, step).start()

        later = list(range(spot + 1, 4))
        for turn in range(size + len(later)):
            for age in range(min(turn, len(later)), -1, -1):
                far = turn - age
                if far >= size:
                    continue
                for step in (-1, 1) if far else (1,):
                    line = here - step * far
                    valid = (line >= 0) & (line < size)

                    def advance(line=line, step=step, far=far, age=age):
                        if age == 0 and far:
                            self.copy(spot, line, line, step).wait_recv()

                            @pl.when(place.can(LINE, step))
                            def _():
                                self.copy(spot, line, line, step).start()

                        if age:
                            self.finish(later[age - 1], line)
                        if age < len(later):
                            self.launch(later[age], line)

                    pl.when(valid)(advance) if far else advance()
            yield

    def drain(self):
        place = self.place
        size, here = place.sizes[LINE], place.here[LINE]
        spot = self.order.index(LINE)
        for line in range(size):
            for step in (-1, 1):

                @pl.when(place.can(LINE, step) & ((line <= here) if step > 0 else (line >= here)))
                def _(line=line, step=step):
                    self.copy(spot, line, line, step).wait_send()

        for stage in range(4):
            if stage == spot:
                continue
            axis = self.order[stage]
            lines = [here] if stage < spot else list(range(size))
            for line in lines:
                if place.sizes[axis] == 1:
                    continue
                if place.sizes[axis] == 2:
                    self.copy(stage, line, place.here[axis], 1 - 2 * place.here[axis]).wait_send()
                    continue
                for step in (-1, 1):
                    for along in range(place.sizes[axis]):
                        at = place.here[axis]

                        @pl.when(place.can(axis, step) & ((along <= at) if step > 0 else (along >= at)))
                        def _(line=line, step=step, along=along, stage=stage):
                            self.copy(stage, line, along, step).wait_send()


ORDERS = ((2, 0, 1), (1, 0, 2), (0, 2, 1), (0, 1, 2))


def gather_kernel(sizes, parts, count, *refs):
    shards, buffers = refs[:count], refs[count : 2 * count]
    send, recv, own = refs[2 * count :]
    place = Place(sizes)
    locals_ = [
        pltpu.make_async_copy(shard, buffer.at[tuple(place.here)], own.at[k])
        for k, (shard, buffer) in enumerate(zip(shards, buffers))
    ]
    for copy in locals_:
        copy.start()
    place.greet()
    for copy in locals_:
        copy.wait()
    gathers = [
        Gather(place, k, order, buffers[which], columns, send, recv)
        for k, (which, columns, order) in enumerate(parts)
    ]
    run_all([g.steps() for g in gathers])
    for g in gathers:
        g.drain()


def lanes_of(sizes):
    return max([1] + [size for size in sizes[1:] if size > 2])


def gather_all(shards, parts, sizes, collective_id):
    lanes = lanes_of(sizes)
    out = pl.pallas_call(
        functools.partial(gather_kernel, sizes, parts, len(shards)),
        out_shape=[jax.ShapeDtypeStruct(sizes + s.shape, s.dtype) for s in shards],
        in_specs=[pl.BlockSpec(memory_space=pltpu.VMEM)] * len(shards),
        out_specs=[pl.BlockSpec(memory_space=pl.ANY)] * len(shards),
        scratch_shapes=[
            pltpu.SemaphoreType.DMA((len(parts), 4, sizes[0], lanes, 2)),
            pltpu.SemaphoreType.DMA((len(parts), 4, sizes[0], lanes)),
            pltpu.SemaphoreType.DMA((len(shards),)),
        ],
        compiler_params=pltpu.CompilerParams(collective_id=collective_id, has_side_effects=True),
    )(*shards)
    return [o.reshape((-1,) + o.shape[5:]) for o in out]


PACE = 1


class Scatter:
    def __init__(self, place, part, order, partial, columns, held, bufs, out, load, send, recv):
        self.place, self.part, self.order = place, part, (CORE,) + order
        self.partial, self.columns, self.held, self.bufs, self.out = partial, columns, held, bufs, out
        self.load, self.send, self.recv = load, send, recv

    def lines(self):
        size = self.place.sizes[LINE]
        return [k // 2 if k % 2 == 0 else size - 1 - k // 2 for k in range(size)]

    def own(self, line):
        first, width = self.columns
        where = (line, slice(None), slice(None), self.place.here[CORE], slice(None), pl.ds(first, width))
        return pltpu.make_async_copy(
            self.partial.at[where], self.bufs[0].at[self.lines().index(line) % (2 * PACE)], self.load.at[self.part, line]
        )

    def block(self, stage, line, along):
        where, done = [], self.order[:stage]
        for a in range(3):
            if a == self.order[stage]:
                where.append(along)
            elif a in done:
                where.append(self.place.here[a])
            elif a == LINE:
                where.append(line)
            else:
                where.append(slice(None))
        return tuple(where)

    def slot(self, stage, line, slot):
        axis = self.order[stage]
        if axis == LINE:
            return (slot,)
        if LINE in self.order[:stage]:
            line = 0
        return (line, 0 if self.place.sizes[axis] == 2 else slot)

    def copy(self, stage, line, along, step):
        place, axis = self.place, self.order[stage]
        size = place.sizes[axis]
        first, width = self.columns
        if axis == CORE:
            where = (line, slice(None), slice(None), along, slice(None), pl.ds(first, width))
            source = self.partial.at[where]
        else:
            source = self.held.at[self.block(stage, line, along)]
        arrives = place.here[axis] + step == along
        number = jnp.where(arrives & (step < 0), size, along) if size > 2 else 0
        sem = self.slot(stage, line, along)
        if axis == LINE:
            sem = sem + (0,)
        there = self.slot(stage, line, number)
        return pltpu.make_async_remote_copy(
            src_ref=source,
            dst_ref=self.held.at[line] if axis == CORE else self.bufs[stage].at[there],
            send_sem=self.send.at[(self.part, stage) + sem],
            recv_sem=self.recv.at[(self.part, stage) + there + ((0,) if axis == LINE else ())],
            device_id=place.toward(axis, step),
            device_id_type=MESH,
        )

    def wait(self, stage, line, number):
        there = self.slot(stage, line, number)
        axis = self.order[stage]
        buf = self.held.at[line] if axis == CORE else self.bufs[stage].at[there]
        pltpu.make_async_copy(
            buf, buf, self.recv.at[(self.part, stage) + there + ((0,) if axis == LINE else ())]
        ).wait()
        return self.bufs[stage], there

    def add(self, stage, line, along, number, last=False):
        buf, there = self.wait(stage, line, number)
        if last:
            first, width = self.columns
            self.out[:, pl.ds(first, width)] += buf[there].astype(jnp.float32)
            return
        where = self.block(stage, line, along)
        if self.order[stage] == CORE:
            where = (line, slice(None), slice(None))
            there = (self.lines().index(line) % (2 * PACE),)
        total = self.held[where].astype(jnp.float32) + buf[there].astype(jnp.float32)
        self.held[where] = total.astype(self.held.dtype)

    def launch(self, stage, line):
        axis, place = self.order[stage], self.place
        size, here = place.sizes[axis], place.here[axis]
        if size == 2:
            self.copy(stage, line, 1 - here, 1 - 2 * here).start()
        elif size > 2:
            for turn in range(1, size):
                for step, along in ((1, size - turn), (-1, turn - 1)):

                    @pl.when((here == (0 if step > 0 else size - 1)))
                    def _(step=step, along=along):
                        self.copy(stage, line, along, step).start()

    def pass_on(self, stage, line, turn):
        axis, place = self.order[stage], self.place
        size, here = place.sizes[axis], place.here[axis]
        for step, along in ((1, size - turn), (-1, turn - 1)):
            ahead = (along > here) if step > 0 else (along < here)

            @pl.when(ahead & place.can(axis, -step))
            def _(step=step, along=along):
                self.add(stage, line, along, along)
                self.copy(stage, line, along, step).start()

    def finish(self, stage, line):
        axis, place = self.order[stage], self.place
        size, here = place.sizes[axis], place.here[axis]
        if size == 2:
            self.add(stage, line, here, 0, stage == 3)
        elif size > 2:
            for step, number in ((-1, here), (1, size)):

                @pl.when(place.can(axis, step))
                def _(number=number):
                    self.add(stage, line, here, number, stage == 3)

    def whole(self, stage, line):
        for turn in range(1, self.place.sizes[self.order[stage]]):
            if self.place.sizes[self.order[stage]] > 2:
                self.pass_on(stage, line, turn)
        self.finish(stage, line)

    def line_hop(self, along, hop):
        place, stage = self.place, self.order.index(LINE)
        size, here = place.sizes[LINE], place.here[LINE]
        for step, at, ahead in ((1, hop, along > hop), (-1, size - 1 - hop, along < size - 1 - hop)):
            if not ahead:
                continue

            @pl.when(here == at)
            def _(step=step):
                if hop:
                    self.add(stage, here, along, along)
                self.copy(stage, here, along, step).start()

    def steps(self):
        place = self.place
        size, here = place.sizes[LINE], place.here[LINE]
        lines = self.lines()
        spot = self.order.index(LINE)

        groups = [lines[k : k + PACE] for k in range(0, size, PACE)]

        def begin(group):
            for line in group:
                self.own(line).start()
                self.launch(0, line)

        begin(groups[0])
        yield
        for turn in range(len(groups) + spot + size - 2):
            if turn + 1 < len(groups):
                begin(groups[turn + 1])
            for k, group in enumerate(groups):
                hop = turn - k - spot
                if 0 <= hop < size - 1:
                    for line in group:
                        self.line_hop(line, hop)
            for stage in range(spot - 1, -1, -1):
                k = turn - stage
                if not 0 <= k < len(groups):
                    continue
                for line in groups[k]:
                    if stage == 0:
                        self.own(line).wait()
                    self.whole(stage, line)
                    if stage + 1 < spot:
                        self.launch(stage + 1, line)
            yield
        if spot == 3:
            self.begin_out()
        self.finish(spot, here)
        for stage in range(spot + 1, 4):
            if stage == 3:
                self.begin_out()
            self.launch(stage, here)
            yield
            self.whole(stage, here)

    def begin_out(self):
        first, width = self.columns
        mine = self.held[tuple(self.place.here[:3])]
        self.out[:, pl.ds(first, width)] = mine.astype(jnp.float32)

    def drain(self):
        place = self.place
        spot = self.order.index(LINE)
        for stage in range(4):
            axis = self.order[stage]
            size, here = place.sizes[axis], place.here[axis]
            for line in range(place.sizes[LINE]) if stage < spot else [place.here[LINE]]:
                if size == 2:
                    self.copy(stage, line, 1 - here, 1 - 2 * here).wait_send()
                elif size > 2:
                    for along in range(size):
                        for step in (-1, 1):

                            @pl.when((along > here) if step > 0 else (along < here))
                            def _(along=along, step=step, line=line, stage=stage):
                                self.copy(stage, line, along, step).wait_send()


def scatter_kernel(sizes, parts, count, *refs):
    partials, outs = refs[:count], refs[count : 2 * count]
    load, send, recv = refs[2 * count : 2 * count + 3]
    scratch = list(refs[2 * count + 3 :])
    place = Place(sizes)
    place.greet()
    scatters = []
    for k, (which, columns, order) in enumerate(parts):
        held, *bufs = scratch[5 * k : 5 * k + 5]
        scatters.append(
            Scatter(place, k, order, partials[which], columns, held, bufs, outs[which], load, send, recv)
        )
    run_all([s.steps() for s in scatters])
    for s in scatters:
        s.drain()


def scatter_scratch(sizes, parts, shapes, dtype):
    scratch = []
    for which, (_, width), order in parts:
        rows = shapes[which][-2]
        scratch.append(pltpu.VMEM(sizes[:3] + (rows, width), dtype))
        stages = (CORE,) + order
        for stage, axis in enumerate(stages):
            free = tuple(sizes[a] for a in range(1, 3) if a not in stages[: stage + 1])
            slots = 1 if sizes[axis] <= 2 else sizes[axis] + 1
            if axis == LINE:
                lead = (slots,)
            elif axis == CORE:
                lead = (2 * PACE,)
            else:
                lead = (1 if LINE in stages[:stage] else sizes[LINE], slots)
            scratch.append(pltpu.VMEM(lead + free + (rows, width), dtype))
    return scratch


def scatter_all(partials, parts, sizes, collective_id):
    count = 1
    for size in sizes:
        count *= size
    partials = [p.reshape(sizes + (p.shape[0] // count, p.shape[1])) for p in partials]
    lanes = max([1] + [size + 1 for size in sizes[1:] if size > 2])
    sems = (len(parts), 4, sizes[0] + 1, lanes)
    return pl.pallas_call(
        functools.partial(scatter_kernel, sizes, parts, len(partials)),
        out_shape=[jax.ShapeDtypeStruct(p.shape[4:], jnp.float32) for p in partials],
        in_specs=[pl.BlockSpec(memory_space=pl.ANY)] * len(partials),
        out_specs=[pl.BlockSpec(memory_space=pltpu.VMEM)] * len(partials),
        scratch_shapes=[
            pltpu.SemaphoreType.DMA((len(parts), sizes[0])),
            pltpu.SemaphoreType.DMA(sems),
            pltpu.SemaphoreType.DMA(sems),
        ]
        + scatter_scratch(sizes, parts, [p.shape for p in partials], partials[0].dtype),
        compiler_params=pltpu.CompilerParams(
            collective_id=collective_id, has_side_effects=True, vmem_limit_bytes=60 << 20
        ),
    )(*partials)


def partners_of(sizes):
    hops = []
    for axis in (2, 1, 0):
        stride = 1
        while stride < sizes[axis]:
            hops.append((axis, stride))
            stride *= 2
    return hops


def scan_kernel(sizes, backward, *refs):
    place = Place(sizes)
    place.greet(partners_of(sizes))
    scan_states(place, backward, lambda hop: None, *refs)


def scan_states(
    place, backward, between, state_ref, logs_ref, out_ref,
    sib, sib_logs, first, first_logs, pre, pre_logs, total, total_logs, wire, wire_logs, got, got_logs, other, send, recv,
):
    core = place.here[CORE]
    hops = partners_of(place.sizes)
    half = HEADS // 2
    mine, theirs = pl.ds(half * core, half), pl.ds(half * (1 - core), half)
    sibling = place.toward(CORE, 1 - 2 * core)
    bit, partner = place.bit, place.partner

    def remote(source, target, number, device):
        return pltpu.make_async_remote_copy(
            src_ref=source, dst_ref=target, send_sem=send.at[number], recv_sem=recv.at[number],
            device_id=device, device_id_type=MESH,
        )

    def scaled(logs, states, added):
        return [jnp.exp(logs[h, 0:1, :]) * states[h] + added[h] for h in range(half)]

    swap = [
        remote(state_ref.at[theirs], sib, 0, sibling),
        remote(logs_ref.at[theirs], sib_logs, 1, sibling),
    ]
    for copy in swap:
        copy.start()
    for copy in swap:
        copy.wait_recv()
    starts = core == (1 if backward else 0)

    @pl.when(starts)
    def _():
        first[...] = state_ref[mine]
        first_logs[...] = logs_ref[mine]
        new = scaled(sib_logs, first, sib)
        for h in range(half):
            total[h] = new[h]

    @pl.when(jnp.logical_not(starts))
    def _():
        first[...] = sib[...]
        first_logs[...] = sib_logs[...]
        new = scaled(logs_ref.at[mine], first, state_ref.at[mine])
        for h in range(half):
            total[h] = new[h]

    total_logs[...] = logs_ref[mine] + sib_logs[...]
    pre[...] = jnp.zeros_like(pre)
    pre_logs[...] = jnp.zeros_like(pre_logs)
    pending = list(swap)
    for k, (axis, stride) in enumerate(hops):
        between(k)
        last = k == len(hops) - 1
        wire[k] = total[...].astype(wire.dtype)
        wire_logs[k] = total_logs[...]
        copies = [
            remote(wire.at[k], got.at[k], 2 + 2 * k, partner(axis, stride)),
            remote(wire_logs.at[k], got_logs.at[k], 3 + 2 * k, partner(axis, stride)),
        ]
        for copy in copies:
            copy.start()
        pending += copies
        for copy in copies:
            copy.wait_recv()
        earlier = bit(axis, stride) == (1 if backward else 0)
        arrived = [got[k, h].astype(jnp.float32) for h in range(half)]

        @pl.when(jnp.logical_not(earlier))
        def _(k=k, arrived=arrived, last=last):
            new = scaled(pre_logs, arrived, pre)
            for h in range(half):
                pre[h] = new[h]
            pre_logs[...] = pre_logs[...] + got_logs[k]
            if not last:
                new = scaled(total_logs, arrived, total)
                for h in range(half):
                    total[h] = new[h]

        if not last:

            @pl.when(earlier)
            def _(k=k, arrived=arrived):
                new = scaled(got_logs.at[k], total, arrived)
                for h in range(half):
                    total[h] = new[h]

            total_logs[...] = total_logs[...] + got_logs[k]
    second = scaled(first_logs, pre, first)

    @pl.when(starts)
    def _():
        for h in range(half):
            other[h] = second[h]
        out_ref[mine] = pre[...]

    @pl.when(jnp.logical_not(starts))
    def _():
        other[...] = pre[...]
        for h in range(half):
            out_ref[half * core + h] = second[h]

    back = remote(other, out_ref.at[mine], 2 + 2 * len(hops), sibling)
    back.start()
    back.wait_recv()
    for copy in pending + [back]:
        copy.wait_send()


def scan_scratch(sizes):
    half, hops = HEADS // 2, len(partners_of(sizes))
    block, tile = (half, HV, HK), (half, 8, HK)
    return [
        pltpu.VMEM(block, jnp.float32), pltpu.VMEM(tile, jnp.float32),
        pltpu.VMEM(block, jnp.float32), pltpu.VMEM(tile, jnp.float32),
        pltpu.VMEM(block, jnp.float32), pltpu.VMEM(tile, jnp.float32),
        pltpu.VMEM(block, jnp.float32), pltpu.VMEM(tile, jnp.float32),
        pltpu.VMEM((hops,) + block, jnp.bfloat16), pltpu.VMEM((hops,) + tile, jnp.float32),
        pltpu.VMEM((hops,) + block, jnp.bfloat16), pltpu.VMEM((hops,) + tile, jnp.float32),
        pltpu.VMEM(block, jnp.float32),
        pltpu.SemaphoreType.DMA((3 + 2 * hops,)),
        pltpu.SemaphoreType.DMA((3 + 2 * hops,)),
    ]


def entering(state, logs, sizes, backward, collective_id):
    return pl.pallas_call(
        functools.partial(scan_kernel, sizes, backward),
        out_shape=jax.ShapeDtypeStruct(state.shape, jnp.float32),
        in_specs=[pl.BlockSpec(memory_space=pltpu.VMEM)] * 2,
        out_specs=pl.BlockSpec(memory_space=pltpu.VMEM),
        scratch_shapes=scan_scratch(sizes),
        compiler_params=pltpu.CompilerParams(
            collective_id=collective_id, has_side_effects=True, vmem_limit_bytes=32 << 20
        ),
    )(state, logs)


CHUNK = 128
ROWS = 256
FTILE = 256
F32, BF16 = jnp.float32, jnp.bfloat16


def nn(left, right):
    return jnp.dot(left, right, preferred_element_type=F32)


def nt(left, right):
    return lax.dot_general(left, right, (((1,), (1,)), ((), ())), preferred_element_type=F32)


def tn(left, right):
    return lax.dot_general(left, right, (((0,), (0,)), ((), ())), preferred_element_type=F32)


def sigmoid(v):
    return 1.0 / (1.0 + jnp.exp(-v))


def causal_mask(size):
    return lax.broadcasted_iota(jnp.int32, (size, size), 0) >= lax.broadcasted_iota(jnp.int32, (size, size), 1)


def triangle(upper):
    rows = lax.broadcasted_iota(jnp.int32, (CHUNK, CHUNK), 0)
    columns = lax.broadcasted_iota(jnp.int32, (CHUNK, CHUNK), 1)
    kept = (columns >= rows) if upper else (columns <= rows)
    return jnp.where(kept, 1.0, 0.0).astype(BF16)


def running(matrix, values):
    high = values.astype(BF16)
    low = (values - high.astype(F32)).astype(BF16)
    return nn(matrix, high) + nn(matrix, low)


def halves(values):
    high = values.astype(BF16)
    return high, (values - high.astype(F32)).astype(BF16)


def fine_nt(left, right):
    (high, low), (other, rest) = left, right
    return nt(high, other) + (nt(high, rest) + nt(low, other))


def inverse_rms(values):
    return lax.rsqrt(jnp.mean(values * values, axis=-1, keepdims=True) + 1e-06)


def heads_of(width):
    return [slice(h * width, (h + 1) * width) for h in range(HEADS)]


def small_rows(extra):
    lanes = lax.broadcasted_iota(jnp.int32, (8, extra.shape[1]), 1)
    rows = lax.broadcasted_iota(jnp.int32, (8, extra.shape[1]), 0)
    return nt(jnp.where(lanes == rows + RANK, 1.0, 0.0).astype(BF16), extra)


def with_one(mid):
    lanes = lax.broadcasted_iota(jnp.int32, mid.shape, 1)
    return jnp.where(lanes < RANK, mid, jnp.where(lanes == RANK, 1.0, 0.0)).astype(BF16)


def project_rows(tokens, gain, weight, up, outs, final_ref, logs_ref):
    normed_ref, query_ref, key_ref, value_ref, gate_ref, mid_ref, logit_ref, within_ref, update_ref = outs
    inputs = tokens[...].astype(F32)
    normed = inputs * inverse_rms(inputs) * gain
    normed_ref[...] = (normed.T if normed_ref.shape[0] != tokens.shape[0] else normed).astype(BF16)
    normed = normed.astype(BF16)
    keys = HEADS * HK
    values = HEADS * HV
    mid = with_one(nn(normed, weight(2 * keys + 2 * values, 128)))
    mid_ref[...] = mid
    logit = nt(mid, up)
    logit_ref[...] = logit
    query_ref[...] = nn(normed, weight(0, keys)).astype(BF16)
    key_ref[...] = nn(normed, weight(keys, keys)).astype(BF16)
    value_ref[...] = nn(normed, weight(2 * keys, values)).astype(BF16)
    gate_ref[...] = nn(normed, weight(2 * keys + values, values)).astype(BF16)
    decay = (jnp.minimum(logit, 0.0) - jnp.log1p(jnp.exp(-jnp.abs(logit)))) * (1.0 / 16.0)
    lower = triangle(False)
    for c in range(ROWS // CHUNK):
        rows = pl.ds(c * CHUNK, CHUNK)
        within = running(lower, decay[c * CHUNK : (c + 1) * CHUNK])
        within_ref[rows, :] = within
        total = within[CHUNK - 1 : CHUNK]
        ending = (key_ref[rows, :].astype(F32) * jnp.exp(total - within)).astype(BF16)
        for h, (ks, vs) in enumerate(zip(heads_of(HK), heads_of(HV))):
            update = tn(value_ref[rows, vs], ending[:, ks])
            update_ref[c, h] = update.astype(BF16)
            final_ref[h] = final_ref[h] * jnp.exp(total[:, ks]) + update
            logs_ref[h] = logs_ref[h] + total[:, ks]


def project_kernel(tokens, gains, weights, up, *refs):
    outs, (final_ref, logs_ref) = refs[:9], refs[9:]

    @pl.when(pl.program_id(0) == 0)
    def _():
        final_ref[...] = jnp.zeros_like(final_ref)
        logs_ref[...] = jnp.zeros_like(logs_ref)

    project_rows(
        tokens, gains[0:1], lambda first, width: weights[:, first : first + width], up[...], outs, final_ref, logs_ref
    )


def mix_rows(tokens, query, key, value, gate, within_all, update, state, head_gain, out_weight, ffn_gain, outs):
    mixed_ref, gated_ref, hidden_ref, ffn_ref, starts_ref = outs
    mask = causal_mask(CHUNK)
    for c in range(ROWS // CHUNK):
        rows = pl.ds(c * CHUNK, CHUNK)
        within = within_all[rows, :]
        middle = within[CHUNK // 2 - 1 : CHUNK // 2]
        total = within[CHUNK - 1 : CHUNK]
        scaled = query[rows, :].astype(F32) * HK**-0.5
        from_start = (scaled * jnp.exp(within)).astype(BF16)
        left = halves(scaled * jnp.exp(within - middle))
        right = halves(key[rows, :].astype(F32) * jnp.exp(middle - within))
        for h, (ks, vs) in enumerate(zip(heads_of(HK), heads_of(HV))):
            start = state[h].astype(BF16)
            starts_ref[c, h] = start
            scores = jnp.where(mask, fine_nt([p[:, ks] for p in left], [p[:, ks] for p in right]), 0.0).astype(BF16)
            mixed = nn(scores, value[rows, vs]) + nt(from_start[:, ks], start)
            state[h] = state[h] * jnp.exp(total[:, ks]) + update[c, h].astype(F32)
            mixed_ref[rows, vs] = mixed
            gates = gate[rows, vs].astype(F32)
            gated = mixed * inverse_rms(mixed) * head_gain[:, vs] * (gates * sigmoid(gates))
            gated_ref[rows, vs] = gated.astype(BF16)
    hidden = tokens[...].astype(F32) + nn(gated_ref[...], out_weight)
    hidden_ref[...] = hidden
    ffn_in = hidden * inverse_rms(hidden) * ffn_gain
    ffn_ref[...] = ffn_in.astype(BF16)
    return ffn_in


def mix_kernel(tokens, query, key, value, gate, within_all, update, entering_ref, gains, out_weight, *refs):
    outs, state = refs[:5], refs[5]

    @pl.when(pl.program_id(0) == 0)
    def _():
        state[...] = entering_ref[...]

    mix_rows(
        tokens, query, key, value, gate, within_all, update, state, gains[1:2], out_weight[...], gains[2:3], outs
    )


def ffn_kernel(
    ffn_in, ffn_in_t, cotangent, hidden, gate_weight, up_weight, down_weight,
    out_ref, back_ref, gate_grad, up_grad, down_grad,
):
    @pl.when(pl.program_id(0) == 0)
    def _():
        out_ref[...] = hidden[...]
        back_ref[...] = jnp.zeros_like(back_ref)

    gate, up = nn(ffn_in[...], gate_weight[...]), nn(ffn_in[...], up_weight[...])
    back = nt(cotangent[...], down_weight[...])
    share = sigmoid(gate)
    passed = gate * share
    inner = (passed * up).astype(BF16)
    d_up = (back * passed).astype(BF16)
    d_gate = (back * up * (share * (1.0 + gate * (1.0 - share)))).astype(BF16)
    out_ref[...] += nn(inner, down_weight[...])
    back_ref[...] += nt(d_gate, gate_weight[...]) + nt(d_up, up_weight[...])
    gate_grad[...] = nn(ffn_in_t[...], d_gate).astype(BF16)
    up_grad[...] = nn(ffn_in_t[...], d_up).astype(BF16)
    down_grad[...] = tn(inner, cotangent[...]).astype(BF16)


def norm_back(values, gain, grad):
    scale = inverse_rms(values)
    inner = grad * gain
    along = jnp.mean(inner * values, axis=-1, keepdims=True)
    return scale * inner - values * (scale * scale * scale * along), grad * values * scale


def unmix_kernel(
    ffn_back, hidden, cotangent, gate, mixed, query, within_all, gains, out_weight,
    d_hidden_ref, low_ref, d_gate_ref, d_mixed_ref, update_ref, enters_ref, ffn_gain_ref, head_gain_ref,
):
    @pl.when(pl.program_id(0) == 0)
    def _():
        enters_ref[...] = jnp.zeros_like(enters_ref)
        ffn_gain_ref[...] = jnp.zeros_like(ffn_gain_ref)
        head_gain_ref[...] = jnp.zeros_like(head_gain_ref)

    through, terms = norm_back(hidden[...], gains[2:3], ffn_back[...])
    ffn_gain_ref[...] += jnp.sum(terms, axis=0, keepdims=True)
    d_hidden = cotangent[...].astype(F32) + through
    d_hidden_ref[...] = d_hidden
    low = d_hidden.astype(BF16)
    low_ref[...] = low
    d_gated = nt(low, out_weight[...])
    for vs in heads_of(HV):
        value = mixed[:, vs]
        scale = inverse_rms(value)
        headed = value * scale
        gates = gate[:, vs].astype(F32)
        share = sigmoid(gates)
        passed = gates * share
        grad, gain = d_gated[:, vs], gains[1:2, vs]
        head_gain_ref[:, vs] += jnp.sum(grad * headed * passed, axis=0, keepdims=True)
        d_gate_ref[:, vs] = (grad * headed * gain * (share * (1.0 + gates * (1.0 - share)))).astype(BF16)
        d_headed = grad * gain * passed
        along = jnp.mean(d_headed * headed, axis=-1, keepdims=True)
        d_mixed_ref[:, vs] = scale * (d_headed - headed * along)
    for c in reversed(range(ROWS // CHUNK)):
        rows = slice(c * CHUNK, (c + 1) * CHUNK)
        within = within_all[rows]
        total = within[CHUNK - 1 : CHUNK]
        from_start = (query[rows].astype(F32) * HK**-0.5 * jnp.exp(within)).astype(BF16)
        for h, (ks, vs) in enumerate(zip(heads_of(HK), heads_of(HV))):
            update = tn(d_mixed_ref[rows, vs].astype(BF16), from_start[:, ks])
            update_ref[c, h] = update.astype(BF16)
            enters_ref[h] = enters_ref[h] * jnp.exp(total[:, ks]) + update


def back_rows(
    tokens, query, key, value, logit, within_all, d_mixed, starts, update, d_gate, d_hidden, gains, weights, up,
    d_proj_ref, d_logit_ref, tokens_grad_ref, gain_ref, state,
):
    mask = causal_mask(CHUNK)
    upper = triangle(True)
    keys = HEADS * HK
    for c in reversed(range(ROWS // CHUNK)):
        rows = slice(c * CHUNK, (c + 1) * CHUNK)
        within = within_all[rows]
        middle = within[CHUNK // 2 - 1 : CHUNK // 2]
        total = within[CHUNK - 1 : CHUNK]
        factor = jnp.exp(total)
        queries, keys_f = query[rows].astype(F32), key[rows].astype(F32)
        q_start, q_middle = jnp.exp(within) * HK**-0.5, jnp.exp(within - middle) * HK**-0.5
        k_middle, k_end = jnp.exp(middle - within), jnp.exp(total - within)
        lefts, rights = halves(queries * q_middle), halves(keys_f * k_middle)
        left, right = lefts[0], rights[0]
        ending = (keys_f * k_end).astype(BF16)
        moves, extras = [], []
        for h, (ks, vs) in enumerate(zip(heads_of(HK), heads_of(HV))):
            start, after = starts[c, h], state[h].astype(BF16)
            (grad, rest), values = halves(d_mixed[rows, vs]), value[rows, vs]
            scores = jnp.where(mask, fine_nt([p[:, ks] for p in lefts], [p[:, ks] for p in rights]), 0.0).astype(BF16)
            d_scores = jnp.where(mask, nt(grad, values) + nt(rest, values), 0.0).astype(BF16)
            d_value = tn(scores, grad) + nt(ending[:, ks], after)
            d_query = nn(d_scores, right[:, ks]) * q_middle[:, ks] + nn(grad, start) * q_start[:, ks]
            d_end = nn(values, after) * k_end[:, ks]
            d_key = tn(d_scores, left[:, ks]) * k_middle[:, ks] + d_end
            d_proj_ref[rows, ks] = d_query.astype(BF16)
            d_proj_ref[rows, slice(keys + ks.start, keys + ks.stop)] = d_key.astype(BF16)
            d_proj_ref[rows, slice(2 * keys + vs.start, 2 * keys + vs.stop)] = d_value.astype(BF16)
            moves.append(queries[:, ks] * d_query - keys_f[:, ks] * d_key)
            extras.append(
                jnp.sum(keys_f[:, ks] * d_end, axis=0, keepdims=True)
                + factor[:, ks] * jnp.sum(start.astype(F32) * state[h], axis=0, keepdims=True)
            )
            state[h] = state[h] * factor[:, ks] + update[c, h].astype(F32)
        d_decay = running(upper, jnp.concatenate(moves, axis=1)) + jnp.concatenate(extras, axis=1)
        d_logit = d_decay * sigmoid(-logit[rows]) * (1.0 / 16.0)
        d_logit_ref[rows] = d_logit.astype(BF16)
    d_mid = nn(d_logit_ref[...], up[...])
    d_mid = jnp.where(lax.broadcasted_iota(jnp.int32, d_mid.shape, 1) < RANK, d_mid, 0.0).astype(BF16)
    inner = 2 * keys + HEADS * HV
    outer = inner + HEADS * HV
    d_proj_ref[:, inner:outer] = d_gate[...]
    d_proj_ref[:, outer:] = d_mid
    d_normed = nt(d_proj_ref[...], weights[...])
    through, terms = norm_back(tokens[...].astype(F32), gains[0:1], d_normed)
    gain_ref[...] += jnp.sum(terms, axis=0, keepdims=True)
    tokens_grad_ref[...] = d_hidden[...] + through


def back_kernel(*refs):
    tiles, leaving_ref, refs = refs[:11], refs[11], refs[12:]
    gain_ref, state = refs[-2:]

    @pl.when(pl.program_id(0) == 0)
    def _():
        state[...] = leaving_ref[...]
        gain_ref[...] = jnp.zeros_like(gain_ref)

    back_rows(*tiles, *refs)


def tail_kernel(sizes, steps, count, *refs):
    tiles, (enters, logs), refs = refs[:11], refs[11:13], refs[13:]
    kept, partials, refs = refs[:3], refs[3 : 3 + count], refs[3 + count :]
    outs, gain_ref, sums, refs = refs[:3], refs[3], refs[4 : 4 + count], refs[4 + count :]
    state, load, send, recv = refs[:4]
    scratch, scan = refs[4 : 4 + 5 * len(TAIL_PARTS)], refs[4 + 5 * len(TAIL_PARTS) :]
    place = Place(sizes)
    step = pl.program_id(0)
    scatters = []
    for k, (which, columns, order) in enumerate(TAIL_PARTS):
        held, *bufs = scratch[5 * k : 5 * k + 5]
        scatters.append(
            Scatter(place, k, order, partials[which], columns, held, bufs, sums[which], load, send, recv)
        )
    moves = [s.steps() for s in scatters]

    def turn():
        for move in moves:
            next(move, None)

    def during(hop):
        for _ in range(TAIL_TURNS[0].count(hop)):
            turn()

    @pl.when(step == 0)
    def _():
        gain_ref[...] = jnp.zeros_like(gain_ref)
        place.greet(partners_of(sizes))
        turn()
        scan_states(place, True, during, enters, logs, state, *scan)

    for k in range(1, steps + 1):

        @pl.when(step == k)
        def _(k=k):
            for _ in range(TAIL_TURNS[1].count(k)):
                turn()

    @pl.when(step > 0)
    def _():
        back_rows(*tiles, *kept, *outs, gain_ref, state)

    @pl.when(step == steps)
    def _():
        run_all(moves)
        for s in scatters:
            s.drain()


def rows_spec(width, steps, backward):
    return pl.BlockSpec((ROWS, width), (lambda i: (steps - 1 - i, 0)) if backward else (lambda i: (i, 0)))


def chunks_spec(steps, backward):
    return pl.BlockSpec(
        (ROWS // CHUNK, HEADS, HV, HK),
        (lambda i: (steps - 1 - i, 0, 0, 0)) if backward else (lambda i: (i, 0, 0, 0)),
    )


def kept_spec(shape):
    return pl.BlockSpec(shape, lambda i: (0,) * len(shape), pipeline_mode=pl.Buffered(1))


def kept_out(shape):
    return pl.BlockSpec(shape, lambda i: (0,) * len(shape))


PARAMS = dict(vmem_limit_bytes=60 << 20)
STATE = (HEADS, HV, HK)


def project(tokens, gains, weights, up):
    length, width = tokens.shape
    steps, keys, values = length // ROWS, HEADS * HK, HEADS * HV
    row = lambda w: rows_spec(w, steps, False)
    chunks = (length // CHUNK,) + STATE
    shape = jax.ShapeDtypeStruct
    return pl.pallas_call(
        project_kernel,
        grid=(steps,),
        in_specs=[row(width)] + [kept_spec(a.shape) for a in (gains, weights, up)],
        out_specs=[row(w) for w in (width, keys, keys, values, values, 128, keys, keys)]
        + [chunks_spec(steps, False), kept_out(STATE), kept_out((HEADS, 8, HK))],
        out_shape=[shape((length, w), BF16) for w in (width, keys, keys, values, values, 128)]
        + [shape((length, keys), F32)] * 2
        + [shape(chunks, BF16), shape(STATE, F32), shape((HEADS, 8, HK), F32)],
        compiler_params=pltpu.CompilerParams(**PARAMS),
    )(tokens, gains, weights, up)


def mix(tokens, query, key, value, gate, within, update, entered, gains, out_weight):
    length, width = tokens.shape
    steps, keys, values = length // ROWS, HEADS * HK, HEADS * HV
    row = lambda w: rows_spec(w, steps, False)
    shape = jax.ShapeDtypeStruct
    return pl.pallas_call(
        mix_kernel,
        grid=(steps,),
        in_specs=[row(w) for w in (width, keys, keys, values, values, keys)]
        + [chunks_spec(steps, False)]
        + [kept_spec(a.shape) for a in (entered, gains, out_weight)],
        out_specs=[row(w) for w in (values, values, width, width)] + [chunks_spec(steps, False)],
        out_shape=[
            shape((length, values), F32), shape((length, values), BF16),
            shape((length, width), F32), shape((length, width), BF16), shape(update.shape, BF16),
        ],
        scratch_shapes=[pltpu.VMEM(STATE, F32)],
        compiler_params=pltpu.CompilerParams(**PARAMS),
    )(tokens, query, key, value, gate, within, update, entered, gains, out_weight)


FRONT_PARTS = (
    (0, (0, 128), ORDERS[0]),
    (1, (0, 1024), ORDERS[0]),
    (1, (1024, 1024), ORDERS[1]),
    (1, (2048, 1152), ORDERS[2]),
    (2, (0, 1024), ORDERS[3]),
    (3, (0, 2816), ORDERS[0]),
    (4, (0, 2816), ORDERS[1]),
    (5, (0, 512), ORDERS[2]),
    (5, (512, 512), ORDERS[3]),
)
FIRST_PARTS = 5
FRONT_TURNS = (1, 2, (2,), 1)


def front_kernel(sizes, steps, *refs):
    tokens, shards, refs = refs[0], refs[1:7], refs[7:]
    buffers, refs = refs[:6], refs[6:]
    outs, mixed_outs, (logs_out, gains_out, ffn_t_ref), refs = refs[:8], refs[8:13], refs[13:16], refs[16:]
    up_all, proj_all, out_all, query, key, value, gate, within, update, state, final, logs, gains, refs = *refs[:13], refs[13:]
    send, recv, own, flush = refs[:4]
    scan = refs[4:]
    place = Place(sizes)
    step = pl.program_id(0)
    here = tuple(place.here)
    held = (up_all, proj_all, out_all) + tuple(buffers[3:])
    gathers = [
        Gather(place, k, order, held[which], columns, send, recv)
        for k, (which, columns, order) in enumerate(FRONT_PARTS)
    ]
    owned = [pltpu.make_async_copy(shards[k], buffers[k].at[here], own.at[k]) for k in (3, 4, 5)]
    flushes = [pltpu.make_async_copy(held[k], buffers[k], flush.at[k]) for k in range(3)]
    later = [g.steps() for g in gathers[FIRST_PARTS:]]

    def turn():
        for g in later:
            next(g, None)

    def during(hop):
        if hop in FRONT_TURNS[2]:
            turn()

    @pl.when(step == 0)
    def _():
        for copy in owned:
            copy.start()
        for k in range(3):
            held[k][here] = shards[k][...]
        place.greet(partners_of(sizes))
        for copy in owned:
            copy.wait()
        run_all([g.steps() for g in gathers[:FIRST_PARTS]])
        turn()
        flushes[0].start()
        flushes[1].start()
        flushes[2].start()
        extra = 2 * HEADS * (HK + HV)
        gains[...] = small_rows(proj_all[..., pl.ds(extra, 128)].reshape(-1, 128))
        gains_out[...] = gains[...]
        final[...] = jnp.zeros_like(final)
        logs[...] = jnp.zeros_like(logs)
        for _ in range(FRONT_TURNS[0]):
            turn()

    @pl.when(step < steps)
    def _():
        rows = pl.ds(pl.multiple_of(step * ROWS, ROWS), ROWS)
        chunks = pl.ds(step * (ROWS // CHUNK), ROWS // CHUNK)
        normed_ref, query_ref, key_ref, value_ref, gate_ref, mid_ref, logit_ref, within_ref = outs
        kept = (query, key, value, gate, within)
        tiles = (query_ref, key_ref, value_ref, gate_ref, within_ref)
        project_rows(
            tokens, gains[0:1],
            lambda first, width: proj_all[..., pl.ds(first, width)].reshape(-1, width),
            up_all[...].reshape(-1, 128),
            (normed_ref, query_ref, key_ref, value_ref, gate_ref, mid_ref, logit_ref, within_ref, update.at[chunks]),
            final, logs,
        )
        for whole, tile in zip(kept, tiles):
            whole[rows, :] = tile[...]

    @pl.when(step == steps)
    def _():
        for _ in range(FRONT_TURNS[1]):
            turn()
        logs_out[...] = logs[...]
        scan_states(place, False, during, final, logs, state, *scan)
        for _ in range(FRONT_TURNS[3]):
            turn()

    @pl.when(step >= steps)
    def _():
        at = step - steps
        rows = pl.ds(pl.multiple_of(at * ROWS, ROWS), ROWS)
        chunks = pl.ds(at * (ROWS // CHUNK), ROWS // CHUNK)
        ffn_in = mix_rows(
            tokens, query.at[rows], key.at[rows], value.at[rows], gate.at[rows], within.at[rows], update.at[chunks], state,
            gains[1:2], out_all[...].reshape(-1, out_all.shape[-1]), gains[2:3], mixed_outs,
        )
        ffn_t_ref[...] = ffn_in.T.astype(BF16)

    @pl.when(step == 2 * steps - 1)
    def _():
        run_all(later)
        for g in gathers:
            g.drain()
        for copy in flushes:
            copy.wait()


def front(tokens, shards, sizes, collective_id):
    length, width = tokens.shape
    steps, keys, values = length // ROWS, HEADS * HK, HEADS * HV
    shape, chunks = jax.ShapeDtypeStruct, (length // CHUNK,) + STATE
    first = lambda w: pl.BlockSpec((ROWS, w), lambda i: (jnp.minimum(i, steps - 1), 0))
    second = lambda w: pl.BlockSpec((ROWS, w), lambda i: (jnp.maximum(i - steps, 0), 0))
    lanes = lanes_of(sizes)
    parts = len(FRONT_PARTS)
    one = lambda w, t: ((length, w), t)
    turned = lambda first: pl.BlockSpec((width, ROWS), lambda i: (0, jnp.minimum(i, steps - 1) if first else jnp.maximum(i - steps, 0)))
    results = [one(keys, BF16), one(keys, BF16), one(values, BF16), one(values, BF16), one(128, BF16), one(keys, F32), one(keys, F32)]
    mixes = [one(values, F32), one(values, BF16), one(width, F32), one(width, BF16)]
    out = pl.pallas_call(
        functools.partial(front_kernel, sizes, steps),
        grid=(2 * steps,),
        in_specs=[pl.BlockSpec((ROWS, width), lambda i: (lax.rem(i, steps), 0))] + [kept_spec(s.shape) for s in shards],
        out_specs=[pl.BlockSpec(memory_space=pl.ANY)] * len(shards)
        + [turned(True)] + [first(s[1]) for s, _ in results]
        + [second(s[1]) for s, _ in mixes]
        + [pl.BlockSpec((ROWS // CHUNK,) + STATE, lambda i: (jnp.maximum(i - steps, 0), 0, 0, 0))]
        + [kept_out((HEADS, 8, HK)), kept_out((8, width)), turned(False)],
        out_shape=[shape(sizes + s.shape, s.dtype) for s in shards]
        + [shape((width, length), BF16)]
        + [shape(s, t) for s, t in results + mixes]
        + [shape(chunks, BF16), shape((HEADS, 8, HK), F32), shape((8, width), F32), shape((width, length), BF16)],
        scratch_shapes=[pltpu.VMEM(sizes + s.shape, s.dtype) for s in shards[:3]]
        + [pltpu.VMEM((length, w), t) for w, t in ((keys, BF16), (keys, BF16), (values, BF16), (values, BF16), (keys, F32))]
        + [pltpu.VMEM(chunks, BF16), pltpu.VMEM(STATE, F32), pltpu.VMEM(STATE, F32), pltpu.VMEM((HEADS, 8, HK), F32), pltpu.VMEM((8, width), F32)]
        + [
            pltpu.SemaphoreType.DMA((parts, 4, sizes[0], lanes, 2)),
            pltpu.SemaphoreType.DMA((parts, 4, sizes[0], lanes)),
            pltpu.SemaphoreType.DMA((len(shards),)),
            pltpu.SemaphoreType.DMA((3,)),
        ]
        + scan_scratch(sizes),
        compiler_params=pltpu.CompilerParams(collective_id=collective_id, has_side_effects=True, **PARAMS),
    )(tokens, *shards)
    weights = [o.reshape(-1, o.shape[-1]) for o in out[: len(shards)]]
    return weights, out[len(shards) :]


def feed_forward(ffn_in, ffn_t, cotangent, hidden, gate_weight, up_weight, down_weight):
    length, width = ffn_in.shape
    inner = gate_weight.shape[1]
    whole = [ffn_in, ffn_t, cotangent, hidden]
    wide = pl.BlockSpec((width, FTILE), lambda i: (0, i))
    tall = pl.BlockSpec((FTILE, width), lambda i: (i, 0))
    shape = jax.ShapeDtypeStruct
    return pl.pallas_call(
        ffn_kernel,
        grid=(inner // FTILE,),
        in_specs=[kept_spec(a.shape) for a in whole] + [wide, wide, tall],
        out_specs=[kept_out((length, width))] * 2 + [wide, wide, tall],
        out_shape=[shape((length, width), F32)] * 2
        + [shape((width, inner), BF16)] * 2 + [shape((inner, width), BF16)],
        compiler_params=pltpu.CompilerParams(**PARAMS),
    )(*whole, gate_weight, up_weight, down_weight)


def unmix(ffn_back, hidden, cotangent, gate, mixed, query, within, gains, out_weight):
    length, width = hidden.shape
    steps, keys, values = length // ROWS, HEADS * HK, HEADS * HV
    row = lambda w: rows_spec(w, steps, True)
    chunks = (length // CHUNK,) + STATE
    shape = jax.ShapeDtypeStruct
    return pl.pallas_call(
        unmix_kernel,
        grid=(steps,),
        in_specs=[row(w) for w in (width, width, width, values, values, keys, keys)]
        + [kept_spec(a.shape) for a in (gains, out_weight)],
        out_specs=[row(w) for w in (width, width, values, values)]
        + [chunks_spec(steps, True), kept_out(STATE), kept_out((1, width)), kept_out((1, values))],
        out_shape=[
            shape((length, width), F32), shape((length, width), BF16), shape((length, values), BF16),
            shape((length, values), F32), shape(chunks, BF16), shape(STATE, F32),
            shape((1, width), F32), shape((1, values), F32),
        ],
        compiler_params=pltpu.CompilerParams(**PARAMS),
    )(ffn_back, hidden, cotangent, gate, mixed, query, within, gains, out_weight)


def back(tiles, leaving, gains, weights, up):
    length, width = tiles[0].shape
    steps, keys, values = length // ROWS, HEADS * HK, HEADS * HV
    row = lambda w: rows_spec(w, steps, True)
    shape = jax.ShapeDtypeStruct
    return pl.pallas_call(
        back_kernel,
        grid=(steps,),
        in_specs=[row(w) for w in (width, keys, keys, values, keys, keys, values)]
        + [chunks_spec(steps, True)] * 2 + [row(values), row(width)]
        + [kept_spec(a.shape) for a in (leaving, gains, weights, up)],
        out_specs=[row(w) for w in (weights.shape[1], keys, width)] + [kept_out((1, width))],
        out_shape=[
            shape((length, weights.shape[1]), BF16), shape((length, keys), BF16),
            shape((length, width), F32), shape((1, width), F32),
        ],
        scratch_shapes=[pltpu.VMEM(STATE, F32)],
        compiler_params=pltpu.CompilerParams(**PARAMS),
    )(*tiles, leaving, gains, weights, up)


TAIL_PARTS = (
    (2, (0, 512), (0, 2, 1)),
    (3, (0, 1024), (0, 1, 2)),
    (0, (0, 2816), (1, 2, 0)),
    (1, (0, 2816), (2, 1, 0)),
    (2, (512, 512), (1, 2, 0)),
)
TAIL_TURNS = ((3, 5), (1, 2, 3, 4))
LAST_PARTS = (
    (0, (0, 128), ORDERS[0][::-1]),
    (1, (0, 1024), ORDERS[0][::-1]),
    (1, (1024, 1024), ORDERS[1][::-1]),
    (1, (2048, 640), ORDERS[2][::-1]),
    (1, (2688, 512), ORDERS[3][::-1]),
)


def tail(tiles, enters, logs, gains, weights, up, partials, sizes, collective_id):
    length, width = tiles[0].shape
    steps, keys, values = length // ROWS, HEADS * HK, HEADS * HV
    shape, at = jax.ShapeDtypeStruct, lambda i: steps - jnp.maximum(i, 1)
    row = lambda w: pl.BlockSpec((ROWS, w), lambda i: (at(i), 0))
    chunk = pl.BlockSpec((ROWS // CHUNK,) + STATE, lambda i: (at(i), 0, 0, 0))
    count = len(partials)
    devices = sizes[0] * sizes[1] * sizes[2] * sizes[3]
    partials = [p.reshape(sizes + (p.shape[0] // devices, p.shape[1])) for p in partials]
    lanes = max([1] + [size + 1 for size in sizes[1:] if size > 2])
    sems = (len(TAIL_PARTS), 4, sizes[0] + 1, lanes)
    out = pl.pallas_call(
        functools.partial(tail_kernel, sizes, steps, count),
        grid=(steps + 1,),
        in_specs=[row(w) for w in (width, keys, keys, values, keys, keys, values)]
        + [chunk] * 2 + [row(values), row(width)]
        + [kept_spec(a.shape) for a in (enters, logs, gains, weights, up)]
        + [pl.BlockSpec(memory_space=pl.ANY)] * count,
        out_specs=[row(w) for w in (weights.shape[1], keys, width)] + [kept_out((1, width))]
        + [kept_out(p.shape[4:]) for p in partials],
        out_shape=[
            shape((length, weights.shape[1]), BF16), shape((length, keys), BF16),
            shape((length, width), F32), shape((1, width), F32),
        ] + [shape(p.shape[4:], F32) for p in partials],
        scratch_shapes=[
            pltpu.VMEM(STATE, F32),
            pltpu.SemaphoreType.DMA((len(TAIL_PARTS), sizes[0])),
            pltpu.SemaphoreType.DMA(sems),
            pltpu.SemaphoreType.DMA(sems),
        ]
        + scatter_scratch(sizes, TAIL_PARTS, [p.shape for p in partials], BF16)
        + scan_scratch(sizes),
        compiler_params=pltpu.CompilerParams(collective_id=collective_id, has_side_effects=True, **PARAMS),
    )(*tiles, enters, logs, gains, weights, up, *partials)
    return out[:4], out[4:]


def last_kernel(sizes, *refs):
    normed_t, d_proj, small, small_out, proj_out, load, send, recv = refs[:8]
    scratch = refs[8 : 8 + 5 * len(LAST_PARTS)]
    partials = [small] + list(refs[8 + 5 * len(LAST_PARTS) :])
    place = Place(sizes)
    place.greet()
    moves, scatters = [], []
    for k, (which, (first, width), order) in enumerate(LAST_PARTS):
        for move in moves:
            next(move, None)
        out = small_out
        if which:
            out = proj_out.at[:, pl.ds(first, width)]
            for at in range(0, width, 512):
                tile = min(512, width - at)
                grad = nn(normed_t[...], d_proj[:, first + at : first + at + tile]).astype(BF16)
                partials[k][..., pl.ds(at, tile)] = grad.reshape(partials[k].shape[:-1] + (tile,))
        held, *bufs = scratch[5 * k : 5 * k + 5]
        scatters.append(Scatter(place, k, order, partials[k], (0, width), held, bufs, out, load, send, recv))
        moves.append(scatters[-1].steps())
        next(moves[-1])
    run_all(moves)
    for s in scatters:
        s.drain()


def project_grads(normed_t, d_proj, small, sizes, collective_id):
    devices = sizes[0] * sizes[1] * sizes[2] * sizes[3]
    small = small.reshape(sizes + (small.shape[0] // devices, small.shape[1]))
    rows = d_proj.shape[1], normed_t.shape[0] // devices
    shapes = [small.shape, sizes + (rows[1], rows[0])]
    lanes = max([1] + [size + 1 for size in sizes[1:] if size > 2])
    sems = (len(LAST_PARTS), 4, sizes[0] + 1, lanes)
    vmem = pl.BlockSpec(memory_space=pltpu.VMEM)
    return pl.pallas_call(
        functools.partial(last_kernel, sizes),
        out_shape=[jax.ShapeDtypeStruct(s[4:], F32) for s in shapes],
        in_specs=[vmem, vmem, pl.BlockSpec(memory_space=pl.ANY)],
        out_specs=[vmem] * 2,
        scratch_shapes=[
            pltpu.SemaphoreType.DMA((len(LAST_PARTS), sizes[0])),
            pltpu.SemaphoreType.DMA(sems),
            pltpu.SemaphoreType.DMA(sems),
        ]
        + scatter_scratch(sizes, LAST_PARTS, shapes, BF16)
        + [pltpu.VMEM(shapes[1][:-1] + (width,), BF16) for which, (_, width), _ in LAST_PARTS if which],
        compiler_params=pltpu.CompilerParams(collective_id=collective_id, has_side_effects=True, **PARAMS),
    )(normed_t, d_proj, small)


def beside(pieces):
    rows, used = pieces[0].shape[0], sum(p.shape[1] for p in pieces)
    return jnp.concatenate(pieces + [jnp.zeros((rows, 128 - used), pieces[0].dtype)], axis=1)


def local(
    tokens,
    norm_gain,
    query_weight,
    key_weight,
    value_weight,
    gate_weight,
    rank_down,
    rank_up,
    gate_bias,
    head_gain,
    out_weight,
    ffn_gain,
    ffn_gate,
    ffn_up,
    ffn_down,
    cotangent,
):
    sizes = grid_of(lax.axis_size("seq"))
    extra = beside([rank_down] + [g[:, None] for g in (norm_gain, head_gain, ffn_gain)])
    projections = jnp.concatenate([query_weight, key_weight, value_weight, gate_weight, extra], axis=1)
    shards = [beside([rank_up.T, gate_bias[:, None]]), projections, out_weight, ffn_gate, ffn_up, ffn_down]
    if rank_up.shape[1] % 16 == 0:
        weights, kept = front(tokens, shards, sizes, 0)
        up, proj, out, full_fgate, full_fup, full_fdown = weights
        normed_t, query, key, value, gate, mid, logit, within, mixed, gated, hidden, ffn_in, starts, logs, gains, ffn_t = kept
    else:
        up, proj, out, full_fgate, full_fup, full_fdown = gather_all(shards, FRONT_PARTS, sizes, 0)
        gains = jnp.pad(proj[:, -128 + RANK : -128 + RANK + 3].astype(F32).T, ((0, 5), (0, 0)))
        normed, query, key, value, gate, mid, logit, within, update, final, logs = project(tokens, gains, proj, up)
        incoming = entering(final, logs, sizes, False, 2)
        mixed, gated, hidden, ffn_in, starts = mix(
            tokens, query, key, value, gate, within, update, incoming, gains, out
        )
        normed_t, ffn_t = normed.T, ffn_in.T
    block_output, ffn_back, fgate_wgrad, fup_wgrad, fdown_wgrad = feed_forward(
        ffn_in, ffn_t, cotangent, hidden, full_fgate, full_fup, full_fdown
    )
    d_hidden, hidden_low, d_gate, d_mixed, back_update, enters, ffn_gain_grad, head_gain_grad = unmix(
        ffn_back, hidden, cotangent, gate, mixed, query, within, gains, out
    )
    out_wgrad = tn(gated, hidden_low).astype(BF16)
    early = [fgate_wgrad, fup_wgrad, fdown_wgrad, out_wgrad]
    tiles = (tokens, query, key, value, logit, within, d_mixed, starts, back_update, d_gate, d_hidden)
    if rank_up.shape[1] % 16 == 0:
        backs, early_sums = tail(tiles, enters, logs, gains, proj, up, early, sizes, 3)
    else:
        leaving = entering(enters, logs, sizes, True, 3)
        backs = back(tiles, leaving, gains, proj, up)
        early_sums = scatter_all(early, TAIL_PARTS, sizes, 4)
    d_proj, d_logit, tokens_grad, gain_grad = backs
    fgate_sum, fup_sum, fdown_sum, out_sum = early_sums
    keys_here = rank_up.shape[1]
    gain_grads = jnp.concatenate([gain_grad, head_gain_grad, ffn_gain_grad]).reshape(3, -1, norm_gain.shape[0] // keys_here, keys_here)
    gain_grads = gain_grads.transpose(1, 3, 0, 2).reshape(HEADS * HK, -1)
    up_wgrad = beside([tn(d_logit, mid)[:, : RANK + 1], gain_grads]).astype(BF16)
    if keys_here % 16 == 0:
        up_sum, proj_sum = project_grads(normed_t, d_proj, up_wgrad, sizes, 1)
    else:
        up_sum, proj_sum = scatter_all([up_wgrad, nn(normed_t, d_proj).astype(BF16)], LAST_PARTS, sizes, 1)
    keys, values = HEADS * HK, HEADS * HV
    last = 2 * (keys + values)
    gain_sum, head_sum, ffn_sum = (
        up_sum[:, RANK + 1 : RANK + 1 + 3 * (norm_gain.shape[0] // keys_here)].reshape(keys_here, 3, -1).transpose(1, 2, 0).reshape(3, -1)
    )
    return (
        block_output,
        tokens_grad,
        gain_sum,
        proj_sum[:, :keys],
        proj_sum[:, keys : 2 * keys],
        proj_sum[:, 2 * keys : 2 * keys + values],
        proj_sum[:, 2 * keys + values : last],
        proj_sum[:, last : last + RANK],
        up_sum[:, :RANK].T,
        up_sum[:, RANK],
        head_sum,
        out_sum,
        ffn_sum,
        fgate_sum,
        fup_sum,
        fdown_sum,
    )


def solution(mesh):
    return jax.shard_map(
        local,
        mesh=mesh,
        in_specs=(
            P("seq", None),
            P("seq"),
            P("seq", None),
            P("seq", None),
            P("seq", None),
            P("seq", None),
            P("seq", None),
            P(None, "seq"),
            P("seq"),
            P("seq"),
            P("seq", None),
            P("seq"),
            P("seq", None),
            P("seq", None),
            P("seq", None),
            P("seq", None),
        ),
        out_specs=(
            P("seq", None),
            P("seq", None),
            P("seq"),
            P("seq", None),
            P("seq", None),
            P("seq", None),
            P("seq", None),
            P("seq", None),
            P(None, "seq"),
            P("seq"),
            P("seq"),
            P("seq", None),
            P("seq"),
            P("seq", None),
            P("seq", None),
            P("seq", None),
        ),
        check_vma=False,
    )
```
